32 devices in a mesh: section: 2 (over core), seq: 4 (over z), head: 4 (over y, x).
Axes of the slice: x: 2, y: 2, z: 4, core: 2. Of those that a mesh axis runs over, the one named last changes fastest.
Arguments:
- tokens: bfloat16 [2, 1024, 2048], P(None, 'seq'), may hold values from -6 to 6
- cotangent: bfloat16 [2, 1024, 2048], P(None, 'seq'), may hold values from -6 to 6
- doc_starts: int32 [2, 8], replicated, may hold values from 0 to 1023, as said below
- valid_mask: int32 [2, 1024], P(None, 'seq'), may hold values 0 or 1
- gain_attn: bfloat16 [2, 2048], P('section', 'seq'), may hold values from 0.099609375 to 1.8984375
- w_query: bfloat16 [2, 2048, 2048], P('section', 'seq', 'head'), may hold values from -0.125 to 0.125
- w_key: bfloat16 [2, 2048, 2048], P('section', 'seq', 'head'), may hold values from -0.125 to 0.125
- w_value: bfloat16 [2, 2048, 4096], P('section', 'seq', 'head'), may hold values from -0.125 to 0.125
- w_gate_out: bfloat16 [2, 2048, 4096], P('section', 'seq', 'head'), may hold values from -0.125 to 0.125
- w_decay: bfloat16 [2, 2048, 16], P('section', 'seq', 'head'), may hold values from -0.125 to 0.125
- w_beta: bfloat16 [2, 2048, 16], P('section', 'seq', 'head'), may hold values from -0.125 to 0.125
- conv_query: bfloat16 [2, 4, 2048], P('section', None, 'head'), may hold values from -3 to 3
- conv_key: bfloat16 [2, 4, 2048], P('section', None, 'head'), may hold values from -3 to 3
- conv_value: bfloat16 [2, 4, 4096], P('section', None, 'head'), may hold values from -3 to 3
- decay_log: float32 [2, 16], P('section', 'head'), may hold values from -3 to 1.5
- decay_bias: float32 [2, 16], P('section', 'head'), may hold values from -7 to -3
- out_norm: bfloat16 [2, 256], P('section'), may hold values from 0.099609375 to 1.8984375
- w_output: bfloat16 [2, 4096, 2048], P('section', 'head', 'seq'), may hold values from -0.125 to 0.125
- gain_mlp: bfloat16 [2, 2048], P('section', 'seq'), may hold values from 0.099609375 to 1.8984375
- w_gate: bfloat16 [2, 2048, 5632], P('section', 'seq', 'head'), may hold values from -0.125 to 0.125
- w_up: bfloat16 [2, 2048, 5632], P('section', 'seq', 'head'), may hold values from -0.125 to 0.125
- w_down: bfloat16 [2, 5632, 2048], P('section', 'head', 'seq'), may hold values from -0.109375 to 0.109375
Outputs:
- activations: bfloat16 [2, 2, 1024, 2048], P('section', None, 'seq')
- input_grads: bfloat16 [2, 2, 1024, 2048], P('section', None, 'seq')
- branch_rms: float32 [2, 2, 3], P('section')
- grad_gain_attn: float32 [2, 2048], P('section', 'seq')
- grad_w_query: float32 [2, 2048, 2048], P('section', 'seq', 'head')
- grad_w_key: float32 [2, 2048, 2048], P('section', 'seq', 'head')
- grad_w_value: float32 [2, 2048, 4096], P('section', 'seq', 'head')
- grad_w_gate_out: float32 [2, 2048, 4096], P('section', 'seq', 'head')
- grad_w_decay: float32 [2, 2048, 16], P('section', 'seq', 'head')
- grad_w_beta: float32 [2, 2048, 16], P('section', 'seq', 'head')
- grad_conv_query: float32 [2, 4, 2048], P('section', None, 'head')
- grad_conv_key: float32 [2, 4, 2048], P('section', None, 'head')
- grad_conv_value: float32 [2, 4, 4096], P('section', None, 'head')
- grad_decay_log: float32 [2, 16], P('section', 'head')
- grad_decay_bias: float32 [2, 16], P('section', 'head')
- grad_out_norm: float32 [2, 256], P('section')
- grad_w_output: float32 [2, 4096, 2048], P('section', 'head', 'seq')
- grad_gain_mlp: float32 [2, 2048], P('section', 'seq')
- grad_w_gate: float32 [2, 2048, 5632], P('section', 'seq', 'head')
- grad_w_up: float32 [2, 2048, 5632], P('section', 'seq', 'head')
- grad_w_down: float32 [2, 5632, 2048], P('section', 'head', 'seq')
The draws below stay inside these ranges and needn't reach their ends.
Inputs may be any that keep to these rules, and one draw needn't show every extreme that they name: doc_starts[m] lists the first positions of the documents of micro-batch m in non-decreasing order; a repeated value adds no document; the first entry is 0; in one micro-batch all entries are 0, so one document spans all 1024 tokens; in each other micro-batch the last entry is 1023.
All inputs are finite; a program needn't handle non-finite values. No bound on the sum of `valid_mask` on one device may be relied on, other than what follows from the above.
Results may differ from the reference program's by a relative error of at most 0.04.
Values may be sent and summed in bfloat16 or wider, within the bound.
No kernel may reach another device: no remote copies, remote signals or barrier semaphores. Data moves between devices by JAX's collectives and lax.ppermute only.
A program may use at most 384 MiB of HBM per device.

```python
import jax
import jax.numpy as jnp
from jax import lax

D = 2048
H = 16
HEAD_K = 128
HEAD_V = 256
FF = 5632
CONVK = 4
BLOCK = 64
M = 2
DOCS = 8
HK = 2048
HV = 4096
TOKENS = 1024


def draw_doc_starts(key, part):
    key = jax.random.fold_in(key, 11)
    whole_key, place_key = jax.random.split(key)
    whole = jax.random.randint(whole_key, (), 0, M)
    inner = jax.random.randint(place_key, (M, DOCS - 1), 1, TOKENS)
    inner = jnp.sort(inner, axis=1)
    inner = inner.at[:, DOCS - 2].set(TOKENS - 1)
    inner = jnp.where((jnp.arange(M) == whole)[:, None], 0, inner)
    return jnp.concatenate([jnp.zeros((M, 1), jnp.int32), inner], axis=1).astype(jnp.int32)


def with_ends(values, key, smallest, top_value):
    dims = values.shape
    spot = [jax.random.randint(jax.random.fold_in(key, axis), (), 0, dims[axis]) for axis in range(len(dims))]
    values = values.at[tuple(spot)].set(smallest)
    longest = dims.index(max(dims))
    spot[longest] = (spot[longest] + 1) % dims[longest]
    return values.at[tuple(spot)].set(top_value)


def levels(rng, dims, shards, least, largest):
    gain, own = 1.0, jax.random.fold_in(rng, 6)
    for axis_at, shards_of in shards:
        heights = jnp.exp(jax.random.uniform(jax.random.fold_in(own, axis_at), (shards_of,), jnp.float32, least / len(shards), largest / len(shards)))
        gain = gain * jnp.repeat(heights, dims[axis_at] // shards_of).reshape([-1 if axis == axis_at else 1 for axis in range(len(dims))])
    return gain


def gaussian(key, extent, width, bound, pieces=(), kind=jnp.bfloat16):
    values = jax.random.normal(key, extent, jnp.float32) * width
    if len(pieces) > 0:
        values = levels(key, extent, pieces, -0.22, 0.18) * values
    return jnp.clip(values, min=-bound, max=bound).astype(kind)


def setup_inputs(seed: int = 0) -> dict:
    keys = jax.random.split(jax.random.key(seed), 23)
    tokens = gaussian(keys[0], (M, TOKENS, D), 1.0, 6.0, ((1, 4),))
    cotangent = gaussian(keys[1], (M, TOKENS, D), 1.0, 6.0, ((1, 4),))
    doc_starts = draw_doc_starts(jax.random.fold_in(keys[22], 71), 0)
    valid_mask = with_ends((jax.random.randint(keys[3], (M, TOKENS), 0, 4) < 3).astype(jnp.int32), jax.random.fold_in(keys[3], 1), 0, 1)
    gain_attn = jnp.clip(1.0 + 0.18 * jax.random.normal(keys[4], (2, D), jnp.float32), 0.099609375, 1.8984375).astype(jnp.bfloat16)
    w_query = gaussian(keys[5], (2, D, HK), D ** -0.5, 0.125, ((0, 2), (1, 4), (2, 4)))
    w_key = gaussian(keys[6], (2, D, HK), D ** -0.5, 0.125, ((0, 2), (1, 4), (2, 4)))
    w_value = gaussian(keys[7], (2, D, HV), D ** -0.5, 0.125, ((0, 2), (1, 4), (2, 4)))
    w_gate_out = gaussian(keys[8], (2, D, HV), D ** -0.5, 0.125, ((0, 2), (1, 4), (2, 4)))
    w_decay = gaussian(keys[9], (2, D, H), D ** -0.5, 0.125, ((0, 2), (1, 4), (2, 4)))
    w_beta = gaussian(keys[10], (2, D, H), D ** -0.5, 0.125, ((0, 2), (1, 4), (2, 4)))
    conv_query = gaussian(keys[11], (2, CONVK, HK), CONVK ** -0.5, 3.0, ((0, 2), (2, 4)))
    conv_key = gaussian(keys[12], (2, CONVK, HK), CONVK ** -0.5, 3.0, ((0, 2), (2, 4)))
    conv_value = gaussian(keys[13], (2, CONVK, HV), CONVK ** -0.5, 3.0, ((0, 2), (2, 4)))
    decay_log = jnp.clip(-3.0 + 4.5 * jax.random.uniform(keys[14], (2, H), jnp.float32) ** levels(keys[14], (2, H), ((0, 2), (1, 4)), -0.2, 0.2), -3.0, 1.5)
    decay_bias = jnp.clip(-7.0 + 4.0 * jax.random.uniform(keys[15], (2, H), jnp.float32) ** levels(keys[15], (2, H), ((0, 2), (1, 4)), -0.2, 0.2), -7.0, -3.0)
    out_norm = jnp.clip(1.0 + 0.18 * jax.random.normal(keys[16], (2, HEAD_V), jnp.float32), 0.099609375, 1.8984375).astype(jnp.bfloat16)
    w_output = gaussian(keys[17], (2, HV, D), (HV // 2) ** -0.5, 0.125, ((0, 2), (1, 4), (2, 4)))
    gain_mlp = jnp.clip(1.0 + 0.18 * jax.random.normal(keys[18], (2, D), jnp.float32), 0.099609375, 1.8984375).astype(jnp.bfloat16)
    w_gate = gaussian(keys[19], (2, D, FF), D ** -0.5, 0.125, ((0, 2), (1, 4), (2, 4)))
    w_up = gaussian(keys[20], (2, D, FF), D ** -0.5, 0.125, ((0, 2), (1, 4), (2, 4)))
    w_down = gaussian(keys[21], (2, FF, D), (FF // 2) ** -0.5, 0.109375, ((0, 2), (1, 4), (2, 4)))
    return {"tokens": tokens, "cotangent": cotangent, "doc_starts": doc_starts, "valid_mask": valid_mask, "gain_attn": gain_attn, "w_query": w_query, "w_key": w_key, "w_value": w_value, "w_gate_out": w_gate_out, "w_decay": w_decay, "w_beta": w_beta, "conv_query": conv_query, "conv_key": conv_key, "conv_value": conv_value, "decay_log": decay_log, "decay_bias": decay_bias, "out_norm": out_norm, "w_output": w_output, "gain_mlp": gain_mlp, "w_gate": w_gate, "w_up": w_up, "w_down": w_down}


epsilon = 1e-06
highest_precision = lax.Precision.HIGHEST

@jax.custom_vjp
def low(v):
    return lax.optimization_barrier(v.astype(jnp.bfloat16)).astype(jnp.float32)

@jax.custom_vjp
def low_back(v):
    return v

def low_keep(v):
    return (low(v), None)

def low_pass(kept, grad):
    return (grad,)

def back_keep(v):
    return (v, None)

def back_low(kept, grad):
    return (low(grad),)
low.defvjp(low_keep, low_pass)
low_back.defvjp(back_keep, back_low)

def matmul(left, right):
    return jnp.dot(left.astype(jnp.float32), right.astype(jnp.float32), precision=highest_precision, preferred_element_type=jnp.float32)

def rms_norm(values, weight):
    return values * lax.rsqrt(lax.optimization_barrier(jnp.mean(values * values, axis=-1, keepdims=True)) + epsilon) * weight

def doc_index(starts, positions):
    counted = lax.optimization_barrier(jnp.sum((starts.astype(jnp.int32)[None, :] <= positions.astype(jnp.int32)[:, None]).astype(jnp.int32), axis=1, dtype=jnp.int32))
    return (counted - 1).astype(jnp.int32)

def unit_rows(values):
    return values * lax.rsqrt(lax.optimization_barrier(jnp.sum(values * values, axis=-1, keepdims=True)) + epsilon)

def conv_front(extended, doc_ext, conv_weight):
    length = extended.shape[0] - (CONVK - 1)
    summed = jnp.zeros((length, extended.shape[1]), extended.dtype)
    for tap_index in range(CONVK):
        same_doc = doc_ext[tap_index:tap_index + length] == doc_ext[CONVK - 1:]
        summed = summed + jnp.where(same_doc[:, None], extended[tap_index:tap_index + length], 0.0) * conv_weight[tap_index]
    return jax.nn.silu(summed)

def heads_front(extended, doc_ext, mix_pre, conv_weight, decay_scale, decay_shift, head_count):
    activated = conv_front(extended, doc_ext, conv_weight)
    length = activated.shape[0]
    width_k = head_count * HEAD_K
    queries = unit_rows(activated[:, :width_k].reshape(length, head_count, HEAD_K)) * HEAD_K ** (-0.5)
    key_rows = unit_rows(activated[:, width_k:2 * width_k].reshape(length, head_count, HEAD_K))
    value_rows = activated[:, 2 * width_k:].reshape(length, head_count, HEAD_V)
    write_rate = jax.nn.sigmoid(mix_pre[:, head_count:])
    log_decay = -jnp.exp(decay_scale) * jax.nn.softplus(mix_pre[:, :head_count] + decay_shift)
    return (queries, key_rows, value_rows, write_rate, log_decay)

def block_terms(queries, key_rows, value_rows, write_rate, log_decay, doc_ids, prev_doc):
    length = queries.shape[1]
    cumulated = jnp.cumsum(log_decay, axis=1)
    row_iota = lax.broadcasted_iota(jnp.int32, (length, length), 0)
    col_iota = lax.broadcasted_iota(jnp.int32, (length, length), 1)
    same_doc = (doc_ids[:, :, None] == doc_ids[:, None, :]) & (col_iota <= row_iota)[None]
    same_mask = same_doc[:, :, :, None]
    exponent = jnp.where(same_mask, cumulated[:, :, None, :] - cumulated[:, None, :, :], 0.0)
    decay_full = jnp.where(same_mask, jnp.exp(exponent), 0.0)
    initial_decay = jnp.where((doc_ids == prev_doc[:, None])[:, :, None], jnp.exp(cumulated), 0.0)
    decay_heads = jnp.transpose(decay_full, (0, 3, 1, 2))
    key_gram = jnp.einsum('nthk,nihk->nhti', key_rows, key_rows, precision=highest_precision)
    strict_mask = (col_iota < row_iota)[None, None]
    lower_part = jnp.where(strict_mask, jnp.transpose(write_rate, (0, 2, 1))[:, :, :, None] * decay_heads * key_gram, 0.0)
    system = lower_part + jnp.eye(length, dtype=lower_part.dtype)
    scaled_values = jnp.transpose(write_rate[..., None] * value_rows, (0, 2, 1, 3))
    scaled_keys = jnp.transpose((write_rate * initial_decay)[..., None] * key_rows, (0, 2, 1, 3))
    resolved_values = lax.linalg.triangular_solve(system, scaled_values, left_side=True, lower=True, unit_diagonal=True)
    resolved_keys = lax.linalg.triangular_solve(system, scaled_keys, left_side=True, lower=True, unit_diagonal=True)
    query_key = jnp.einsum('nthk,nihk->nhti', queries, key_rows, precision=highest_precision) * decay_heads
    return (resolved_values, resolved_keys, query_key, decay_heads, initial_decay)

def gate_norm(mixed_out, gate_pre, norm_weight, head_count):
    length = mixed_out.shape[0]
    per_head = mixed_out.reshape(length, head_count, HEAD_V)
    gates = gate_pre.reshape(length, head_count, HEAD_V)
    normed = rms_norm(per_head, norm_weight) * jax.nn.silu(gates)
    return normed.reshape(length, head_count * HEAD_V)

def recurrence(queries, key_rows, value_rows, write_rate, log_decay, doc_ids):
    length, head_count = write_rate.shape
    blocks = length // BLOCK
    previous = jnp.concatenate([jnp.full((1,), -1, jnp.int32), doc_ids[:-1].astype(jnp.int32)])[::BLOCK]

    def as_blocks(values):
        return values.reshape((blocks, 1, BLOCK) + values.shape[1:])

    def step(running_state, item):
        block_query_rows, block_key_rows, block_v, block_w, block_g, block_d, block_p = item
        resolved_values, resolved_keys, query_key, decay_heads, initial_decay = block_terms(block_query_rows, block_key_rows, block_v, block_w, block_g, block_d, block_p)
        written_values = resolved_values - jnp.einsum('xrqs,rst->xrqt', resolved_keys, running_state, precision=highest_precision)
        direct_term = jnp.einsum('iawt,wts->iwas', block_query_rows, running_state, precision=highest_precision) * jnp.transpose(initial_decay, (0, 2, 1))[..., None]
        result = direct_term + jnp.einsum('nhti,nhiv->nhtv', query_key, written_values, precision=highest_precision)
        final_row = decay_heads[:, :, -1, :]
        updated_state = initial_decay[0, -1, :][:, None, None] * running_state + jnp.einsum('zab,zbaf,zabl->afl', final_row, block_key_rows, written_values, precision=highest_precision)
        return (updated_state, result[0])
    initial = jnp.zeros((head_count, HEAD_K, HEAD_V), queries.dtype)
    items = (as_blocks(queries), as_blocks(key_rows), as_blocks(value_rows), as_blocks(write_rate), as_blocks(log_decay), as_blocks(doc_ids.astype(jnp.int32)), previous[:, None])
    _, results = lax.scan(jax.checkpoint(step), initial, items)
    return jnp.transpose(results, (0, 2, 1, 3)).reshape(length, head_count * HEAD_V)

def layer(resid, weights, doc_ids):
    gain_attn, w_query, w_key, w_value, w_gate_out, w_decay, w_beta, conv_query, conv_key, conv_value, decay_log, decay_bias, out_norm, w_output, gain_mlp, w_gate, w_up, w_down = weights
    normed = low(rms_norm(resid, gain_attn))
    q_pre = low_back(matmul(normed, w_query))
    k_pre = low_back(matmul(normed, w_key))
    v_pre = low_back(matmul(normed, w_value))
    g_pre = low_back(matmul(normed, w_gate_out))
    mix_pre = matmul(normed, jnp.concatenate([w_decay, w_beta], axis=1))
    qkv_pre = jnp.concatenate([q_pre, k_pre, v_pre], axis=1)
    extended = jnp.pad(qkv_pre, ((CONVK - 1, 0), (0, 0)))
    doc_ext = jnp.concatenate([jnp.full((CONVK - 1,), -1, jnp.int32), doc_ids.astype(jnp.int32)])
    conv_weight = jnp.concatenate([conv_query, conv_key, conv_value], axis=1)
    queries, key_rows, value_rows, write_rate, log_decay = heads_front(extended, doc_ext, mix_pre, conv_weight, decay_log, decay_bias, H)
    mixed_out = recurrence(queries, key_rows, value_rows, write_rate, log_decay, doc_ids)
    gated = low(gate_norm(mixed_out, g_pre, out_norm, H))
    attn = low_back(matmul(gated, w_output))
    resid_mid = resid + attn
    ffn_in = low(rms_norm(resid_mid, gain_mlp))
    gate_act = low_back(matmul(ffn_in, w_gate))
    up_act = low_back(matmul(ffn_in, w_up))
    hidden = low(jax.nn.silu(gate_act) * up_act)
    ffn = low_back(matmul(hidden, w_down))
    return (resid_mid + ffn, attn, ffn)

def rms_stat(values, weights_valid):
    return jnp.sqrt(jnp.sum(weights_valid * lax.optimization_barrier(jnp.mean(values * values, axis=-1))) / jnp.maximum(jnp.sum(weights_valid), 1.0))

def reference(tokens, cotangent, doc_starts, valid_mask, gain_attn, w_query, w_key, w_value, w_gate_out, w_decay, w_beta, conv_query, conv_key, conv_value, decay_log, decay_bias, out_norm, w_output, gain_mlp, w_gate, w_up, w_down):
    params = [array.astype(jnp.float32) for array in (gain_attn, w_query, w_key, w_value, w_gate_out, w_decay, w_beta, conv_query, conv_key, conv_value, decay_log, decay_bias, out_norm, w_output, gain_mlp, w_gate, w_up, w_down)]
    positions = jnp.arange(TOKENS, dtype=jnp.int32)
    doc_all = [doc_index(doc_starts[micro_index], positions) for micro_index in range(M)]
    masks = valid_mask.astype(jnp.float32)
    cot_float = cotangent.astype(jnp.float32)
    inputs = tokens.astype(jnp.float32)
    shift_zero = jnp.zeros((M, TOKENS, D), jnp.float32)

    def forward(inputs_in, weights_in, shift_in):
        loss = jnp.zeros((), jnp.float32)
        records = []
        for micro_index in range(M):
            first_out, first_attn, first_ffn = layer(inputs_in[micro_index], [weight[0] for weight in weights_in], doc_all[micro_index])
            handed = low_back(low(first_out)) + shift_in[micro_index]
            second_out, second_attn, second_ffn = layer(handed, [weight[1] for weight in weights_in], doc_all[micro_index])
            loss = loss + jnp.sum(second_out * cot_float[micro_index] * masks[micro_index][:, None])
            records.append(((first_out, first_attn, first_ffn), (second_out, second_attn, second_ffn)))
        return (loss, records)
    loss, pullback, records = jax.vjp(forward, inputs, params, shift_zero, has_aux=True)
    grad_tokens, grad_params, grad_shift = pullback(jnp.ones_like(loss))
    activations = jnp.stack([jnp.stack([records[micro_index][layer_index][0] for micro_index in range(M)]) for layer_index in range(2)]).astype(jnp.bfloat16)
    input_grads = jnp.stack([grad_tokens, grad_shift]).astype(jnp.bfloat16)
    branch_rms = jnp.stack([jnp.stack([jnp.stack([rms_stat(values, masks[micro_index]) for values in records[micro_index][layer_index]]) for micro_index in range(M)]) for layer_index in range(2)])
    return (activations, input_grads, branch_rms, grad_params[0], grad_params[1], grad_params[2], grad_params[3], grad_params[4], grad_params[5], grad_params[6], grad_params[7], grad_params[8], grad_params[9], grad_params[10], grad_params[11], grad_params[12], grad_params[13], grad_params[14], grad_params[15], grad_params[16], grad_params[17])
```

```python
import functools

import jax
import jax.numpy as jnp
from jax import lax
from jax.experimental import pallas as pl
from jax.experimental.pallas import tpu as pltpu
from jax.sharding import PartitionSpec as P

HEAD_K = 128
HEAD_V = 256
CONVK = 4
BLOCK = 64
HALO = 8
EXTRA = 128
GROUP = 4


epsilon = 1e-06
highest_precision = lax.Precision.HIGHEST


def swapped(value, axis, stride):
    return lax.ppermute(value, axis, [(i, i ^ 1 << stride) for i in range(lax.axis_size(axis))])


def carried_in(value, axis, combine, identity):
    devices, position = (lax.axis_size(axis), lax.axis_index(axis))
    everything = jax.tree.map(
        lambda part, kind: lax.all_gather(part.astype(kind), axis),
        value,
        (jnp.bfloat16, jnp.bfloat16),
    )
    start = jax.tree.map(
        lambda part, zero: jnp.broadcast_to(jnp.asarray(zero, part.dtype), part.shape),
        value,
        identity,
    )

    def step(k, before):
        reached = k < position
        new = combine(
            before, jax.tree.map(lambda part, own: part[k].astype(own.dtype), everything, value)
        )
        return jax.tree.map(lambda a, b: jnp.where(reached, a, b), new, before)

    return lax.fori_loop(0, devices, step, start)


def entering(value, axis, join, neutral):
    count = lax.axis_size(axis)
    place = lax.axis_index(axis)
    ahead = count - 1 - place
    gathered = jax.tree.map(
        lambda a, kind: lax.all_gather(a.astype(kind), axis),
        value,
        jax.tree.map(lambda a: jnp.bfloat16 if a.dtype == jnp.float32 else a.dtype, value),
    )
    state = jax.tree.map(lambda a, e: jnp.zeros_like(a) + jnp.asarray(e, a.dtype), value, neutral)

    def one(step, state):
        source = count - 1 - step
        return join(
            state,
            jax.tree.map(
                lambda a, own: lax.dynamic_index_in_dim(a, source, 0, False).astype(own.dtype),
                gathered,
                value,
            ),
        )

    return lax.fori_loop(0, ahead, one, state)


def passed_along(value, axis, steps):
    count = lax.axis_size(axis)
    first, last = (max(0, -steps), min(count, count - steps))
    return lax.ppermute(value, axis, [(source, source + steps) for source in range(first, last)])


def rms_norm(values, weight):
    return values * lax.rsqrt(jnp.mean(values * values, axis=-1, keepdims=True) + epsilon) * weight


def doc_index(starts, positions):
    counted = jnp.sum(
        (starts[None, :] <= positions[:, None]).astype(jnp.int32), axis=1, dtype=jnp.int32
    )
    return counted - 1


def unit_rows(values):
    return values * lax.rsqrt(jnp.sum(values * values, axis=-1, keepdims=True) + epsilon)


def conv_front(extended, doc_ext, conv_weight):
    length = extended.shape[0] - (CONVK - 1)
    summed = jnp.zeros((length, extended.shape[1]), extended.dtype)
    for tap_index in range(CONVK):
        same_doc = doc_ext[tap_index : tap_index + length] == doc_ext[CONVK - 1 :]
        summed = (
            summed
            + jnp.where(same_doc[:, None], extended[tap_index : tap_index + length], 0.0)
            * conv_weight[tap_index]
        )
    return jax.nn.silu(summed)


def heads_front(extended, doc_ext, mix_pre, conv_weight, decay_scale, decay_shift, head_count):
    activated = conv_front(extended, doc_ext, conv_weight)
    length = activated.shape[0]
    width_k = head_count * HEAD_K
    queries = unit_rows(activated[:, :width_k].reshape(length, head_count, HEAD_K)) * HEAD_K ** (
        -0.5
    )
    key_rows = unit_rows(activated[:, width_k : 2 * width_k].reshape(length, head_count, HEAD_K))
    value_rows = activated[:, 2 * width_k :].reshape(length, head_count, HEAD_V)
    write_rate = jax.nn.sigmoid(mix_pre[:, head_count:])
    log_decay = -jnp.exp(decay_scale) * jax.nn.softplus(mix_pre[:, :head_count] + decay_shift)
    return (queries, key_rows, value_rows, write_rate, log_decay)


def block_terms(queries, key_rows, value_rows, write_rate, log_decay, doc_ids, prev_doc):
    length = queries.shape[1]
    cumulated = jnp.cumsum(log_decay, axis=1)
    row_iota = lax.broadcasted_iota(jnp.int32, (length, length), 0)
    col_iota = lax.broadcasted_iota(jnp.int32, (length, length), 1)
    same_doc = (doc_ids[:, :, None] == doc_ids[:, None, :]) & (col_iota <= row_iota)[None]
    same_mask = same_doc[:, :, :, None]
    exponent = jnp.where(same_mask, cumulated[:, :, None, :] - cumulated[:, None, :, :], 0.0)
    decay_full = jnp.where(same_mask, jnp.exp(exponent), 0.0)
    initial_decay = jnp.where((doc_ids == prev_doc[:, None])[:, :, None], jnp.exp(cumulated), 0.0)
    decay_heads = jnp.transpose(decay_full, (0, 3, 1, 2))
    key_gram = jnp.einsum("nthk,nihk->nhti", key_rows, key_rows, precision=highest_precision)
    strict_mask = (col_iota < row_iota)[None, None]
    lower_part = jnp.where(
        strict_mask,
        jnp.transpose(write_rate, (0, 2, 1))[:, :, :, None] * decay_heads * key_gram,
        0.0,
    )
    system = lower_part + jnp.eye(length, dtype=lower_part.dtype)
    scaled_values = jnp.transpose(write_rate[..., None] * value_rows, (0, 2, 1, 3))
    scaled_keys = jnp.transpose((write_rate * initial_decay)[..., None] * key_rows, (0, 2, 1, 3))
    resolved_values = lax.linalg.triangular_solve(
        system, scaled_values, left_side=True, lower=True, unit_diagonal=True
    )
    resolved_keys = lax.linalg.triangular_solve(
        system, scaled_keys, left_side=True, lower=True, unit_diagonal=True
    )
    query_key = (
        jnp.einsum("nthk,nihk->nhti", queries, key_rows, precision=highest_precision) * decay_heads
    )
    return (resolved_values, resolved_keys, query_key, decay_heads, initial_decay)


def gate_norm(mixed_out, gate_pre, norm_weight, head_count):
    length = mixed_out.shape[0]
    per_head = mixed_out.reshape(length, head_count, HEAD_V)
    gates = gate_pre.reshape(length, head_count, HEAD_V)
    normed = rms_norm(per_head, norm_weight) * jax.nn.silu(gates)
    return normed.reshape(length, head_count * HEAD_V)


def summary(
    extended, mix_pre, conv_weight, decay_scale, decay_shift, doc_ext, prev_docs, head_count
):
    queries, key_rows, value_rows, write_rate, log_decay = heads_front(
        extended, doc_ext, mix_pre, conv_weight, decay_scale, decay_shift, head_count
    )
    length = write_rate.shape[0]
    blocks = length // BLOCK

    def as_blocks(values):
        return values.reshape((blocks, BLOCK) + values.shape[1:])

    block_query_rows = as_blocks(queries)
    block_key_rows = as_blocks(key_rows)
    resolved_values, resolved_keys, query_key, decay_heads, initial_decay = block_terms(
        block_query_rows,
        block_key_rows,
        as_blocks(value_rows),
        as_blocks(write_rate),
        as_blocks(log_decay),
        as_blocks(doc_ext[CONVK - 1 :]),
        prev_docs,
    )
    final_row = decay_heads[:, :, -1, :]
    identity = jnp.eye(HEAD_K, dtype=extended.dtype)
    transfer_blocks = initial_decay[:, -1, :][:, :, None, None] * identity - jnp.einsum(
        "nhi,nihk,nhil->nhkl", final_row, block_key_rows, resolved_keys, precision=highest_precision
    )
    add_blocks = jnp.einsum(
        "nhi,nihk,nhiv->nhkv",
        final_row,
        block_key_rows,
        resolved_values,
        precision=highest_precision,
    )
    local_out = jnp.einsum(
        "nhti,nhiv->nhtv", query_key, resolved_values, precision=highest_precision
    )
    response = jnp.transpose(initial_decay, (0, 2, 1))[..., None] * jnp.transpose(
        block_query_rows, (0, 2, 1, 3)
    ) - jnp.einsum("nhti,nhik->nhtk", query_key, resolved_keys, precision=highest_precision)
    carry_map = jnp.broadcast_to(identity, (head_count, HEAD_K, HEAD_K))
    carried_addend = jnp.zeros((head_count, HEAD_K, HEAD_V), extended.dtype)
    entry_maps = []
    entry_adds = []
    for block_number in range(blocks):
        entry_maps.append(carry_map)
        entry_adds.append(carried_addend)
        carried_addend = (
            jnp.einsum(
                "jme,jed->jmd",
                transfer_blocks[block_number],
                carried_addend,
                precision=highest_precision,
            )
            + add_blocks[block_number]
        )
        carry_map = jnp.einsum(
            "hkl,hlm->hkm", transfer_blocks[block_number], carry_map, precision=highest_precision
        )
    kept = (local_out, response, jnp.stack(entry_maps), jnp.stack(entry_adds))
    return (carry_map, carried_addend, kept)


def finish(kept, running_state):
    local_out, response, entry_maps, entry_adds = kept
    entry_states = (
        jnp.einsum("nhkl,hlv->nhkv", entry_maps, running_state, precision=highest_precision)
        + entry_adds
    )
    result = local_out + jnp.einsum(
        "nhck,nhkv->nhcv", response, entry_states, precision=highest_precision
    )
    blocks, head_count, length, width_v = result.shape
    return jnp.transpose(result, (0, 2, 1, 3)).reshape(blocks * length, head_count * width_v)


def compose(earlier_blocks, later_blocks):
    return (
        jnp.einsum("hkl,hlm->hkm", later_blocks[0], earlier_blocks[0], precision=highest_precision),
        jnp.einsum("jme,jed->jmd", later_blocks[0], earlier_blocks[1], precision=highest_precision)
        + later_blocks[1],
    )


def head_total(values):
    return lax.psum(values.astype(jnp.bfloat16), "head").astype(jnp.float32)


def partner(values):
    return swapped(values, "section", 0)


def proj_t(left, right):
    return lax.dot_general(
        left, right, (((1,), (1,)), ((), ())), preferred_element_type=jnp.float32
    )


def inner_t(left, right):
    return lax.dot_general(
        left, right, (((0,), (0,)), ((), ())), preferred_element_type=jnp.float32
    )


def spread(rows_grads, cols_grads):
    rows_part = (
        lax.psum_scatter(
            rows_grads[0].astype(jnp.bfloat16), "seq", scatter_dimension=0, tiled=True
        ).astype(jnp.float32),
        lax.psum_scatter(
            rows_grads[1].astype(jnp.bfloat16), "seq", scatter_dimension=0, tiled=True
        ).astype(jnp.float32),
        lax.psum_scatter(
            rows_grads[2].astype(jnp.bfloat16), "seq", scatter_dimension=0, tiled=True
        ).astype(jnp.float32),
        lax.psum_scatter(
            rows_grads[3].astype(jnp.bfloat16), "seq", scatter_dimension=0, tiled=True
        ).astype(jnp.float32),
        lax.psum_scatter(
            rows_grads[4].astype(jnp.bfloat16), "seq", scatter_dimension=0, tiled=True
        ).astype(jnp.float32),
    )
    cols_part = (
        lax.psum_scatter(
            cols_grads[0].astype(jnp.bfloat16), "seq", scatter_dimension=1, tiled=True
        ).astype(jnp.float32),
        lax.psum_scatter(
            cols_grads[1].astype(jnp.bfloat16), "seq", scatter_dimension=1, tiled=True
        ).astype(jnp.float32),
    )
    return (rows_part, cols_part)


def shards(
    tokens,
    cotangent,
    doc_starts,
    valid_mask,
    gain_attn,
    w_query,
    w_key,
    w_value,
    w_gate_out,
    w_decay,
    w_beta,
    conv_query,
    conv_key,
    conv_value,
    decay_log,
    decay_bias,
    out_norm,
    w_output,
    gain_mlp,
    w_gate,
    w_up,
    w_down,
):
    micro_count = tokens.shape[0]
    row_count = tokens.shape[1]
    model_width = tokens.shape[2]
    head_count = w_decay.shape[2]
    width_qk = w_query.shape[2]
    width_qkv = 2 * width_qk + w_value.shape[2]
    hidden_width = w_gate.shape[2]
    block_count = row_count // BLOCK
    section_index = lax.axis_index("section")
    shard_index = lax.axis_index("seq")
    full_rows = (
        lax.all_gather(gain_attn[0], "seq", axis=0, tiled=True),
        lax.all_gather(gain_mlp[0], "seq", axis=0, tiled=True),
        lax.all_gather(w_query[0], "seq", axis=0, tiled=True),
        lax.all_gather(w_key[0], "seq", axis=0, tiled=True),
        lax.all_gather(w_value[0], "seq", axis=0, tiled=True),
        lax.all_gather(w_gate_out[0], "seq", axis=0, tiled=True),
        lax.all_gather(w_decay[0], "seq", axis=0, tiled=True),
        lax.all_gather(w_beta[0], "seq", axis=0, tiled=True),
        lax.all_gather(w_gate[0], "seq", axis=0, tiled=True),
        lax.all_gather(w_up[0], "seq", axis=0, tiled=True),
    )
    full_cols = (
        lax.all_gather(w_output[0], "seq", axis=1, tiled=True),
        lax.all_gather(w_down[0], "seq", axis=1, tiled=True),
    )
    attn_gain = full_rows[0].astype(jnp.float32)
    mlp_gain = full_rows[1].astype(jnp.float32)
    proj_weight = jnp.concatenate([full_rows[2], full_rows[3], full_rows[4], full_rows[5]], axis=1)
    mix_weight = jnp.concatenate([full_rows[6], full_rows[7]], axis=1).astype(jnp.float32)
    gate_up_weight = jnp.concatenate([full_rows[8], full_rows[9]], axis=1)
    out_weight = full_cols[0]
    down_weight = full_cols[1]
    conv_weight = jnp.concatenate([conv_query[0], conv_key[0], conv_value[0]], axis=1).astype(
        jnp.float32
    )
    decay_scale = decay_log[0]
    decay_shift = decay_bias[0]
    norm_weight = out_norm[0].astype(jnp.float32)
    ext_pos = (
        shard_index * row_count - (CONVK - 1) + jnp.arange(row_count + CONVK - 1, dtype=jnp.int32)
    )
    block_pos = shard_index * row_count + jnp.arange(block_count, dtype=jnp.int32) * BLOCK - 1

    def carry_backward(shard_map_t, shard_adj):
        identity = jnp.broadcast_to(
            jnp.eye(shard_map_t.shape[1], dtype=jnp.float32), shard_map_t.shape
        )
        suffix = entering(
            (shard_map_t, shard_adj), "seq", compose, (identity, jnp.zeros_like(shard_adj))
        )
        result = suffix[1]
        return result

    def layer_backward(saved, upstream, starts):
        (
            resid_in,
            normed,
            mix_pre,
            extended,
            gate_pre,
            kept,
            running_state,
            shard_map,
            mixed_out,
            gated,
            resid_mid,
            ffn_in,
            gate_up,
            hidden,
        ) = saved
        doc_ext = doc_index(starts, ext_pos)
        prev_docs = doc_index(starts, block_pos)
        grad_ffn = upstream.astype(jnp.bfloat16)
        grad_hidden = proj_t(grad_ffn, down_weight)
        grad_down = inner_t(hidden, grad_ffn)
        _, act_back = jax.vjp(
            lambda gate_in, up_in: jax.nn.silu(gate_in) * up_in,
            gate_up[:, :hidden_width],
            gate_up[:, hidden_width:],
        )
        grad_gate, grad_up = act_back(grad_hidden)
        grad_gate_up = jnp.concatenate([grad_gate, grad_up], axis=1).astype(jnp.bfloat16)
        grad_gu_weight = inner_t(ffn_in, grad_gate_up)
        grad_ffn_in = head_total(proj_t(grad_gate_up, gate_up_weight))
        _, mlp_norm_back = jax.vjp(rms_norm, resid_mid, mlp_gain)
        grad_mid_norm, grad_mlp_gain = mlp_norm_back(grad_ffn_in)
        grad_mid = upstream + grad_mid_norm
        grad_attn = grad_mid.astype(jnp.bfloat16)
        grad_gated = proj_t(grad_attn, out_weight)
        grad_out_weight = inner_t(gated, grad_attn)
        _, gate_back = jax.vjp(
            lambda mixed_in, gate_in, weight_in: gate_norm(
                mixed_in, gate_in, weight_in, head_count
            ),
            mixed_out,
            gate_pre,
            norm_weight,
        )
        grad_mixed, grad_gate_pre, grad_norm_weight = gate_back(grad_gated)
        _, finish_back = jax.vjp(finish, kept, running_state)
        grad_kept, grad_state = finish_back(grad_mixed)
        later_blocks = carry_backward(jnp.swapaxes(shard_map, 1, 2), grad_state)
        gradient_transfer = jnp.einsum(
            "rgm,ram->rga", later_blocks, running_state, precision=highest_precision
        )

        def local_summary(ext_in, mix_in, conv_in, scale_in, shift_in):
            return summary(
                ext_in, mix_in, conv_in, scale_in, shift_in, doc_ext, prev_docs, head_count
            )

        _, summary_back = jax.vjp(
            local_summary, extended, mix_pre, conv_weight, decay_scale, decay_shift
        )
        grad_ext, grad_mix, grad_conv, grad_scale, grad_shift = summary_back(
            (gradient_transfer, later_blocks, grad_kept)
        )
        returned = passed_along(grad_ext[: CONVK - 1], "seq", -1)
        grad_qkv = grad_ext[CONVK - 1 :] + jnp.pad(returned, ((row_count - (CONVK - 1), 0), (0, 0)))
        grad_pre = jnp.concatenate([grad_qkv, grad_gate_pre], axis=1).astype(jnp.bfloat16)
        grad_proj_weight = inner_t(normed, grad_pre)
        normed_float = normed.astype(jnp.float32)
        grad_mix_weight = lax.dot_general(
            normed_float, grad_mix, (((0,), (0,)), ((), ())), precision=highest_precision
        )
        grad_normed = head_total(
            proj_t(grad_pre, proj_weight)
            + lax.dot_general(
                grad_mix, mix_weight, (((1,), (1,)), ((), ())), precision=highest_precision
            )
        )
        _, attn_norm_back = jax.vjp(rms_norm, resid_in.astype(jnp.float32), attn_gain)
        grad_resid_norm, grad_attn_gain = attn_norm_back(grad_normed)
        grad_resid = grad_mid + grad_resid_norm
        rows_grads = (
            grad_attn_gain,
            grad_mlp_gain,
            grad_proj_weight,
            grad_mix_weight,
            grad_gu_weight,
        )
        cols_grads = (grad_out_weight, grad_down)
        small_grads = (grad_conv, grad_scale, grad_shift, grad_norm_weight)
        return (grad_resid, rows_grads, cols_grads, small_grads)

    zero_in = jnp.zeros((row_count, model_width), jnp.bfloat16)
    incoming = zero_in
    stored = None
    activations_buf = jnp.zeros(tokens.shape, jnp.bfloat16)
    stat_sums = jnp.zeros((micro_count, 3), jnp.float32)
    stat_counts = jnp.zeros((micro_count,), jnp.float32)
    for slot_index in range(micro_count + 1):
        chosen_raw = slot_index - section_index
        active = (chosen_raw >= 0) & (chosen_raw < micro_count)
        chosen = jnp.clip(chosen_raw, 0, micro_count - 1)
        resid_in = jnp.where(section_index == 0, tokens[min(slot_index, micro_count - 1)], incoming)
        layer_starts = doc_starts[chosen]
        layer_doc_ext = doc_index(layer_starts, ext_pos)
        layer_prev_docs = doc_index(layer_starts, block_pos)
        resid = resid_in.astype(jnp.float32)
        layer_normed = rms_norm(resid, attn_gain).astype(jnp.bfloat16)
        projected = jnp.dot(layer_normed, proj_weight, preferred_element_type=jnp.float32)
        layer_mix_pre = jnp.dot(
            layer_normed.astype(jnp.float32), mix_weight, precision=highest_precision
        )
        qkv_pre = projected[:, :width_qkv]
        layer_gate_pre = projected[:, width_qkv:]
        rim_rows = passed_along(qkv_pre[row_count - (CONVK - 1) :], "seq", 1)
        layer_extended = jnp.concatenate([rim_rows, qkv_pre], axis=0)
        layer_shard_map, layer_shard_add, layer_kept = summary(
            layer_extended,
            layer_mix_pre,
            conv_weight,
            decay_scale,
            decay_shift,
            layer_doc_ext,
            layer_prev_docs,
            head_count,
        )
        carry_identity = jnp.broadcast_to(
            jnp.eye(layer_shard_map.shape[1], dtype=jnp.float32), layer_shard_map.shape
        )
        prefix = carried_in(
            (layer_shard_map, layer_shard_add),
            "seq",
            compose,
            (carry_identity, jnp.zeros_like(layer_shard_add)),
        )
        carry_result = prefix[1]
        layer_mixed_out = finish(layer_kept, carry_result)
        layer_gated = gate_norm(layer_mixed_out, layer_gate_pre, norm_weight, head_count).astype(
            jnp.bfloat16
        )
        attn = head_total(jnp.dot(layer_gated, out_weight, preferred_element_type=jnp.float32))
        layer_resid_mid = resid + attn
        layer_ffn_in = rms_norm(layer_resid_mid, mlp_gain).astype(jnp.bfloat16)
        layer_gate_up = jnp.dot(layer_ffn_in, gate_up_weight, preferred_element_type=jnp.float32)
        layer_hidden = (
            jax.nn.silu(layer_gate_up[:, :hidden_width]) * layer_gate_up[:, hidden_width:]
        ).astype(jnp.bfloat16)
        ffn = head_total(jnp.dot(layer_hidden, down_weight, preferred_element_type=jnp.float32))
        layer_out = layer_resid_mid + ffn
        layer_saved = (
            resid_in,
            layer_normed,
            layer_mix_pre,
            layer_extended,
            layer_gate_pre,
            layer_kept,
            carry_result,
            layer_shard_map,
            layer_mixed_out,
            layer_gated,
            layer_resid_mid,
            layer_ffn_in,
            layer_gate_up,
            layer_hidden,
        )
        saved, layer_out, attn_out, ffn_out = (layer_saved, layer_out, attn, ffn)
        if stored is None:
            stored = jax.tree.map(
                lambda part_new: jnp.zeros((micro_count,) + part_new.shape, part_new.dtype), saved
            )
        stored = jax.tree.map(
            lambda buffer, part_new: buffer.at[chosen].set(
                jnp.where(active, part_new, buffer[chosen])
            ),
            stored,
            saved,
        )
        outgoing = layer_out.astype(jnp.bfloat16)
        activations_buf = activations_buf.at[chosen].set(
            jnp.where(active, outgoing, activations_buf[chosen])
        )
        weights_valid = valid_mask[chosen].astype(jnp.float32)
        sums_now = jnp.stack(
            [
                jnp.sum(weights_valid * jnp.mean(branch_val * branch_val, axis=-1))
                for branch_val in (layer_out, attn_out, ffn_out)
            ]
        )
        stat_sums = stat_sums.at[chosen].set(jnp.where(active, sums_now, stat_sums[chosen]))
        stat_counts = stat_counts.at[chosen].set(
            jnp.where(active, jnp.sum(weights_valid), stat_counts[chosen])
        )
        if slot_index < micro_count:
            incoming = partner(outgoing)
    rows_acc = None
    cols_acc = None
    small_acc = None
    back_in = zero_in
    grad_inputs = jnp.zeros(tokens.shape, jnp.bfloat16)
    for slot_index in range(micro_count + 1):
        chosen_raw = slot_index - (1 - section_index)
        active = (chosen_raw >= 0) & (chosen_raw < micro_count)
        chosen = jnp.clip(chosen_raw, 0, micro_count - 1)
        saved = jax.tree.map(lambda buffer: buffer[chosen], stored)
        from_loss = (
            cotangent[chosen].astype(jnp.float32) * valid_mask[chosen].astype(jnp.float32)[:, None]
        )
        upstream = jnp.where(section_index == 1, from_loss, back_in.astype(jnp.float32))
        grad_resid, rows_grads, cols_grads, small_grads = layer_backward(
            saved, upstream, doc_starts[chosen]
        )
        rows_grads = jax.tree.map(lambda grad_part: jnp.where(active, grad_part, 0.0), rows_grads)
        cols_grads = jax.tree.map(lambda grad_part: jnp.where(active, grad_part, 0.0), cols_grads)
        small_grads = jax.tree.map(lambda grad_part: jnp.where(active, grad_part, 0.0), small_grads)
        if rows_acc is None:
            rows_acc, cols_acc, small_acc = (rows_grads, cols_grads, small_grads)
        else:
            rows_acc = jax.tree.map(jnp.add, rows_acc, rows_grads)
            cols_acc = jax.tree.map(jnp.add, cols_acc, cols_grads)
            small_acc = jax.tree.map(jnp.add, small_acc, small_grads)
        outgoing = grad_resid.astype(jnp.bfloat16)
        grad_inputs = grad_inputs.at[chosen].set(jnp.where(active, outgoing, grad_inputs[chosen]))
        if slot_index < micro_count:
            back_in = partner(outgoing)
    rows_part, cols_part = spread(rows_acc, cols_acc)
    norm_heads = lax.psum(small_acc[3], "head")
    conv_sum, scale_sum, shift_sum, norm_sum, sums_all, counts_all = (
        lax.psum(small_acc[0].astype(jnp.bfloat16), "seq").astype(jnp.float32),
        lax.psum(small_acc[1].astype(jnp.bfloat16), "seq").astype(jnp.float32),
        lax.psum(small_acc[2].astype(jnp.bfloat16), "seq").astype(jnp.float32),
        lax.psum(norm_heads.astype(jnp.bfloat16), "seq").astype(jnp.float32),
        lax.psum(stat_sums.astype(jnp.bfloat16), "seq").astype(jnp.float32),
        lax.psum(stat_counts.astype(jnp.bfloat16), "seq").astype(jnp.float32),
    )
    branch_rms = jnp.sqrt(sums_all / jnp.maximum(counts_all, 1.0)[:, None])
    proj_part = rows_part[2]
    mix_part = rows_part[3]
    gu_part = rows_part[4]
    return (
        activations_buf[None],
        grad_inputs[None],
        branch_rms[None],
        rows_part[0][None],
        proj_part[:, :width_qk][None],
        proj_part[:, width_qk : 2 * width_qk][None],
        proj_part[:, 2 * width_qk : width_qkv][None],
        proj_part[:, width_qkv:][None],
        mix_part[:, :head_count][None],
        mix_part[:, head_count:][None],
        conv_sum[:, :width_qk][None],
        conv_sum[:, width_qk : 2 * width_qk][None],
        conv_sum[:, 2 * width_qk :][None],
        scale_sum[None],
        shift_sum[None],
        norm_sum[None],
        cols_part[0][None],
        rows_part[1][None],
        gu_part[:, :hidden_width][None],
        gu_part[:, hidden_width:][None],
        cols_part[1][None],
    )


exact = lax.Precision.HIGHEST


def dot_nn(a, b):
    return lax.dot_general(
        a, b, (((1,), (0,)), ((), ())), precision=exact, preferred_element_type=jnp.float32
    )


def dot_nt(a, b):
    return lax.dot_general(
        a, b, (((1,), (1,)), ((), ())), precision=exact, preferred_element_type=jnp.float32
    )


def dot_tn(a, b):
    return lax.dot_general(
        a, b, (((0,), (0,)), ((), ())), precision=exact, preferred_element_type=jnp.float32
    )


@functools.partial(jax.custom_vjp, nondiff_argnums=(1,))
def shifted(window, steps):
    if steps == 0:
        return window[HALO:]
    return pltpu.roll(window, steps, 0)[HALO:]


def shifted_fwd(window, steps):
    return shifted(window, steps), None


def shifted_bwd(steps, _, grad):
    padded = jnp.concatenate([jnp.zeros((HALO, grad.shape[1]), grad.dtype), grad], axis=0)
    if steps == 0:
        return (padded,)
    return (pltpu.roll(padded, padded.shape[0] - steps, 0),)


shifted.defvjp(shifted_fwd, shifted_bwd)


def iotas(length):
    rows = lax.broadcasted_iota(jnp.int32, (length, length), 0)
    cols = lax.broadcasted_iota(jnp.int32, (length, length), 1)
    return rows, cols


def as_row(column):
    rows, cols = iotas(column.shape[0])
    return jnp.sum(jnp.where(rows == cols, column, 0.0), axis=0, keepdims=True)


def unit_inverse(lower):
    length = lower.shape[0]
    rows, cols = iotas(length)
    near = jnp.where((rows >> 3) == (cols >> 3), lower, 0.0)
    result = jnp.where(rows == cols, 1.0, 0.0) - near
    square = dot_nn(near, near)
    result = result + dot_nn(result, square)
    result = result + dot_nn(result, dot_nn(square, square))
    shift = 3
    while (1 << shift) < length:
        off = ((rows >> (shift + 1)) == (cols >> (shift + 1))) & ((rows >> shift) != (cols >> shift))
        result = result - dot_nn(result, dot_nn(jnp.where(off, lower, 0.0), result))
        shift += 1
    return result


@jax.custom_vjp
def inverse_known(lower, inverse):
    return inverse


def inverse_known_fwd(lower, inverse):
    return inverse, inverse


def inverse_known_bwd(inverse, grad):
    return -dot_nt(dot_tn(inverse, grad), inverse), jnp.zeros_like(grad)


inverse_known.defvjp(inverse_known_fwd, inverse_known_bwd)


def silu(values):
    return values / (1.0 + jnp.exp(-values))


def sigmoid(values):
    return 1.0 / (1.0 + jnp.exp(-values))


@jax.custom_vjp
def softplus(values):
    return jnp.maximum(values, 0.0) + jnp.log1p(jnp.exp(-jnp.abs(values)))


def softplus_fwd(values):
    return softplus(values), values


def softplus_bwd(values, grad):
    return (grad * sigmoid(values),)


softplus.defvjp(softplus_fwd, softplus_bwd)


def block_front(window, mix_decay, mix_write, taps, decay_log, decay_bias, aux):
    summed = shifted(window, 0) * taps[3]
    for steps in range(1, CONVK):
        summed = summed + jnp.where(aux[:, steps : steps + 1] > 0.0, shifted(window, steps), 0.0) * taps[3 - steps]
    active = silu(summed)
    queries = unit_rows(active[:, :HEAD_K]) * HEAD_K ** (-0.5)
    keys = unit_rows(active[:, HEAD_K : 2 * HEAD_K])
    values = active[:, 2 * HEAD_K :]
    write = sigmoid(mix_write)
    log_decay = -jnp.exp(decay_log) * softplus(mix_decay + decay_bias)
    rows, cols = iotas(BLOCK)
    cum = jnp.sum(jnp.where(cols <= rows, as_row(log_decay), 0.0), axis=1, keepdims=True)
    total = jnp.sum(log_decay, axis=0, keepdims=True)
    doc = aux[:, 0:1]
    same = (doc == as_row(doc)) & (cols <= rows)
    decay = jnp.where(same, jnp.exp(jnp.where(same, cum - as_row(cum), 0.0)), 0.0)
    entry = jnp.where(aux[:, 4:5] > 0.0, jnp.exp(cum), 0.0)
    leave = jnp.where(aux[:, 5:6] > 0.0, jnp.exp(total - cum), 0.0)
    through = jnp.where(aux[BLOCK - 1 : BLOCK, 4:5] > 0.0, jnp.exp(total), 0.0)
    grams = dot_nt(jnp.concatenate([keys, queries], axis=0), keys)
    lower = jnp.where(cols < rows, write * decay * grams[:BLOCK], 0.0)
    mixing = grams[BLOCK:] * decay
    scaled = jnp.concatenate([write * values, (write * entry) * keys], axis=1)
    return lower, mixing, scaled, entry * queries, leave * keys, through


def block_step(window, mix_decay, mix_write, taps, decay_log, decay_bias, state, aux, inverse):
    lower, mixing, scaled, queries, keys, through = block_front(
        window, mix_decay, mix_write, taps, decay_log, decay_bias, aux
    )
    if inverse is None:
        inverse = unit_inverse(lower)
    else:
        inverse = inverse_known(lower, inverse)
    resolved = dot_nn(inverse, scaled)
    read = dot_nn(jnp.concatenate([resolved[:, HEAD_V:], queries], axis=0), state)
    written = resolved[:, :HEAD_V] - read[:BLOCK]
    mixed = read[BLOCK:] + dot_nn(mixing, written)
    return mixed, through * state + dot_tn(keys, written), inverse


def stored_at(number, blocks, parts):
    shards, slices = parts
    each = blocks // (shards * slices)
    shard = number // (slices * each)
    rest = number - shard * slices * each
    place = (rest // each * shards + shard) * each + rest % each
    return pl.multiple_of(place * BLOCK, BLOCK)


def fill_window(xh_ref, xbuf, parts):
    width = xbuf.shape[1]
    length = xh_ref.shape[0]
    blocks = length // BLOCK
    xbuf[0:HALO, :] = jnp.zeros((HALO, width), jnp.float32)

    def copy(index, carry):
        base = pl.multiple_of(index * BLOCK, BLOCK)
        stored = stored_at(index, blocks, parts)
        xbuf[pl.ds(base + HALO, BLOCK), :] = xh_ref[pl.ds(stored, BLOCK), :width].astype(jnp.float32)
        return carry

    lax.fori_loop(0, length // BLOCK, copy, 0)


def load_block(xh_ref, aux_ref, xbuf, base, stored):
    window = xbuf[pl.ds(base, BLOCK + HALO), :]
    mix = xh_ref[pl.ds(stored, BLOCK), xbuf.shape[1] :].astype(jnp.float32)
    aux = aux_ref[pl.ds(base, BLOCK), :]
    return window, mix[:, 0:1] + mix[:, 2:3], mix[:, 1:2] + mix[:, 3:4], aux


def load_taps(taps_ref):
    return [taps_ref[j : j + 1, :] for j in range(CONVK)]


def forward_kernel(parts, xh_ref, aux_ref, taps_ref, scal_ref, mixed_ref, states_ref, inverse_ref, xbuf, state_ref):
    fill_window(xh_ref, xbuf, parts)
    state_ref[...] = jnp.zeros_like(state_ref)
    blocks = xh_ref.shape[0] // BLOCK
    taps = load_taps(taps_ref)
    decay_log = scal_ref[0:1, 0:1]
    decay_bias = scal_ref[0:1, 1:2]

    def group(index, carry):
        state = state_ref[...]
        for inner in range(GROUP):
            number = index * GROUP + inner
            base = pl.multiple_of(number * BLOCK, BLOCK)
            stored = stored_at(number, blocks, parts)
            window, mix_decay, mix_write, aux = load_block(xh_ref, aux_ref, xbuf, base, stored)
            states_ref[number] = state
            mixed, state, inverse = block_step(
                window, mix_decay, mix_write, taps, decay_log, decay_bias, state, aux, None
            )
            mixed_ref[pl.ds(stored, BLOCK), :] = mixed.astype(mixed_ref.dtype)
            inverse_ref[pl.ds(base, BLOCK), :] = inverse
        state_ref[...] = state
        return carry

    lax.fori_loop(0, blocks // GROUP, group, 0)


def backward_kernel(
    parts, xh_ref, aux_ref, taps_ref, scal_ref, states_ref, inverse_ref, grad_ref,
    dxh_ref, dtaps_ref, dscal_ref, xbuf, adjoint_ref, halo_ref,
):
    fill_window(xh_ref, xbuf, parts)
    adjoint_ref[...] = jnp.zeros_like(adjoint_ref)
    halo_ref[...] = jnp.zeros_like(halo_ref)
    dtaps_ref[...] = jnp.zeros_like(dtaps_ref)
    dscal_ref[...] = jnp.zeros_like(dscal_ref)
    blocks = xh_ref.shape[0] // BLOCK
    width = xbuf.shape[1]
    taps = load_taps(taps_ref)
    decay_log = scal_ref[0:1, 0:1]
    decay_bias = scal_ref[0:1, 1:2]
    lanes = lax.broadcasted_iota(jnp.int32, (BLOCK, EXTRA), 1)

    def group(index, carry):
        adjoint = adjoint_ref[...]
        halo = halo_ref[...]
        dtaps = [dtaps_ref[j : j + 1, :] for j in range(CONVK)]
        dlog = dscal_ref[0:1, 0:1]
        dbias = dscal_ref[0:1, 1:2]
        for inner in range(GROUP):
            number = blocks - 1 - (index * GROUP + inner)
            base = pl.multiple_of(number * BLOCK, BLOCK)
            stored = stored_at(number, blocks, parts)
            window, mix_decay, mix_write, aux = load_block(xh_ref, aux_ref, xbuf, base, stored)
            inverse = inverse_ref[pl.ds(base, BLOCK), :]
            grad = grad_ref[pl.ds(stored, BLOCK), :].astype(jnp.float32)

            def run(*inputs):
                return block_step(*inputs, aux, inverse)[:2]

            _, pull = jax.vjp(
                run, window, mix_decay, mix_write, taps, decay_log, decay_bias, states_ref[number]
            )
            dwindow, ddecay, dwrite, dtaps_now, dlog_now, dbias_now, adjoint = pull((grad, adjoint))
            own = dwindow[HALO:]
            own = jnp.concatenate([own[: BLOCK - HALO], own[BLOCK - HALO :] + halo], axis=0)
            halo = dwindow[:HALO]
            dtaps = [a + b for a, b in zip(dtaps, dtaps_now)]
            dlog = dlog + dlog_now
            dbias = dbias + dbias_now
            dxh_ref[pl.ds(stored, BLOCK), :width] = own.astype(dxh_ref.dtype)
            high_decay = ddecay.astype(jnp.bfloat16).astype(jnp.float32)
            high_write = dwrite.astype(jnp.bfloat16).astype(jnp.float32)
            mix = jnp.where(lanes == 0, high_decay, jnp.where(lanes == 1, high_write, 0.0))
            mix = jnp.where(lanes == 2, ddecay - high_decay, jnp.where(lanes == 3, dwrite - high_write, mix))
            dxh_ref[pl.ds(stored, BLOCK), width:] = mix.astype(dxh_ref.dtype)
        adjoint_ref[...] = adjoint
        halo_ref[...] = halo
        for j in range(CONVK):
            dtaps_ref[j : j + 1, :] = dtaps[j]
        dscal_ref[0:1, 0:1] = dlog
        dscal_ref[0:1, 1:2] = dbias
        return carry

    lax.fori_loop(0, blocks // GROUP, group, 0)


WIDTH = 2 * HEAD_K + HEAD_V


def whole():
    return pl.BlockSpec(memory_space=pltpu.VMEM)


def recur_forward(xh, aux, taps, scal, parts):
    length = xh.shape[0]
    blocks = length // BLOCK
    return pl.pallas_call(
        functools.partial(forward_kernel, parts),
        out_shape=(
            jax.ShapeDtypeStruct((length, HEAD_V), jnp.bfloat16),
            jax.ShapeDtypeStruct((blocks, HEAD_K, HEAD_V), jnp.float32),
            jax.ShapeDtypeStruct((length, BLOCK), jnp.float32),
        ),
        in_specs=[whole()] * 4,
        out_specs=(whole(),) * 3,
        scratch_shapes=[
            pltpu.VMEM((length + HALO, WIDTH), jnp.float32),
            pltpu.VMEM((HEAD_K, HEAD_V), jnp.float32),
        ],
        compiler_params=pltpu.CompilerParams(vmem_limit_bytes=48 * 1024 * 1024),
        name="recur_forward",
    )(xh, aux, taps, scal)


def recur_backward(xh, aux, taps, scal, states, inverse, grad, parts):
    length = xh.shape[0]
    return pl.pallas_call(
        functools.partial(backward_kernel, parts),
        out_shape=(
            jax.ShapeDtypeStruct((length, WIDTH + EXTRA), jnp.bfloat16),
            jax.ShapeDtypeStruct((8, WIDTH), jnp.float32),
            jax.ShapeDtypeStruct((8, 128), jnp.float32),
        ),
        in_specs=[whole()] * 7,
        out_specs=(whole(),) * 3,
        scratch_shapes=[
            pltpu.VMEM((length + HALO, WIDTH), jnp.float32),
            pltpu.VMEM((HEAD_K, HEAD_V), jnp.float32),
            pltpu.VMEM((HALO, WIDTH), jnp.float32),
        ],
        compiler_params=pltpu.CompilerParams(vmem_limit_bytes=48 * 1024 * 1024),
        name="recur_backward",
    )(xh, aux, taps, scal, states, inverse, grad)


def make_aux(starts, length):
    positions = jnp.arange(length, dtype=jnp.int32)
    doc = jnp.sum((starts[None, :] <= positions[:, None]).astype(jnp.int32), axis=1)
    def back(steps):
        earlier = jnp.concatenate([jnp.full((steps,), -1, jnp.int32), doc[:-steps]])
        return (earlier == doc).astype(jnp.float32)
    blocks = doc.reshape(-1, BLOCK)
    before = jnp.concatenate([jnp.full((1,), -1, jnp.int32), blocks[:-1, -1]])
    entering = (blocks == before[:, None]).reshape(-1).astype(jnp.float32)
    leaving = (blocks == blocks[:, -1:]).reshape(-1).astype(jnp.float32)
    zero = jnp.zeros((length,), jnp.float32)
    return jnp.stack([doc.astype(jnp.float32), back(1), back(2), back(3), entering, leaving, zero, zero], axis=1)


def halves(value, axis):
    step = 1
    while step < lax.axis_size(axis):
        value = value + swapped(value, axis, step.bit_length() - 1)
        step *= 2
    return value


def by_partner(value, axis):
    size = lax.axis_size(axis)
    return [value] + [
        lax.ppermute(value, axis, [(i, i ^ k) for i in range(size)]) for k in range(1, size)
    ]


def in_order(parts, axis):
    position = lax.axis_index(axis)
    parts = list(parts)
    step = 1
    while step < len(parts):
        odd = (position & step) != 0
        parts = [jnp.where(odd, parts[i ^ step], parts[i]) for i in range(len(parts))]
        step *= 2
    return parts


def gathered(value, axis):
    return jnp.concatenate(in_order(by_partner(value, axis), axis), axis=0)


def shard_total(partial):
    size = lax.axis_size("seq")
    rows, width = partial.shape
    pieces = partial.astype(jnp.bfloat16).reshape(size, rows // size, width)
    pieces = lax.all_to_all(pieces, "seq", 0, 0)
    total = jnp.sum(pieces.astype(jnp.float32), axis=0).astype(jnp.bfloat16)
    return gathered(total, "seq").astype(jnp.float32)


def pick(flag, when, otherwise):
    return jnp.where(flag, when, otherwise)


def both_layers(local, axis):
    core = lax.axis_index("section")
    half = local.shape[axis] // 2
    own = lax.dynamic_slice_in_dim(local, core * half, half, axis)
    received = partner(lax.dynamic_slice_in_dim(local, (1 - core) * half, half, axis))
    first = core == 0
    return pick(first, own, received), pick(first, received, own)


def spread_rows(part):
    part = lax.all_to_all(part, "seq", 0, 0)
    part = part.reshape(-1, part.shape[2])
    full = lax.all_gather(part, ("head", "section"), axis=0, tiled=True)
    return full.reshape(lax.axis_size("head"), -1, part.shape[1])


def spread_cols(part):
    part = lax.all_to_all(part, "seq", 0, 0)
    part = jnp.swapaxes(part, 0, 1).reshape(part.shape[1], -1)
    full = lax.all_gather(part, ("section", "head"), axis=0, tiled=True)
    return full.reshape(2, -1, part.shape[1])


def collect_rows(grad):
    part = lax.psum_scatter(
        grad.reshape(-1, grad.shape[2]), ("head", "section"), scatter_dimension=0, tiled=True
    )
    shards = lax.axis_size("seq")
    part = lax.all_to_all(part.reshape(shards, -1, part.shape[1]), "seq", 0, 0)
    return jnp.swapaxes(part, 0, 1)


def collect_cols(grad):
    part = lax.psum_scatter(
        grad.reshape(-1, grad.shape[2]), ("section", "head"), scatter_dimension=0, tiled=True
    )
    shards = lax.axis_size("seq")
    part = jnp.swapaxes(part.reshape(part.shape[0], shards, -1), 0, 1)
    return lax.all_to_all(part, "seq", 0, 0)


def dot(left, right):
    return jnp.dot(left, right, preferred_element_type=jnp.float32)


def over_halves(value, weight):
    return jnp.concatenate([dot(value, weight[half]) for half in range(2)], axis=1)


def from_halves(value, weight):
    width = weight.shape[2]
    return sum(proj_t(value[:, half * width : (half + 1) * width], weight[half]) for half in range(2))


def grad_halves(value, grad):
    width = grad.shape[1] // 2
    return jnp.stack(
        [inner_t(value, grad[:, half * width : (half + 1) * width]).astype(jnp.bfloat16) for half in range(2)]
    )


def head_norm(mixed, gate_pre, norm_weight):
    return rms_norm(mixed, norm_weight) * jax.nn.silu(gate_pre)


def layer_forward(resid, gains, weights, small, aux, parts):
    attn_gain, mlp_gain = gains
    w_proj, w_mix, w_out, w_gu, w_down = weights
    taps, scal, norm_weight = small
    rows = resid.shape[0]
    slices = w_proj.shape[0]
    normed = rms_norm(resid, attn_gain).astype(jnp.bfloat16)
    projected = jnp.stack([dot(normed, w_proj[j]) for j in range(slices)])
    gate_pre = projected[:, :, WIDTH:]
    mix = proj_t(normed, w_mix).T.reshape(slices, 2, rows)
    mix = jnp.swapaxes(mix, 1, 2)
    mix_high = mix.astype(jnp.bfloat16)
    mix_low = (mix - mix_high.astype(jnp.float32)).astype(jnp.bfloat16)
    packed = jnp.concatenate(
        [
            projected[:, :, :WIDTH].astype(jnp.bfloat16),
            mix_high,
            mix_low,
            jnp.zeros((slices, rows, EXTRA - 4), jnp.bfloat16),
        ],
        axis=2,
    )
    xh = lax.all_to_all(packed, "head", 0, 0).reshape(slices * rows, WIDTH + EXTRA)
    mixed_head, states, inverse = recur_forward(xh, aux, taps, scal, parts)
    mixed = lax.all_to_all(mixed_head.reshape(slices, rows, HEAD_V), "head", 0, 0)
    gated = head_norm(mixed.astype(jnp.float32), gate_pre, norm_weight).astype(jnp.bfloat16)
    gated = jnp.swapaxes(gated, 0, 1).reshape(rows, slices * HEAD_V)
    attn = shard_total(over_halves(gated, w_out))
    resid_mid = resid + attn
    ffn_in = rms_norm(resid_mid, mlp_gain).astype(jnp.bfloat16)
    gate_up = jnp.stack([dot(ffn_in, w_gu[j]) for j in range(slices)])
    hidden_width = w_gu.shape[2] // 2
    hidden = (jax.nn.silu(gate_up[:, :, :hidden_width]) * gate_up[:, :, hidden_width:]).astype(
        jnp.bfloat16
    )
    hidden = jnp.swapaxes(hidden, 0, 1).reshape(rows, slices * hidden_width)
    ffn = shard_total(over_halves(hidden, w_down))
    out = resid_mid + ffn
    saved = (resid, normed, gate_pre, xh, states, inverse, mixed, gated, resid_mid, ffn_in, gate_up, hidden)
    return out, attn, ffn, saved


def layer_backward_fast(upstream, saved, gains, weights, small, aux, parts):
    attn_gain, mlp_gain = gains
    w_proj, w_mix, w_out, w_gu, w_down = weights
    taps, scal, norm_weight = small
    resid, normed, gate_pre, xh, states, inverse, mixed, gated, resid_mid, ffn_in, gate_up, hidden = saved
    rows = resid.shape[0]
    slices = w_proj.shape[0]
    hidden_width = w_gu.shape[2] // 2

    def by_slice(value):
        return jnp.swapaxes(value.reshape(rows, slices, -1), 0, 1)

    grad_ffn = upstream.astype(jnp.bfloat16)
    grad_hidden = by_slice(from_halves(grad_ffn, w_down))
    grad_down = grad_halves(hidden, grad_ffn)
    _, act_back = jax.vjp(
        lambda gate_in, up_in: jax.nn.silu(gate_in) * up_in,
        gate_up[:, :, :hidden_width],
        gate_up[:, :, hidden_width:],
    )
    grad_gate, grad_up = act_back(grad_hidden)
    grad_gate_up = jnp.concatenate([grad_gate, grad_up], axis=2).astype(jnp.bfloat16)
    grad_ffn_in = shard_total(sum(proj_t(grad_gate_up[j], w_gu[j]) for j in range(slices)))
    grad_gu = jnp.stack([inner_t(ffn_in, grad_gate_up[j]).astype(jnp.bfloat16) for j in range(slices)])
    _, mlp_norm_back = jax.vjp(rms_norm, resid_mid, mlp_gain)
    grad_mid_norm, grad_mlp_gain = mlp_norm_back(grad_ffn_in)
    grad_mid = upstream + grad_mid_norm
    grad_attn = grad_mid.astype(jnp.bfloat16)
    grad_gated = by_slice(from_halves(grad_attn, w_out))
    grad_out = grad_halves(gated, grad_attn)
    _, gate_back = jax.vjp(head_norm, mixed.astype(jnp.float32), gate_pre, norm_weight)
    grad_mixed, grad_gate_pre, grad_norm_weight = gate_back(grad_gated)
    grad_head = lax.all_to_all(grad_mixed.astype(jnp.bfloat16), "head", 0, 0)
    dxh, dtaps, dscal = recur_backward(
        xh, aux, taps, scal, states, inverse, grad_head.reshape(slices * rows, HEAD_V), parts
    )
    grad_packed = lax.all_to_all(dxh.reshape(slices, rows, WIDTH + EXTRA), "head", 0, 0)
    grad_mix = grad_packed[:, :, WIDTH : WIDTH + 4].reshape(slices, rows, 2, 2)
    grad_mix = jnp.transpose(grad_mix, (1, 2, 0, 3)).reshape(rows, 4 * slices)
    grad_pre = jnp.concatenate(
        [grad_packed[:, :, :WIDTH], grad_gate_pre.astype(jnp.bfloat16)], axis=2
    )
    grad_proj = jnp.stack([inner_t(normed, grad_pre[j]).astype(jnp.bfloat16) for j in range(slices)])
    grad_w_mix = inner_t(grad_mix, normed)
    grad_w_mix = grad_w_mix[: 2 * slices] + grad_w_mix[2 * slices :]
    grad_normed = shard_total(
        sum(proj_t(grad_pre[j], w_proj[j]) for j in range(slices))
        + dot(grad_mix, jnp.concatenate([w_mix, w_mix], axis=0))
    )
    _, attn_norm_back = jax.vjp(rms_norm, resid, attn_gain)
    grad_resid_norm, grad_attn_gain = attn_norm_back(grad_normed)
    grad_resid = grad_mid + grad_resid_norm
    small_grads = (dtaps[:CONVK], dscal[0, :2], grad_norm_weight, grad_attn_gain, grad_mlp_gain, grad_w_mix)
    return grad_resid, (grad_proj, grad_out, grad_gu, grad_down), small_grads


def fast_shards(
    tokens,
    cotangent,
    doc_starts,
    valid_mask,
    gain_attn,
    w_query,
    w_key,
    w_value,
    w_gate_out,
    w_decay,
    w_beta,
    conv_query,
    conv_key,
    conv_value,
    decay_log,
    decay_bias,
    out_norm,
    w_output,
    gain_mlp,
    w_gate,
    w_up,
    w_down,
):
    core = lax.axis_index("section")
    first = core == 0
    shard = lax.axis_index("seq")
    piece = lax.axis_index("head")
    shards, slices = lax.axis_size("seq"), lax.axis_size("head")
    parts = (shards, slices)
    shard_rows = w_query.shape[1]
    model_width = tokens.shape[2]
    sub = tokens.shape[1] // slices
    length = tokens.shape[1] * shards
    hidden_width = w_gate.shape[2] // shards
    hidden_padded = -(-hidden_width // 128) * 128

    def columns(value, width):
        return jnp.stack([value[:, s * width : (s + 1) * width] for s in range(shards)])

    def halved(value):
        shape = value.shape[:-1]
        value = value.reshape(shape + (shards, 2, model_width // (2 * shards)))
        return jnp.swapaxes(value, -3, -2).reshape(shape + (model_width,))

    proj_local = jnp.concatenate(
        [
            columns(w_query[0], HEAD_K),
            columns(w_key[0], HEAD_K),
            columns(w_value[0], HEAD_V),
            columns(w_gate_out[0], HEAD_V),
        ],
        axis=2,
    )
    fill = ((0, 0), (0, 0), (0, hidden_padded - hidden_width))
    gu_local = jnp.concatenate(
        [jnp.pad(columns(w_gate[0], hidden_width), fill), jnp.pad(columns(w_up[0], hidden_width), fill)],
        axis=2,
    )
    out_local = w_output[0].reshape(shards, HEAD_V, shard_rows)
    down_local = jnp.pad(
        w_down[0].reshape(shards, hidden_width, shard_rows),
        ((0, 0), (0, hidden_padded - hidden_width), (0, 0)),
    )
    proj_parts = both_layers(proj_local, 1)
    out_parts = both_layers(out_local, 2)
    gu_parts = both_layers(gu_local, 1)
    down_parts = both_layers(down_local, 2)

    conv = jnp.concatenate(
        [
            columns(conv_query[0], HEAD_K),
            columns(conv_key[0], HEAD_K),
            columns(conv_value[0], HEAD_V),
        ],
        axis=2,
    )
    taps_own = lax.dynamic_index_in_dim(conv, shard, 0, False).astype(jnp.float32)
    small_own = jnp.concatenate(
        [
            taps_own.reshape(-1),
            jnp.stack([decay_log[0, shard], decay_bias[0, shard]]),
            out_norm[0].astype(jnp.float32),
            gain_attn[0].astype(jnp.float32),
            gain_mlp[0].astype(jnp.float32),
            w_decay[0].astype(jnp.float32).T.reshape(-1),
            w_beta[0].astype(jnp.float32).T.reshape(-1),
        ]
    )
    small_other = partner(small_own)
    small_layers = (pick(first, small_own, small_other), pick(first, small_other, small_own))
    taps_size = CONVK * WIDTH
    norm_at = taps_size + 2
    gain_at = norm_at + HEAD_V
    wide = jnp.stack([vector[gain_at:] for vector in small_layers])
    wide = jnp.concatenate([wide.reshape(-1), valid_mask[core].astype(jnp.float32)])
    wide = gathered(wide[None], "seq")
    valid_all = wide[:, wide.shape[1] - tokens.shape[1] :].reshape(shards, slices, sub)
    valid = lax.dynamic_index_in_dim(valid_all, piece, 1, False).reshape(-1)
    wide = wide[:, : wide.shape[1] - tokens.shape[1]].reshape(shards, 2, 2 + 2 * shards, 2, shard_rows // 2)
    gains_all = jnp.transpose(wide[:, :, :2], (1, 2, 3, 0, 4)).reshape(2, 2, model_width)
    mix_all = wide[:, :, 2:].reshape(shards, 2, 2, shards, 2, shard_rows // 2)
    mix_all = lax.dynamic_index_in_dim(mix_all, shard, 3, False)
    mix_all = jnp.transpose(mix_all, (1, 2, 3, 0, 4)).reshape(2, 2, model_width).astype(jnp.bfloat16)
    mix_all = gathered(mix_all[None], "head")
    small = []
    gains = []
    weights = []
    for layer in range(2):
        vector = small_layers[layer]
        taps = jnp.pad(vector[:taps_size].reshape(CONVK, WIDTH), ((0, 8 - CONVK), (0, 0)))
        scal = jnp.pad(vector[taps_size:norm_at][None], ((0, 7), (0, 126)))
        small.append((taps, scal, vector[norm_at:gain_at]))
        gains.append((gains_all[layer, 0], gains_all[layer, 1]))
        weights.append(
            (
                spread_rows(proj_parts[layer]),
                mix_all[:, layer].reshape(2 * slices, model_width),
                spread_cols(out_parts[layer]),
                spread_rows(gu_parts[layer]),
                spread_cols(down_parts[layer]),
            )
        )

    def my_tokens(value):
        mine = lax.dynamic_slice_in_dim(value, piece * sub, sub, 0)
        return halved(gathered(mine, "seq"))

    aux = make_aux(doc_starts[core], length)
    resid = my_tokens(tokens[core]).astype(jnp.float32)
    masked = cotangent[core] * valid_mask[core].astype(jnp.bfloat16)[:, None]
    upstream = my_tokens(masked).astype(jnp.float32)

    def stats(values):
        return jnp.stack([jnp.sum(valid * jnp.mean(v * v, axis=-1)) for v in values])

    out0, attn0, ffn0, saved0 = layer_forward(resid, gains[0], weights[0], small[0], aux, parts)
    stats0 = stats((out0, attn0, ffn0))
    h1 = out0.astype(jnp.bfloat16)
    out1, attn1, ffn1, saved1 = layer_forward(
        h1.astype(jnp.float32), gains[1], weights[1], small[1], aux, parts
    )
    stats1 = stats((out1, attn1, ffn1))
    act1 = out1.astype(jnp.bfloat16)

    grad_h1, big1, small1 = layer_backward_fast(
        upstream, saved1, gains[1], weights[1], small[1], aux, parts
    )
    grad_h1 = grad_h1.astype(jnp.bfloat16)
    grad_tokens, big0, small0 = layer_backward_fast(
        grad_h1.astype(jnp.float32), saved0, gains[0], weights[0], small[0], aux, parts
    )
    grad_tokens = grad_tokens.astype(jnp.bfloat16)

    def placed_tokens(layer0, layer1):
        layer0, layer1 = (
            lax.dynamic_slice_in_dim(value, shard * sub, sub, 0) for value in (layer0, layer1)
        )
        keep = pick(first, layer0, layer1)
        received = partner(pick(first, layer1, layer0))
        both = jnp.stack([pick(first, keep, received), pick(first, received, keep)])
        pieces = jnp.stack(in_order(by_partner(both, "head"), "head"), axis=1)
        pieces = pieces.reshape(2, slices * sub, 2, shards, model_width // (2 * shards))
        return jnp.swapaxes(pieces, 2, 3).reshape(2, slices * sub, model_width)

    activations = placed_tokens(h1, act1)
    input_grads = placed_tokens(grad_tokens, grad_h1)

    def joined(layer0, layer1, axis):
        keep = pick(first, layer0, layer1)
        received = partner(pick(first, layer1, layer0))
        return jnp.concatenate(
            [pick(first, keep, received), pick(first, received, keep)], axis=axis
        ).astype(jnp.float32)

    grad_down = joined(collect_cols(big0[3]), collect_cols(big1[3]), 2)
    grad_gu = joined(collect_rows(big0[2]), collect_rows(big1[2]), 0)
    grad_out = joined(collect_cols(big0[1]), collect_cols(big1[1]), 2)
    grad_proj = joined(collect_rows(big0[0]), collect_rows(big1[0]), 0)

    def pack(grads, sums):
        dtaps, dscal, dnorm, dattn, dmlp, dmix = grads
        place = (jnp.arange(2) == core)[:, None]
        marked = jnp.where(place, jnp.concatenate([sums, jnp.sum(valid)[None]])[None], 0.0)
        return jnp.concatenate(
            [dtaps.reshape(-1), dscal, dnorm, marked.reshape(-1), dattn, dmlp, dmix.reshape(-1)]
        )

    packs = (pack(small0, stats0), pack(small1, stats1))
    vector = pick(first, packs[0], packs[1]) + partner(pick(first, packs[1], packs[0]))
    gain_end = norm_at + HEAD_V + 8 + 2 * model_width
    per_head = gathered(vector[None, :norm_at], "seq")
    sums_all = halves(vector[norm_at:gain_end], "head")
    norm_sum = halves(sums_all[:HEAD_V], "seq")
    stat_sums = sums_all[HEAD_V : HEAD_V + 8].reshape(2, 4)
    gain_sums = sums_all[HEAD_V + 8 :].reshape(2, 2, shards, shard_rows // 2)
    gain_sums = lax.dynamic_index_in_dim(gain_sums, shard, 2, False).reshape(2, shard_rows)
    branch_rms = jnp.sqrt(stat_sums[:, :3] / jnp.maximum(stat_sums[:, 3:], 1.0))
    mix_grad = vector[gain_end:].reshape(slices, 2, 2, shards, shard_rows // 2)
    mix_grad = jnp.sum(lax.all_to_all(mix_grad, "head", 0, 0), axis=0)
    mix_grad = lax.all_to_all(jnp.transpose(mix_grad, (2, 0, 1, 3)), "seq", 0, 0)
    mix_grad = jnp.transpose(mix_grad, (1, 2, 3, 0)).reshape(2, shard_rows, shards)
    conv_grad = jnp.swapaxes(per_head[:, :taps_size].reshape(shards, CONVK, WIDTH), 0, 1)

    def conv_part(start, width):
        return conv_grad[:, :, start : start + width].reshape(1, CONVK, shards * width)

    def proj_part(start, width):
        return grad_proj[:, :, start : start + width].reshape(1, shard_rows, shards * width)

    def gu_part(start):
        return grad_gu[:, :, start : start + hidden_width].reshape(1, shard_rows, shards * hidden_width)

    return (
        activations[None],
        input_grads[None],
        branch_rms[None],
        gain_sums[0][None],
        proj_part(0, HEAD_K),
        proj_part(HEAD_K, HEAD_K),
        proj_part(2 * HEAD_K, HEAD_V),
        proj_part(2 * HEAD_K + HEAD_V, HEAD_V),
        mix_grad[0][None],
        mix_grad[1][None],
        conv_part(0, HEAD_K),
        conv_part(HEAD_K, HEAD_K),
        conv_part(2 * HEAD_K, HEAD_V),
        per_head[:, taps_size][None],
        per_head[:, taps_size + 1][None],
        norm_sum[None],
        grad_out.reshape(1, shards * HEAD_V, shard_rows),
        gain_sums[1][None],
        gu_part(0),
        gu_part(hidden_padded),
        grad_down[:, :hidden_width].reshape(1, shards * hidden_width, shard_rows),
    )


def per_device(*args):
    tokens, w_decay = args[0], args[9]
    rows = tokens.shape[1]
    seq, head, section = (lax.axis_size(axis) for axis in ("seq", "head", "section"))
    one_head_each = w_decay.shape[2] == seq
    micro_each = tokens.shape[0] == section == 2
    powers = seq & (seq - 1) == 0 and head & (head - 1) == 0
    even = rows % (head * BLOCK) == 0 and rows * seq % (BLOCK * GROUP) == 0
    if one_head_each and micro_each and powers and even:
        return fast_shards(*args)
    return shards(*args)


def solution(mesh):
    placed = (
        P(None, "seq", None),
        P(None, "seq", None),
        P(),
        P(None, "seq"),
        P("section", "seq"),
        P("section", "seq", "head"),
        P("section", "seq", "head"),
        P("section", "seq", "head"),
        P("section", "seq", "head"),
        P("section", "seq", "head"),
        P("section", "seq", "head"),
        P("section", None, "head"),
        P("section", None, "head"),
        P("section", None, "head"),
        P("section", "head"),
        P("section", "head"),
        P("section", None),
        P("section", "head", "seq"),
        P("section", "seq"),
        P("section", "seq", "head"),
        P("section", "seq", "head"),
        P("section", "head", "seq"),
    )
    return jax.shard_map(
        per_device,
        mesh=mesh,
        in_specs=placed,
        out_specs=(
            P("section", None, "seq", None),
            P("section", None, "seq", None),
            P("section", None, None),
            P("section", "seq"),
            P("section", "seq", "head"),
            P("section", "seq", "head"),
            P("section", "seq", "head"),
            P("section", "seq", "head"),
            P("section", "seq", "head"),
            P("section", "seq", "head"),
            P("section", None, "head"),
            P("section", None, "head"),
            P("section", None, "head"),
            P("section", "head"),
            P("section", "head"),
            P("section", None),
            P("section", "head", "seq"),
            P("section", "seq"),
            P("section", "seq", "head"),
            P("section", "seq", "head"),
            P("section", "head", "seq"),
        ),
        check_vma=False,
    )
```

```python
import functools

import jax
import jax.numpy as jnp
from jax import lax
from jax.experimental import pallas as pl
from jax.experimental.pallas import tpu as pltpu
from jax.sharding import PartitionSpec as P

HEAD_K = 128
HEAD_V = 256
CONVK = 4
BLOCK = 64
RECUR_FLOPS = 40_000_000
VMEM_LIMIT = 48 * 1024 * 1024
HALO = 8
EXTRA = 128
GROUP = 4


epsilon = 1e-06
highest_precision = lax.Precision.HIGHEST


def swapped(value, axis, stride):
    return lax.ppermute(value, axis, [(i, i ^ 1 << stride) for i in range(lax.axis_size(axis))])


def carried_in(value, axis, combine, identity):
    devices, position = (lax.axis_size(axis), lax.axis_index(axis))
    everything = jax.tree.map(
        lambda part, kind: lax.all_gather(part.astype(kind), axis),
        value,
        (jnp.bfloat16, jnp.bfloat16),
    )
    start = jax.tree.map(
        lambda part, zero: jnp.broadcast_to(jnp.asarray(zero, part.dtype), part.shape),
        value,
        identity,
    )

    def step(k, before):
        reached = k < position
        new = combine(
            before, jax.tree.map(lambda part, own: part[k].astype(own.dtype), everything, value)
        )
        return jax.tree.map(lambda a, b: jnp.where(reached, a, b), new, before)

    return lax.fori_loop(0, devices, step, start)


def entering(value, axis, join, neutral):
    count = lax.axis_size(axis)
    place = lax.axis_index(axis)
    ahead = count - 1 - place
    gathered = jax.tree.map(
        lambda a, kind: lax.all_gather(a.astype(kind), axis),
        value,
        jax.tree.map(lambda a: jnp.bfloat16 if a.dtype == jnp.float32 else a.dtype, value),
    )
    state = jax.tree.map(lambda a, e: jnp.zeros_like(a) + jnp.asarray(e, a.dtype), value, neutral)

    def one(step, state):
        source = count - 1 - step
        return join(
            state,
            jax.tree.map(
                lambda a, own: lax.dynamic_index_in_dim(a, source, 0, False).astype(own.dtype),
                gathered,
                value,
            ),
        )

    return lax.fori_loop(0, ahead, one, state)


def passed_along(value, axis, steps):
    count = lax.axis_size(axis)
    first, last = (max(0, -steps), min(count, count - steps))
    return lax.ppermute(value, axis, [(source, source + steps) for source in range(first, last)])


def rms_norm(values, weight):
    return values * lax.rsqrt(jnp.mean(values * values, axis=-1, keepdims=True) + epsilon) * weight


def doc_index(starts, positions):
    counted = jnp.sum(
        (starts[None, :] <= positions[:, None]).astype(jnp.int32), axis=1, dtype=jnp.int32
    )
    return counted - 1


def unit_rows(values):
    return values * lax.rsqrt(jnp.sum(values * values, axis=-1, keepdims=True) + epsilon)


def conv_front(extended, doc_ext, conv_weight):
    length = extended.shape[0] - (CONVK - 1)
    summed = jnp.zeros((length, extended.shape[1]), extended.dtype)
    for tap_index in range(CONVK):
        same_doc = doc_ext[tap_index : tap_index + length] == doc_ext[CONVK - 1 :]
        summed = (
            summed
            + jnp.where(same_doc[:, None], extended[tap_index : tap_index + length], 0.0)
            * conv_weight[tap_index]
        )
    return jax.nn.silu(summed)


def heads_front(extended, doc_ext, mix_pre, conv_weight, decay_scale, decay_shift, head_count):
    activated = conv_front(extended, doc_ext, conv_weight)
    length = activated.shape[0]
    width_k = head_count * HEAD_K
    queries = unit_rows(activated[:, :width_k].reshape(length, head_count, HEAD_K)) * HEAD_K ** (
        -0.5
    )
    key_rows = unit_rows(activated[:, width_k : 2 * width_k].reshape(length, head_count, HEAD_K))
    value_rows = activated[:, 2 * width_k :].reshape(length, head_count, HEAD_V)
    write_rate = jax.nn.sigmoid(mix_pre[:, head_count:])
    log_decay = -jnp.exp(decay_scale) * jax.nn.softplus(mix_pre[:, :head_count] + decay_shift)
    return (queries, key_rows, value_rows, write_rate, log_decay)


def block_terms(queries, key_rows, value_rows, write_rate, log_decay, doc_ids, prev_doc):
    length = queries.shape[1]
    cumulated = jnp.cumsum(log_decay, axis=1)
    row_iota = lax.broadcasted_iota(jnp.int32, (length, length), 0)
    col_iota = lax.broadcasted_iota(jnp.int32, (length, length), 1)
    same_doc = (doc_ids[:, :, None] == doc_ids[:, None, :]) & (col_iota <= row_iota)[None]
    same_mask = same_doc[:, :, :, None]
    exponent = jnp.where(same_mask, cumulated[:, :, None, :] - cumulated[:, None, :, :], 0.0)
    decay_full = jnp.where(same_mask, jnp.exp(exponent), 0.0)
    initial_decay = jnp.where((doc_ids == prev_doc[:, None])[:, :, None], jnp.exp(cumulated), 0.0)
    decay_heads = jnp.transpose(decay_full, (0, 3, 1, 2))
    key_gram = jnp.einsum("nthk,nihk->nhti", key_rows, key_rows, precision=highest_precision)
    strict_mask = (col_iota < row_iota)[None, None]
    lower_part = jnp.where(
        strict_mask,
        jnp.transpose(write_rate, (0, 2, 1))[:, :, :, None] * decay_heads * key_gram,
        0.0,
    )
    system = lower_part + jnp.eye(length, dtype=lower_part.dtype)
    scaled_values = jnp.transpose(write_rate[..., None] * value_rows, (0, 2, 1, 3))
    scaled_keys = jnp.transpose((write_rate * initial_decay)[..., None] * key_rows, (0, 2, 1, 3))
    resolved_values = lax.linalg.triangular_solve(
        system, scaled_values, left_side=True, lower=True, unit_diagonal=True
    )
    resolved_keys = lax.linalg.triangular_solve(
        system, scaled_keys, left_side=True, lower=True, unit_diagonal=True
    )
    query_key = (
        jnp.einsum("nthk,nihk->nhti", queries, key_rows, precision=highest_precision) * decay_heads
    )
    return (resolved_values, resolved_keys, query_key, decay_heads, initial_decay)


def gate_norm(mixed_out, gate_pre, norm_weight, head_count):
    length = mixed_out.shape[0]
    per_head = mixed_out.reshape(length, head_count, HEAD_V)
    gates = gate_pre.reshape(length, head_count, HEAD_V)
    normed = rms_norm(per_head, norm_weight) * jax.nn.silu(gates)
    return normed.reshape(length, head_count * HEAD_V)


def summary(
    extended, mix_pre, conv_weight, decay_scale, decay_shift, doc_ext, prev_docs, head_count
):
    queries, key_rows, value_rows, write_rate, log_decay = heads_front(
        extended, doc_ext, mix_pre, conv_weight, decay_scale, decay_shift, head_count
    )
    length = write_rate.shape[0]
    blocks = length // BLOCK

    def as_blocks(values):
        return values.reshape((blocks, BLOCK) + values.shape[1:])

    block_query_rows = as_blocks(queries)
    block_key_rows = as_blocks(key_rows)
    resolved_values, resolved_keys, query_key, decay_heads, initial_decay = block_terms(
        block_query_rows,
        block_key_rows,
        as_blocks(value_rows),
        as_blocks(write_rate),
        as_blocks(log_decay),
        as_blocks(doc_ext[CONVK - 1 :]),
        prev_docs,
    )
    final_row = decay_heads[:, :, -1, :]
    identity = jnp.eye(HEAD_K, dtype=extended.dtype)
    transfer_blocks = initial_decay[:, -1, :][:, :, None, None] * identity - jnp.einsum(
        "nhi,nihk,nhil->nhkl", final_row, block_key_rows, resolved_keys, precision=highest_precision
    )
    add_blocks = jnp.einsum(
        "nhi,nihk,nhiv->nhkv",
        final_row,
        block_key_rows,
        resolved_values,
        precision=highest_precision,
    )
    local_out = jnp.einsum(
        "nhti,nhiv->nhtv", query_key, resolved_values, precision=highest_precision
    )
    response = jnp.transpose(initial_decay, (0, 2, 1))[..., None] * jnp.transpose(
        block_query_rows, (0, 2, 1, 3)
    ) - jnp.einsum("nhti,nhik->nhtk", query_key, resolved_keys, precision=highest_precision)
    carry_map = jnp.broadcast_to(identity, (head_count, HEAD_K, HEAD_K))
    carried_addend = jnp.zeros((head_count, HEAD_K, HEAD_V), extended.dtype)
    entry_maps = []
    entry_adds = []
    for block_number in range(blocks):
        entry_maps.append(carry_map)
        entry_adds.append(carried_addend)
        carried_addend = (
            jnp.einsum(
                "jme,jed->jmd",
                transfer_blocks[block_number],
                carried_addend,
                precision=highest_precision,
            )
            + add_blocks[block_number]
        )
        carry_map = jnp.einsum(
            "hkl,hlm->hkm", transfer_blocks[block_number], carry_map, precision=highest_precision
        )
    kept = (local_out, response, jnp.stack(entry_maps), jnp.stack(entry_adds))
    return (carry_map, carried_addend, kept)


def finish(kept, running_state):
    local_out, response, entry_maps, entry_adds = kept
    entry_states = (
        jnp.einsum("nhkl,hlv->nhkv", entry_maps, running_state, precision=highest_precision)
        + entry_adds
    )
    result = local_out + jnp.einsum(
        "nhck,nhkv->nhcv", response, entry_states, precision=highest_precision
    )
    blocks, head_count, length, width_v = result.shape
    return jnp.transpose(result, (0, 2, 1, 3)).reshape(blocks * length, head_count * width_v)


def compose(earlier_blocks, later_blocks):
    return (
        jnp.einsum("hkl,hlm->hkm", later_blocks[0], earlier_blocks[0], precision=highest_precision),
        jnp.einsum("jme,jed->jmd", later_blocks[0], earlier_blocks[1], precision=highest_precision)
        + later_blocks[1],
    )


def head_total(values):
    return lax.psum(values.astype(jnp.bfloat16), "head").astype(jnp.float32)


def partner(values):
    return swapped(values, "section", 0)


def proj_t(left, right):
    return lax.dot_general(
        left, right, (((1,), (1,)), ((), ())), preferred_element_type=jnp.float32
    )


def inner_t(left, right):
    return lax.dot_general(
        left, right, (((0,), (0,)), ((), ())), preferred_element_type=jnp.float32
    )


def spread(rows_grads, cols_grads):
    rows_part = (
        lax.psum_scatter(
            rows_grads[0].astype(jnp.bfloat16), "seq", scatter_dimension=0, tiled=True
        ).astype(jnp.float32),
        lax.psum_scatter(
            rows_grads[1].astype(jnp.bfloat16), "seq", scatter_dimension=0, tiled=True
        ).astype(jnp.float32),
        lax.psum_scatter(
            rows_grads[2].astype(jnp.bfloat16), "seq", scatter_dimension=0, tiled=True
        ).astype(jnp.float32),
        lax.psum_scatter(
            rows_grads[3].astype(jnp.bfloat16), "seq", scatter_dimension=0, tiled=True
        ).astype(jnp.float32),
        lax.psum_scatter(
            rows_grads[4].astype(jnp.bfloat16), "seq", scatter_dimension=0, tiled=True
        ).astype(jnp.float32),
    )
    cols_part = (
        lax.psum_scatter(
            cols_grads[0].astype(jnp.bfloat16), "seq", scatter_dimension=1, tiled=True
        ).astype(jnp.float32),
        lax.psum_scatter(
            cols_grads[1].astype(jnp.bfloat16), "seq", scatter_dimension=1, tiled=True
        ).astype(jnp.float32),
    )
    return (rows_part, cols_part)


def shards(
    tokens,
    cotangent,
    doc_starts,
    valid_mask,
    gain_attn,
    w_query,
    w_key,
    w_value,
    w_gate_out,
    w_decay,
    w_beta,
    conv_query,
    conv_key,
    conv_value,
    decay_log,
    decay_bias,
    out_norm,
    w_output,
    gain_mlp,
    w_gate,
    w_up,
    w_down,
):
    micro_count = tokens.shape[0]
    row_count = tokens.shape[1]
    model_width = tokens.shape[2]
    head_count = w_decay.shape[2]
    width_qk = w_query.shape[2]
    width_qkv = 2 * width_qk + w_value.shape[2]
    hidden_width = w_gate.shape[2]
    block_count = row_count // BLOCK
    section_index = lax.axis_index("section")
    shard_index = lax.axis_index("seq")
    full_rows = (
        lax.all_gather(gain_attn[0], "seq", axis=0, tiled=True),
        lax.all_gather(gain_mlp[0], "seq", axis=0, tiled=True),
        lax.all_gather(w_query[0], "seq", axis=0, tiled=True),
        lax.all_gather(w_key[0], "seq", axis=0, tiled=True),
        lax.all_gather(w_value[0], "seq", axis=0, tiled=True),
        lax.all_gather(w_gate_out[0], "seq", axis=0, tiled=True),
        lax.all_gather(w_decay[0], "seq", axis=0, tiled=True),
        lax.all_gather(w_beta[0], "seq", axis=0, tiled=True),
        lax.all_gather(w_gate[0], "seq", axis=0, tiled=True),
        lax.all_gather(w_up[0], "seq", axis=0, tiled=True),
    )
    full_cols = (
        lax.all_gather(w_output[0], "seq", axis=1, tiled=True),
        lax.all_gather(w_down[0], "seq", axis=1, tiled=True),
    )
    attn_gain = full_rows[0].astype(jnp.float32)
    mlp_gain = full_rows[1].astype(jnp.float32)
    proj_weight = jnp.concatenate([full_rows[2], full_rows[3], full_rows[4], full_rows[5]], axis=1)
    mix_weight = jnp.concatenate([full_rows[6], full_rows[7]], axis=1).astype(jnp.float32)
    gate_up_weight = jnp.concatenate([full_rows[8], full_rows[9]], axis=1)
    out_weight = full_cols[0]
    down_weight = full_cols[1]
    conv_weight = jnp.concatenate([conv_query[0], conv_key[0], conv_value[0]], axis=1).astype(
        jnp.float32
    )
    decay_scale = decay_log[0]
    decay_shift = decay_bias[0]
    norm_weight = out_norm[0].astype(jnp.float32)
    ext_pos = (
        shard_index * row_count - (CONVK - 1) + jnp.arange(row_count + CONVK - 1, dtype=jnp.int32)
    )
    block_pos = shard_index * row_count + jnp.arange(block_count, dtype=jnp.int32) * BLOCK - 1

    def carry_backward(shard_map_t, shard_adj):
        identity = jnp.broadcast_to(
            jnp.eye(shard_map_t.shape[1], dtype=jnp.float32), shard_map_t.shape
        )
        suffix = entering(
            (shard_map_t, shard_adj), "seq", compose, (identity, jnp.zeros_like(shard_adj))
        )
        result = suffix[1]
        return result

    def layer_backward(saved, upstream, starts):
        (
            resid_in,
            normed,
            mix_pre,
            extended,
            gate_pre,
            kept,
            running_state,
            shard_map,
            mixed_out,
            gated,
            resid_mid,
            ffn_in,
            gate_up,
            hidden,
        ) = saved
        doc_ext = doc_index(starts, ext_pos)
        prev_docs = doc_index(starts, block_pos)
        grad_ffn = upstream.astype(jnp.bfloat16)
        grad_hidden = proj_t(grad_ffn, down_weight)
        grad_down = inner_t(hidden, grad_ffn)
        _, act_back = jax.vjp(
            lambda gate_in, up_in: jax.nn.silu(gate_in) * up_in,
            gate_up[:, :hidden_width],
            gate_up[:, hidden_width:],
        )
        grad_gate, grad_up = act_back(grad_hidden)
        grad_gate_up = jnp.concatenate([grad_gate, grad_up], axis=1).astype(jnp.bfloat16)
        grad_gu_weight = inner_t(ffn_in, grad_gate_up)
        grad_ffn_in = head_total(proj_t(grad_gate_up, gate_up_weight))
        _, mlp_norm_back = jax.vjp(rms_norm, resid_mid, mlp_gain)
        grad_mid_norm, grad_mlp_gain = mlp_norm_back(grad_ffn_in)
        grad_mid = upstream + grad_mid_norm
        grad_attn = grad_mid.astype(jnp.bfloat16)
        grad_gated = proj_t(grad_attn, out_weight)
        grad_out_weight = inner_t(gated, grad_attn)
        _, gate_back = jax.vjp(
            lambda mixed_in, gate_in, weight_in: gate_norm(
                mixed_in, gate_in, weight_in, head_count
            ),
            mixed_out,
            gate_pre,
            norm_weight,
        )
        grad_mixed, grad_gate_pre, grad_norm_weight = gate_back(grad_gated)
        _, finish_back = jax.vjp(finish, kept, running_state)
        grad_kept, grad_state = finish_back(grad_mixed)
        later_blocks = carry_backward(jnp.swapaxes(shard_map, 1, 2), grad_state)
        gradient_transfer = jnp.einsum(
            "rgm,ram->rga", later_blocks, running_state, precision=highest_precision
        )

        def local_summary(ext_in, mix_in, conv_in, scale_in, shift_in):
            return summary(
                ext_in, mix_in, conv_in, scale_in, shift_in, doc_ext, prev_docs, head_count
            )

        _, summary_back = jax.vjp(
            local_summary, extended, mix_pre, conv_weight, decay_scale, decay_shift
        )
        grad_ext, grad_mix, grad_conv, grad_scale, grad_shift = summary_back(
            (gradient_transfer, later_blocks, grad_kept)
        )
        returned = passed_along(grad_ext[: CONVK - 1], "seq", -1)
        grad_qkv = grad_ext[CONVK - 1 :] + jnp.pad(returned, ((row_count - (CONVK - 1), 0), (0, 0)))
        grad_pre = jnp.concatenate([grad_qkv, grad_gate_pre], axis=1).astype(jnp.bfloat16)
        grad_proj_weight = inner_t(normed, grad_pre)
        normed_float = normed.astype(jnp.float32)
        grad_mix_weight = lax.dot_general(
            normed_float, grad_mix, (((0,), (0,)), ((), ())), precision=highest_precision
        )
        grad_normed = head_total(
            proj_t(grad_pre, proj_weight)
            + lax.dot_general(
                grad_mix, mix_weight, (((1,), (1,)), ((), ())), precision=highest_precision
            )
        )
        _, attn_norm_back = jax.vjp(rms_norm, resid_in.astype(jnp.float32), attn_gain)
        grad_resid_norm, grad_attn_gain = attn_norm_back(grad_normed)
        grad_resid = grad_mid + grad_resid_norm
        rows_grads = (
            grad_attn_gain,
            grad_mlp_gain,
            grad_proj_weight,
            grad_mix_weight,
            grad_gu_weight,
        )
        cols_grads = (grad_out_weight, grad_down)
        small_grads = (grad_conv, grad_scale, grad_shift, grad_norm_weight)
        return (grad_resid, rows_grads, cols_grads, small_grads)

    zero_in = jnp.zeros((row_count, model_width), jnp.bfloat16)
    incoming = zero_in
    stored = None
    activations_buf = jnp.zeros(tokens.shape, jnp.bfloat16)
    stat_sums = jnp.zeros((micro_count, 3), jnp.float32)
    stat_counts = jnp.zeros((micro_count,), jnp.float32)
    for slot_index in range(micro_count + 1):
        chosen_raw = slot_index - section_index
        active = (chosen_raw >= 0) & (chosen_raw < micro_count)
        chosen = jnp.clip(chosen_raw, 0, micro_count - 1)
        resid_in = jnp.where(section_index == 0, tokens[min(slot_index, micro_count - 1)], incoming)
        layer_starts = doc_starts[chosen]
        layer_doc_ext = doc_index(layer_starts, ext_pos)
        layer_prev_docs = doc_index(layer_starts, block_pos)
        resid = resid_in.astype(jnp.float32)
        layer_normed = rms_norm(resid, attn_gain).astype(jnp.bfloat16)
        projected = jnp.dot(layer_normed, proj_weight, preferred_element_type=jnp.float32)
        layer_mix_pre = jnp.dot(
            layer_normed.astype(jnp.float32), mix_weight, precision=highest_precision
        )
        qkv_pre = projected[:, :width_qkv]
        layer_gate_pre = projected[:, width_qkv:]
        rim_rows = passed_along(qkv_pre[row_count - (CONVK - 1) :], "seq", 1)
        layer_extended = jnp.concatenate([rim_rows, qkv_pre], axis=0)
        layer_shard_map, layer_shard_add, layer_kept = summary(
            layer_extended,
            layer_mix_pre,
            conv_weight,
            decay_scale,
            decay_shift,
            layer_doc_ext,
            layer_prev_docs,
            head_count,
        )
        carry_identity = jnp.broadcast_to(
            jnp.eye(layer_shard_map.shape[1], dtype=jnp.float32), layer_shard_map.shape
        )
        prefix = carried_in(
            (layer_shard_map, layer_shard_add),
            "seq",
            compose,
            (carry_identity, jnp.zeros_like(layer_shard_add)),
        )
        carry_result = prefix[1]
        layer_mixed_out = finish(layer_kept, carry_result)
        layer_gated = gate_norm(layer_mixed_out, layer_gate_pre, norm_weight, head_count).astype(
            jnp.bfloat16
        )
        attn = head_total(jnp.dot(layer_gated, out_weight, preferred_element_type=jnp.float32))
        layer_resid_mid = resid + attn
        layer_ffn_in = rms_norm(layer_resid_mid, mlp_gain).astype(jnp.bfloat16)
        layer_gate_up = jnp.dot(layer_ffn_in, gate_up_weight, preferred_element_type=jnp.float32)
        layer_hidden = (
            jax.nn.silu(layer_gate_up[:, :hidden_width]) * layer_gate_up[:, hidden_width:]
        ).astype(jnp.bfloat16)
        ffn = head_total(jnp.dot(layer_hidden, down_weight, preferred_element_type=jnp.float32))
        layer_out = layer_resid_mid + ffn
        layer_saved = (
            resid_in,
            layer_normed,
            layer_mix_pre,
            layer_extended,
            layer_gate_pre,
            layer_kept,
            carry_result,
            layer_shard_map,
            layer_mixed_out,
            layer_gated,
            layer_resid_mid,
            layer_ffn_in,
            layer_gate_up,
            layer_hidden,
        )
        saved, layer_out, attn_out, ffn_out = (layer_saved, layer_out, attn, ffn)
        if stored is None:
            stored = jax.tree.map(
                lambda part_new: jnp.zeros((micro_count,) + part_new.shape, part_new.dtype), saved
            )
        stored = jax.tree.map(
            lambda buffer, part_new: buffer.at[chosen].set(
                jnp.where(active, part_new, buffer[chosen])
            ),
            stored,
            saved,
        )
        outgoing = layer_out.astype(jnp.bfloat16)
        activations_buf = activations_buf.at[chosen].set(
            jnp.where(active, outgoing, activations_buf[chosen])
        )
        weights_valid = valid_mask[chosen].astype(jnp.float32)
        sums_now = jnp.stack(
            [
                jnp.sum(weights_valid * jnp.mean(branch_val * branch_val, axis=-1))
                for branch_val in (layer_out, attn_out, ffn_out)
            ]
        )
        stat_sums = stat_sums.at[chosen].set(jnp.where(active, sums_now, stat_sums[chosen]))
        stat_counts = stat_counts.at[chosen].set(
            jnp.where(active, jnp.sum(weights_valid), stat_counts[chosen])
        )
        if slot_index < micro_count:
            incoming = partner(outgoing)
    rows_acc = None
    cols_acc = None
    small_acc = None
    back_in = zero_in
    grad_inputs = jnp.zeros(tokens.shape, jnp.bfloat16)
    for slot_index in range(micro_count + 1):
        chosen_raw = slot_index - (1 - section_index)
        active = (chosen_raw >= 0) & (chosen_raw < micro_count)
        chosen = jnp.clip(chosen_raw, 0, micro_count - 1)
        saved = jax.tree.map(lambda buffer: buffer[chosen], stored)
        from_loss = (
            cotangent[chosen].astype(jnp.float32) * valid_mask[chosen].astype(jnp.float32)[:, None]
        )
        upstream = jnp.where(section_index == 1, from_loss, back_in.astype(jnp.float32))
        grad_resid, rows_grads, cols_grads, small_grads = layer_backward(
            saved, upstream, doc_starts[chosen]
        )
        rows_grads = jax.tree.map(lambda grad_part: jnp.where(active, grad_part, 0.0), rows_grads)
        cols_grads = jax.tree.map(lambda grad_part: jnp.where(active, grad_part, 0.0), cols_grads)
        small_grads = jax.tree.map(lambda grad_part: jnp.where(active, grad_part, 0.0), small_grads)
        if rows_acc is None:
            rows_acc, cols_acc, small_acc = (rows_grads, cols_grads, small_grads)
        else:
            rows_acc = jax.tree.map(jnp.add, rows_acc, rows_grads)
            cols_acc = jax.tree.map(jnp.add, cols_acc, cols_grads)
            small_acc = jax.tree.map(jnp.add, small_acc, small_grads)
        outgoing = grad_resid.astype(jnp.bfloat16)
        grad_inputs = grad_inputs.at[chosen].set(jnp.where(active, outgoing, grad_inputs[chosen]))
        if slot_index < micro_count:
            back_in = partner(outgoing)
    rows_part, cols_part = spread(rows_acc, cols_acc)
    norm_heads = lax.psum(small_acc[3], "head")
    conv_sum, scale_sum, shift_sum, norm_sum, sums_all, counts_all = (
        lax.psum(small_acc[0].astype(jnp.bfloat16), "seq").astype(jnp.float32),
        lax.psum(small_acc[1].astype(jnp.bfloat16), "seq").astype(jnp.float32),
        lax.psum(small_acc[2].astype(jnp.bfloat16), "seq").astype(jnp.float32),
        lax.psum(norm_heads.astype(jnp.bfloat16), "seq").astype(jnp.float32),
        lax.psum(stat_sums.astype(jnp.bfloat16), "seq").astype(jnp.float32),
        lax.psum(stat_counts.astype(jnp.bfloat16), "seq").astype(jnp.float32),
    )
    branch_rms = jnp.sqrt(sums_all / jnp.maximum(counts_all, 1.0)[:, None])
    proj_part = rows_part[2]
    mix_part = rows_part[3]
    gu_part = rows_part[4]
    return (
        activations_buf[None],
        grad_inputs[None],
        branch_rms[None],
        rows_part[0][None],
        proj_part[:, :width_qk][None],
        proj_part[:, width_qk : 2 * width_qk][None],
        proj_part[:, 2 * width_qk : width_qkv][None],
        proj_part[:, width_qkv:][None],
        mix_part[:, :head_count][None],
        mix_part[:, head_count:][None],
        conv_sum[:, :width_qk][None],
        conv_sum[:, width_qk : 2 * width_qk][None],
        conv_sum[:, 2 * width_qk :][None],
        scale_sum[None],
        shift_sum[None],
        norm_sum[None],
        cols_part[0][None],
        rows_part[1][None],
        gu_part[:, :hidden_width][None],
        gu_part[:, hidden_width:][None],
        cols_part[1][None],
    )


exact = lax.Precision.HIGHEST


def dot_nn(a, b):
    return lax.dot_general(
        a, b, (((1,), (0,)), ((), ())), precision=exact, preferred_element_type=jnp.float32
    )


def dot_nt(a, b):
    return lax.dot_general(
        a, b, (((1,), (1,)), ((), ())), precision=exact, preferred_element_type=jnp.float32
    )


def dot_tn(a, b):
    return lax.dot_general(
        a, b, (((0,), (0,)), ((), ())), precision=exact, preferred_element_type=jnp.float32
    )


@functools.partial(jax.custom_vjp, nondiff_argnums=(1,))
def shifted(window, steps):
    if steps == 0:
        return window[HALO:]
    return pltpu.roll(window, steps, 0)[HALO:]


def shifted_fwd(window, steps):
    return shifted(window, steps), None


def shifted_bwd(steps, _, grad):
    padded = jnp.concatenate([jnp.zeros((HALO, grad.shape[1]), grad.dtype), grad], axis=0)
    if steps == 0:
        return (padded,)
    return (pltpu.roll(padded, padded.shape[0] - steps, 0),)


shifted.defvjp(shifted_fwd, shifted_bwd)


def iotas(length):
    rows = lax.broadcasted_iota(jnp.int32, (length, length), 0)
    cols = lax.broadcasted_iota(jnp.int32, (length, length), 1)
    return rows, cols


def as_row(column):
    rows, cols = iotas(column.shape[0])
    return jnp.sum(jnp.where(rows == cols, column, 0.0), axis=0, keepdims=True)


def unit_inverse(lower):
    length = lower.shape[0]
    rows, cols = iotas(length)
    near = jnp.where((rows >> 3) == (cols >> 3), lower, 0.0)
    result = jnp.where(rows == cols, 1.0, 0.0) - near
    square = dot_nn(near, near)
    result = result + dot_nn(result, square)
    result = result + dot_nn(result, dot_nn(square, square))
    shift = 3
    while (1 << shift) < length:
        off = ((rows >> (shift + 1)) == (cols >> (shift + 1))) & ((rows >> shift) != (cols >> shift))
        result = result - dot_nn(result, dot_nn(jnp.where(off, lower, 0.0), result))
        shift += 1
    return result


@jax.custom_vjp
def inverse_known(lower, inverse):
    return inverse


def inverse_known_fwd(lower, inverse):
    return inverse, inverse


def inverse_known_bwd(inverse, grad):
    return -dot_nt(dot_tn(inverse, grad), inverse), jnp.zeros_like(grad)


inverse_known.defvjp(inverse_known_fwd, inverse_known_bwd)


def silu(values):
    return values / (1.0 + jnp.exp(-values))


def sigmoid(values):
    return 1.0 / (1.0 + jnp.exp(-values))


@jax.custom_vjp
def softplus(values):
    return jnp.maximum(values, 0.0) + jnp.log1p(jnp.exp(-jnp.abs(values)))


def softplus_fwd(values):
    return softplus(values), values


def softplus_bwd(values, grad):
    return (grad * sigmoid(values),)


softplus.defvjp(softplus_fwd, softplus_bwd)


def block_front(window, mix_decay, mix_write, taps, decay_log, decay_bias, aux):
    summed = shifted(window, 0) * taps[3]
    for steps in range(1, CONVK):
        summed = summed + jnp.where(aux[:, steps : steps + 1] > 0.0, shifted(window, steps), 0.0) * taps[3 - steps]
    active = silu(summed)
    queries = unit_rows(active[:, :HEAD_K]) * HEAD_K ** (-0.5)
    keys = unit_rows(active[:, HEAD_K : 2 * HEAD_K])
    values = active[:, 2 * HEAD_K :]
    write = sigmoid(mix_write)
    log_decay = -jnp.exp(decay_log) * softplus(mix_decay + decay_bias)
    rows, cols = iotas(BLOCK)
    cum = jnp.sum(jnp.where(cols <= rows, as_row(log_decay), 0.0), axis=1, keepdims=True)
    total = jnp.sum(log_decay, axis=0, keepdims=True)
    doc = aux[:, 0:1]
    same = (doc == as_row(doc)) & (cols <= rows)
    decay = jnp.where(same, jnp.exp(jnp.where(same, cum - as_row(cum), 0.0)), 0.0)
    entry = jnp.where(aux[:, 4:5] > 0.0, jnp.exp(cum), 0.0)
    leave = jnp.where(aux[:, 5:6] > 0.0, jnp.exp(total - cum), 0.0)
    through = jnp.where(aux[BLOCK - 1 : BLOCK, 4:5] > 0.0, jnp.exp(total), 0.0)
    grams = dot_nt(jnp.concatenate([keys, queries], axis=0), keys)
    lower = jnp.where(cols < rows, write * decay * grams[:BLOCK], 0.0)
    mixing = grams[BLOCK:] * decay
    scaled = jnp.concatenate([write * values, (write * entry) * keys], axis=1)
    return lower, mixing, scaled, entry * queries, leave * keys, through


def block_step(window, mix_decay, mix_write, taps, decay_log, decay_bias, state, aux, inverse):
    lower, mixing, scaled, queries, keys, through = block_front(
        window, mix_decay, mix_write, taps, decay_log, decay_bias, aux
    )
    if inverse is None:
        inverse = unit_inverse(lower)
    else:
        inverse = inverse_known(lower, inverse)
    resolved = dot_nn(inverse, scaled)
    read = dot_nn(jnp.concatenate([resolved[:, HEAD_V:], queries], axis=0), state)
    written = resolved[:, :HEAD_V] - read[:BLOCK]
    mixed = read[BLOCK:] + dot_nn(mixing, written)
    return mixed, through * state + dot_tn(keys, written), inverse


def stored_at(number, blocks, parts):
    shards, slices = parts
    each = blocks // (shards * slices)
    shard = number // (slices * each)
    rest = number - shard * slices * each
    place = (rest // each * shards + shard) * each + rest % each
    return pl.multiple_of(place * BLOCK, BLOCK)


def fill_window(xh_ref, xbuf, parts):
    width = xbuf.shape[1]
    length = xh_ref.shape[0]
    blocks = length // BLOCK
    xbuf[0:HALO, :] = jnp.zeros((HALO, width), jnp.float32)

    def copy(index, carry):
        base = pl.multiple_of(index * BLOCK, BLOCK)
        stored = stored_at(index, blocks, parts)
        xbuf[pl.ds(base + HALO, BLOCK), :] = xh_ref[pl.ds(stored, BLOCK), :width].astype(jnp.float32)
        return carry

    lax.fori_loop(0, length // BLOCK, copy, 0)


def load_block(xh_ref, aux_ref, xbuf, base, stored):
    window = xbuf[pl.ds(base, BLOCK + HALO), :]
    mix = xh_ref[pl.ds(stored, BLOCK), xbuf.shape[1] :].astype(jnp.float32)
    aux = aux_ref[pl.ds(base, BLOCK), :]
    return window, mix[:, 0:1] + mix[:, 2:3], mix[:, 1:2] + mix[:, 3:4], aux


def load_taps(taps_ref):
    return [taps_ref[j : j + 1, :] for j in range(CONVK)]


def forward_kernel(parts, xh_ref, aux_ref, taps_ref, scal_ref, mixed_ref, states_ref, inverse_ref, xbuf, state_ref):
    fill_window(xh_ref, xbuf, parts)
    state_ref[...] = jnp.zeros_like(state_ref)
    blocks = xh_ref.shape[0] // BLOCK
    taps = load_taps(taps_ref)
    decay_log = scal_ref[0:1, 0:1]
    decay_bias = scal_ref[0:1, 1:2]

    def group(index, carry):
        state = state_ref[...]
        for inner in range(GROUP):
            number = index * GROUP + inner
            base = pl.multiple_of(number * BLOCK, BLOCK)
            stored = stored_at(number, blocks, parts)
            window, mix_decay, mix_write, aux = load_block(xh_ref, aux_ref, xbuf, base, stored)
            states_ref[number] = state
            mixed, state, inverse = block_step(
                window, mix_decay, mix_write, taps, decay_log, decay_bias, state, aux, None
            )
            mixed_ref[pl.ds(stored, BLOCK), :] = mixed.astype(mixed_ref.dtype)
            inverse_ref[pl.ds(base, BLOCK), :] = inverse
        state_ref[...] = state
        return carry

    lax.fori_loop(0, blocks // GROUP, group, 0)


def backward_kernel(
    parts, xh_ref, aux_ref, taps_ref, scal_ref, states_ref, inverse_ref, grad_ref,
    dxh_ref, dtaps_ref, dscal_ref, xbuf, adjoint_ref, halo_ref,
):
    fill_window(xh_ref, xbuf, parts)
    adjoint_ref[...] = jnp.zeros_like(adjoint_ref)
    halo_ref[...] = jnp.zeros_like(halo_ref)
    dtaps_ref[...] = jnp.zeros_like(dtaps_ref)
    dscal_ref[...] = jnp.zeros_like(dscal_ref)
    blocks = xh_ref.shape[0] // BLOCK
    width = xbuf.shape[1]
    taps = load_taps(taps_ref)
    decay_log = scal_ref[0:1, 0:1]
    decay_bias = scal_ref[0:1, 1:2]
    lanes = lax.broadcasted_iota(jnp.int32, (BLOCK, EXTRA), 1)

    def group(index, carry):
        adjoint = adjoint_ref[...]
        halo = halo_ref[...]
        dtaps = [dtaps_ref[j : j + 1, :] for j in range(CONVK)]
        dlog = dscal_ref[0:1, 0:1]
        dbias = dscal_ref[0:1, 1:2]
        for inner in range(GROUP):
            number = blocks - 1 - (index * GROUP + inner)
            base = pl.multiple_of(number * BLOCK, BLOCK)
            stored = stored_at(number, blocks, parts)
            window, mix_decay, mix_write, aux = load_block(xh_ref, aux_ref, xbuf, base, stored)
            inverse = inverse_ref[pl.ds(base, BLOCK), :]
            grad = grad_ref[pl.ds(stored, BLOCK), :].astype(jnp.float32)

            def run(*inputs):
                return block_step(*inputs, aux, inverse)[:2]

            _, pull = jax.vjp(
                run, window, mix_decay, mix_write, taps, decay_log, decay_bias, states_ref[number]
            )
            dwindow, ddecay, dwrite, dtaps_now, dlog_now, dbias_now, adjoint = pull((grad, adjoint))
            own = dwindow[HALO:]
            own = jnp.concatenate([own[: BLOCK - HALO], own[BLOCK - HALO :] + halo], axis=0)
            halo = dwindow[:HALO]
            dtaps = [a + b for a, b in zip(dtaps, dtaps_now)]
            dlog = dlog + dlog_now
            dbias = dbias + dbias_now
            dxh_ref[pl.ds(stored, BLOCK), :width] = own.astype(dxh_ref.dtype)
            high_decay = ddecay.astype(jnp.bfloat16).astype(jnp.float32)
            high_write = dwrite.astype(jnp.bfloat16).astype(jnp.float32)
            mix = jnp.where(lanes == 0, high_decay, jnp.where(lanes == 1, high_write, 0.0))
            mix = jnp.where(lanes == 2, ddecay - high_decay, jnp.where(lanes == 3, dwrite - high_write, mix))
            dxh_ref[pl.ds(stored, BLOCK), width:] = mix.astype(dxh_ref.dtype)
        adjoint_ref[...] = adjoint
        halo_ref[...] = halo
        for j in range(CONVK):
            dtaps_ref[j : j + 1, :] = dtaps[j]
        dscal_ref[0:1, 0:1] = dlog
        dscal_ref[0:1, 1:2] = dbias
        return carry

    lax.fori_loop(0, blocks // GROUP, group, 0)


WIDTH = 2 * HEAD_K + HEAD_V


def whole():
    return pl.BlockSpec(memory_space=pltpu.VMEM)


def recur_forward(xh, aux, taps, scal, parts):
    length = xh.shape[0]
    blocks = length // BLOCK
    return pl.pallas_call(
        functools.partial(forward_kernel, parts),
        out_shape=(
            jax.ShapeDtypeStruct((length, HEAD_V), jnp.bfloat16),
            jax.ShapeDtypeStruct((blocks, HEAD_K, HEAD_V), jnp.float32),
            jax.ShapeDtypeStruct((length, BLOCK), jnp.float32),
        ),
        in_specs=[whole()] * 4,
        out_specs=(whole(),) * 3,
        scratch_shapes=[
            pltpu.VMEM((length + HALO, WIDTH), jnp.float32),
            pltpu.VMEM((HEAD_K, HEAD_V), jnp.float32),
        ],
        compiler_params=pltpu.CompilerParams(vmem_limit_bytes=VMEM_LIMIT),
        cost_estimate=pl.CostEstimate(
            flops=length * RECUR_FLOPS, bytes_accessed=length * 8192, transcendentals=0
        ),
        name="recur_forward",
    )(xh, aux, taps, scal)


def recur_backward(xh, aux, taps, scal, states, inverse, grad, parts):
    length = xh.shape[0]
    return pl.pallas_call(
        functools.partial(backward_kernel, parts),
        out_shape=(
            jax.ShapeDtypeStruct((length, WIDTH + EXTRA), jnp.bfloat16),
            jax.ShapeDtypeStruct((8, WIDTH), jnp.float32),
            jax.ShapeDtypeStruct((8, 128), jnp.float32),
        ),
        in_specs=[whole()] * 7,
        out_specs=(whole(),) * 3,
        scratch_shapes=[
            pltpu.VMEM((length + HALO, WIDTH), jnp.float32),
            pltpu.VMEM((HEAD_K, HEAD_V), jnp.float32),
            pltpu.VMEM((HALO, WIDTH), jnp.float32),
        ],
        compiler_params=pltpu.CompilerParams(vmem_limit_bytes=VMEM_LIMIT),
        cost_estimate=pl.CostEstimate(
            flops=length * RECUR_FLOPS, bytes_accessed=length * 8192, transcendentals=0
        ),
        name="recur_backward",
    )(xh, aux, taps, scal, states, inverse, grad)


def make_aux(starts, length):
    positions = jnp.arange(length, dtype=jnp.int32)
    doc = jnp.sum((starts[None, :] <= positions[:, None]).astype(jnp.int32), axis=1)
    def back(steps):
        earlier = jnp.concatenate([jnp.full((steps,), -1, jnp.int32), doc[:-steps]])
        return (earlier == doc).astype(jnp.float32)
    blocks = doc.reshape(-1, BLOCK)
    before = jnp.concatenate([jnp.full((1,), -1, jnp.int32), blocks[:-1, -1]])
    entering = (blocks == before[:, None]).reshape(-1).astype(jnp.float32)
    leaving = (blocks == blocks[:, -1:]).reshape(-1).astype(jnp.float32)
    zero = jnp.zeros((length,), jnp.float32)
    return jnp.stack([doc.astype(jnp.float32), back(1), back(2), back(3), entering, leaving, zero, zero], axis=1)


def dot(left, right):
    return lax.dot_general(
        left, right, (((1,), (0,)), ((), ())), preferred_element_type=jnp.float32
    )


def in_vmem():
    return pl.BlockSpec(memory_space=pltpu.VMEM)


def in_smem():
    return pl.BlockSpec(memory_space=pltpu.SMEM)


def held(shape):
    return pl.BlockSpec(shape, lambda step: (0,) * len(shape))


def slab(shape, axis):
    return pl.BlockSpec(shape, lambda step: tuple(step if d == axis else 0 for d in range(len(shape))))


def like(shape, dtype):
    return jax.ShapeDtypeStruct(shape, dtype)


def run(kernel, grid, in_specs, out_specs, out_shape, scratch, name, flops, moved, args):
    return pl.pallas_call(
        kernel,
        grid=grid,
        in_specs=in_specs,
        out_specs=out_specs,
        out_shape=out_shape,
        scratch_shapes=scratch,
        compiler_params=pltpu.CompilerParams(vmem_limit_bytes=VMEM_LIMIT),
        cost_estimate=pl.CostEstimate(flops=flops, bytes_accessed=moved, transcendentals=0),
        name=name,
    )(*args)


def row_scale(value):
    return lax.rsqrt(jnp.mean(value * value, axis=-1, keepdims=True) + epsilon)


def mean_square(value, valid):
    return jnp.sum(valid * jnp.mean(value * value, axis=-1, keepdims=True), axis=0, keepdims=True)


def norm_adjoint(value, gain, grad):
    scale = row_scale(value)
    unit = value * scale
    scaled = grad * gain
    dvalue = scale * (scaled - unit * jnp.mean(scaled * unit, axis=-1, keepdims=True))
    return dvalue, jnp.sum(grad * unit, axis=0, keepdims=True)


def each_piece(me_ref, part_refs):
    rows = part_refs[0].shape[0]
    for number, part in enumerate(part_refs):
        start = (me_ref[0] ^ number) * rows
        yield pl.ds(pl.multiple_of(start, rows), rows), part


def put_stat(stat_ref, column, value):
    stat_ref[0:1, column : column + 1] += value


def mix_rows(mix_ref):
    mix = mix_ref[0]
    return jnp.concatenate([mix, jnp.zeros((EXTRA - mix.shape[0], mix.shape[1]), mix.dtype)], axis=0)


def project_kernel(kind, pieces, *refs):
    me_ref, valid_ref, gain_ref = refs[:3]
    part_refs = refs[3 : 3 + pieces]
    refs = refs[3 + pieces :]
    if kind == "next":
        base_ref, refs = refs[0], refs[1:]
    w_ref, mix_ref, resid_ref, normed_ref, packed_ref, gate_ref, stat_ref = refs

    @pl.when(pl.program_id(0) == 0)
    def _():
        stat_ref[...] = jnp.zeros_like(stat_ref)
        for where, part in each_piece(me_ref, part_refs):
            value = part[...].astype(jnp.float32)
            if kind == "next":
                valid = valid_ref[where, :]
                put_stat(stat_ref, 1, mean_square(value, valid))
                value = value + base_ref[where, :]
                put_stat(stat_ref, 0, mean_square(value, valid))
            rounded = value.astype(jnp.bfloat16)
            resid_ref[where, :] = rounded
            value = rounded.astype(jnp.float32)
            normed_ref[where, :] = (value * row_scale(value) * gain_ref[...]).astype(jnp.bfloat16)

    normed = normed_ref[...]
    result = dot(normed, w_ref[0])
    packed_ref[0, :, :WIDTH] = result[:, :WIDTH].astype(jnp.bfloat16)
    gate_ref[0] = result[:, WIDTH:]
    mix = proj_t(normed, mix_rows(mix_ref))
    lanes = lax.broadcasted_iota(jnp.int32, mix.shape, 1)
    low = mix - mix.astype(jnp.bfloat16).astype(jnp.float32)
    mix = jnp.where(lanes < 2, mix, jnp.where(lanes < 4, low, 0.0))
    packed_ref[0, :, WIDTH:] = mix.astype(jnp.bfloat16)


def project(me, valid, gain, parts, base, w_proj, w_mix):
    slices, width, columns = w_proj.shape
    sub = parts[0].shape[0]
    rows = sub * len(parts)
    kind = "first" if base is None else "next"
    return run(
        functools.partial(project_kernel, kind, len(parts)),
        (slices,),
        [in_smem(), held((rows, 1)), held((1, width))]
        + [held((sub, width))] * len(parts)
        + ([] if base is None else [held((rows, width))])
        + [slab((1, width, columns), 0), slab((1, 16, width), 0)],
        (
            held((rows, width)),
            held((rows, width)),
            slab((1, rows, WIDTH + EXTRA), 0),
            slab((1, rows, HEAD_V), 0),
            held((8, 128)),
        ),
        (
            like((rows, width), jnp.bfloat16),
            like((rows, width), jnp.bfloat16),
            like((slices, rows, WIDTH + EXTRA), jnp.bfloat16),
            like((slices, rows, HEAD_V), jnp.float32),
            like((8, 128), jnp.float32),
        ),
        [],
        "project_" + kind,
        2 * rows * width * columns * slices,
        w_proj.size * 2 + rows * width * 12,
        [me, valid, gain] + list(parts) + ([] if base is None else [base]) + [w_proj, w_mix],
    )


def output_kernel(mixed_ref, gate_ref, norm_ref, w_ref, gated_ref, pieces_ref):
    slices = mixed_ref.shape[0]

    @pl.when(pl.program_id(0) == 0)
    def _():
        for j in range(slices):
            value = mixed_ref[j].astype(jnp.float32)
            normed = value * row_scale(value) * norm_ref[...] * silu(gate_ref[j])
            gated_ref[:, j * HEAD_V : (j + 1) * HEAD_V] = normed.astype(jnp.bfloat16)

    result = dot(gated_ref[...], w_ref[0]).astype(jnp.bfloat16)
    pieces_ref[...] = result.reshape(pieces_ref.shape)


def output(mixed, gate_pre, norm_weight, w_out, shards):
    slices, rows, _ = mixed.shape
    _, inner, half = w_out.shape
    return run(
        output_kernel,
        (2,),
        [held(mixed.shape), held(gate_pre.shape), held((1, HEAD_V)), slab((1, inner, half), 0)],
        (held((rows, inner)), slab((shards, rows // shards, half), 2)),
        (like((rows, inner), jnp.bfloat16), like((shards, rows // shards, 2 * half), jnp.bfloat16)),
        [],
        "output",
        4 * rows * inner * half,
        w_out.size * 2 + rows * inner * 12,
        [mixed, gate_pre, norm_weight, w_out],
    )


def feed_kernel(pieces, *refs):
    me_ref, valid_ref, gain_ref = refs[:3]
    part_refs = refs[3 : 3 + pieces]
    base_ref, w_gu_ref, w_down_ref, mid_ref, normed_ref, gate_up_ref, hidden_ref, pieces_ref, stat_ref, total = refs[
        3 + pieces :
    ]
    step = pl.program_id(0)
    half = w_down_ref.shape[2]

    @pl.when(step == 0)
    def _():
        stat_ref[...] = jnp.zeros_like(stat_ref)
        total[...] = jnp.zeros_like(total)
        for where, part in each_piece(me_ref, part_refs):
            value = part[...].astype(jnp.float32)
            put_stat(stat_ref, 0, mean_square(value, valid_ref[where, :]))
            value = value + base_ref[where, :].astype(jnp.float32)
            mid_ref[where, :] = value
            normed_ref[where, :] = (value * row_scale(value) * gain_ref[...]).astype(jnp.bfloat16)

    result = dot(normed_ref[...], w_gu_ref[0])
    gate_up_ref[0] = result
    width = result.shape[1] // 2
    hidden = (silu(result[:, :width]) * result[:, width:]).astype(jnp.bfloat16)
    hidden_ref[...] = hidden
    for c in range(2):
        total[:, c * half : (c + 1) * half] += dot(hidden, w_down_ref[c])

    @pl.when(step == pl.num_programs(0) - 1)
    def _():
        pieces_ref[...] = total[...].astype(jnp.bfloat16).reshape(pieces_ref.shape)


def feed(me, valid, gain, parts, base, w_gu, w_down, shards):
    slices, width, columns = w_gu.shape
    sub = parts[0].shape[0]
    rows = sub * len(parts)
    hidden = columns // 2
    half = width // 2
    return run(
        functools.partial(feed_kernel, len(parts)),
        (slices,),
        [in_smem(), held((rows, 1)), held((1, width))]
        + [held((sub, width))] * len(parts)
        + [held((rows, width)), slab((1, width, columns), 0), slab((2, hidden, half), 1)],
        (
            held((rows, width)),
            held((rows, width)),
            slab((1, rows, columns), 0),
            slab((rows, hidden), 1),
            held((shards, rows // shards, width)),
            held((8, 128)),
        ),
        (
            like((rows, width), jnp.float32),
            like((rows, width), jnp.bfloat16),
            like((slices, rows, columns), jnp.float32),
            like((rows, slices * hidden), jnp.bfloat16),
            like((shards, rows // shards, width), jnp.bfloat16),
            like((8, 128), jnp.float32),
        ),
        [pltpu.VMEM((rows, width), jnp.float32)],
        "feed",
        2 * rows * width * (columns + hidden) * slices,
        (w_gu.size + w_down.size) * 2 + rows * width * 16,
        [me, valid, gain] + list(parts) + [base, w_gu, w_down],
    )


def close_kernel(pieces, *refs):
    me_ref, valid_ref = refs[:2]
    part_refs = refs[2 : 2 + pieces]
    base_ref, out_ref, stat_ref = refs[2 + pieces :]
    stat_ref[...] = jnp.zeros_like(stat_ref)
    for where, part in each_piece(me_ref, part_refs):
        value = part[...].astype(jnp.float32)
        valid = valid_ref[where, :]
        put_stat(stat_ref, 1, mean_square(value, valid))
        value = value + base_ref[where, :]
        put_stat(stat_ref, 0, mean_square(value, valid))
        out_ref[where, :] = value.astype(jnp.bfloat16)


def close(me, valid, parts, base):
    return run(
        functools.partial(close_kernel, len(parts)),
        (),
        [in_smem()] + [in_vmem()] * (2 + len(parts)),
        (in_vmem(), in_vmem()),
        (like(base.shape, jnp.bfloat16), like((8, 128), jnp.float32)),
        [],
        "close",
        base.size * 6,
        base.size * 8,
        [me, valid] + list(parts) + [base],
    )


def sum_kernel(pieces_ref, total_ref):
    total = pieces_ref[0].astype(jnp.float32)
    for k in range(1, pieces_ref.shape[0]):
        total = total + pieces_ref[k].astype(jnp.float32)
    total_ref[...] = total.astype(total_ref.dtype)


def sum_pieces(pieces):
    return run(
        sum_kernel,
        (),
        [in_vmem()],
        in_vmem(),
        like(pieces.shape[1:], pieces.dtype),
        [],
        "sum_pieces",
        pieces.size,
        pieces.size * 3,
        [pieces],
    )


def feed_back_kernel(up_ref, gate_up_ref, w_gu_ref, w_down_ref, grad_ref, pieces_ref, total):
    step = pl.program_id(0)
    half = w_down_ref.shape[2]
    width = gate_up_ref.shape[2] // 2
    upstream = up_ref[...]
    grad_hidden = proj_t(upstream[:, :half], w_down_ref[0]) + proj_t(upstream[:, half:], w_down_ref[1])
    gate = gate_up_ref[0, :, :width]
    up = gate_up_ref[0, :, width:]
    sig = sigmoid(gate)
    grad_ref[0, :, :width] = (grad_hidden * up * (sig * (1.0 + gate * (1.0 - sig)))).astype(jnp.bfloat16)
    grad_ref[0, :, width:] = (grad_hidden * (gate * sig)).astype(jnp.bfloat16)
    part = proj_t(grad_ref[0], w_gu_ref[0])

    @pl.when(step == 0)
    def _():
        total[...] = part

    @pl.when(step > 0)
    def _():
        total[...] += part

    @pl.when(step == pl.num_programs(0) - 1)
    def _():
        pieces_ref[...] = total[...].astype(jnp.bfloat16).reshape(pieces_ref.shape)


def feed_back(upstream, gate_up, w_gu, w_down, shards):
    slices, width, columns = w_gu.shape
    rows = upstream.shape[0]
    hidden = columns // 2
    half = width // 2
    return run(
        feed_back_kernel,
        (slices,),
        [
            held((rows, width)),
            slab((1, rows, columns), 0),
            slab((1, width, columns), 0),
            slab((2, hidden, half), 1),
        ],
        (slab((1, rows, columns), 0), held((shards, rows // shards, width))),
        (
            like((slices, rows, columns), jnp.bfloat16),
            like((shards, rows // shards, width), jnp.bfloat16),
        ),
        [pltpu.VMEM((rows, width), jnp.float32)],
        "feed_back",
        2 * rows * width * (columns + hidden) * slices,
        (w_gu.size + w_down.size) * 2 + gate_up.size * 6 + rows * width * 4,
        [upstream, gate_up, w_gu, w_down],
    )


def mid_back_kernel(pieces, *refs):
    me_ref, gain_ref = refs[:2]
    part_refs = refs[2 : 2 + pieces]
    (
        mid_ref, up_ref, w_ref, mixed_ref, gate_ref, norm_ref,
        grad_mid_ref, grad_attn_ref, dgain_ref, dmixed_ref, dgate_ref, dnorm_ref,
    ) = refs[2 + pieces :]
    half = w_ref.shape[2]

    @pl.when(pl.program_id(0) == 0)
    def _():
        dgain_ref[...] = jnp.zeros_like(dgain_ref)
        dnorm_ref[...] = jnp.zeros_like(dnorm_ref)
        for where, part in each_piece(me_ref, part_refs):
            dvalue, dgain = norm_adjoint(mid_ref[where, :], gain_ref[...], part[...].astype(jnp.float32))
            dvalue = dvalue + up_ref[where, :].astype(jnp.float32)
            grad_mid_ref[where, :] = dvalue
            grad_attn_ref[where, :] = dvalue.astype(jnp.bfloat16)
            dgain_ref[...] += dgain

    grad = grad_attn_ref[...]
    grad_gated = proj_t(grad[:, :half], w_ref[0]) + proj_t(grad[:, half:], w_ref[1])
    value = mixed_ref[0].astype(jnp.float32)
    scale = row_scale(value)
    unit = value * scale
    weight = norm_ref[...]
    gate = gate_ref[0]
    sig = sigmoid(gate)
    dgate_ref[0] = (grad_gated * unit * weight * (sig * (1.0 + gate * (1.0 - sig)))).astype(jnp.bfloat16)
    dscaled = grad_gated * (gate * sig)
    dnorm_ref[...] += jnp.sum(dscaled * unit, axis=0, keepdims=True)
    dunit = dscaled * weight
    dmixed = scale * (dunit - unit * jnp.mean(dunit * unit, axis=-1, keepdims=True))
    dmixed_ref[0] = dmixed.astype(jnp.bfloat16)


def mid_back(me, gain, parts, mid, upstream, w_out, mixed, gate_pre, norm_weight):
    slices, rows, _ = mixed.shape
    width = mid.shape[1]
    half = width // 2
    sub = parts[0].shape[0]
    return run(
        functools.partial(mid_back_kernel, len(parts)),
        (slices,),
        [in_smem(), held((1, width))]
        + [held((sub, width))] * len(parts)
        + [
            held((rows, width)),
            held((rows, width)),
            slab((2, HEAD_V, half), 1),
            slab((1, rows, HEAD_V), 0),
            slab((1, rows, HEAD_V), 0),
            held((1, HEAD_V)),
        ],
        (
            held((rows, width)),
            held((rows, width)),
            held((1, width)),
            slab((1, rows, HEAD_V), 0),
            slab((1, rows, HEAD_V), 0),
            held((1, HEAD_V)),
        ),
        (
            like((rows, width), jnp.float32),
            like((rows, width), jnp.bfloat16),
            like((1, width), jnp.float32),
            like((slices, rows, HEAD_V), jnp.bfloat16),
            like((slices, rows, HEAD_V), jnp.bfloat16),
            like((1, HEAD_V), jnp.float32),
        ),
        [],
        "mid_back",
        2 * rows * width * HEAD_V * slices,
        w_out.size * 2 + rows * width * 20,
        [me, gain] + list(parts) + [mid, upstream, w_out, mixed, gate_pre, norm_weight],
    )


def project_back_kernel(packed_ref, dgate_ref, w_ref, mix_ref, normed_ref, grad_ref, pieces_ref, dmix_ref, total):
    step = pl.program_id(0)
    grad_ref[0, :, :WIDTH] = packed_ref[0, :, :WIDTH]
    grad_ref[0, :, WIDTH:] = dgate_ref[0]
    mix = packed_ref[0, :, WIDTH:]
    part = proj_t(grad_ref[0], w_ref[0]) + dot(mix, mix_rows(mix_ref))
    dmix = inner_t(mix, normed_ref[...])
    dmix_ref[0] = jnp.concatenate([dmix[0:2] + dmix[2:4], dmix[2:8]], axis=0)

    @pl.when(step == 0)
    def _():
        total[...] = part

    @pl.when(step > 0)
    def _():
        total[...] += part

    @pl.when(step == pl.num_programs(0) - 1)
    def _():
        pieces_ref[...] = total[...].astype(jnp.bfloat16).reshape(pieces_ref.shape)


def project_back(packed, dgate, w_proj, w_mix, normed, shards):
    slices, width, columns = w_proj.shape
    rows = normed.shape[0]
    return run(
        project_back_kernel,
        (slices,),
        [
            slab((1, rows, WIDTH + EXTRA), 0),
            slab((1, rows, HEAD_V), 0),
            slab((1, width, columns), 0),
            slab((1, 16, width), 0),
            held((rows, width)),
        ],
        (
            slab((1, rows, columns), 0),
            held((shards, rows // shards, width)),
            slab((1, 8, width), 0),
        ),
        (
            like((slices, rows, columns), jnp.bfloat16),
            like((shards, rows // shards, width), jnp.bfloat16),
            like((slices, 8, width), jnp.float32),
        ),
        [pltpu.VMEM((rows, width), jnp.float32)],
        "project_back",
        2 * rows * width * columns * slices,
        w_proj.size * 2 + rows * width * 12,
        [packed, dgate, w_proj, w_mix, normed],
    )


def norm_back_kernel(pieces, *refs):
    me_ref, gain_ref = refs[:2]
    part_refs = refs[2 : 2 + pieces]
    resid_ref, mid_ref, out_ref, dgain_ref = refs[2 + pieces :]
    dgain_ref[...] = jnp.zeros_like(dgain_ref)
    for where, part in each_piece(me_ref, part_refs):
        value = resid_ref[where, :].astype(jnp.float32)
        dvalue, dgain = norm_adjoint(value, gain_ref[...], part[...].astype(jnp.float32))
        out_ref[where, :] = (dvalue + mid_ref[where, :]).astype(jnp.bfloat16)
        dgain_ref[...] += dgain


def norm_back(me, gain, parts, resid, grad_mid):
    return run(
        functools.partial(norm_back_kernel, len(parts)),
        (),
        [in_smem()] + [in_vmem()] * (3 + len(parts)),
        (in_vmem(), in_vmem()),
        (like(resid.shape, jnp.bfloat16), like(gain.shape, jnp.float32)),
        [],
        "norm_back",
        resid.size * 10,
        resid.size * 10,
        [me, gain] + list(parts) + [resid, grad_mid],
    )


def weight_grad_kernel(left_ref, right_ref, out_ref):
    right = right_ref[0] if len(right_ref.shape) == 3 else right_ref[...]
    out_ref[0] = inner_t(left_ref[...], right).astype(jnp.bfloat16)


def grad_rows(left, right):
    rows, width = left.shape
    slices, _, columns = right.shape
    return run(
        weight_grad_kernel,
        (slices,),
        [held((rows, width)), slab((1, rows, columns), 0)],
        slab((1, width, columns), 0),
        like((slices, width, columns), jnp.bfloat16),
        [],
        "grad_rows",
        2 * rows * width * columns * slices,
        slices * width * columns * 2 + rows * width * 2 + right.size * 2,
        [left, right],
    )


def grad_cols_kernel(hidden_ref, up_ref, gated_ref, grad_ref, out_ref):
    rows = hidden_ref.shape[1]
    out_ref[0, 0, :rows] = inner_t(hidden_ref[...], up_ref[...]).astype(jnp.bfloat16)
    out_ref[0, 0, rows:] = inner_t(gated_ref[...], grad_ref[...]).astype(jnp.bfloat16)


def grad_cols(hidden, upstream, gated, grad_attn, slices):
    rows, width = upstream.shape
    half = width // 2
    first, second = hidden.shape[1] // slices, gated.shape[1] // slices

    def piece(columns):
        return pl.BlockSpec((rows, columns), lambda c, j: (0, j))

    def side():
        return pl.BlockSpec((rows, half), lambda c, j: (0, c))

    result = run(
        grad_cols_kernel,
        (2, slices),
        [piece(first), side(), piece(second), side()],
        pl.BlockSpec((1, 1, first + second, half), lambda c, j: (c, j, 0, 0)),
        like((2, slices, first + second, half), jnp.bfloat16),
        [],
        "grad_cols",
        4 * rows * (first + second) * slices * half,
        2 * slices * (first + second) * half * 2 + rows * width * 4,
        [hidden, upstream, gated, grad_attn],
    )
    return result.reshape(2, slices * (first + second), half)


def place_kernel(pieces, *refs):
    me_ref, out_ref = refs[0], refs[-1]
    for where, part in each_piece(me_ref, refs[1:-1]):
        out_ref[where, :] = part[...]


def place(me, parts):
    sub, width = parts[0].shape
    shape = (sub * len(parts), width)
    return run(
        functools.partial(place_kernel, len(parts)),
        (),
        [in_smem()] + [in_vmem()] * len(parts),
        in_vmem(),
        like(shape, parts[0].dtype),
        [],
        "place",
        0,
        4 * sub * width * len(parts),
        [me] + list(parts),
    )


def place_cols_kernel(pieces, *refs):
    me_ref, out_ref = refs[0], refs[-1]
    width = refs[1].shape[1]
    for number, part in enumerate(refs[1:-1]):
        start = pl.multiple_of((me_ref[0] ^ number) * width, width)
        out_ref[:, pl.ds(start, width)] = part[...]


def place_cols(me, parts):
    rows, width = parts[0].shape
    shape = (rows, width * len(parts))
    return run(
        functools.partial(place_cols_kernel, len(parts)),
        (),
        [in_smem()] + [in_vmem()] * len(parts),
        in_vmem(),
        like(shape, parts[0].dtype),
        [],
        "place_cols",
        0,
        4 * rows * width * len(parts),
        [me] + list(parts),
    )


def finish_rows_kernel(widths, side_ref, layer0_ref, layer1_ref, received_ref, *out_refs):
    side = side_ref[0]
    own = jnp.where(side == 0, layer0_ref[0], layer1_ref[0]).astype(jnp.float32)
    other = received_ref[0].astype(jnp.float32)
    rows = own.shape[0]
    start = 0
    for width, out_ref in zip(widths, out_refs):
        out_ref[pl.ds(pl.multiple_of(side * rows, rows), rows), :] = own[:, start : start + width]
        out_ref[pl.ds(pl.multiple_of((1 - side) * rows, rows), rows), :] = other[:, start : start + width]
        start += width


def finish_rows(side, layer0, layer1, received, widths):
    shards, rows, columns = layer0.shape
    return run(
        functools.partial(finish_rows_kernel, widths),
        (shards,),
        [in_smem()] + [slab((1, rows, columns), 0)] * 3,
        tuple(slab((2 * rows, width), 1) for width in widths),
        tuple(like((2 * rows, shards * width), jnp.float32) for width in widths),
        [],
        "finish_rows",
        0,
        layer0.size * 14,
        [side, layer0, layer1, received],
    )


def finish_cols_kernel(hidden, side_ref, layer0_ref, layer1_ref, received_ref, down_ref, out_ref):
    side = side_ref[0]
    own = jnp.where(side == 0, layer0_ref[0], layer1_ref[0]).astype(jnp.float32)
    other = received_ref[0].astype(jnp.float32)
    first = own.shape[0] - out_ref.shape[0]
    columns = own.shape[1]
    here = pl.ds(pl.multiple_of(side * columns, columns), columns)
    there = pl.ds(pl.multiple_of((1 - side) * columns, columns), columns)
    down_ref[:, here] = own[:hidden]
    down_ref[:, there] = other[:hidden]
    out_ref[:, here] = own[first:]
    out_ref[:, there] = other[first:]


def finish_cols(side, layer0, layer1, received, hidden):
    shards, rows, columns = layer0.shape
    return run(
        functools.partial(finish_cols_kernel, hidden),
        (shards,),
        [in_smem()] + [slab((1, rows, columns), 0)] * 3,
        (slab((hidden, 2 * columns), 0), slab((HEAD_V, 2 * columns), 0)),
        (
            like((shards * hidden, 2 * columns), jnp.float32),
            like((shards * HEAD_V, 2 * columns), jnp.float32),
        ),
        [],
        "finish_cols",
        0,
        layer0.size * 14,
        [side, layer0, layer1, received],
    )


def halves(value, axis):
    step = 1
    while step < lax.axis_size(axis):
        value = value + swapped(value, axis, step.bit_length() - 1)
        step *= 2
    return value


def by_partner(value, axis):
    size = lax.axis_size(axis)
    return [value] + [
        lax.ppermute(value, axis, [(i, i ^ k) for i in range(size)]) for k in range(1, size)
    ]


def in_order(parts, axis):
    position = lax.axis_index(axis)
    parts = list(parts)
    step = 1
    while step < len(parts):
        odd = (position & step) != 0
        parts = [jnp.where(odd, parts[i ^ step], parts[i]) for i in range(len(parts))]
        step *= 2
    return parts


def gathered(value, axis):
    return jnp.concatenate(in_order(by_partner(value, axis), axis), axis=0)


def move_pieces(pieces):
    return lax.all_to_all(pieces, "seq", 0, 0)


def exchange(pieces, beside=()):
    pieces, beside = lax.optimization_barrier((move_pieces(pieces), beside))
    return by_partner(sum_pieces(pieces), "seq"), beside


def pick(flag, when, otherwise):
    return jnp.where(flag, when, otherwise)


def both_layers(local, axis):
    core = lax.axis_index("section")
    half = local.shape[axis] // 2
    own = lax.dynamic_slice_in_dim(local, core * half, half, axis)
    received = partner(lax.dynamic_slice_in_dim(local, (1 - core) * half, half, axis))
    first = core == 0
    return pick(first, own, received), pick(first, received, own)


def move_rows(part):
    return lax.all_to_all(part, "seq", 0, 0).reshape(-1, part.shape[2])


def move_cols(part):
    part = lax.all_to_all(part, "seq", 0, 0)
    return jnp.swapaxes(part, 0, 1).reshape(part.shape[1], -1)


def sent_pieces(part, me):
    size = lax.axis_size("seq")
    own = lax.dynamic_index_in_dim(part, me[0], 0, False)
    return [own] + [
        lax.ppermute(
            lax.dynamic_index_in_dim(part, me[0] ^ k, 0, False),
            "seq",
            [(i, i ^ k) for i in range(size)],
        )
        for k in range(1, size)
    ]


def move_rows_freely(part, me):
    return place(me, sent_pieces(part, me))


def move_cols_freely(part, me):
    return place_cols(me, sent_pieces(part, me))


def spread_rows(part):
    full = lax.all_gather(part, ("head", "section"), axis=0, tiled=True)
    return full.reshape(lax.axis_size("head"), -1, part.shape[1])


def spread_cols(part):
    full = lax.all_gather(part, ("section", "head"), axis=0, tiled=True)
    return full.reshape(2, -1, part.shape[1])


def reduce_rows(grad):
    return lax.psum_scatter(
        grad.reshape(-1, grad.shape[2]), ("head", "section"), scatter_dimension=0, tiled=True
    )


def reduce_cols(grad):
    return lax.psum_scatter(
        grad.reshape(-1, grad.shape[2]), ("section", "head"), scatter_dimension=0, tiled=True
    )


def collect_rows(part):
    shards = lax.axis_size("seq")
    return lax.all_to_all(part.reshape(shards, -1, part.shape[1]), "seq", 0, 0)


def collect_cols(part):
    shards = lax.axis_size("seq")
    part = jnp.swapaxes(part.reshape(part.shape[0], shards, -1), 0, 1)
    return lax.all_to_all(part, "seq", 0, 0)


def collect_cols_freely(part, me):
    shards = lax.axis_size("seq")
    part = jnp.swapaxes(part.reshape(part.shape[0], shards, -1), 0, 1)
    return place(me, sent_pieces(part, me)).reshape(part.shape)


def after(value, other):
    return lax.optimization_barrier((value, other))[0]


def layer_backward_fast(me, upstream, saved, gains, weights, small, aux, parts, plan):
    before_mid, early_gu, start, then = plan
    attn_gain, mlp_gain = gains
    w_proj, w_mix, w_out, w_gu, w_down = weights
    taps, scal, norm_weight = small
    resid, normed, gate_pre, mixer, mid, ffn_in, gate_up, hidden = saved
    xh, states, inverse, mixed, gated = mixer
    shards = parts[0]
    slices, rows, _ = mixed.shape
    grad_gate_up, pieces = feed_back(upstream, gate_up, w_gu, w_down, shards)
    grad_gu = grad_rows(ffn_in, grad_gate_up)
    sums, _ = exchange(pieces, grad_gu)
    sums, sum_gu = before_mid(sums, grad_gu)
    grad_mid, grad_attn, dmlp, dmixed, dgate, dnorm = mid_back(
        me, mlp_gain, sums, mid, upstream, w_out, mixed, gate_pre, norm_weight
    )
    grad_both = grad_cols(hidden, upstream, gated, grad_attn, slices)
    grad_head = lax.all_to_all(dmixed, "head", 0, 0).reshape(slices * rows, HEAD_V)
    grad_head, grad_both, sum_gu = early_gu(grad_head, grad_both, sum_gu)
    running = start(grad_head)
    dxh, dtaps, dscal = recur_backward(xh, aux, taps, scal, states, inverse, grad_head, parts)
    dxh, running = lax.optimization_barrier((dxh, running))
    packed = lax.all_to_all(dxh.reshape(slices, rows, WIDTH + EXTRA), "head", 0, 0)
    packed, sum_gu = lax.optimization_barrier((packed, sum_gu))
    sum_both = reduce_cols(after(grad_both, sum_gu))
    running = then(running)
    grad_pre, pieces, dmix = project_back(packed, dgate, w_proj, w_mix, normed, shards)
    grad_proj = grad_rows(normed, grad_pre)
    sums, _ = exchange(pieces, grad_proj)
    sums, sum_both, running = lax.optimization_barrier((sums, sum_both, running))
    sum_proj = reduce_rows(after(grad_proj, sum_both))
    grad_resid, dattn = norm_back(me, attn_gain, sums, resid, grad_mid)
    small_grads = (dtaps[:CONVK], dscal[0, :2], dnorm[0], dattn[0], dmlp[0], dmix[:, :2])
    return grad_resid, (sum_proj, sum_gu, sum_both), small_grads, running


def fast_shards(
    tokens,
    cotangent,
    doc_starts,
    valid_mask,
    gain_attn,
    w_query,
    w_key,
    w_value,
    w_gate_out,
    w_decay,
    w_beta,
    conv_query,
    conv_key,
    conv_value,
    decay_log,
    decay_bias,
    out_norm,
    w_output,
    gain_mlp,
    w_gate,
    w_up,
    w_down,
):
    core = lax.axis_index("section")
    first = core == 0
    shard = lax.axis_index("seq")
    piece = lax.axis_index("head")
    shards, slices = lax.axis_size("seq"), lax.axis_size("head")
    parts = (shards, slices)
    shard_rows = w_query.shape[1]
    model_width = tokens.shape[2]
    sub = tokens.shape[1] // slices
    length = tokens.shape[1] * shards
    hidden_width = w_gate.shape[2] // shards
    hidden_padded = -(-hidden_width // 128) * 128

    def columns(value, width):
        return jnp.stack([value[:, s * width : (s + 1) * width] for s in range(shards)])

    def halved(value):
        shape = value.shape[:-1]
        value = value.reshape(shape + (shards, 2, model_width // (2 * shards)))
        return jnp.swapaxes(value, -3, -2).reshape(shape + (model_width,))

    proj_local = jnp.concatenate(
        [
            columns(w_query[0], HEAD_K),
            columns(w_key[0], HEAD_K),
            columns(w_value[0], HEAD_V),
            columns(w_gate_out[0], HEAD_V),
        ],
        axis=2,
    )
    fill = ((0, 0), (0, 0), (0, hidden_padded - hidden_width))
    gu_local = jnp.concatenate(
        [jnp.pad(columns(w_gate[0], hidden_width), fill), jnp.pad(columns(w_up[0], hidden_width), fill)],
        axis=2,
    )
    out_local = w_output[0].reshape(shards, HEAD_V, shard_rows)
    down_local = jnp.pad(
        w_down[0].reshape(shards, hidden_width, shard_rows),
        ((0, 0), (0, hidden_padded - hidden_width), (0, 0)),
    )
    proj_parts = both_layers(proj_local, 1)
    out_parts = both_layers(out_local, 2)
    gu_parts = both_layers(gu_local, 1)
    down_parts = both_layers(down_local, 2)

    conv = jnp.concatenate(
        [
            columns(conv_query[0], HEAD_K),
            columns(conv_key[0], HEAD_K),
            columns(conv_value[0], HEAD_V),
        ],
        axis=2,
    )
    taps_own = lax.dynamic_index_in_dim(conv, shard, 0, False).astype(jnp.float32)
    small_own = jnp.concatenate(
        [
            taps_own.reshape(-1),
            jnp.stack([decay_log[0, shard], decay_bias[0, shard]]),
            out_norm[0].astype(jnp.float32),
            gain_attn[0].astype(jnp.float32),
            gain_mlp[0].astype(jnp.float32),
            w_decay[0].astype(jnp.float32).T.reshape(-1),
            w_beta[0].astype(jnp.float32).T.reshape(-1),
        ]
    )
    small_other = partner(small_own)
    small_layers = (pick(first, small_own, small_other), pick(first, small_other, small_own))
    taps_size = CONVK * WIDTH
    norm_at = taps_size + 2
    gain_at = norm_at + HEAD_V
    wide = jnp.stack([vector[gain_at:] for vector in small_layers])
    wide = jnp.concatenate([wide.reshape(-1), valid_mask[core].astype(jnp.float32)])
    wide = gathered(wide[None], "seq")
    valid_all = wide[:, wide.shape[1] - tokens.shape[1] :].reshape(shards, slices, sub)
    valid = lax.dynamic_index_in_dim(valid_all, piece, 1, False).reshape(-1)
    wide = wide[:, : wide.shape[1] - tokens.shape[1]].reshape(shards, 2, 2 + 2 * shards, 2, shard_rows // 2)
    gains_all = jnp.transpose(wide[:, :, :2], (1, 2, 3, 0, 4)).reshape(2, 2, model_width)
    mix_all = wide[:, :, 2:].reshape(shards, 2, 2, shards, 2, shard_rows // 2)
    mix_all = lax.dynamic_index_in_dim(mix_all, shard, 3, False)
    mix_all = jnp.transpose(mix_all, (1, 2, 3, 0, 4)).reshape(2, 2, model_width).astype(jnp.bfloat16)
    mix_all = gathered(mix_all[None], "head")
    mix_all = jnp.swapaxes(mix_all, 0, 1)
    mix_all = jnp.concatenate(
        [mix_all, mix_all, jnp.zeros((2, slices, 12, model_width), jnp.bfloat16)], axis=2
    )
    small = []
    gains = []
    weights = []
    for layer in range(2):
        vector = small_layers[layer]
        taps = jnp.pad(vector[:taps_size].reshape(CONVK, WIDTH), ((0, 8 - CONVK), (0, 0)))
        scal = jnp.pad(vector[taps_size:norm_at][None], ((0, 7), (0, 126)))
        small.append((taps, scal, vector[None, norm_at:gain_at]))
        gains.append((gains_all[layer, 0][None], gains_all[layer, 1][None]))

    def my_tokens(value):
        mine = lax.dynamic_slice_in_dim(value, piece * sub, sub, 0)
        return by_partner(halved(mine), "seq")

    me = shard[None].astype(jnp.int32)
    valid = valid[:, None]
    aux = make_aux(doc_starts[core], length)
    masked = cotangent[core] * valid_mask[core].astype(jnp.bfloat16)[:, None]

    token_parts, base = my_tokens(tokens[core]), None
    proj0 = after(move_rows(proj_parts[0]), (token_parts, gains, small, valid))
    out0 = move_cols(after(out_parts[0], proj0))
    gu0 = move_rows(after(gu_parts[0], out0))
    down0 = move_cols_freely(after(down_parts[0], gu0), me)
    weights = [
        (spread_rows(proj0), mix_all[0], spread_cols(out0), spread_rows(gu0), None)
    ]

    saved = []
    stats = []
    for layer in range(2):
        w_proj, w_mix, w_out, w_gu, w_down = weights[layer]
        attn_gain, mlp_gain = gains[layer]
        resid, normed, packed, gate_pre, stat = project(
            me, valid, attn_gain, token_parts, base, w_proj, w_mix
        )
        stats.append(stat)
        xh = lax.all_to_all(packed, "head", 0, 0).reshape(slices * valid.shape[0], WIDTH + EXTRA)
        if layer == 0:
            xh, down0 = lax.optimization_barrier((xh, down0))
            w_down = spread_cols(down0)
            weights[0] = (w_proj, w_mix, w_out, w_gu, w_down)
            proj1 = move_rows(after(proj_parts[1], xh))
            out1 = move_cols_freely(after(out_parts[1], xh), me)
            down1 = move_cols_freely(after(down_parts[1], xh), me)
        else:
            gu1 = move_rows_freely(after(gu_parts[1], xh), me)
            masked = my_tokens(after(masked, xh))
        mixed_head, states, inverse = recur_forward(xh, aux, *small[layer][:2], parts)
        if layer == 0:
            mixed_head, proj1 = lax.optimization_barrier((mixed_head, proj1))
        else:
            mixed_head, gu1, masked = lax.optimization_barrier((mixed_head, gu1, masked))
            w_gu = spread_rows(gu1)
            weights[1] = (w_proj, w_mix, w_out, w_gu, w_down)
        mixed = lax.all_to_all(mixed_head.reshape(gate_pre.shape), "head", 0, 0)
        gated, pieces = output(mixed, gate_pre, small[layer][2], w_out, shards)
        mixer = (xh, states, inverse, mixed, gated)
        mix_parts, _ = exchange(pieces)
        base, ffn_in, gate_up, hidden, pieces, stat = feed(
            me, valid, mlp_gain, mix_parts, resid, w_gu, w_down, shards
        )
        stats.append(stat)
        saved.append((resid, normed, gate_pre, mixer, base, ffn_in, gate_up, hidden))
        if layer == 0:
            pieces, out1, down1 = lax.optimization_barrier((pieces, out1, down1))
            weights.append(
                (spread_rows(proj1), mix_all[1], spread_cols(out1), None, spread_cols(down1))
            )
            token_parts, _ = exchange(pieces)
    h1 = saved[1][0]
    stats0 = jnp.stack([stats[2][0, 0], stats[1][0, 0], stats[2][0, 1]])
    upstream = place(me, masked)
    def placed_tokens(layer0, layer1):
        layer0, layer1 = (
            lax.dynamic_slice_in_dim(value, shard * sub, sub, 0) for value in (layer0, layer1)
        )
        keep = pick(first, layer0, layer1)
        received = partner(pick(first, layer1, layer0))
        both = jnp.stack([pick(first, keep, received), pick(first, received, keep)])
        pieces = jnp.stack(in_order(by_partner(both, "head"), "head"), axis=1)
        pieces = pieces.reshape(2, slices * sub, 2, shards, model_width // (2 * shards))
        return jnp.swapaxes(pieces, 2, 3).reshape(2, slices * sub, model_width)

    def plan_last():
        def before_mid(sums, grad_gu):
            return sums, reduce_rows(grad_gu)

        def early_gu(grad_head, grad_both, sum_gu):
            return lax.optimization_barrier((grad_head, grad_both, sum_gu))

        def start(anchor):
            return move_pieces(after(pieces, anchor))

        def then(moved):
            return by_partner(sum_pieces(moved), "seq")

        return before_mid, early_gu, start, then

    grad_h1, big1, small1, last_parts = layer_backward_fast(
        me, upstream, saved[1], gains[1], weights[1], small[1], aux, parts, plan_last()
    )
    sum_proj1, sum_gu1, sum_both1 = big1
    act1, stat = close(me, valid, last_parts, base)
    stats1 = jnp.stack([stat[0, 0], stats[3][0, 0], stat[0, 1]])
    activations = placed_tokens(h1, act1)
    early = {}

    def plan_first():
        def before_mid(sums, grad_gu):
            sums, early["proj"], early["activations"] = lax.optimization_barrier(
                (sums, sum_proj1, activations)
            )
            return sums, reduce_rows(after(grad_gu, early["proj"]))

        def early_gu(grad_head, grad_both, sum_gu):
            grad_head, grad_both = lax.optimization_barrier((grad_head, grad_both))
            return grad_head, grad_both, sum_gu

        def start(anchor):
            gu = collect_rows(after(sum_gu1, anchor))
            both = collect_cols_freely(after(sum_both1, anchor), me)
            early["both"] = both
            return gu

        def then(moved):
            return moved, early["both"]

        return before_mid, early_gu, start, then

    grad_tokens, big0, small0, (moved_gu1, moved_both1) = layer_backward_fast(
        me, grad_h1, saved[0], gains[0], weights[0], small[0], aux, parts, plan_first()
    )
    sum_proj0, sum_gu0, sum_both0 = big0
    activations = early["activations"]
    moved_proj1 = collect_rows(after(early["proj"], sum_both0))
    moved_gu0 = collect_rows(after(sum_gu0, moved_proj1))
    moved_both0 = collect_cols(after(sum_both0, moved_gu0))
    moved_proj0 = collect_rows(sum_proj0)

    input_grads = placed_tokens(grad_tokens, grad_h1)

    def joined(layer0, layer1, axis):
        keep = pick(first, layer0, layer1)
        received = partner(pick(first, layer1, layer0))
        return jnp.concatenate(
            [pick(first, keep, received), pick(first, received, keep)], axis=axis
        ).astype(jnp.float32)

    side = core[None].astype(jnp.int32)
    grad_down, grad_out = finish_cols(
        side, moved_both0, moved_both1, partner(pick(first, moved_both1, moved_both0)), hidden_width
    )
    grad_gu = joined(moved_gu0, moved_gu1, 1)
    grad_proj = finish_rows(
        side, moved_proj0, moved_proj1, partner(pick(first, moved_proj1, moved_proj0)),
        (HEAD_K, HEAD_K, HEAD_V, HEAD_V),
    )

    def pack(grads, sums):
        dtaps, dscal, dnorm, dattn, dmlp, dmix = grads
        place = (jnp.arange(2) == core)[:, None]
        marked = jnp.where(place, jnp.concatenate([sums, jnp.sum(valid)[None]])[None], 0.0)
        return jnp.concatenate(
            [dtaps.reshape(-1), dscal, dnorm, marked.reshape(-1), dattn, dmlp, dmix.reshape(-1)]
        )

    packs = (pack(small0, stats0), pack(small1, stats1))
    vector = pick(first, packs[0], packs[1]) + partner(pick(first, packs[1], packs[0]))
    gain_end = norm_at + HEAD_V + 8 + 2 * model_width
    per_head = gathered(vector[None, :norm_at], "seq")
    sums_all = halves(vector[norm_at:gain_end], "head")
    norm_sum = halves(sums_all[:HEAD_V], "seq")
    stat_sums = sums_all[HEAD_V : HEAD_V + 8].reshape(2, 4)
    gain_sums = sums_all[HEAD_V + 8 :].reshape(2, 2, shards, shard_rows // 2)
    gain_sums = lax.dynamic_index_in_dim(gain_sums, shard, 2, False).reshape(2, shard_rows)
    branch_rms = jnp.sqrt(stat_sums[:, :3] / jnp.maximum(stat_sums[:, 3:], 1.0))
    mix_grad = vector[gain_end:].reshape(slices, 2, 2, shards, shard_rows // 2)
    mix_grad = jnp.sum(lax.all_to_all(mix_grad, "head", 0, 0), axis=0)
    mix_grad = lax.all_to_all(jnp.transpose(mix_grad, (2, 0, 1, 3)), "seq", 0, 0)
    mix_grad = jnp.transpose(mix_grad, (1, 2, 3, 0)).reshape(2, shard_rows, shards)
    conv_grad = jnp.swapaxes(per_head[:, :taps_size].reshape(shards, CONVK, WIDTH), 0, 1)

    def conv_part(start, width):
        return conv_grad[:, :, start : start + width].reshape(1, CONVK, shards * width)

    def gu_part(start):
        part = jnp.swapaxes(grad_gu[:, :, start : start + hidden_width], 0, 1)
        return part.reshape(1, shard_rows, shards * hidden_width)

    return (
        activations[None],
        input_grads[None],
        branch_rms[None],
        gain_sums[0][None],
        grad_proj[0][None],
        grad_proj[1][None],
        grad_proj[2][None],
        grad_proj[3][None],
        mix_grad[0][None],
        mix_grad[1][None],
        conv_part(0, HEAD_K),
        conv_part(HEAD_K, HEAD_K),
        conv_part(2 * HEAD_K, HEAD_V),
        per_head[:, taps_size][None],
        per_head[:, taps_size + 1][None],
        norm_sum[None],
        grad_out[None],
        gain_sums[1][None],
        gu_part(0),
        gu_part(hidden_padded),
        grad_down[None],
    )


def per_device(*args):
    tokens, w_decay = args[0], args[9]
    rows = tokens.shape[1]
    seq, head, section = (lax.axis_size(axis) for axis in ("seq", "head", "section"))
    one_head_each = w_decay.shape[2] == seq
    micro_each = tokens.shape[0] == section == 2
    powers = seq & (seq - 1) == 0 and head & (head - 1) == 0
    even = rows % (head * BLOCK) == 0 and rows * seq % (BLOCK * GROUP) == 0
    if one_head_each and micro_each and powers and even:
        return fast_shards(*args)
    return shards(*args)


def solution(mesh):
    placed = (
        P(None, "seq", None),
        P(None, "seq", None),
        P(),
        P(None, "seq"),
        P("section", "seq"),
        P("section", "seq", "head"),
        P("section", "seq", "head"),
        P("section", "seq", "head"),
        P("section", "seq", "head"),
        P("section", "seq", "head"),
        P("section", "seq", "head"),
        P("section", None, "head"),
        P("section", None, "head"),
        P("section", None, "head"),
        P("section", "head"),
        P("section", "head"),
        P("section", None),
        P("section", "head", "seq"),
        P("section", "seq"),
        P("section", "seq", "head"),
        P("section", "seq", "head"),
        P("section", "head", "seq"),
    )
    return jax.shard_map(
        per_device,
        mesh=mesh,
        in_specs=placed,
        out_specs=(
            P("section", None, "seq", None),
            P("section", None, "seq", None),
            P("section", None, None),
            P("section", "seq"),
            P("section", "seq", "head"),
            P("section", "seq", "head"),
            P("section", "seq", "head"),
            P("section", "seq", "head"),
            P("section", "seq", "head"),
            P("section", "seq", "head"),
            P("section", None, "head"),
            P("section", None, "head"),
            P("section", None, "head"),
            P("section", "head"),
            P("section", "head"),
            P("section", None),
            P("section", "head", "seq"),
            P("section", "seq"),
            P("section", "seq", "head"),
            P("section", "seq", "head"),
            P("section", "head", "seq"),
        ),
        check_vma=False,
    )
```

```python
import functools

import jax
import jax.numpy as jnp
from jax import lax
from jax.experimental import pallas as pl
from jax.experimental.pallas import tpu as pltpu
from jax.sharding import PartitionSpec as P

HEAD_K = 128
HEAD_V = 256
CONVK = 4
BLOCK = 64
SECTION = "section"
SEQ = "seq"
HEAD = "head"
LANES = 128
RECUR_FLOPS = 40_000_000
VMEM_LIMIT = 48 * 1024 * 1024
HALO = 8
EXTRA = 128
GROUP = 8


epsilon = 1e-06
highest_precision = lax.Precision.HIGHEST


def swapped(value, axis, stride):
    return lax.ppermute(value, axis, [(i, i ^ 1 << stride) for i in range(lax.axis_size(axis))])


def carried_in(value, axis, combine, identity):
    devices, position = (lax.axis_size(axis), lax.axis_index(axis))
    everything = jax.tree.map(
        lambda part, kind: lax.all_gather(part.astype(kind), axis),
        value,
        (jnp.bfloat16, jnp.bfloat16),
    )
    start = jax.tree.map(
        lambda part, zero: jnp.broadcast_to(jnp.asarray(zero, part.dtype), part.shape),
        value,
        identity,
    )

    def step(k, before):
        reached = k < position
        new = combine(
            before, jax.tree.map(lambda part, own: part[k].astype(own.dtype), everything, value)
        )
        return jax.tree.map(lambda a, b: jnp.where(reached, a, b), new, before)

    return lax.fori_loop(0, devices, step, start)


def entering(value, axis, join, neutral):
    count = lax.axis_size(axis)
    place = lax.axis_index(axis)
    ahead = count - 1 - place
    gathered = jax.tree.map(
        lambda a, kind: lax.all_gather(a.astype(kind), axis),
        value,
        jax.tree.map(lambda a: jnp.bfloat16 if a.dtype == jnp.float32 else a.dtype, value),
    )
    state = jax.tree.map(lambda a, e: jnp.zeros_like(a) + jnp.asarray(e, a.dtype), value, neutral)

    def one(step, state):
        source = count - 1 - step
        return join(
            state,
            jax.tree.map(
                lambda a, own: lax.dynamic_index_in_dim(a, source, 0, False).astype(own.dtype),
                gathered,
                value,
            ),
        )

    return lax.fori_loop(0, ahead, one, state)


def passed_along(value, axis, steps):
    count = lax.axis_size(axis)
    first, last = (max(0, -steps), min(count, count - steps))
    return lax.ppermute(value, axis, [(source, source + steps) for source in range(first, last)])


def rms_norm(values, weight):
    return values * lax.rsqrt(jnp.mean(values * values, axis=-1, keepdims=True) + epsilon) * weight


def doc_index(starts, positions):
    counted = jnp.sum(
        (starts[None, :] <= positions[:, None]).astype(jnp.int32), axis=1, dtype=jnp.int32
    )
    return counted - 1


def unit_rows(values):
    return values * lax.rsqrt(jnp.sum(values * values, axis=-1, keepdims=True) + epsilon)


def conv_front(extended, doc_ext, conv_weight):
    length = extended.shape[0] - (CONVK - 1)
    summed = jnp.zeros((length, extended.shape[1]), extended.dtype)
    for tap_index in range(CONVK):
        same_doc = doc_ext[tap_index : tap_index + length] == doc_ext[CONVK - 1 :]
        summed = (
            summed
            + jnp.where(same_doc[:, None], extended[tap_index : tap_index + length], 0.0)
            * conv_weight[tap_index]
        )
    return jax.nn.silu(summed)


def heads_front(extended, doc_ext, mix_pre, conv_weight, decay_scale, decay_shift, head_count):
    activated = conv_front(extended, doc_ext, conv_weight)
    length = activated.shape[0]
    width_k = head_count * HEAD_K
    queries = unit_rows(activated[:, :width_k].reshape(length, head_count, HEAD_K)) * HEAD_K ** (
        -0.5
    )
    key_rows = unit_rows(activated[:, width_k : 2 * width_k].reshape(length, head_count, HEAD_K))
    value_rows = activated[:, 2 * width_k :].reshape(length, head_count, HEAD_V)
    write_rate = jax.nn.sigmoid(mix_pre[:, head_count:])
    log_decay = -jnp.exp(decay_scale) * jax.nn.softplus(mix_pre[:, :head_count] + decay_shift)
    return (queries, key_rows, value_rows, write_rate, log_decay)


def block_terms(queries, key_rows, value_rows, write_rate, log_decay, doc_ids, prev_doc):
    length = queries.shape[1]
    cumulated = jnp.cumsum(log_decay, axis=1)
    row_iota = lax.broadcasted_iota(jnp.int32, (length, length), 0)
    col_iota = lax.broadcasted_iota(jnp.int32, (length, length), 1)
    same_doc = (doc_ids[:, :, None] == doc_ids[:, None, :]) & (col_iota <= row_iota)[None]
    same_mask = same_doc[:, :, :, None]
    exponent = jnp.where(same_mask, cumulated[:, :, None, :] - cumulated[:, None, :, :], 0.0)
    decay_full = jnp.where(same_mask, jnp.exp(exponent), 0.0)
    initial_decay = jnp.where((doc_ids == prev_doc[:, None])[:, :, None], jnp.exp(cumulated), 0.0)
    decay_heads = jnp.transpose(decay_full, (0, 3, 1, 2))
    key_gram = jnp.einsum("nthk,nihk->nhti", key_rows, key_rows, precision=highest_precision)
    strict_mask = (col_iota < row_iota)[None, None]
    lower_part = jnp.where(
        strict_mask,
        jnp.transpose(write_rate, (0, 2, 1))[:, :, :, None] * decay_heads * key_gram,
        0.0,
    )
    system = lower_part + jnp.eye(length, dtype=lower_part.dtype)
    scaled_values = jnp.transpose(write_rate[..., None] * value_rows, (0, 2, 1, 3))
    scaled_keys = jnp.transpose((write_rate * initial_decay)[..., None] * key_rows, (0, 2, 1, 3))
    resolved_values = lax.linalg.triangular_solve(
        system, scaled_values, left_side=True, lower=True, unit_diagonal=True
    )
    resolved_keys = lax.linalg.triangular_solve(
        system, scaled_keys, left_side=True, lower=True, unit_diagonal=True
    )
    query_key = (
        jnp.einsum("nthk,nihk->nhti", queries, key_rows, precision=highest_precision) * decay_heads
    )
    return (resolved_values, resolved_keys, query_key, decay_heads, initial_decay)


def gate_norm(mixed_out, gate_pre, norm_weight, head_count):
    length = mixed_out.shape[0]
    per_head = mixed_out.reshape(length, head_count, HEAD_V)
    gates = gate_pre.reshape(length, head_count, HEAD_V)
    normed = rms_norm(per_head, norm_weight) * jax.nn.silu(gates)
    return normed.reshape(length, head_count * HEAD_V)


def summary(
    extended, mix_pre, conv_weight, decay_scale, decay_shift, doc_ext, prev_docs, head_count
):
    queries, key_rows, value_rows, write_rate, log_decay = heads_front(
        extended, doc_ext, mix_pre, conv_weight, decay_scale, decay_shift, head_count
    )
    length = write_rate.shape[0]
    blocks = length // BLOCK

    def as_blocks(values):
        return values.reshape((blocks, BLOCK) + values.shape[1:])

    block_query_rows = as_blocks(queries)
    block_key_rows = as_blocks(key_rows)
    resolved_values, resolved_keys, query_key, decay_heads, initial_decay = block_terms(
        block_query_rows,
        block_key_rows,
        as_blocks(value_rows),
        as_blocks(write_rate),
        as_blocks(log_decay),
        as_blocks(doc_ext[CONVK - 1 :]),
        prev_docs,
    )
    final_row = decay_heads[:, :, -1, :]
    identity = jnp.eye(HEAD_K, dtype=extended.dtype)
    transfer_blocks = initial_decay[:, -1, :][:, :, None, None] * identity - jnp.einsum(
        "nhi,nihk,nhil->nhkl", final_row, block_key_rows, resolved_keys, precision=highest_precision
    )
    add_blocks = jnp.einsum(
        "nhi,nihk,nhiv->nhkv",
        final_row,
        block_key_rows,
        resolved_values,
        precision=highest_precision,
    )
    local_out = jnp.einsum(
        "nhti,nhiv->nhtv", query_key, resolved_values, precision=highest_precision
    )
    response = jnp.transpose(initial_decay, (0, 2, 1))[..., None] * jnp.transpose(
        block_query_rows, (0, 2, 1, 3)
    ) - jnp.einsum("nhti,nhik->nhtk", query_key, resolved_keys, precision=highest_precision)
    carry_map = jnp.broadcast_to(identity, (head_count, HEAD_K, HEAD_K))
    carried_addend = jnp.zeros((head_count, HEAD_K, HEAD_V), extended.dtype)
    entry_maps = []
    entry_adds = []
    for block_number in range(blocks):
        entry_maps.append(carry_map)
        entry_adds.append(carried_addend)
        carried_addend = (
            jnp.einsum(
                "jme,jed->jmd",
                transfer_blocks[block_number],
                carried_addend,
                precision=highest_precision,
            )
            + add_blocks[block_number]
        )
        carry_map = jnp.einsum(
            "hkl,hlm->hkm", transfer_blocks[block_number], carry_map, precision=highest_precision
        )
    kept = (local_out, response, jnp.stack(entry_maps), jnp.stack(entry_adds))
    return (carry_map, carried_addend, kept)


def finish(kept, running_state):
    local_out, response, entry_maps, entry_adds = kept
    entry_states = (
        jnp.einsum("nhkl,hlv->nhkv", entry_maps, running_state, precision=highest_precision)
        + entry_adds
    )
    result = local_out + jnp.einsum(
        "nhck,nhkv->nhcv", response, entry_states, precision=highest_precision
    )
    blocks, head_count, length, width_v = result.shape
    return jnp.transpose(result, (0, 2, 1, 3)).reshape(blocks * length, head_count * width_v)


def compose(earlier_blocks, later_blocks):
    return (
        jnp.einsum("hkl,hlm->hkm", later_blocks[0], earlier_blocks[0], precision=highest_precision),
        jnp.einsum("jme,jed->jmd", later_blocks[0], earlier_blocks[1], precision=highest_precision)
        + later_blocks[1],
    )


def head_total(values):
    return lax.psum(values.astype(jnp.bfloat16), HEAD).astype(jnp.float32)


def partner(values):
    return swapped(values, SECTION, 0)


def proj_t(left, right):
    return lax.dot_general(
        left, right, (((1,), (1,)), ((), ())), preferred_element_type=jnp.float32
    )


def inner_t(left, right):
    return lax.dot_general(
        left, right, (((0,), (0,)), ((), ())), preferred_element_type=jnp.float32
    )


def spread(rows_grads, cols_grads):
    rows_part = (
        lax.psum_scatter(
            rows_grads[0].astype(jnp.bfloat16), SEQ, scatter_dimension=0, tiled=True
        ).astype(jnp.float32),
        lax.psum_scatter(
            rows_grads[1].astype(jnp.bfloat16), SEQ, scatter_dimension=0, tiled=True
        ).astype(jnp.float32),
        lax.psum_scatter(
            rows_grads[2].astype(jnp.bfloat16), SEQ, scatter_dimension=0, tiled=True
        ).astype(jnp.float32),
        lax.psum_scatter(
            rows_grads[3].astype(jnp.bfloat16), SEQ, scatter_dimension=0, tiled=True
        ).astype(jnp.float32),
        lax.psum_scatter(
            rows_grads[4].astype(jnp.bfloat16), SEQ, scatter_dimension=0, tiled=True
        ).astype(jnp.float32),
    )
    cols_part = (
        lax.psum_scatter(
            cols_grads[0].astype(jnp.bfloat16), SEQ, scatter_dimension=1, tiled=True
        ).astype(jnp.float32),
        lax.psum_scatter(
            cols_grads[1].astype(jnp.bfloat16), SEQ, scatter_dimension=1, tiled=True
        ).astype(jnp.float32),
    )
    return (rows_part, cols_part)


def shards(
    tokens,
    cotangent,
    doc_starts,
    valid_mask,
    gain_attn,
    w_query,
    w_key,
    w_value,
    w_gate_out,
    w_decay,
    w_beta,
    conv_query,
    conv_key,
    conv_value,
    decay_log,
    decay_bias,
    out_norm,
    w_output,
    gain_mlp,
    w_gate,
    w_up,
    w_down,
):
    micro_count = tokens.shape[0]
    row_count = tokens.shape[1]
    model_width = tokens.shape[2]
    head_count = w_decay.shape[2]
    width_qk = w_query.shape[2]
    width_qkv = 2 * width_qk + w_value.shape[2]
    hidden_width = w_gate.shape[2]
    block_count = row_count // BLOCK
    section_index = lax.axis_index(SECTION)
    shard_index = lax.axis_index(SEQ)
    full_rows = (
        lax.all_gather(gain_attn[0], SEQ, axis=0, tiled=True),
        lax.all_gather(gain_mlp[0], SEQ, axis=0, tiled=True),
        lax.all_gather(w_query[0], SEQ, axis=0, tiled=True),
        lax.all_gather(w_key[0], SEQ, axis=0, tiled=True),
        lax.all_gather(w_value[0], SEQ, axis=0, tiled=True),
        lax.all_gather(w_gate_out[0], SEQ, axis=0, tiled=True),
        lax.all_gather(w_decay[0], SEQ, axis=0, tiled=True),
        lax.all_gather(w_beta[0], SEQ, axis=0, tiled=True),
        lax.all_gather(w_gate[0], SEQ, axis=0, tiled=True),
        lax.all_gather(w_up[0], SEQ, axis=0, tiled=True),
    )
    full_cols = (
        lax.all_gather(w_output[0], SEQ, axis=1, tiled=True),
        lax.all_gather(w_down[0], SEQ, axis=1, tiled=True),
    )
    attn_gain = full_rows[0].astype(jnp.float32)
    mlp_gain = full_rows[1].astype(jnp.float32)
    proj_weight = jnp.concatenate([full_rows[2], full_rows[3], full_rows[4], full_rows[5]], axis=1)
    mix_weight = jnp.concatenate([full_rows[6], full_rows[7]], axis=1).astype(jnp.float32)
    gate_up_weight = jnp.concatenate([full_rows[8], full_rows[9]], axis=1)
    out_weight = full_cols[0]
    down_weight = full_cols[1]
    conv_weight = jnp.concatenate([conv_query[0], conv_key[0], conv_value[0]], axis=1).astype(
        jnp.float32
    )
    decay_scale = decay_log[0]
    decay_shift = decay_bias[0]
    norm_weight = out_norm[0].astype(jnp.float32)
    ext_pos = (
        shard_index * row_count - (CONVK - 1) + jnp.arange(row_count + CONVK - 1, dtype=jnp.int32)
    )
    block_pos = shard_index * row_count + jnp.arange(block_count, dtype=jnp.int32) * BLOCK - 1

    def carry_backward(shard_map_t, shard_adj):
        identity = jnp.broadcast_to(
            jnp.eye(shard_map_t.shape[1], dtype=jnp.float32), shard_map_t.shape
        )
        suffix = entering(
            (shard_map_t, shard_adj), SEQ, compose, (identity, jnp.zeros_like(shard_adj))
        )
        result = suffix[1]
        return result

    def layer_backward(saved, upstream, starts):
        (
            resid_in,
            normed,
            mix_pre,
            extended,
            gate_pre,
            kept,
            running_state,
            shard_map,
            mixed_out,
            gated,
            resid_mid,
            ffn_in,
            gate_up,
            hidden,
        ) = saved
        doc_ext = doc_index(starts, ext_pos)
        prev_docs = doc_index(starts, block_pos)
        grad_ffn = upstream.astype(jnp.bfloat16)
        grad_hidden = proj_t(grad_ffn, down_weight)
        grad_down = inner_t(hidden, grad_ffn)
        _, act_back = jax.vjp(
            lambda gate_in, up_in: jax.nn.silu(gate_in) * up_in,
            gate_up[:, :hidden_width],
            gate_up[:, hidden_width:],
        )
        grad_gate, grad_up = act_back(grad_hidden)
        grad_gate_up = jnp.concatenate([grad_gate, grad_up], axis=1).astype(jnp.bfloat16)
        grad_gu_weight = inner_t(ffn_in, grad_gate_up)
        grad_ffn_in = head_total(proj_t(grad_gate_up, gate_up_weight))
        _, mlp_norm_back = jax.vjp(rms_norm, resid_mid, mlp_gain)
        grad_mid_norm, grad_mlp_gain = mlp_norm_back(grad_ffn_in)
        grad_mid = upstream + grad_mid_norm
        grad_attn = grad_mid.astype(jnp.bfloat16)
        grad_gated = proj_t(grad_attn, out_weight)
        grad_out_weight = inner_t(gated, grad_attn)
        _, gate_back = jax.vjp(
            lambda mixed_in, gate_in, weight_in: gate_norm(
                mixed_in, gate_in, weight_in, head_count
            ),
            mixed_out,
            gate_pre,
            norm_weight,
        )
        grad_mixed, grad_gate_pre, grad_norm_weight = gate_back(grad_gated)
        _, finish_back = jax.vjp(finish, kept, running_state)
        grad_kept, grad_state = finish_back(grad_mixed)
        later_blocks = carry_backward(jnp.swapaxes(shard_map, 1, 2), grad_state)
        gradient_transfer = jnp.einsum(
            "rgm,ram->rga", later_blocks, running_state, precision=highest_precision
        )

        def local_summary(ext_in, mix_in, conv_in, scale_in, shift_in):
            return summary(
                ext_in, mix_in, conv_in, scale_in, shift_in, doc_ext, prev_docs, head_count
            )

        _, summary_back = jax.vjp(
            local_summary, extended, mix_pre, conv_weight, decay_scale, decay_shift
        )
        grad_ext, grad_mix, grad_conv, grad_scale, grad_shift = summary_back(
            (gradient_transfer, later_blocks, grad_kept)
        )
        returned = passed_along(grad_ext[: CONVK - 1], SEQ, -1)
        grad_qkv = grad_ext[CONVK - 1 :] + jnp.pad(returned, ((row_count - (CONVK - 1), 0), (0, 0)))
        grad_pre = jnp.concatenate([grad_qkv, grad_gate_pre], axis=1).astype(jnp.bfloat16)
        grad_proj_weight = inner_t(normed, grad_pre)
        normed_float = normed.astype(jnp.float32)
        grad_mix_weight = lax.dot_general(
            normed_float, grad_mix, (((0,), (0,)), ((), ())), precision=highest_precision
        )
        grad_normed = head_total(
            proj_t(grad_pre, proj_weight)
            + lax.dot_general(
                grad_mix, mix_weight, (((1,), (1,)), ((), ())), precision=highest_precision
            )
        )
        _, attn_norm_back = jax.vjp(rms_norm, resid_in.astype(jnp.float32), attn_gain)
        grad_resid_norm, grad_attn_gain = attn_norm_back(grad_normed)
        grad_resid = grad_mid + grad_resid_norm
        rows_grads = (
            grad_attn_gain,
            grad_mlp_gain,
            grad_proj_weight,
            grad_mix_weight,
            grad_gu_weight,
        )
        cols_grads = (grad_out_weight, grad_down)
        small_grads = (grad_conv, grad_scale, grad_shift, grad_norm_weight)
        return (grad_resid, rows_grads, cols_grads, small_grads)

    zero_in = jnp.zeros((row_count, model_width), jnp.bfloat16)
    incoming = zero_in
    stored = None
    activations_buf = jnp.zeros(tokens.shape, jnp.bfloat16)
    stat_sums = jnp.zeros((micro_count, 3), jnp.float32)
    stat_counts = jnp.zeros((micro_count,), jnp.float32)
    for slot_index in range(micro_count + 1):
        chosen_raw = slot_index - section_index
        active = (chosen_raw >= 0) & (chosen_raw < micro_count)
        chosen = jnp.clip(chosen_raw, 0, micro_count - 1)
        resid_in = jnp.where(section_index == 0, tokens[min(slot_index, micro_count - 1)], incoming)
        layer_starts = doc_starts[chosen]
        layer_doc_ext = doc_index(layer_starts, ext_pos)
        layer_prev_docs = doc_index(layer_starts, block_pos)
        resid = resid_in.astype(jnp.float32)
        layer_normed = rms_norm(resid, attn_gain).astype(jnp.bfloat16)
        projected = jnp.dot(layer_normed, proj_weight, preferred_element_type=jnp.float32)
        layer_mix_pre = jnp.dot(
            layer_normed.astype(jnp.float32), mix_weight, precision=highest_precision
        )
        qkv_pre = projected[:, :width_qkv]
        layer_gate_pre = projected[:, width_qkv:]
        rim_rows = passed_along(qkv_pre[row_count - (CONVK - 1) :], SEQ, 1)
        layer_extended = jnp.concatenate([rim_rows, qkv_pre], axis=0)
        layer_shard_map, layer_shard_add, layer_kept = summary(
            layer_extended,
            layer_mix_pre,
            conv_weight,
            decay_scale,
            decay_shift,
            layer_doc_ext,
            layer_prev_docs,
            head_count,
        )
        carry_identity = jnp.broadcast_to(
            jnp.eye(layer_shard_map.shape[1], dtype=jnp.float32), layer_shard_map.shape
        )
        prefix = carried_in(
            (layer_shard_map, layer_shard_add),
            SEQ,
            compose,
            (carry_identity, jnp.zeros_like(layer_shard_add)),
        )
        carry_result = prefix[1]
        layer_mixed_out = finish(layer_kept, carry_result)
        layer_gated = gate_norm(layer_mixed_out, layer_gate_pre, norm_weight, head_count).astype(
            jnp.bfloat16
        )
        attn = head_total(jnp.dot(layer_gated, out_weight, preferred_element_type=jnp.float32))
        layer_resid_mid = resid + attn
        layer_ffn_in = rms_norm(layer_resid_mid, mlp_gain).astype(jnp.bfloat16)
        layer_gate_up = jnp.dot(layer_ffn_in, gate_up_weight, preferred_element_type=jnp.float32)
        layer_hidden = (
            jax.nn.silu(layer_gate_up[:, :hidden_width]) * layer_gate_up[:, hidden_width:]
        ).astype(jnp.bfloat16)
        ffn = head_total(jnp.dot(layer_hidden, down_weight, preferred_element_type=jnp.float32))
        layer_out = layer_resid_mid + ffn
        layer_saved = (
            resid_in,
            layer_normed,
            layer_mix_pre,
            layer_extended,
            layer_gate_pre,
            layer_kept,
            carry_result,
            layer_shard_map,
            layer_mixed_out,
            layer_gated,
            layer_resid_mid,
            layer_ffn_in,
            layer_gate_up,
            layer_hidden,
        )
        saved, layer_out, attn_out, ffn_out = (layer_saved, layer_out, attn, ffn)
        if stored is None:
            stored = jax.tree.map(
                lambda part_new: jnp.zeros((micro_count,) + part_new.shape, part_new.dtype), saved
            )
        stored = jax.tree.map(
            lambda buffer, part_new: buffer.at[chosen].set(
                jnp.where(active, part_new, buffer[chosen])
            ),
            stored,
            saved,
        )
        outgoing = layer_out.astype(jnp.bfloat16)
        activations_buf = activations_buf.at[chosen].set(
            jnp.where(active, outgoing, activations_buf[chosen])
        )
        weights_valid = valid_mask[chosen].astype(jnp.float32)
        sums_now = jnp.stack(
            [
                jnp.sum(weights_valid * jnp.mean(branch_val * branch_val, axis=-1))
                for branch_val in (layer_out, attn_out, ffn_out)
            ]
        )
        stat_sums = stat_sums.at[chosen].set(jnp.where(active, sums_now, stat_sums[chosen]))
        stat_counts = stat_counts.at[chosen].set(
            jnp.where(active, jnp.sum(weights_valid), stat_counts[chosen])
        )
        if slot_index < micro_count:
            incoming = partner(outgoing)
    rows_acc = None
    cols_acc = None
    small_acc = None
    back_in = zero_in
    grad_inputs = jnp.zeros(tokens.shape, jnp.bfloat16)
    for slot_index in range(micro_count + 1):
        chosen_raw = slot_index - (1 - section_index)
        active = (chosen_raw >= 0) & (chosen_raw < micro_count)
        chosen = jnp.clip(chosen_raw, 0, micro_count - 1)
        saved = jax.tree.map(lambda buffer: buffer[chosen], stored)
        from_loss = (
            cotangent[chosen].astype(jnp.float32) * valid_mask[chosen].astype(jnp.float32)[:, None]
        )
        upstream = jnp.where(section_index == 1, from_loss, back_in.astype(jnp.float32))
        grad_resid, rows_grads, cols_grads, small_grads = layer_backward(
            saved, upstream, doc_starts[chosen]
        )
        rows_grads = jax.tree.map(lambda grad_part: jnp.where(active, grad_part, 0.0), rows_grads)
        cols_grads = jax.tree.map(lambda grad_part: jnp.where(active, grad_part, 0.0), cols_grads)
        small_grads = jax.tree.map(lambda grad_part: jnp.where(active, grad_part, 0.0), small_grads)
        if rows_acc is None:
            rows_acc, cols_acc, small_acc = (rows_grads, cols_grads, small_grads)
        else:
            rows_acc = jax.tree.map(jnp.add, rows_acc, rows_grads)
            cols_acc = jax.tree.map(jnp.add, cols_acc, cols_grads)
            small_acc = jax.tree.map(jnp.add, small_acc, small_grads)
        outgoing = grad_resid.astype(jnp.bfloat16)
        grad_inputs = grad_inputs.at[chosen].set(jnp.where(active, outgoing, grad_inputs[chosen]))
        if slot_index < micro_count:
            back_in = partner(outgoing)
    rows_part, cols_part = spread(rows_acc, cols_acc)
    norm_heads = lax.psum(small_acc[3], HEAD)
    conv_sum, scale_sum, shift_sum, norm_sum, sums_all, counts_all = (
        lax.psum(small_acc[0].astype(jnp.bfloat16), SEQ).astype(jnp.float32),
        lax.psum(small_acc[1].astype(jnp.bfloat16), SEQ).astype(jnp.float32),
        lax.psum(small_acc[2].astype(jnp.bfloat16), SEQ).astype(jnp.float32),
        lax.psum(norm_heads.astype(jnp.bfloat16), SEQ).astype(jnp.float32),
        lax.psum(stat_sums.astype(jnp.bfloat16), SEQ).astype(jnp.float32),
        lax.psum(stat_counts.astype(jnp.bfloat16), SEQ).astype(jnp.float32),
    )
    branch_rms = jnp.sqrt(sums_all / jnp.maximum(counts_all, 1.0)[:, None])
    proj_part = rows_part[2]
    mix_part = rows_part[3]
    gu_part = rows_part[4]
    return (
        activations_buf[None],
        grad_inputs[None],
        branch_rms[None],
        rows_part[0][None],
        proj_part[:, :width_qk][None],
        proj_part[:, width_qk : 2 * width_qk][None],
        proj_part[:, 2 * width_qk : width_qkv][None],
        proj_part[:, width_qkv:][None],
        mix_part[:, :head_count][None],
        mix_part[:, head_count:][None],
        conv_sum[:, :width_qk][None],
        conv_sum[:, width_qk : 2 * width_qk][None],
        conv_sum[:, 2 * width_qk :][None],
        scale_sum[None],
        shift_sum[None],
        norm_sum[None],
        cols_part[0][None],
        rows_part[1][None],
        gu_part[:, :hidden_width][None],
        gu_part[:, hidden_width:][None],
        cols_part[1][None],
    )


def high_low(value):
    high = value.astype(jnp.bfloat16)
    return high, (value - high.astype(jnp.float32)).astype(jnp.bfloat16)


@functools.partial(jax.custom_vjp, nondiff_argnums=(2,))
def fine_dot(a, b, dims):
    a_high, a_low = high_low(a)
    b_high, b_low = high_low(b)

    def part(x, y):
        return lax.dot_general(x, y, (dims, ((), ())), preferred_element_type=jnp.float32)

    return part(a_high, b_high) + (part(a_high, b_low) + part(a_low, b_high))


def fine_dot_fwd(a, b, dims):
    return fine_dot(a, b, dims), (a, b)


def fine_dot_bwd(dims, kept, grad):
    a, b = kept
    (a_dim,), (b_dim,) = dims
    if a_dim == 1:
        da = fine_dot(grad, b, ((1,), (1 - b_dim,)))
    else:
        da = fine_dot(b, grad, ((1 - b_dim,), (1,)))
    if b_dim == 0:
        db = fine_dot(a, grad, ((1 - a_dim,), (0,)))
    else:
        db = fine_dot(grad, a, ((0,), (1 - a_dim,)))
    return da, db


fine_dot.defvjp(fine_dot_fwd, fine_dot_bwd)


def dot_nn(a, b):
    return fine_dot(a, b, ((1,), (0,)))


def dot_nt(a, b):
    return fine_dot(a, b, ((1,), (1,)))


def dot_tn(a, b):
    return fine_dot(a, b, ((0,), (0,)))


@functools.partial(jax.custom_vjp, nondiff_argnums=(1,))
def shifted(window, steps):
    if steps == 0:
        return window[HALO:]
    return pltpu.roll(window, steps, 0)[HALO:]


def shifted_fwd(window, steps):
    return shifted(window, steps), None


def shifted_bwd(steps, _, grad):
    padded = jnp.concatenate([jnp.zeros((HALO, grad.shape[1]), grad.dtype), grad], axis=0)
    if steps == 0:
        return (padded,)
    return (pltpu.roll(padded, padded.shape[0] - steps, 0),)


shifted.defvjp(shifted_fwd, shifted_bwd)


def iotas(length):
    rows = lax.broadcasted_iota(jnp.int32, (length, length), 0)
    cols = lax.broadcasted_iota(jnp.int32, (length, length), 1)
    return rows, cols


def as_row(column):
    rows, cols = iotas(column.shape[0])
    return jnp.sum(jnp.where(rows == cols, column, 0.0), axis=0, keepdims=True)


def unit_inverses(lowers):
    length = lowers[0].shape[0]
    rows, cols = iotas(length)
    eye = jnp.where(rows == cols, 1.0, 0.0)
    near = [jnp.where((rows >> 3) == (cols >> 3), lower, 0.0) for lower in lowers]
    results = [eye - part for part in near]
    squares = [dot_nn(part, part) for part in near]
    steps = [dot_nn(result, square) for result, square in zip(results, squares)]
    squares = [dot_nn(square, square) for square in squares]
    results = [result + step for result, step in zip(results, steps)]
    steps = [dot_nn(result, square) for result, square in zip(results, squares)]
    results = [result + step for result, step in zip(results, steps)]
    shift = 3
    while (1 << shift) < length:
        off = ((rows >> (shift + 1)) == (cols >> (shift + 1))) & ((rows >> shift) != (cols >> shift))
        steps = [
            dot_nn(jnp.where(off, lower, 0.0), result) for lower, result in zip(lowers, results)
        ]
        steps = [dot_nn(result, step) for result, step in zip(results, steps)]
        results = [result - step for result, step in zip(results, steps)]
        shift += 1
    return results


@jax.custom_vjp
def inverse_known(lower, inverse):
    return inverse


def inverse_known_fwd(lower, inverse):
    return inverse, inverse


def inverse_known_bwd(inverse, grad):
    return -dot_nt(dot_tn(inverse, grad), inverse), jnp.zeros_like(grad)


inverse_known.defvjp(inverse_known_fwd, inverse_known_bwd)


def silu(values):
    return values / (1.0 + jnp.exp(-values))


def sigmoid(values):
    return 1.0 / (1.0 + jnp.exp(-values))


@jax.custom_vjp
def softplus(values):
    return jnp.maximum(values, 0.0) + jnp.log1p(jnp.exp(-jnp.abs(values)))


def softplus_fwd(values):
    return softplus(values), values


def softplus_bwd(values, grad):
    return (grad * sigmoid(values),)


softplus.defvjp(softplus_fwd, softplus_bwd)


def block_front(window, mix_decay, mix_write, taps, decay_log, decay_bias, aux):
    summed = shifted(window, 0) * taps[3]
    for steps in range(1, CONVK):
        summed = summed + jnp.where(aux[:, steps : steps + 1] > 0.0, shifted(window, steps), 0.0) * taps[3 - steps]
    active = silu(summed)
    queries = unit_rows(active[:, :HEAD_K]) * HEAD_K ** (-0.5)
    keys = unit_rows(active[:, HEAD_K : 2 * HEAD_K])
    values = active[:, 2 * HEAD_K :]
    write = sigmoid(mix_write)
    log_decay = -jnp.exp(decay_log) * softplus(mix_decay + decay_bias)
    rows, cols = iotas(BLOCK)
    cum = jnp.sum(jnp.where(cols <= rows, as_row(log_decay), 0.0), axis=1, keepdims=True)
    total = jnp.sum(log_decay, axis=0, keepdims=True)
    doc = aux[:, 0:1]
    same = (doc == as_row(doc)) & (cols <= rows)
    decay = jnp.where(same, jnp.exp(jnp.where(same, cum - as_row(cum), 0.0)), 0.0)
    entry = jnp.where(aux[:, 4:5] > 0.0, jnp.exp(cum), 0.0)
    leave = jnp.where(aux[:, 5:6] > 0.0, jnp.exp(total - cum), 0.0)
    through = jnp.where(aux[BLOCK - 1 : BLOCK, 4:5] > 0.0, jnp.exp(total), 0.0)
    grams = dot_nt(jnp.concatenate([keys, queries], axis=0), keys)
    lower = jnp.where(cols < rows, write * decay * grams[:BLOCK], 0.0)
    mixing = grams[BLOCK:] * decay
    scaled = jnp.concatenate([write * values, (write * entry) * keys], axis=1)
    return lower, mixing, scaled, entry * queries, leave * keys, through


def block_prepare(window, mix_decay, mix_write, taps, decay_log, decay_bias, aux, inverse):
    lower, mixing, scaled, queries, keys, through = block_front(
        window, mix_decay, mix_write, taps, decay_log, decay_bias, aux
    )
    return mixing, dot_nn(inverse_known(lower, inverse), scaled), queries, keys, through


def block_core(mixing, resolved, queries, keys, through, state):
    read = dot_nn(jnp.concatenate([resolved[:, HEAD_V:], queries], axis=0), state)
    written = resolved[:, :HEAD_V] - read[:BLOCK]
    mixed = read[BLOCK:] + dot_nn(mixing, written)
    return mixed, through * state + dot_tn(keys, written)


def each_slice(piece_ref, refs, parts):
    shards, slices = parts
    sub = refs[0].shape[0] // shards
    for number, ref in enumerate(refs):
        for shard in range(shards):
            start = (shard * slices + (piece_ref[0] ^ number)) * sub
            yield pl.multiple_of(start, sub), pl.ds(shard * sub, sub), sub, ref


def fill_inputs(piece_ref, xh_refs, parts, xbuf, mixbuf):
    width = xbuf.shape[1]
    xbuf[0:HALO, :] = jnp.zeros((HALO, width), jnp.float32)
    for start, there, sub, ref in each_slice(piece_ref, xh_refs, parts):
        here = pl.ds(pl.multiple_of(start + HALO, HALO), sub)
        xbuf[here, :] = ref[there, :width].astype(jnp.float32)
        mixbuf[pl.ds(start, sub), :] = ref[there, width:].astype(jnp.float32)


def load_block(aux_ref, xbuf, mixbuf, base):
    window = xbuf[pl.ds(base, BLOCK + HALO), :]
    mix = mixbuf[pl.ds(base, BLOCK), :]
    aux = aux_ref[pl.ds(base, BLOCK), :]
    return window, mix[:, 0:1] + mix[:, 2:3], mix[:, 1:2] + mix[:, 3:4], aux


def load_taps(taps_ref):
    return [taps_ref[j : j + 1, :] for j in range(CONVK)]


def forward_kernel(parts, piece_ref, *refs):
    slices = parts[1]
    xh_refs, refs = refs[:slices], refs[slices:]
    aux_ref, taps_ref, scal_ref, *mixed_refs = refs[: 3 + slices]
    states_ref, inverse_ref, xbuf, mixbuf, mixed_buf, state_ref = refs[3 + slices :]
    fill_inputs(piece_ref, xh_refs, parts, xbuf, mixbuf)
    state_ref[...] = jnp.zeros_like(state_ref)
    blocks = aux_ref.shape[0] // BLOCK
    taps = load_taps(taps_ref)
    decay_log = scal_ref[0:1, 0:1]
    decay_bias = scal_ref[0:1, 1:2]

    def group(index, carry):
        state = state_ref[...]
        places, fronts = [], []
        for inner in range(GROUP):
            number = index * GROUP + inner
            base = pl.multiple_of(number * BLOCK, BLOCK)
            window, mix_decay, mix_write, aux = load_block(aux_ref, xbuf, mixbuf, base)
            places.append((number, base))
            fronts.append(block_front(window, mix_decay, mix_write, taps, decay_log, decay_bias, aux))
        inverses = unit_inverses([front[0] for front in fronts])
        resolved = [dot_nn(inverse, front[2]) for inverse, front in zip(inverses, fronts)]
        for (number, base), front, inverse, solved in zip(places, fronts, inverses, resolved):
            states_ref[number] = state
            inverse_ref[pl.ds(base, BLOCK), :] = inverse
            mixed, state = block_core(front[1], solved, *front[3:], state)
            mixed_buf[pl.ds(base, BLOCK), :] = mixed.astype(mixed_buf.dtype)
        state_ref[...] = state
        return carry

    lax.fori_loop(0, blocks // GROUP, group, 0)
    for start, there, sub, ref in each_slice(piece_ref, mixed_refs, parts):
        ref[there, :] = mixed_buf[pl.ds(start, sub), :]


def backward_kernel(parts, piece_ref, *refs):
    slices = parts[1]
    xh_refs, grad_refs, refs = refs[:slices], refs[slices : 2 * slices], refs[2 * slices :]
    aux_ref, taps_ref, scal_ref, states_ref, inverse_ref, *dxh_refs = refs[: 5 + slices]
    dtaps_ref, dscal_ref, xbuf, mixbuf, grad_buf, dxh_buf, adjoint_ref, halo_ref = refs[5 + slices :]
    fill_inputs(piece_ref, xh_refs, parts, xbuf, mixbuf)
    for start, there, sub, ref in each_slice(piece_ref, grad_refs, parts):
        grad_buf[pl.ds(start, sub), :] = ref[there, :]
    adjoint_ref[...] = jnp.zeros_like(adjoint_ref)
    halo_ref[...] = jnp.zeros_like(halo_ref)
    dtaps_ref[...] = jnp.zeros_like(dtaps_ref)
    dscal_ref[...] = jnp.zeros_like(dscal_ref)
    blocks = aux_ref.shape[0] // BLOCK
    width = xbuf.shape[1]
    taps = load_taps(taps_ref)
    decay_log = scal_ref[0:1, 0:1]
    decay_bias = scal_ref[0:1, 1:2]
    lanes = lax.broadcasted_iota(jnp.int32, (BLOCK, EXTRA), 1)

    def group(index, carry):
        adjoint = adjoint_ref[...]
        halo = halo_ref[...]
        dtaps = [dtaps_ref[j : j + 1, :] for j in range(CONVK)]
        dlog = dscal_ref[0:1, 0:1]
        dbias = dscal_ref[0:1, 1:2]
        places, prepares, cores = [], [], []
        for inner in range(GROUP):
            number = blocks - 1 - (index * GROUP + inner)
            base = pl.multiple_of(number * BLOCK, BLOCK)
            window, mix_decay, mix_write, aux = load_block(aux_ref, xbuf, mixbuf, base)
            inverse = inverse_ref[pl.ds(base, BLOCK), :]
            prepared, pull = jax.vjp(
                functools.partial(block_prepare, aux=aux, inverse=inverse),
                window, mix_decay, mix_write, taps, decay_log, decay_bias,
            )
            places.append(base)
            prepares.append(pull)
            cores.append(jax.vjp(block_core, *prepared, states_ref[number])[1])
        dprepared = []
        for base, pull in zip(places, cores):
            grad = grad_buf[pl.ds(base, BLOCK), :].astype(jnp.float32)
            *dparts, adjoint = pull((grad, adjoint))
            dprepared.append(tuple(dparts))
        for base, pull, dparts in zip(places, prepares, dprepared):
            dwindow, ddecay, dwrite, dtaps_now, dlog_now, dbias_now = pull(dparts)
            own = dwindow[HALO:]
            own = jnp.concatenate([own[: BLOCK - HALO], own[BLOCK - HALO :] + halo], axis=0)
            halo = dwindow[:HALO]
            dtaps = [a + b for a, b in zip(dtaps, dtaps_now)]
            dlog = dlog + dlog_now
            dbias = dbias + dbias_now
            dxh_buf[pl.ds(base, BLOCK), :width] = own.astype(dxh_buf.dtype)
            high_decay = ddecay.astype(jnp.bfloat16).astype(jnp.float32)
            high_write = dwrite.astype(jnp.bfloat16).astype(jnp.float32)
            mix = jnp.where(lanes == 0, high_decay, jnp.where(lanes == 1, high_write, 0.0))
            mix = jnp.where(lanes == 2, ddecay - high_decay, jnp.where(lanes == 3, dwrite - high_write, mix))
            dxh_buf[pl.ds(base, BLOCK), width:] = mix.astype(dxh_buf.dtype)
        adjoint_ref[...] = adjoint
        halo_ref[...] = halo
        for j in range(CONVK):
            dtaps_ref[j : j + 1, :] = dtaps[j]
        dscal_ref[0:1, 0:1] = dlog
        dscal_ref[0:1, 1:2] = dbias
        return carry

    lax.fori_loop(0, blocks // GROUP, group, 0)
    for start, there, sub, ref in each_slice(piece_ref, dxh_refs, parts):
        ref[there, :] = dxh_buf[pl.ds(start, sub), :]


WIDTH = 2 * HEAD_K + HEAD_V


def whole():
    return pl.BlockSpec(memory_space=pltpu.VMEM)


def recur_cost(length):
    return pl.CostEstimate(flops=length * RECUR_FLOPS, bytes_accessed=length * 8192, transcendentals=0)


def recur_forward(piece, xh, aux, taps, scal, parts):
    length = aux.shape[0]
    blocks = length // BLOCK
    slices = len(xh)
    *mixed, states, inverse = pl.pallas_call(
        functools.partial(forward_kernel, parts),
        out_shape=(jax.ShapeDtypeStruct((length // slices, HEAD_V), jnp.bfloat16),) * slices
        + (
            jax.ShapeDtypeStruct((blocks, HEAD_K, HEAD_V), jnp.float32),
            jax.ShapeDtypeStruct((length, BLOCK), jnp.float32),
        ),
        in_specs=[pl.BlockSpec(memory_space=pltpu.SMEM)] + [whole()] * (slices + 3),
        out_specs=(whole(),) * (slices + 2),
        scratch_shapes=[
            pltpu.VMEM((length + HALO, WIDTH), jnp.float32),
            pltpu.VMEM((length, EXTRA), jnp.float32),
            pltpu.VMEM((length, HEAD_V), jnp.bfloat16),
            pltpu.VMEM((HEAD_K, HEAD_V), jnp.float32),
        ],
        compiler_params=pltpu.CompilerParams(vmem_limit_bytes=VMEM_LIMIT),
        cost_estimate=recur_cost(length),
        name="recur_forward",
    )(piece, *xh, aux, taps, scal)
    return mixed, states, inverse


def recur_backward(piece, xh, grad, aux, taps, scal, states, inverse, parts):
    length = aux.shape[0]
    slices = len(xh)
    *dxh, dtaps, dscal = pl.pallas_call(
        functools.partial(backward_kernel, parts),
        out_shape=(jax.ShapeDtypeStruct((length // slices, WIDTH + EXTRA), jnp.bfloat16),) * slices
        + (
            jax.ShapeDtypeStruct((8, WIDTH), jnp.float32),
            jax.ShapeDtypeStruct((8, 128), jnp.float32),
        ),
        in_specs=[pl.BlockSpec(memory_space=pltpu.SMEM)] + [whole()] * (2 * slices + 5),
        out_specs=(whole(),) * (slices + 2),
        scratch_shapes=[
            pltpu.VMEM((length + HALO, WIDTH), jnp.float32),
            pltpu.VMEM((length, EXTRA), jnp.float32),
            pltpu.VMEM((length, HEAD_V), jnp.bfloat16),
            pltpu.VMEM((length, WIDTH + EXTRA), jnp.bfloat16),
            pltpu.VMEM((HEAD_K, HEAD_V), jnp.float32),
            pltpu.VMEM((HALO, WIDTH), jnp.float32),
        ],
        compiler_params=pltpu.CompilerParams(vmem_limit_bytes=VMEM_LIMIT),
        cost_estimate=recur_cost(length),
        name="recur_backward",
    )(piece, *xh, *grad, aux, taps, scal, states, inverse)
    return dxh, dtaps, dscal


def make_aux(starts, length):
    positions = jnp.arange(length, dtype=jnp.int32)
    doc = jnp.sum((starts[None, :] <= positions[:, None]).astype(jnp.int32), axis=1)
    def back(steps):
        earlier = jnp.concatenate([jnp.full((steps,), -1, jnp.int32), doc[:-steps]])
        return (earlier == doc).astype(jnp.float32)
    blocks = doc.reshape(-1, BLOCK)
    before = jnp.concatenate([jnp.full((1,), -1, jnp.int32), blocks[:-1, -1]])
    entering = (blocks == before[:, None]).reshape(-1).astype(jnp.float32)
    leaving = (blocks == blocks[:, -1:]).reshape(-1).astype(jnp.float32)
    zero = jnp.zeros((length,), jnp.float32)
    return jnp.stack([doc.astype(jnp.float32), back(1), back(2), back(3), entering, leaving, zero, zero], axis=1)


def dot(left, right):
    return lax.dot_general(
        left, right, (((1,), (0,)), ((), ())), preferred_element_type=jnp.float32
    )


def in_vmem():
    return pl.BlockSpec(memory_space=pltpu.VMEM)


def in_smem():
    return pl.BlockSpec(memory_space=pltpu.SMEM)


def held(shape):
    return pl.BlockSpec(shape, lambda step: (0,) * len(shape))


def slab(shape, axis):
    return pl.BlockSpec(shape, lambda step: tuple(step if d == axis else 0 for d in range(len(shape))))


def like(shape, dtype):
    return jax.ShapeDtypeStruct(shape, dtype)


def run(kernel, grid, in_specs, out_specs, out_shape, scratch, name, flops, moved, args):
    return pl.pallas_call(
        kernel,
        grid=grid,
        in_specs=in_specs,
        out_specs=out_specs,
        out_shape=out_shape,
        scratch_shapes=scratch,
        compiler_params=pltpu.CompilerParams(vmem_limit_bytes=VMEM_LIMIT),
        cost_estimate=pl.CostEstimate(flops=flops, bytes_accessed=moved, transcendentals=0),
        name=name,
    )(*args)


def row_scale(value):
    return lax.rsqrt(jnp.mean(value * value, axis=-1, keepdims=True) + epsilon)


def mean_square(value, valid):
    return jnp.sum(valid * jnp.mean(value * value, axis=-1, keepdims=True), axis=0, keepdims=True)


def norm_adjoint(value, gain, grad):
    scale = row_scale(value)
    unit = value * scale
    scaled = grad * gain
    dvalue = scale * (scaled - unit * jnp.mean(scaled * unit, axis=-1, keepdims=True))
    return dvalue, jnp.sum(grad * unit, axis=0, keepdims=True)


def each_piece(me_ref, part_refs):
    rows = part_refs[0].shape[0]
    for number, part in enumerate(part_refs):
        start = (me_ref[0] ^ number) * rows
        yield pl.ds(pl.multiple_of(start, rows), rows), part


def hand_out(me_ref, total_ref, piece_refs):
    for where, piece in each_piece(me_ref, piece_refs):
        piece[...] = total_ref[where, :].astype(piece.dtype)


def put_stat(stat_ref, column, value):
    stat_ref[0:1, column : column + 1] += value


def mix_rows(mix_ref):
    mix = mix_ref[0]
    return jnp.concatenate([mix, jnp.zeros((EXTRA - mix.shape[0], mix.shape[1]), mix.dtype)], axis=0)


def project_kernel(kind, pieces, *refs):
    me_ref, valid_ref, gain_ref = refs[:3]
    part_refs = refs[3 : 3 + pieces]
    refs = refs[3 + pieces :]
    if kind == "next":
        base_ref, refs = refs[0], refs[1:]
    w_ref, mix_ref, resid_ref, normed_ref, packed_ref, gate_ref, stat_ref = refs

    @pl.when(pl.program_id(0) == 0)
    def _():
        stat_ref[...] = jnp.zeros_like(stat_ref)
        for where, part in each_piece(me_ref, part_refs):
            value = part[...].astype(jnp.float32)
            if kind == "next":
                valid = valid_ref[where, :]
                put_stat(stat_ref, 1, mean_square(value, valid))
                value = value + base_ref[where, :]
                put_stat(stat_ref, 0, mean_square(value, valid))
            rounded = value.astype(jnp.bfloat16)
            resid_ref[where, :] = rounded
            value = rounded.astype(jnp.float32)
            normed_ref[where, :] = (value * row_scale(value) * gain_ref[...]).astype(jnp.bfloat16)

    normed = normed_ref[...]
    result = dot(normed, w_ref[0])
    packed_ref[0, :, :WIDTH] = result[:, :WIDTH].astype(jnp.bfloat16)
    gate_ref[0] = result[:, WIDTH:]
    mix = proj_t(normed, mix_rows(mix_ref))
    lanes = lax.broadcasted_iota(jnp.int32, mix.shape, 1)
    low = mix - mix.astype(jnp.bfloat16).astype(jnp.float32)
    mix = jnp.where(lanes < 2, mix, jnp.where(lanes < 4, low, 0.0))
    packed_ref[0, :, WIDTH:] = mix.astype(jnp.bfloat16)


def project(me, valid, gain, parts, base, w_proj, w_mix):
    slices, width, columns = w_proj.shape
    sub = parts[0].shape[0]
    rows = sub * len(parts)
    kind = "first" if base is None else "next"
    return run(
        functools.partial(project_kernel, kind, len(parts)),
        (slices,),
        [in_smem(), held((rows, 1)), held((1, width))]
        + [held((sub, width))] * len(parts)
        + ([] if base is None else [held((rows, width))])
        + [slab((1, width, columns), 0), slab((1, 16, width), 0)],
        (
            held((rows, width)),
            held((rows, width)),
            slab((1, rows, WIDTH + EXTRA), 0),
            slab((1, rows, HEAD_V), 0),
            held((8, 128)),
        ),
        (
            like((rows, width), jnp.bfloat16),
            like((rows, width), jnp.bfloat16),
            like((slices, rows, WIDTH + EXTRA), jnp.bfloat16),
            like((slices, rows, HEAD_V), jnp.float32),
            like((8, 128), jnp.float32),
        ),
        [],
        "project_" + kind,
        2 * rows * width * columns * slices,
        w_proj.size * 2 + rows * width * 12,
        [me, valid, gain] + list(parts) + ([] if base is None else [base]) + [w_proj, w_mix],
    )


def output_kernel(slices, me_ref, piece_ref, *refs):
    mixed_refs, refs = refs[:slices], refs[slices:]
    gate_ref, norm_ref, w_ref, gated_ref, kept_ref, *piece_refs, total = refs

    @pl.when(pl.program_id(0) == 0)
    def _():
        for number, mixed_ref in enumerate(mixed_refs):
            j = piece_ref[0] ^ number
            kept_ref[j] = mixed_ref[...]
            value = mixed_ref[...].astype(jnp.float32)
            normed = value * row_scale(value) * norm_ref[...] * silu(gate_ref[j])
            start = pl.multiple_of(j * HEAD_V, HEAD_V)
            gated_ref[:, pl.ds(start, HEAD_V)] = normed.astype(jnp.bfloat16)

    weight = w_ref[0].reshape(gated_ref.shape[1], w_ref.shape[3])
    total[...] = dot(gated_ref[...], weight)
    hand_out(me_ref, total, piece_refs)


def output(me, piece, mixed, gate_pre, norm_weight, w_cols, shards):
    slices, rows, _ = gate_pre.shape
    inner, half = slices * HEAD_V, w_cols.shape[3]
    sub = rows // shards
    gated, kept, *pieces = run(
        functools.partial(output_kernel, slices),
        (2,),
        [in_smem(), in_smem()]
        + [held((rows, HEAD_V))] * slices
        + [held(gate_pre.shape), held((1, HEAD_V)), slab((1, slices, HEAD_V, half), 0)],
        (held((rows, inner)), held(gate_pre.shape)) + (slab((sub, half), 1),) * shards,
        (like((rows, inner), jnp.bfloat16), like(gate_pre.shape, jnp.bfloat16))
        + (like((sub, 2 * half), jnp.bfloat16),) * shards,
        [pltpu.VMEM((rows, half), jnp.float32)],
        "output",
        4 * rows * inner * half,
        inner * half * 4 + rows * inner * 12,
        [me, piece] + list(mixed) + [gate_pre, norm_weight, w_cols],
    )
    return gated, kept, pieces


def feed_kernel(pieces, *refs):
    me_ref, valid_ref, gain_ref = refs[:3]
    part_refs = refs[3 : 3 + pieces]
    base_ref, w_gu_ref = refs[3 + pieces : 5 + pieces]
    down_refs = refs[5 + pieces : -6 - pieces]
    mid_ref, normed_ref, gate_up_ref, hidden_ref, *piece_refs, stat_ref, total = refs[-6 - pieces :]
    step = pl.program_id(0)
    half = down_refs[0].shape[3]

    @pl.when(step == 0)
    def _():
        stat_ref[...] = jnp.zeros_like(stat_ref)
        total[...] = jnp.zeros_like(total)
        for where, part in each_piece(me_ref, part_refs):
            value = part[...].astype(jnp.float32)
            put_stat(stat_ref, 0, mean_square(value, valid_ref[where, :]))
            value = value + base_ref[where, :].astype(jnp.float32)
            mid_ref[where, :] = value
            normed_ref[where, :] = (value * row_scale(value) * gain_ref[...]).astype(jnp.bfloat16)

    result = dot(normed_ref[...], w_gu_ref[0])
    gate_up_ref[0] = result
    width = result.shape[1] // 2
    hidden = (silu(result[:, :width]) * result[:, width:]).astype(jnp.bfloat16)
    hidden_ref[...] = hidden
    for c in range(2):
        part = sum(
            dot(hidden[:, k * LANES : (k + 1) * LANES], ref[c, 0]) for k, ref in enumerate(down_refs)
        )
        total[:, c * half : (c + 1) * half] += part

    @pl.when(step == pl.num_programs(0) - 1)
    def _():
        hand_out(me_ref, total, piece_refs)


def down_slabs(w_cols, hidden):
    half = w_cols.shape[3]

    def block(number):
        return pl.BlockSpec((2, 1, LANES, half), lambda step: (0, step, number, 0))

    first = HEAD_V // LANES
    return [block(first + k) for k in range(hidden // LANES)]


def feed(me, valid, gain, parts, base, w_gu, w_cols):
    slices, width, columns = w_gu.shape
    sub = parts[0].shape[0]
    rows = sub * len(parts)
    hidden = columns // 2
    mid, normed, gate_up, hidden, *pieces, stat = run(
        functools.partial(feed_kernel, len(parts)),
        (slices,),
        [in_smem(), held((rows, 1)), held((1, width))]
        + [held((sub, width))] * len(parts)
        + [held((rows, width)), slab((1, width, columns), 0)]
        + down_slabs(w_cols, hidden),
        (
            held((rows, width)),
            held((rows, width)),
            slab((1, rows, columns), 0),
            slab((rows, hidden), 1),
        )
        + (held((sub, width)),) * len(parts)
        + (held((8, 128)),),
        (
            like((rows, width), jnp.float32),
            like((rows, width), jnp.bfloat16),
            like((slices, rows, columns), jnp.float32),
            like((rows, slices * hidden), jnp.bfloat16),
        )
        + (like((sub, width), jnp.bfloat16),) * len(parts)
        + (like((8, 128), jnp.float32),),
        [pltpu.VMEM((rows, width), jnp.float32)],
        "feed",
        2 * rows * width * (columns + hidden) * slices,
        (w_gu.size + hidden * slices * width) * 2 + rows * width * 16,
        [me, valid, gain] + list(parts) + [base, w_gu] + [w_cols] * (hidden // LANES),
    )
    return mid, normed, gate_up, hidden, pieces, stat


def close_kernel(valid_ref, part_ref, base_ref, out_ref, stat_ref):
    stat_ref[...] = jnp.zeros_like(stat_ref)
    value = part_ref[...].astype(jnp.float32)
    valid = valid_ref[...]
    put_stat(stat_ref, 1, mean_square(value, valid))
    value = value + base_ref[...]
    put_stat(stat_ref, 0, mean_square(value, valid))
    out_ref[...] = value.astype(jnp.bfloat16)


def close(valid, part, base):
    return run(
        close_kernel,
        (),
        [in_vmem()] * 3,
        (in_vmem(), in_vmem()),
        (like(base.shape, jnp.bfloat16), like((8, 128), jnp.float32)),
        [],
        "close",
        base.size * 6,
        base.size * 8,
        [valid, part, base],
    )


def sum_kernel(*refs):
    total = refs[0][...].astype(jnp.float32)
    for ref in refs[1:-1]:
        total = total + ref[...].astype(jnp.float32)
    refs[-1][...] = total.astype(refs[-1].dtype)


def sum_pieces(pieces):
    size = pieces[0].size
    return run(
        sum_kernel,
        (),
        [in_vmem()] * len(pieces),
        in_vmem(),
        like(pieces[0].shape, pieces[0].dtype),
        [],
        "sum_pieces",
        size * len(pieces),
        size * 2 * (len(pieces) + 1),
        list(pieces),
    )


def feed_back_kernel(shards, me_ref, up_ref, gate_up_ref, w_gu_ref, *refs):
    down_refs, (grad_ref, *piece_refs, total) = refs[: -2 - shards], refs[-2 - shards :]
    step = pl.program_id(0)
    half = down_refs[0].shape[3]
    width = gate_up_ref.shape[2] // 2
    upstream = up_ref[...]
    grad_hidden = jnp.concatenate(
        [
            proj_t(upstream[:, :half], ref[0, 0]) + proj_t(upstream[:, half:], ref[1, 0])
            for ref in down_refs
        ],
        axis=1,
    )
    gate = gate_up_ref[0, :, :width]
    up = gate_up_ref[0, :, width:]
    sig = sigmoid(gate)
    grad_ref[0, :, :width] = (grad_hidden * up * (sig * (1.0 + gate * (1.0 - sig)))).astype(jnp.bfloat16)
    grad_ref[0, :, width:] = (grad_hidden * (gate * sig)).astype(jnp.bfloat16)
    part = proj_t(grad_ref[0], w_gu_ref[0])

    @pl.when(step == 0)
    def _():
        total[...] = part

    @pl.when(step > 0)
    def _():
        total[...] += part

    @pl.when(step == pl.num_programs(0) - 1)
    def _():
        hand_out(me_ref, total, piece_refs)


def feed_back(me, upstream, gate_up, w_gu, w_cols, shards):
    slices, width, columns = w_gu.shape
    rows = upstream.shape[0]
    hidden = columns // 2
    sub = rows // shards
    grad, *pieces = run(
        functools.partial(feed_back_kernel, shards),
        (slices,),
        [
            in_smem(),
            held((rows, width)),
            slab((1, rows, columns), 0),
            slab((1, width, columns), 0),
        ]
        + down_slabs(w_cols, hidden),
        (slab((1, rows, columns), 0),) + (held((sub, width)),) * shards,
        (like((slices, rows, columns), jnp.bfloat16),) + (like((sub, width), jnp.bfloat16),) * shards,
        [pltpu.VMEM((rows, width), jnp.float32)],
        "feed_back",
        2 * rows * width * (columns + hidden) * slices,
        (w_gu.size + hidden * slices * width) * 2 + gate_up.size * 6 + rows * width * 4,
        [me, upstream, gate_up, w_gu] + [w_cols] * (hidden // LANES),
    )
    return grad, pieces


def mid_back_kernel(pieces, *refs):
    me_ref, gain_ref = refs[:2]
    part_refs = refs[2 : 2 + pieces]
    (
        mid_ref, up_ref, w_ref, mixed_ref, gate_ref, norm_ref,
        grad_mid_ref, grad_attn_ref, dgain_ref, dmixed_ref, dgate_ref, dnorm_ref,
    ) = refs[2 + pieces :]
    half = w_ref.shape[3]

    @pl.when(pl.program_id(0) == 0)
    def _():
        dgain_ref[...] = jnp.zeros_like(dgain_ref)
        dnorm_ref[...] = jnp.zeros_like(dnorm_ref)
        for where, part in each_piece(me_ref, part_refs):
            dvalue, dgain = norm_adjoint(mid_ref[where, :], gain_ref[...], part[...].astype(jnp.float32))
            dvalue = dvalue + up_ref[where, :].astype(jnp.float32)
            grad_mid_ref[where, :] = dvalue
            grad_attn_ref[where, :] = dvalue.astype(jnp.bfloat16)
            dgain_ref[...] += dgain

    grad = grad_attn_ref[...]
    grad_gated = proj_t(grad[:, :half], w_ref[0, 0]) + proj_t(grad[:, half:], w_ref[1, 0])
    value = mixed_ref[0].astype(jnp.float32)
    scale = row_scale(value)
    unit = value * scale
    weight = norm_ref[...]
    gate = gate_ref[0]
    sig = sigmoid(gate)
    dgate_ref[0] = (grad_gated * unit * weight * (sig * (1.0 + gate * (1.0 - sig)))).astype(jnp.bfloat16)
    dscaled = grad_gated * (gate * sig)
    dnorm_ref[...] += jnp.sum(dscaled * unit, axis=0, keepdims=True)
    dunit = dscaled * weight
    dmixed = scale * (dunit - unit * jnp.mean(dunit * unit, axis=-1, keepdims=True))
    dmixed_ref[0] = dmixed.astype(jnp.bfloat16)


def mid_back(me, gain, parts, mid, upstream, w_cols, mixed, gate_pre, norm_weight):
    slices, rows, _ = mixed.shape
    width = mid.shape[1]
    half = width // 2
    sub = parts[0].shape[0]
    return run(
        functools.partial(mid_back_kernel, len(parts)),
        (slices,),
        [in_smem(), held((1, width))]
        + [held((sub, width))] * len(parts)
        + [
            held((rows, width)),
            held((rows, width)),
            slab((2, 1, HEAD_V, half), 1),
            slab((1, rows, HEAD_V), 0),
            slab((1, rows, HEAD_V), 0),
            held((1, HEAD_V)),
        ],
        (
            held((rows, width)),
            held((rows, width)),
            held((1, width)),
            slab((1, rows, HEAD_V), 0),
            slab((1, rows, HEAD_V), 0),
            held((1, HEAD_V)),
        ),
        (
            like((rows, width), jnp.float32),
            like((rows, width), jnp.bfloat16),
            like((1, width), jnp.float32),
            like((slices, rows, HEAD_V), jnp.bfloat16),
            like((slices, rows, HEAD_V), jnp.bfloat16),
            like((1, HEAD_V), jnp.float32),
        ),
        [],
        "mid_back",
        2 * rows * width * HEAD_V * slices,
        slices * HEAD_V * width * 2 + rows * width * 20,
        [me, gain] + list(parts) + [mid, upstream, w_cols, mixed, gate_pre, norm_weight],
    )


def project_back_kernel(shards, slices, me_ref, piece_ref, *refs):
    part_refs, refs = refs[:slices], refs[slices:]
    dgate_ref, w_ref, mix_ref, normed_ref, grad_ref, dmix_ref, *piece_refs, packed, total = refs
    step = pl.program_id(0)

    @pl.when(step == 0)
    def _():
        for number, part in enumerate(part_refs):
            packed[piece_ref[0] ^ number] = part[...]
        total[...] = jnp.zeros_like(total)

    grad_ref[0, :, :WIDTH] = packed[step, :, :WIDTH]
    grad_ref[0, :, WIDTH:] = dgate_ref[0]
    mix = packed[step, :, WIDTH:]
    total[...] += proj_t(grad_ref[0], w_ref[0]) + dot(mix, mix_rows(mix_ref))
    dmix = inner_t(mix, normed_ref[...])
    dmix_ref[0] = jnp.concatenate([dmix[0:2] + dmix[2:4], dmix[2:8]], axis=0)

    @pl.when(step == pl.num_programs(0) - 1)
    def _():
        hand_out(me_ref, total, piece_refs)


def project_back(me, piece, packed, dgate, w_proj, w_mix, normed, shards):
    slices, width, columns = w_proj.shape
    rows = normed.shape[0]
    sub = rows // shards
    grad, dmix, *pieces = run(
        functools.partial(project_back_kernel, shards, slices),
        (slices,),
        [in_smem(), in_smem()]
        + [held((rows, WIDTH + EXTRA))] * slices
        + [
            slab((1, rows, HEAD_V), 0),
            slab((1, width, columns), 0),
            slab((1, 16, width), 0),
            held((rows, width)),
        ],
        (slab((1, rows, columns), 0), slab((1, 8, width), 0)) + (held((sub, width)),) * shards,
        (like((slices, rows, columns), jnp.bfloat16), like((slices, 8, width), jnp.float32))
        + (like((sub, width), jnp.bfloat16),) * shards,
        [
            pltpu.VMEM((slices, rows, WIDTH + EXTRA), jnp.bfloat16),
            pltpu.VMEM((rows, width), jnp.float32),
        ],
        "project_back",
        2 * rows * width * columns * slices,
        w_proj.size * 2 + rows * width * 12,
        [me, piece] + list(packed) + [dgate, w_proj, w_mix, normed],
    )
    return grad, pieces, dmix


def norm_back_kernel(pieces, *refs):
    me_ref, gain_ref = refs[:2]
    part_refs = refs[2 : 2 + pieces]
    resid_ref, mid_ref, out_ref, dgain_ref = refs[2 + pieces :]
    dgain_ref[...] = jnp.zeros_like(dgain_ref)
    for where, part in each_piece(me_ref, part_refs):
        value = resid_ref[where, :].astype(jnp.float32)
        dvalue, dgain = norm_adjoint(value, gain_ref[...], part[...].astype(jnp.float32))
        out_ref[where, :] = (dvalue + mid_ref[where, :]).astype(jnp.bfloat16)
        dgain_ref[...] += dgain


def norm_back(me, gain, parts, resid, grad_mid):
    return run(
        functools.partial(norm_back_kernel, len(parts)),
        (),
        [in_smem()] + [in_vmem()] * (3 + len(parts)),
        (in_vmem(), in_vmem()),
        (like(resid.shape, jnp.bfloat16), like(gain.shape, jnp.float32)),
        [],
        "norm_back",
        resid.size * 10,
        resid.size * 10,
        [me, gain] + list(parts) + [resid, grad_mid],
    )


def weight_grad_kernel(left_ref, right_ref, out_ref):
    right = right_ref[0] if len(right_ref.shape) == 3 else right_ref[...]
    out_ref[0] = inner_t(left_ref[...], right).astype(jnp.bfloat16)


def grad_rows(left, right):
    rows, width = left.shape
    slices, _, columns = right.shape
    return run(
        weight_grad_kernel,
        (slices,),
        [held((rows, width)), slab((1, rows, columns), 0)],
        slab((1, width, columns), 0),
        like((slices, width, columns), jnp.bfloat16),
        [],
        "grad_rows",
        2 * rows * width * columns * slices,
        slices * width * columns * 2 + rows * width * 2 + right.size * 2,
        [left, right],
    )


def grad_cols_kernel(hidden_ref, up_ref, gated_ref, grad_ref, out_ref):
    rows = hidden_ref.shape[1]
    out_ref[0, 0, :-rows] = inner_t(gated_ref[...], grad_ref[...]).astype(jnp.bfloat16)
    out_ref[0, 0, -rows:] = inner_t(hidden_ref[...], up_ref[...]).astype(jnp.bfloat16)


def grad_cols(hidden, upstream, gated, grad_attn, slices):
    rows, width = upstream.shape
    half = width // 2
    first, second = hidden.shape[1] // slices, gated.shape[1] // slices

    def piece(columns):
        return pl.BlockSpec((rows, columns), lambda c, j: (0, j))

    def side():
        return pl.BlockSpec((rows, half), lambda c, j: (0, c))

    result = run(
        grad_cols_kernel,
        (2, slices),
        [piece(first), side(), piece(second), side()],
        pl.BlockSpec((1, 1, first + second, half), lambda c, j: (c, j, 0, 0)),
        like((2, slices, first + second, half), jnp.bfloat16),
        [],
        "grad_cols",
        4 * rows * (first + second) * slices * half,
        2 * slices * (first + second) * half * 2 + rows * width * 4,
        [hidden, upstream, gated, grad_attn],
    )
    return result.reshape(2, slices * (first + second), half)


def place_kernel(pieces, *refs):
    me_ref, out_ref = refs[0], refs[-1]
    for where, part in each_piece(me_ref, refs[1:-1]):
        out_ref[where, :] = part[...]


def place(me, parts):
    sub, width = parts[0].shape
    shape = (sub * len(parts), width)
    return run(
        functools.partial(place_kernel, len(parts)),
        (),
        [in_smem()] + [in_vmem()] * len(parts),
        in_vmem(),
        like(shape, parts[0].dtype),
        [],
        "place",
        0,
        4 * sub * width * len(parts),
        [me] + list(parts),
    )


def place_cols_kernel(pieces, *refs):
    me_ref, out_ref = refs[0], refs[-1]
    width = refs[1].shape[1]
    for number, part in enumerate(refs[1:-1]):
        start = pl.multiple_of((me_ref[0] ^ number) * width, width)
        out_ref[:, pl.ds(start, width)] = part[...]


def place_cols(me, parts):
    rows, width = parts[0].shape
    shape = (rows, width * len(parts))
    return run(
        functools.partial(place_cols_kernel, len(parts)),
        (),
        [in_smem()] + [in_vmem()] * len(parts),
        in_vmem(),
        like(shape, parts[0].dtype),
        [],
        "place_cols",
        0,
        4 * rows * width * len(parts),
        [me] + list(parts),
    )


def finish_rows_kernel(widths, side_ref, layer0_ref, layer1_ref, received_ref, *out_refs):
    side = side_ref[0]
    own = jnp.where(side == 0, layer0_ref[0], layer1_ref[0]).astype(jnp.float32)
    other = received_ref[0].astype(jnp.float32)
    rows = own.shape[0]
    start = 0
    for width, out_ref in zip(widths, out_refs):
        out_ref[pl.ds(pl.multiple_of(side * rows, rows), rows), :] = own[:, start : start + width]
        out_ref[pl.ds(pl.multiple_of((1 - side) * rows, rows), rows), :] = other[:, start : start + width]
        start += width


def finish_rows(side, layer0, layer1, received, widths):
    shards, rows, columns = layer0.shape
    return run(
        functools.partial(finish_rows_kernel, widths),
        (shards,),
        [in_smem()] + [slab((1, rows, columns), 0)] * 3,
        tuple(slab((2 * rows, width), 1) for width in widths),
        tuple(like((2 * rows, shards * width), jnp.float32) for width in widths),
        [],
        "finish_rows",
        0,
        layer0.size * 14,
        [side, layer0, layer1, received],
    )


def finish_cols_kernel(hidden, side_ref, layer0_ref, layer1_ref, received_ref, down_ref, out_ref):
    side = side_ref[0]
    own = jnp.where(side == 0, layer0_ref[0], layer1_ref[0]).astype(jnp.float32)
    other = received_ref[0].astype(jnp.float32)
    first = out_ref.shape[0]
    columns = own.shape[1]
    here = pl.ds(pl.multiple_of(side * columns, columns), columns)
    there = pl.ds(pl.multiple_of((1 - side) * columns, columns), columns)
    down_ref[:, here] = own[first : first + hidden]
    down_ref[:, there] = other[first : first + hidden]
    out_ref[:, here] = own[:first]
    out_ref[:, there] = other[:first]


def finish_cols(side, layer0, layer1, received, hidden):
    shards, rows, columns = layer0.shape
    return run(
        functools.partial(finish_cols_kernel, hidden),
        (shards,),
        [in_smem()] + [slab((1, rows, columns), 0)] * 3,
        (slab((hidden, 2 * columns), 0), slab((HEAD_V, 2 * columns), 0)),
        (
            like((shards * hidden, 2 * columns), jnp.float32),
            like((shards * HEAD_V, 2 * columns), jnp.float32),
        ),
        [],
        "finish_cols",
        0,
        layer0.size * 14,
        [side, layer0, layer1, received],
    )


def finish_gu_kernel(hidden, side_ref, layer0_ref, layer1_ref, received_ref, gate_ref, up_ref):
    side = side_ref[0]
    shards, rows, columns = layer0_ref.shape
    here = pl.ds(pl.multiple_of(side * rows, rows), rows)
    there = pl.ds(pl.multiple_of((1 - side) * rows, rows), rows)
    for s in range(shards):
        own = jnp.where(side == 0, layer0_ref[s], layer1_ref[s]).astype(jnp.float32)
        other = received_ref[s].astype(jnp.float32)
        for start, out_ref in ((0, gate_ref), (columns // 2, up_ref)):
            out_ref[here, s * hidden : (s + 1) * hidden] = own[:, start : start + hidden]
            out_ref[there, s * hidden : (s + 1) * hidden] = other[:, start : start + hidden]


def finish_gu(side, layer0, layer1, received, hidden):
    shards, rows, _ = layer0.shape
    return run(
        functools.partial(finish_gu_kernel, hidden),
        (),
        [in_smem()] + [in_vmem()] * 3,
        (in_vmem(), in_vmem()),
        (like((2 * rows, shards * hidden), jnp.float32),) * 2,
        [],
        "finish_gu",
        0,
        layer0.size * 14,
        [side, layer0, layer1, received],
    )


def place_tokens_kernel(shards, me_ref, *refs):
    part_refs, out_ref = refs[:-1], refs[-1]
    micros, rows, width = part_refs[0].shape
    columns = width // (2 * shards)
    for number, part in enumerate(part_refs):
        where = pl.ds(pl.multiple_of((me_ref[0] ^ number) * rows, rows), rows)
        for half in range(2):
            for s in range(shards):
                source = (half * shards + s) * columns
                target = (s * 2 + half) * columns
                for m in range(micros):
                    out_ref[m, where, target : target + columns] = part[m, :, source : source + columns]


def place_tokens(me, parts, shards):
    micros, sub, width = parts[0].shape
    shape = (micros, sub * len(parts), width)
    return run(
        functools.partial(place_tokens_kernel, shards),
        (),
        [in_smem()] + [in_vmem()] * len(parts),
        in_vmem(),
        like(shape, parts[0].dtype),
        [],
        "place_tokens",
        0,
        4 * micros * sub * width * len(parts),
        [me] + list(parts),
    )


def join_cols_kernel(part_ref, out_ref):
    out_ref[...] = part_ref[0]


def join_cols(part):
    shards, rows, columns = part.shape
    return run(
        join_cols_kernel,
        (shards,),
        [slab((1, rows, columns), 0)],
        slab((rows, columns), 1),
        like((rows, shards * columns), part.dtype),
        [],
        "join_cols",
        0,
        part.size * 4,
        [part],
    )


def split_cols_kernel(whole_ref, out_ref):
    out_ref[0] = whole_ref[...]


def split_cols(whole, shards):
    rows, width = whole.shape
    columns = width // shards
    return run(
        split_cols_kernel,
        (shards,),
        [slab((rows, columns), 1)],
        slab((1, rows, columns), 0),
        like((shards, rows, columns), whole.dtype),
        [],
        "split_cols",
        0,
        whole.size * 4,
        [whole],
    )


def halves(value, axis):
    step = 1
    while step < lax.axis_size(axis):
        value = value + swapped(value, axis, step.bit_length() - 1)
        step *= 2
    return value


def by_partner(value, axis):
    size = lax.axis_size(axis)
    return [value] + [
        lax.ppermute(value, axis, [(i, i ^ k) for i in range(size)]) for k in range(1, size)
    ]


def in_order(parts, axis):
    position = lax.axis_index(axis)
    parts = list(parts)
    step = 1
    while step < len(parts):
        odd = (position & step) != 0
        parts = [jnp.where(odd, parts[i ^ step], parts[i]) for i in range(len(parts))]
        step *= 2
    return parts


def gathered(value, axis):
    return jnp.concatenate(in_order(by_partner(value, axis), axis), axis=0)


def swap_pieces(pieces, axis):
    size = lax.axis_size(axis)
    return [pieces[0]] + [
        lax.ppermute(pieces[n], axis, [(i, i ^ n) for i in range(size)]) for n in range(1, size)
    ]


def for_partners(parts, me):
    return [lax.dynamic_index_in_dim(parts, me[0] ^ n, 0, False) for n in range(parts.shape[0])]


def exchange(pieces):
    return by_partner(sum_pieces(swap_pieces(pieces, SEQ)), SEQ)


def pick(flag, when, otherwise):
    return jnp.where(flag, when, otherwise)


def both_layers(local, axis):
    core = lax.axis_index(SECTION)
    half = local.shape[axis] // 2
    own = lax.dynamic_slice_in_dim(local, core * half, half, axis)
    received = partner(lax.dynamic_slice_in_dim(local, (1 - core) * half, half, axis))
    first = core == 0
    return pick(first, own, received), pick(first, received, own)


def move_rows(part):
    return lax.all_to_all(part, SEQ, 0, 0).reshape(-1, part.shape[2])


def move_cols(part):
    return join_cols(lax.all_to_all(part, SEQ, 0, 0))


def spread_rows(part):
    full = lax.all_gather(part, (HEAD, SECTION), axis=0, tiled=True)
    return full.reshape(lax.axis_size(HEAD), -1, part.shape[1])


def spread_cols(part):
    full = lax.all_gather(part, (SECTION, HEAD), axis=0, tiled=True)
    return full.reshape(2, lax.axis_size(HEAD), -1, part.shape[1])


def reduce_rows(grad):
    return lax.psum_scatter(
        grad.reshape(-1, grad.shape[2]), (HEAD, SECTION), scatter_dimension=0, tiled=True
    )


def reduce_cols(grad):
    return lax.psum_scatter(
        grad.reshape(-1, grad.shape[2]), (SECTION, HEAD), scatter_dimension=0, tiled=True
    )


def collect_rows(part):
    shards = lax.axis_size(SEQ)
    return lax.all_to_all(part.reshape(shards, -1, part.shape[1]), SEQ, 0, 0)


def collect_cols(part):
    return lax.all_to_all(split_cols(part, lax.axis_size(SEQ)), SEQ, 0, 0)


def after(value, other):
    return lax.optimization_barrier((value, other))[0]


def layer_backward_fast(me, piece, upstream, saved, gains, weights, small, aux, parts, plan):
    at_mid, sum_rows, start, at_end, at_out, sum_cols, before_end, last_due = plan
    attn_gain, mlp_gain = gains
    w_proj, w_mix, w_cols, w_gu = weights
    taps, scal, norm_weight = small
    resid, normed, gate_pre, mixer, mid, ffn_in, gate_up, hidden = saved
    xh, states, inverse, mixed, gated = mixer
    shards = parts[0]
    slices, rows, _ = mixed.shape
    grad_gate_up, pieces = feed_back(me, upstream, gate_up, w_gu, w_cols, shards)
    grad_gu = grad_rows(ffn_in, grad_gate_up)
    pieces = swap_pieces(pieces, SEQ)
    pieces, _ = lax.optimization_barrier((pieces, grad_gu))
    sums = at_mid(by_partner(sum_pieces(pieces), SEQ))
    grad_mid, grad_attn, dmlp, dmixed, dgate, dnorm = mid_back(
        me, mlp_gain, sums, mid, upstream, w_cols, mixed, gate_pre, norm_weight
    )
    grad_both = grad_cols(hidden, upstream, gated, grad_attn, slices)
    grad_head = swap_pieces(for_partners(dmixed, piece), HEAD)
    grad_head, grad_both = lax.optimization_barrier((grad_head, grad_both))
    sum_gu = sum_rows(grad_gu, dmixed)
    running = start(grad_head, sum_gu)
    dxh, dtaps, dscal = recur_backward(piece, xh, grad_head, aux, taps, scal, states, inverse, parts)
    dxh, running = at_end(dxh, running, sum_gu)
    packed = swap_pieces(dxh, HEAD)
    grad_pre, pieces, dmix = project_back(me, piece, packed, dgate, w_proj, w_mix, normed, shards)
    pieces, running = at_out(pieces, running)
    grad_proj = grad_rows(normed, grad_pre)
    pieces = swap_pieces(pieces, SEQ)
    pieces, _ = lax.optimization_barrier((pieces, grad_proj))
    sums, sum_both = sum_cols(grad_both, (sum_gu, dxh), pieces)
    sums, running = lax.optimization_barrier((sums, running))
    sums = before_end(sums)
    grad_resid, dattn = norm_back(me, attn_gain, sums, resid, grad_mid)
    sum_proj = reduce_rows(after(grad_proj, last_due(sum_both, sums, sum_gu, grad_resid)))
    small_grads = (dtaps[:CONVK], dscal[0, :2], dnorm[0], dattn[0], dmlp[0], dmix[:, :2])
    return grad_resid, (sum_proj, sum_gu, sum_both), small_grads, running


def fast_shards(
    tokens,
    cotangent,
    doc_starts,
    valid_mask,
    gain_attn,
    w_query,
    w_key,
    w_value,
    w_gate_out,
    w_decay,
    w_beta,
    conv_query,
    conv_key,
    conv_value,
    decay_log,
    decay_bias,
    out_norm,
    w_output,
    gain_mlp,
    w_gate,
    w_up,
    w_down,
):
    core = lax.axis_index(SECTION)
    first = core == 0
    shard = lax.axis_index(SEQ)
    piece = lax.axis_index(HEAD)
    shards, slices = lax.axis_size(SEQ), lax.axis_size(HEAD)
    parts = (shards, slices)
    shard_rows = w_query.shape[1]
    model_width = tokens.shape[2]
    sub = tokens.shape[1] // slices
    length = tokens.shape[1] * shards
    hidden_width = w_gate.shape[2] // shards
    hidden_padded = -(-hidden_width // 128) * 128

    def columns(value, width):
        return jnp.stack([value[:, s * width : (s + 1) * width] for s in range(shards)])

    def halved(value):
        shape = value.shape[:-1]
        value = value.reshape(shape + (shards, 2, model_width // (2 * shards)))
        return jnp.swapaxes(value, -3, -2).reshape(shape + (model_width,))

    proj_local = jnp.concatenate(
        [
            columns(w_query[0], HEAD_K),
            columns(w_key[0], HEAD_K),
            columns(w_value[0], HEAD_V),
            columns(w_gate_out[0], HEAD_V),
        ],
        axis=2,
    )
    fill = ((0, 0), (0, 0), (0, hidden_padded - hidden_width))
    gu_local = jnp.concatenate(
        [jnp.pad(columns(w_gate[0], hidden_width), fill), jnp.pad(columns(w_up[0], hidden_width), fill)],
        axis=2,
    )
    cols_local = jnp.concatenate(
        [
            w_output[0].reshape(shards, HEAD_V, shard_rows),
            w_down[0].reshape(shards, hidden_width, shard_rows),
            jnp.zeros((shards, hidden_padded - hidden_width, shard_rows), jnp.bfloat16),
        ],
        axis=1,
    )
    proj_parts = both_layers(proj_local, 1)
    cols_parts = both_layers(cols_local, 2)
    gu_parts = both_layers(gu_local, 1)

    conv = jnp.concatenate(
        [
            columns(conv_query[0], HEAD_K),
            columns(conv_key[0], HEAD_K),
            columns(conv_value[0], HEAD_V),
        ],
        axis=2,
    )
    taps_own = lax.dynamic_index_in_dim(conv, shard, 0, False).astype(jnp.float32)
    small_own = jnp.concatenate(
        [
            taps_own.reshape(-1),
            jnp.stack([decay_log[0, shard], decay_bias[0, shard]]),
            out_norm[0].astype(jnp.float32),
            gain_attn[0].astype(jnp.float32),
            gain_mlp[0].astype(jnp.float32),
            w_decay[0].astype(jnp.float32).T.reshape(-1),
            w_beta[0].astype(jnp.float32).T.reshape(-1),
        ]
    )
    small_own = after(small_own, proj_parts[0])
    small_other = partner(small_own)
    small_layers = (pick(first, small_own, small_other), pick(first, small_other, small_own))
    taps_size = CONVK * WIDTH
    norm_at = taps_size + 2
    gain_at = norm_at + HEAD_V
    wide = jnp.stack([vector[gain_at:] for vector in small_layers])
    wide = jnp.concatenate([wide.reshape(-1), valid_mask[core].astype(jnp.float32)])
    wide = gathered(wide[None], SEQ)
    valid_all = wide[:, wide.shape[1] - tokens.shape[1] :].reshape(shards, slices, sub)
    valid = lax.dynamic_index_in_dim(valid_all, piece, 1, False).reshape(-1)
    wide = wide[:, : wide.shape[1] - tokens.shape[1]].reshape(shards, 2, 2 + 2 * shards, 2, shard_rows // 2)
    gains_all = jnp.transpose(wide[:, :, :2], (1, 2, 3, 0, 4)).reshape(2, 2, model_width)
    mix_all = wide[:, :, 2:].reshape(shards, 2, 2, shards, 2, shard_rows // 2)
    mix_all = lax.dynamic_index_in_dim(mix_all, shard, 3, False)
    mix_all = jnp.transpose(mix_all, (1, 2, 3, 0, 4)).reshape(2, 2, model_width).astype(jnp.bfloat16)
    mix_all = gathered(mix_all[None], HEAD)
    mix_all = jnp.swapaxes(mix_all, 0, 1)
    mix_all = jnp.concatenate(
        [mix_all, mix_all, jnp.zeros((2, slices, 12, model_width), jnp.bfloat16)], axis=2
    )
    small = []
    gains = []
    weights = []
    for layer in range(2):
        vector = small_layers[layer]
        taps = jnp.pad(vector[:taps_size].reshape(CONVK, WIDTH), ((0, 8 - CONVK), (0, 0)))
        scal = jnp.pad(vector[taps_size:norm_at][None], ((0, 7), (0, 126)))
        small.append((taps, scal, vector[None, norm_at:gain_at]))
        gains.append((gains_all[layer, 0][None], gains_all[layer, 1][None]))

    def my_tokens(value):
        mine = lax.dynamic_slice_in_dim(value, piece * sub, sub, 0)
        return by_partner(halved(mine), SEQ)

    me = shard[None].astype(jnp.int32)
    place_at = piece[None].astype(jnp.int32)
    valid = valid[:, None]
    aux = make_aux(doc_starts[core], length)
    masked = cotangent[core] * valid_mask[core].astype(jnp.bfloat16)[:, None]

    token_parts, base = my_tokens(tokens[core]), None
    proj0 = after(move_rows(proj_parts[0]), (small_layers, cols_parts, gu_parts))
    cols0 = lax.all_to_all(after(cols_parts[0], proj0), SEQ, 0, 0)
    cols0 = join_cols(after(cols0, (token_parts, gains, small, valid, mix_all)))
    gu0 = move_rows(after(gu_parts[0], cols0))
    weights = [(spread_rows(proj0), mix_all[0], spread_cols(cols0), None)]

    saved = []
    stats = []
    for layer in range(2):
        w_proj, w_mix, w_cols, w_gu = weights[layer]
        attn_gain, mlp_gain = gains[layer]
        resid, normed, packed, gate_pre, stat = project(
            me, valid, attn_gain, token_parts, base, w_proj, w_mix
        )
        stats.append(stat)
        xh = swap_pieces(for_partners(packed, place_at), HEAD)
        if layer == 0:
            xh, gu0 = lax.optimization_barrier((xh, gu0))
            w_gu = spread_rows(gu0)
            weights[0] = (w_proj, w_mix, w_cols, w_gu)
            masked = my_tokens(after(masked, gu0))
        mixed, states, inverse = recur_forward(place_at, xh, aux, *small[layer][:2], parts)
        mixed = swap_pieces(mixed, HEAD)
        if layer == 0:
            mixed, masked = lax.optimization_barrier((mixed, masked))
            proj1 = move_rows(after(proj_parts[1], mixed))
        else:
            mixed, gu1 = lax.optimization_barrier((mixed, gu1))
            w_gu = spread_rows(gu1)
            weights[1] = (w_proj, w_mix, w_cols, w_gu)
        gated, kept, pieces = output(me, place_at, mixed, gate_pre, small[layer][2], w_cols, shards)
        mixer = (xh, states, inverse, kept, gated)
        mix_parts = exchange(pieces)
        if layer == 0:
            mix_parts, proj1 = lax.optimization_barrier((mix_parts, proj1))
        base, ffn_in, gate_up, hidden, pieces, stat = feed(
            me, valid, mlp_gain, mix_parts, resid, w_gu, w_cols
        )
        stats.append(stat)
        saved.append((resid, normed, gate_pre, mixer, base, ffn_in, gate_up, hidden))
        if layer == 0:
            cols1 = move_cols(after(cols_parts[1], pieces))
            token_parts = exchange(pieces)
            token_parts, cols1 = lax.optimization_barrier((token_parts, cols1))
            gu1 = move_rows(after(gu_parts[1], token_parts))
            weights.append((spread_rows(proj1), mix_all[1], spread_cols(cols1), None))
    h1 = saved[1][0]
    stats0 = jnp.stack([stats[2][0, 0], stats[1][0, 0], stats[2][0, 1]]) / shards
    upstream = place(me, masked)
    def placed_tokens(layer0, layer1):
        layer0, layer1 = (
            value if value.shape[0] == sub else lax.dynamic_slice_in_dim(value, shard * sub, sub, 0)
            for value in (layer0, layer1)
        )
        keep = pick(first, layer0, layer1)
        received = partner(pick(first, layer1, layer0))
        both = jnp.stack([pick(first, keep, received), pick(first, received, keep)])
        return place_tokens(piece[None].astype(jnp.int32), by_partner(both, HEAD), shards)

    early = {}

    def all_sums(pieces):
        return by_partner(sum_pieces(pieces), SEQ)

    def plan_last():
        def at_mid(sums):
            return sums

        def sum_rows(grad_gu, anchor):
            return reduce_rows(grad_gu)

        def start(anchor, sum_gu):
            return swap_pieces(after(pieces, anchor), SEQ)

        def at_end(dxh, running, sum_gu):
            dxh, running = lax.optimization_barrier((dxh, running))
            return dxh, (running, collect_rows(after(sum_gu, dxh)))

        def at_out(pieces, running):
            return lax.optimization_barrier((pieces, running))

        def sum_cols(grad_both, due, pieces):
            sum_both = reduce_cols(after(grad_both, due))
            return lax.optimization_barrier((all_sums(pieces), sum_both))

        def before_end(sums):
            return sums

        def last_due(sum_both, sums, sum_gu, grad_resid):
            return sum_both, sums

        return at_mid, sum_rows, start, at_end, at_out, sum_cols, before_end, last_due

    grad_h1, big1, small1, (last_sum, moved_gu1) = layer_backward_fast(
        me, place_at, upstream, saved[1], gains[1], weights[1], small[1], aux, parts, plan_last()
    )
    sum_proj1, sum_gu1, sum_both1 = big1
    last_sum = sum_pieces(last_sum)
    moved_both1 = collect_cols(after(sum_both1, grad_h1))
    here = shard * sub
    valid_here = lax.dynamic_slice_in_dim(valid, here, sub, 0)
    act1, stat = close(valid_here, last_sum, lax.dynamic_slice_in_dim(base, here, sub, 0))
    stats1 = jnp.stack([stat[0, 0], stats[3][0, 0] / shards, stat[0, 1]])
    activations = placed_tokens(h1, act1)

    def plan_first():
        def at_mid(sums):
            sums, early["both"] = lax.optimization_barrier((sums, moved_both1))
            return sums

        def sum_rows(grad_gu, anchor):
            return reduce_rows(after(grad_gu, (sum_proj1, anchor)))

        def start(anchor, sum_gu):
            return collect_rows(after(sum_proj1, anchor))

        def at_end(dxh, running, sum_gu):
            return lax.optimization_barrier((dxh, running))

        def at_out(pieces, running):
            return pieces, running

        def sum_cols(grad_both, due, pieces):
            sum_both = reduce_cols(after(grad_both, (due, pieces)))
            return all_sums(pieces), sum_both

        def before_end(sums):
            return sums

        def last_due(sum_both, sums, sum_gu, grad_resid):
            early["gu"] = collect_rows(after(sum_gu, grad_resid))
            return sum_both, early["gu"], placed_tokens(grad_resid, grad_h1)

        return at_mid, sum_rows, start, at_end, at_out, sum_cols, before_end, last_due

    grad_tokens, big0, small0, moved_proj1 = layer_backward_fast(
        me, place_at, grad_h1, saved[0], gains[0], weights[0], small[0], aux, parts, plan_first()
    )
    sum_proj0, sum_gu0, sum_both0 = big0
    moved_both1 = early["both"]
    moved_gu0 = early["gu"]
    moved_both0 = collect_cols(after(sum_both0, moved_gu0))
    input_grads = placed_tokens(grad_tokens, grad_h1)
    side = core[None].astype(jnp.int32)
    grad_down, grad_out = finish_cols(
        side, moved_both0, moved_both1, partner(pick(first, moved_both1, moved_both0)), hidden_width
    )
    grad_gate, grad_up = finish_gu(
        side, moved_gu0, moved_gu1, partner(pick(first, moved_gu1, moved_gu0)), hidden_width
    )

    def pack(grads, sums):
        dtaps, dscal, dnorm, dattn, dmlp, dmix = grads
        place = (jnp.arange(2) == core)[:, None]
        marked = jnp.where(place, jnp.concatenate([sums, (jnp.sum(valid) / shards)[None]])[None], 0.0)
        return jnp.concatenate(
            [dtaps.reshape(-1), dscal, dnorm, marked.reshape(-1), dattn, dmlp, dmix.reshape(-1)]
        )

    packs = (pack(small0, stats0), pack(small1, stats1))
    vector = pick(first, packs[0], packs[1]) + partner(pick(first, packs[1], packs[0]))
    gain_end = norm_at + HEAD_V + 8 + 2 * model_width
    per_head = gathered(vector[None, :norm_at], SEQ)
    sums_all = halves(vector[norm_at:gain_end], HEAD)
    norm_sum = halves(sums_all[: HEAD_V + 8], SEQ)
    stat_sums = norm_sum[HEAD_V:].reshape(2, 4)
    norm_sum = norm_sum[:HEAD_V]
    gain_sums = sums_all[HEAD_V + 8 :].reshape(2, 2, shards, shard_rows // 2)
    gain_sums = lax.dynamic_index_in_dim(gain_sums, shard, 2, False).reshape(2, shard_rows)
    branch_rms = jnp.sqrt(stat_sums[:, :3] / jnp.maximum(stat_sums[:, 3:], 1.0))
    mix_grad = vector[gain_end:].reshape(slices, 2, 2, shards, shard_rows // 2)
    mix_grad = jnp.sum(lax.all_to_all(mix_grad, HEAD, 0, 0), axis=0)
    mix_grad = lax.all_to_all(jnp.transpose(mix_grad, (2, 0, 1, 3)), SEQ, 0, 0)
    mix_grad = jnp.transpose(mix_grad, (1, 2, 3, 0)).reshape(2, shard_rows, shards)
    others = (input_grads, grad_down, grad_out, grad_gate, grad_up, mix_grad, norm_sum, gain_sums, per_head)
    sum_proj0, others = lax.optimization_barrier((sum_proj0, others))
    input_grads, grad_down, grad_out, grad_gate, grad_up, mix_grad, norm_sum, gain_sums, per_head = others
    moved_proj0 = collect_rows(sum_proj0)
    grad_proj = finish_rows(
        side, moved_proj0, moved_proj1, partner(pick(first, moved_proj1, moved_proj0)),
        (HEAD_K, HEAD_K, HEAD_V, HEAD_V),
    )
    conv_grad = jnp.swapaxes(per_head[:, :taps_size].reshape(shards, CONVK, WIDTH), 0, 1)

    def conv_part(start, width):
        return conv_grad[:, :, start : start + width].reshape(1, CONVK, shards * width)

    return (
        activations[None],
        input_grads[None],
        branch_rms[None],
        gain_sums[0][None],
        grad_proj[0][None],
        grad_proj[1][None],
        grad_proj[2][None],
        grad_proj[3][None],
        mix_grad[0][None],
        mix_grad[1][None],
        conv_part(0, HEAD_K),
        conv_part(HEAD_K, HEAD_K),
        conv_part(2 * HEAD_K, HEAD_V),
        per_head[:, taps_size][None],
        per_head[:, taps_size + 1][None],
        norm_sum[None],
        grad_out[None],
        gain_sums[1][None],
        grad_gate[None],
        grad_up[None],
        grad_down[None],
    )


def per_device(*args):
    tokens, w_decay = args[0], args[9]
    rows = tokens.shape[1]
    seq, head, section = (lax.axis_size(axis) for axis in (SEQ, HEAD, SECTION))
    one_head_each = w_decay.shape[2] == seq
    micro_each = tokens.shape[0] == section == 2
    powers = seq & (seq - 1) == 0 and head & (head - 1) == 0
    even = rows % (head * BLOCK) == 0 and rows * seq % (BLOCK * GROUP) == 0
    if one_head_each and micro_each and powers and even:
        return fast_shards(*args)
    return shards(*args)


def solution(mesh):
    placed = (
        P(None, SEQ, None),
        P(None, SEQ, None),
        P(),
        P(None, SEQ),
        P(SECTION, SEQ),
        P(SECTION, SEQ, HEAD),
        P(SECTION, SEQ, HEAD),
        P(SECTION, SEQ, HEAD),
        P(SECTION, SEQ, HEAD),
        P(SECTION, SEQ, HEAD),
        P(SECTION, SEQ, HEAD),
        P(SECTION, None, HEAD),
        P(SECTION, None, HEAD),
        P(SECTION, None, HEAD),
        P(SECTION, HEAD),
        P(SECTION, HEAD),
        P(SECTION, None),
        P(SECTION, HEAD, SEQ),
        P(SECTION, SEQ),
        P(SECTION, SEQ, HEAD),
        P(SECTION, SEQ, HEAD),
        P(SECTION, HEAD, SEQ),
    )
    return jax.shard_map(
        per_device,
        mesh=mesh,
        in_specs=placed,
        out_specs=(
            P(SECTION, None, SEQ, None),
            P(SECTION, None, SEQ, None),
            P(SECTION, None, None),
            P(SECTION, SEQ),
            P(SECTION, SEQ, HEAD),
            P(SECTION, SEQ, HEAD),
            P(SECTION, SEQ, HEAD),
            P(SECTION, SEQ, HEAD),
            P(SECTION, SEQ, HEAD),
            P(SECTION, SEQ, HEAD),
            P(SECTION, None, HEAD),
            P(SECTION, None, HEAD),
            P(SECTION, None, HEAD),
            P(SECTION, HEAD),
            P(SECTION, HEAD),
            P(SECTION, None),
            P(SECTION, HEAD, SEQ),
            P(SECTION, SEQ),
            P(SECTION, SEQ, HEAD),
            P(SECTION, SEQ, HEAD),
            P(SECTION, HEAD, SEQ),
        ),
        check_vma=False,
    )
```

```python
import functools

import jax
import jax.numpy as jnp
from jax import lax
from jax.experimental import pallas as pl
from jax.experimental.pallas import tpu as pltpu
from jax.sharding import PartitionSpec as P

HEAD_K = 128
HEAD_V = 256
CONVK = 4
BLOCK = 64
SECTION = "section"
SEQ = "seq"
HEAD = "head"
LANES = 128
RECUR_FLOPS = 40_000_000
VMEM_LIMIT = 62 * 1024 * 1024
HALO = 8
EXTRA = 128
GROUP = 8


epsilon = 1e-06
highest_precision = lax.Precision.HIGHEST


def swapped(value, axis, stride):
    return lax.ppermute(value, axis, [(i, i ^ 1 << stride) for i in range(lax.axis_size(axis))])


def carried_in(value, axis, combine, identity):
    devices, position = (lax.axis_size(axis), lax.axis_index(axis))
    everything = jax.tree.map(
        lambda part, kind: lax.all_gather(part.astype(kind), axis),
        value,
        (jnp.bfloat16, jnp.bfloat16),
    )
    start = jax.tree.map(
        lambda part, zero: jnp.broadcast_to(jnp.asarray(zero, part.dtype), part.shape),
        value,
        identity,
    )

    def step(k, before):
        reached = k < position
        new = combine(
            before, jax.tree.map(lambda part, own: part[k].astype(own.dtype), everything, value)
        )
        return jax.tree.map(lambda a, b: jnp.where(reached, a, b), new, before)

    return lax.fori_loop(0, devices, step, start)


def entering(value, axis, join, neutral):
    count = lax.axis_size(axis)
    place = lax.axis_index(axis)
    ahead = count - 1 - place
    gathered = jax.tree.map(
        lambda a, kind: lax.all_gather(a.astype(kind), axis),
        value,
        jax.tree.map(lambda a: jnp.bfloat16 if a.dtype == jnp.float32 else a.dtype, value),
    )
    state = jax.tree.map(lambda a, e: jnp.zeros_like(a) + jnp.asarray(e, a.dtype), value, neutral)

    def one(step, state):
        source = count - 1 - step
        return join(
            state,
            jax.tree.map(
                lambda a, own: lax.dynamic_index_in_dim(a, source, 0, False).astype(own.dtype),
                gathered,
                value,
            ),
        )

    return lax.fori_loop(0, ahead, one, state)


def passed_along(value, axis, steps):
    count = lax.axis_size(axis)
    first, last = (max(0, -steps), min(count, count - steps))
    return lax.ppermute(value, axis, [(source, source + steps) for source in range(first, last)])


def rms_norm(values, weight):
    return values * lax.rsqrt(jnp.mean(values * values, axis=-1, keepdims=True) + epsilon) * weight


def doc_index(starts, positions):
    counted = jnp.sum(
        (starts[None, :] <= positions[:, None]).astype(jnp.int32), axis=1, dtype=jnp.int32
    )
    return counted - 1


def unit_rows(values):
    return values * lax.rsqrt(jnp.sum(values * values, axis=-1, keepdims=True) + epsilon)


def conv_front(extended, doc_ext, conv_weight):
    length = extended.shape[0] - (CONVK - 1)
    summed = jnp.zeros((length, extended.shape[1]), extended.dtype)
    for tap_index in range(CONVK):
        same_doc = doc_ext[tap_index : tap_index + length] == doc_ext[CONVK - 1 :]
        summed = (
            summed
            + jnp.where(same_doc[:, None], extended[tap_index : tap_index + length], 0.0)
            * conv_weight[tap_index]
        )
    return jax.nn.silu(summed)


def heads_front(extended, doc_ext, mix_pre, conv_weight, decay_scale, decay_shift, head_count):
    activated = conv_front(extended, doc_ext, conv_weight)
    length = activated.shape[0]
    width_k = head_count * HEAD_K
    queries = unit_rows(activated[:, :width_k].reshape(length, head_count, HEAD_K)) * HEAD_K ** (
        -0.5
    )
    key_rows = unit_rows(activated[:, width_k : 2 * width_k].reshape(length, head_count, HEAD_K))
    value_rows = activated[:, 2 * width_k :].reshape(length, head_count, HEAD_V)
    write_rate = jax.nn.sigmoid(mix_pre[:, head_count:])
    log_decay = -jnp.exp(decay_scale) * jax.nn.softplus(mix_pre[:, :head_count] + decay_shift)
    return (queries, key_rows, value_rows, write_rate, log_decay)


def block_terms(queries, key_rows, value_rows, write_rate, log_decay, doc_ids, prev_doc):
    length = queries.shape[1]
    cumulated = jnp.cumsum(log_decay, axis=1)
    row_iota = lax.broadcasted_iota(jnp.int32, (length, length), 0)
    col_iota = lax.broadcasted_iota(jnp.int32, (length, length), 1)
    same_doc = (doc_ids[:, :, None] == doc_ids[:, None, :]) & (col_iota <= row_iota)[None]
    same_mask = same_doc[:, :, :, None]
    exponent = jnp.where(same_mask, cumulated[:, :, None, :] - cumulated[:, None, :, :], 0.0)
    decay_full = jnp.where(same_mask, jnp.exp(exponent), 0.0)
    initial_decay = jnp.where((doc_ids == prev_doc[:, None])[:, :, None], jnp.exp(cumulated), 0.0)
    decay_heads = jnp.transpose(decay_full, (0, 3, 1, 2))
    key_gram = jnp.einsum("nthk,nihk->nhti", key_rows, key_rows, precision=highest_precision)
    strict_mask = (col_iota < row_iota)[None, None]
    lower_part = jnp.where(
        strict_mask,
        jnp.transpose(write_rate, (0, 2, 1))[:, :, :, None] * decay_heads * key_gram,
        0.0,
    )
    system = lower_part + jnp.eye(length, dtype=lower_part.dtype)
    scaled_values = jnp.transpose(write_rate[..., None] * value_rows, (0, 2, 1, 3))
    scaled_keys = jnp.transpose((write_rate * initial_decay)[..., None] * key_rows, (0, 2, 1, 3))
    resolved_values = lax.linalg.triangular_solve(
        system, scaled_values, left_side=True, lower=True, unit_diagonal=True
    )
    resolved_keys = lax.linalg.triangular_solve(
        system, scaled_keys, left_side=True, lower=True, unit_diagonal=True
    )
    query_key = (
        jnp.einsum("nthk,nihk->nhti", queries, key_rows, precision=highest_precision) * decay_heads
    )
    return (resolved_values, resolved_keys, query_key, decay_heads, initial_decay)


def gate_norm(mixed_out, gate_pre, norm_weight, head_count):
    length = mixed_out.shape[0]
    per_head = mixed_out.reshape(length, head_count, HEAD_V)
    gates = gate_pre.reshape(length, head_count, HEAD_V)
    normed = rms_norm(per_head, norm_weight) * jax.nn.silu(gates)
    return normed.reshape(length, head_count * HEAD_V)


def summary(
    extended, mix_pre, conv_weight, decay_scale, decay_shift, doc_ext, prev_docs, head_count
):
    queries, key_rows, value_rows, write_rate, log_decay = heads_front(
        extended, doc_ext, mix_pre, conv_weight, decay_scale, decay_shift, head_count
    )
    length = write_rate.shape[0]
    blocks = length // BLOCK

    def as_blocks(values):
        return values.reshape((blocks, BLOCK) + values.shape[1:])

    block_query_rows = as_blocks(queries)
    block_key_rows = as_blocks(key_rows)
    resolved_values, resolved_keys, query_key, decay_heads, initial_decay = block_terms(
        block_query_rows,
        block_key_rows,
        as_blocks(value_rows),
        as_blocks(write_rate),
        as_blocks(log_decay),
        as_blocks(doc_ext[CONVK - 1 :]),
        prev_docs,
    )
    final_row = decay_heads[:, :, -1, :]
    identity = jnp.eye(HEAD_K, dtype=extended.dtype)
    transfer_blocks = initial_decay[:, -1, :][:, :, None, None] * identity - jnp.einsum(
        "nhi,nihk,nhil->nhkl", final_row, block_key_rows, resolved_keys, precision=highest_precision
    )
    add_blocks = jnp.einsum(
        "nhi,nihk,nhiv->nhkv",
        final_row,
        block_key_rows,
        resolved_values,
        precision=highest_precision,
    )
    local_out = jnp.einsum(
        "nhti,nhiv->nhtv", query_key, resolved_values, precision=highest_precision
    )
    response = jnp.transpose(initial_decay, (0, 2, 1))[..., None] * jnp.transpose(
        block_query_rows, (0, 2, 1, 3)
    ) - jnp.einsum("nhti,nhik->nhtk", query_key, resolved_keys, precision=highest_precision)
    carry_map = jnp.broadcast_to(identity, (head_count, HEAD_K, HEAD_K))
    carried_addend = jnp.zeros((head_count, HEAD_K, HEAD_V), extended.dtype)
    entry_maps = []
    entry_adds = []
    for block_number in range(blocks):
        entry_maps.append(carry_map)
        entry_adds.append(carried_addend)
        carried_addend = (
            jnp.einsum(
                "jme,jed->jmd",
                transfer_blocks[block_number],
                carried_addend,
                precision=highest_precision,
            )
            + add_blocks[block_number]
        )
        carry_map = jnp.einsum(
            "hkl,hlm->hkm", transfer_blocks[block_number], carry_map, precision=highest_precision
        )
    kept = (local_out, response, jnp.stack(entry_maps), jnp.stack(entry_adds))
    return (carry_map, carried_addend, kept)


def finish(kept, running_state):
    local_out, response, entry_maps, entry_adds = kept
    entry_states = (
        jnp.einsum("nhkl,hlv->nhkv", entry_maps, running_state, precision=highest_precision)
        + entry_adds
    )
    result = local_out + jnp.einsum(
        "nhck,nhkv->nhcv", response, entry_states, precision=highest_precision
    )
    blocks, head_count, length, width_v = result.shape
    return jnp.transpose(result, (0, 2, 1, 3)).reshape(blocks * length, head_count * width_v)


def compose(earlier_blocks, later_blocks):
    return (
        jnp.einsum("hkl,hlm->hkm", later_blocks[0], earlier_blocks[0], precision=highest_precision),
        jnp.einsum("jme,jed->jmd", later_blocks[0], earlier_blocks[1], precision=highest_precision)
        + later_blocks[1],
    )


def head_total(values):
    return lax.psum(values.astype(jnp.bfloat16), HEAD).astype(jnp.float32)


def partner(values):
    return swapped(values, SECTION, 0)


def proj_t(left, right):
    return lax.dot_general(
        left, right, (((1,), (1,)), ((), ())), preferred_element_type=jnp.float32
    )


def inner_t(left, right):
    return lax.dot_general(
        left, right, (((0,), (0,)), ((), ())), preferred_element_type=jnp.float32
    )


def spread(rows_grads, cols_grads):
    rows_part = (
        lax.psum_scatter(
            rows_grads[0].astype(jnp.bfloat16), SEQ, scatter_dimension=0, tiled=True
        ).astype(jnp.float32),
        lax.psum_scatter(
            rows_grads[1].astype(jnp.bfloat16), SEQ, scatter_dimension=0, tiled=True
        ).astype(jnp.float32),
        lax.psum_scatter(
            rows_grads[2].astype(jnp.bfloat16), SEQ, scatter_dimension=0, tiled=True
        ).astype(jnp.float32),
        lax.psum_scatter(
            rows_grads[3].astype(jnp.bfloat16), SEQ, scatter_dimension=0, tiled=True
        ).astype(jnp.float32),
        lax.psum_scatter(
            rows_grads[4].astype(jnp.bfloat16), SEQ, scatter_dimension=0, tiled=True
        ).astype(jnp.float32),
    )
    cols_part = (
        lax.psum_scatter(
            cols_grads[0].astype(jnp.bfloat16), SEQ, scatter_dimension=1, tiled=True
        ).astype(jnp.float32),
        lax.psum_scatter(
            cols_grads[1].astype(jnp.bfloat16), SEQ, scatter_dimension=1, tiled=True
        ).astype(jnp.float32),
    )
    return (rows_part, cols_part)


def shards(
    tokens,
    cotangent,
    doc_starts,
    valid_mask,
    gain_attn,
    w_query,
    w_key,
    w_value,
    w_gate_out,
    w_decay,
    w_beta,
    conv_query,
    conv_key,
    conv_value,
    decay_log,
    decay_bias,
    out_norm,
    w_output,
    gain_mlp,
    w_gate,
    w_up,
    w_down,
):
    micro_count = tokens.shape[0]
    row_count = tokens.shape[1]
    model_width = tokens.shape[2]
    head_count = w_decay.shape[2]
    width_qk = w_query.shape[2]
    width_qkv = 2 * width_qk + w_value.shape[2]
    hidden_width = w_gate.shape[2]
    block_count = row_count // BLOCK
    section_index = lax.axis_index(SECTION)
    shard_index = lax.axis_index(SEQ)
    full_rows = (
        lax.all_gather(gain_attn[0], SEQ, axis=0, tiled=True),
        lax.all_gather(gain_mlp[0], SEQ, axis=0, tiled=True),
        lax.all_gather(w_query[0], SEQ, axis=0, tiled=True),
        lax.all_gather(w_key[0], SEQ, axis=0, tiled=True),
        lax.all_gather(w_value[0], SEQ, axis=0, tiled=True),
        lax.all_gather(w_gate_out[0], SEQ, axis=0, tiled=True),
        lax.all_gather(w_decay[0], SEQ, axis=0, tiled=True),
        lax.all_gather(w_beta[0], SEQ, axis=0, tiled=True),
        lax.all_gather(w_gate[0], SEQ, axis=0, tiled=True),
        lax.all_gather(w_up[0], SEQ, axis=0, tiled=True),
    )
    full_cols = (
        lax.all_gather(w_output[0], SEQ, axis=1, tiled=True),
        lax.all_gather(w_down[0], SEQ, axis=1, tiled=True),
    )
    attn_gain = full_rows[0].astype(jnp.float32)
    mlp_gain = full_rows[1].astype(jnp.float32)
    proj_weight = jnp.concatenate([full_rows[2], full_rows[3], full_rows[4], full_rows[5]], axis=1)
    mix_weight = jnp.concatenate([full_rows[6], full_rows[7]], axis=1).astype(jnp.float32)
    gate_up_weight = jnp.concatenate([full_rows[8], full_rows[9]], axis=1)
    out_weight = full_cols[0]
    down_weight = full_cols[1]
    conv_weight = jnp.concatenate([conv_query[0], conv_key[0], conv_value[0]], axis=1).astype(
        jnp.float32
    )
    decay_scale = decay_log[0]
    decay_shift = decay_bias[0]
    norm_weight = out_norm[0].astype(jnp.float32)
    ext_pos = (
        shard_index * row_count - (CONVK - 1) + jnp.arange(row_count + CONVK - 1, dtype=jnp.int32)
    )
    block_pos = shard_index * row_count + jnp.arange(block_count, dtype=jnp.int32) * BLOCK - 1

    def carry_backward(shard_map_t, shard_adj):
        identity = jnp.broadcast_to(
            jnp.eye(shard_map_t.shape[1], dtype=jnp.float32), shard_map_t.shape
        )
        suffix = entering(
            (shard_map_t, shard_adj), SEQ, compose, (identity, jnp.zeros_like(shard_adj))
        )
        result = suffix[1]
        return result

    def layer_backward(saved, upstream, starts):
        (
            resid_in,
            normed,
            mix_pre,
            extended,
            gate_pre,
            kept,
            running_state,
            shard_map,
            mixed_out,
            gated,
            resid_mid,
            ffn_in,
            gate_up,
            hidden,
        ) = saved
        doc_ext = doc_index(starts, ext_pos)
        prev_docs = doc_index(starts, block_pos)
        grad_ffn = upstream.astype(jnp.bfloat16)
        grad_hidden = proj_t(grad_ffn, down_weight)
        grad_down = inner_t(hidden, grad_ffn)
        _, act_back = jax.vjp(
            lambda gate_in, up_in: jax.nn.silu(gate_in) * up_in,
            gate_up[:, :hidden_width],
            gate_up[:, hidden_width:],
        )
        grad_gate, grad_up = act_back(grad_hidden)
        grad_gate_up = jnp.concatenate([grad_gate, grad_up], axis=1).astype(jnp.bfloat16)
        grad_gu_weight = inner_t(ffn_in, grad_gate_up)
        grad_ffn_in = head_total(proj_t(grad_gate_up, gate_up_weight))
        _, mlp_norm_back = jax.vjp(rms_norm, resid_mid, mlp_gain)
        grad_mid_norm, grad_mlp_gain = mlp_norm_back(grad_ffn_in)
        grad_mid = upstream + grad_mid_norm
        grad_attn = grad_mid.astype(jnp.bfloat16)
        grad_gated = proj_t(grad_attn, out_weight)
        grad_out_weight = inner_t(gated, grad_attn)
        _, gate_back = jax.vjp(
            lambda mixed_in, gate_in, weight_in: gate_norm(
                mixed_in, gate_in, weight_in, head_count
            ),
            mixed_out,
            gate_pre,
            norm_weight,
        )
        grad_mixed, grad_gate_pre, grad_norm_weight = gate_back(grad_gated)
        _, finish_back = jax.vjp(finish, kept, running_state)
        grad_kept, grad_state = finish_back(grad_mixed)
        later_blocks = carry_backward(jnp.swapaxes(shard_map, 1, 2), grad_state)
        gradient_transfer = jnp.einsum(
            "rgm,ram->rga", later_blocks, running_state, precision=highest_precision
        )

        def local_summary(ext_in, mix_in, conv_in, scale_in, shift_in):
            return summary(
                ext_in, mix_in, conv_in, scale_in, shift_in, doc_ext, prev_docs, head_count
            )

        _, summary_back = jax.vjp(
            local_summary, extended, mix_pre, conv_weight, decay_scale, decay_shift
        )
        grad_ext, grad_mix, grad_conv, grad_scale, grad_shift = summary_back(
            (gradient_transfer, later_blocks, grad_kept)
        )
        returned = passed_along(grad_ext[: CONVK - 1], SEQ, -1)
        grad_qkv = grad_ext[CONVK - 1 :] + jnp.pad(returned, ((row_count - (CONVK - 1), 0), (0, 0)))
        grad_pre = jnp.concatenate([grad_qkv, grad_gate_pre], axis=1).astype(jnp.bfloat16)
        grad_proj_weight = inner_t(normed, grad_pre)
        normed_float = normed.astype(jnp.float32)
        grad_mix_weight = lax.dot_general(
            normed_float, grad_mix, (((0,), (0,)), ((), ())), precision=highest_precision
        )
        grad_normed = head_total(
            proj_t(grad_pre, proj_weight)
            + lax.dot_general(
                grad_mix, mix_weight, (((1,), (1,)), ((), ())), precision=highest_precision
            )
        )
        _, attn_norm_back = jax.vjp(rms_norm, resid_in.astype(jnp.float32), attn_gain)
        grad_resid_norm, grad_attn_gain = attn_norm_back(grad_normed)
        grad_resid = grad_mid + grad_resid_norm
        rows_grads = (
            grad_attn_gain,
            grad_mlp_gain,
            grad_proj_weight,
            grad_mix_weight,
            grad_gu_weight,
        )
        cols_grads = (grad_out_weight, grad_down)
        small_grads = (grad_conv, grad_scale, grad_shift, grad_norm_weight)
        return (grad_resid, rows_grads, cols_grads, small_grads)

    zero_in = jnp.zeros((row_count, model_width), jnp.bfloat16)
    incoming = zero_in
    stored = None
    activations_buf = jnp.zeros(tokens.shape, jnp.bfloat16)
    stat_sums = jnp.zeros((micro_count, 3), jnp.float32)
    stat_counts = jnp.zeros((micro_count,), jnp.float32)
    for slot_index in range(micro_count + 1):
        chosen_raw = slot_index - section_index
        active = (chosen_raw >= 0) & (chosen_raw < micro_count)
        chosen = jnp.clip(chosen_raw, 0, micro_count - 1)
        resid_in = jnp.where(section_index == 0, tokens[min(slot_index, micro_count - 1)], incoming)
        layer_starts = doc_starts[chosen]
        layer_doc_ext = doc_index(layer_starts, ext_pos)
        layer_prev_docs = doc_index(layer_starts, block_pos)
        resid = resid_in.astype(jnp.float32)
        layer_normed = rms_norm(resid, attn_gain).astype(jnp.bfloat16)
        projected = jnp.dot(layer_normed, proj_weight, preferred_element_type=jnp.float32)
        layer_mix_pre = jnp.dot(
            layer_normed.astype(jnp.float32), mix_weight, precision=highest_precision
        )
        qkv_pre = projected[:, :width_qkv]
        layer_gate_pre = projected[:, width_qkv:]
        rim_rows = passed_along(qkv_pre[row_count - (CONVK - 1) :], SEQ, 1)
        layer_extended = jnp.concatenate([rim_rows, qkv_pre], axis=0)
        layer_shard_map, layer_shard_add, layer_kept = summary(
            layer_extended,
            layer_mix_pre,
            conv_weight,
            decay_scale,
            decay_shift,
            layer_doc_ext,
            layer_prev_docs,
            head_count,
        )
        carry_identity = jnp.broadcast_to(
            jnp.eye(layer_shard_map.shape[1], dtype=jnp.float32), layer_shard_map.shape
        )
        prefix = carried_in(
            (layer_shard_map, layer_shard_add),
            SEQ,
            compose,
            (carry_identity, jnp.zeros_like(layer_shard_add)),
        )
        carry_result = prefix[1]
        layer_mixed_out = finish(layer_kept, carry_result)
        layer_gated = gate_norm(layer_mixed_out, layer_gate_pre, norm_weight, head_count).astype(
            jnp.bfloat16
        )
        attn = head_total(jnp.dot(layer_gated, out_weight, preferred_element_type=jnp.float32))
        layer_resid_mid = resid + attn
        layer_ffn_in = rms_norm(layer_resid_mid, mlp_gain).astype(jnp.bfloat16)
        layer_gate_up = jnp.dot(layer_ffn_in, gate_up_weight, preferred_element_type=jnp.float32)
        layer_hidden = (
            jax.nn.silu(layer_gate_up[:, :hidden_width]) * layer_gate_up[:, hidden_width:]
        ).astype(jnp.bfloat16)
        ffn = head_total(jnp.dot(layer_hidden, down_weight, preferred_element_type=jnp.float32))
        layer_out = layer_resid_mid + ffn
        layer_saved = (
            resid_in,
            layer_normed,
            layer_mix_pre,
            layer_extended,
            layer_gate_pre,
            layer_kept,
            carry_result,
            layer_shard_map,
            layer_mixed_out,
            layer_gated,
            layer_resid_mid,
            layer_ffn_in,
            layer_gate_up,
            layer_hidden,
        )
        saved, layer_out, attn_out, ffn_out = (layer_saved, layer_out, attn, ffn)
        if stored is None:
            stored = jax.tree.map(
                lambda part_new: jnp.zeros((micro_count,) + part_new.shape, part_new.dtype), saved
            )
        stored = jax.tree.map(
            lambda buffer, part_new: buffer.at[chosen].set(
                jnp.where(active, part_new, buffer[chosen])
            ),
            stored,
            saved,
        )
        outgoing = layer_out.astype(jnp.bfloat16)
        activations_buf = activations_buf.at[chosen].set(
            jnp.where(active, outgoing, activations_buf[chosen])
        )
        weights_valid = valid_mask[chosen].astype(jnp.float32)
        sums_now = jnp.stack(
            [
                jnp.sum(weights_valid * jnp.mean(branch_val * branch_val, axis=-1))
                for branch_val in (layer_out, attn_out, ffn_out)
            ]
        )
        stat_sums = stat_sums.at[chosen].set(jnp.where(active, sums_now, stat_sums[chosen]))
        stat_counts = stat_counts.at[chosen].set(
            jnp.where(active, jnp.sum(weights_valid), stat_counts[chosen])
        )
        if slot_index < micro_count:
            incoming = partner(outgoing)
    rows_acc = None
    cols_acc = None
    small_acc = None
    back_in = zero_in
    grad_inputs = jnp.zeros(tokens.shape, jnp.bfloat16)
    for slot_index in range(micro_count + 1):
        chosen_raw = slot_index - (1 - section_index)
        active = (chosen_raw >= 0) & (chosen_raw < micro_count)
        chosen = jnp.clip(chosen_raw, 0, micro_count - 1)
        saved = jax.tree.map(lambda buffer: buffer[chosen], stored)
        from_loss = (
            cotangent[chosen].astype(jnp.float32) * valid_mask[chosen].astype(jnp.float32)[:, None]
        )
        upstream = jnp.where(section_index == 1, from_loss, back_in.astype(jnp.float32))
        grad_resid, rows_grads, cols_grads, small_grads = layer_backward(
            saved, upstream, doc_starts[chosen]
        )
        rows_grads = jax.tree.map(lambda grad_part: jnp.where(active, grad_part, 0.0), rows_grads)
        cols_grads = jax.tree.map(lambda grad_part: jnp.where(active, grad_part, 0.0), cols_grads)
        small_grads = jax.tree.map(lambda grad_part: jnp.where(active, grad_part, 0.0), small_grads)
        if rows_acc is None:
            rows_acc, cols_acc, small_acc = (rows_grads, cols_grads, small_grads)
        else:
            rows_acc = jax.tree.map(jnp.add, rows_acc, rows_grads)
            cols_acc = jax.tree.map(jnp.add, cols_acc, cols_grads)
            small_acc = jax.tree.map(jnp.add, small_acc, small_grads)
        outgoing = grad_resid.astype(jnp.bfloat16)
        grad_inputs = grad_inputs.at[chosen].set(jnp.where(active, outgoing, grad_inputs[chosen]))
        if slot_index < micro_count:
            back_in = partner(outgoing)
    rows_part, cols_part = spread(rows_acc, cols_acc)
    norm_heads = lax.psum(small_acc[3], HEAD)
    conv_sum, scale_sum, shift_sum, norm_sum, sums_all, counts_all = (
        lax.psum(small_acc[0].astype(jnp.bfloat16), SEQ).astype(jnp.float32),
        lax.psum(small_acc[1].astype(jnp.bfloat16), SEQ).astype(jnp.float32),
        lax.psum(small_acc[2].astype(jnp.bfloat16), SEQ).astype(jnp.float32),
        lax.psum(norm_heads.astype(jnp.bfloat16), SEQ).astype(jnp.float32),
        lax.psum(stat_sums.astype(jnp.bfloat16), SEQ).astype(jnp.float32),
        lax.psum(stat_counts.astype(jnp.bfloat16), SEQ).astype(jnp.float32),
    )
    branch_rms = jnp.sqrt(sums_all / jnp.maximum(counts_all, 1.0)[:, None])
    proj_part = rows_part[2]
    mix_part = rows_part[3]
    gu_part = rows_part[4]
    return (
        activations_buf[None],
        grad_inputs[None],
        branch_rms[None],
        rows_part[0][None],
        proj_part[:, :width_qk][None],
        proj_part[:, width_qk : 2 * width_qk][None],
        proj_part[:, 2 * width_qk : width_qkv][None],
        proj_part[:, width_qkv:][None],
        mix_part[:, :head_count][None],
        mix_part[:, head_count:][None],
        conv_sum[:, :width_qk][None],
        conv_sum[:, width_qk : 2 * width_qk][None],
        conv_sum[:, 2 * width_qk :][None],
        scale_sum[None],
        shift_sum[None],
        norm_sum[None],
        cols_part[0][None],
        rows_part[1][None],
        gu_part[:, :hidden_width][None],
        gu_part[:, hidden_width:][None],
        cols_part[1][None],
    )


def high_low(value):
    high = value.astype(jnp.bfloat16)
    return high, (value - high.astype(jnp.float32)).astype(jnp.bfloat16)


@functools.partial(jax.custom_vjp, nondiff_argnums=(2,))
def fine_dot(a, b, dims):
    a_high, a_low = high_low(a)
    b_high, b_low = high_low(b)

    def part(x, y):
        return lax.dot_general(x, y, (dims, ((), ())), preferred_element_type=jnp.float32)

    return part(a_high, b_high) + (part(a_high, b_low) + part(a_low, b_high))


def fine_dot_fwd(a, b, dims):
    return fine_dot(a, b, dims), (a, b)


def fine_dot_bwd(dims, kept, grad):
    a, b = kept
    (a_dim,), (b_dim,) = dims
    if a_dim == 1:
        da = fine_dot(grad, b, ((1,), (1 - b_dim,)))
    else:
        da = fine_dot(b, grad, ((1 - b_dim,), (1,)))
    if b_dim == 0:
        db = fine_dot(a, grad, ((1 - a_dim,), (0,)))
    else:
        db = fine_dot(grad, a, ((0,), (1 - a_dim,)))
    return da, db


fine_dot.defvjp(fine_dot_fwd, fine_dot_bwd)


def dot_nn(a, b):
    return fine_dot(a, b, ((1,), (0,)))


def dot_nt(a, b):
    return fine_dot(a, b, ((1,), (1,)))


def dot_tn(a, b):
    return fine_dot(a, b, ((0,), (0,)))


@functools.partial(jax.custom_vjp, nondiff_argnums=(1,))
def shifted(window, steps):
    if steps == 0:
        return window[HALO:]
    return pltpu.roll(window, steps, 0)[HALO:]


def shifted_fwd(window, steps):
    return shifted(window, steps), None


def shifted_bwd(steps, _, grad):
    padded = jnp.concatenate([jnp.zeros((HALO, grad.shape[1]), grad.dtype), grad], axis=0)
    if steps == 0:
        return (padded,)
    return (pltpu.roll(padded, padded.shape[0] - steps, 0),)


shifted.defvjp(shifted_fwd, shifted_bwd)


def iotas(length):
    rows = lax.broadcasted_iota(jnp.int32, (length, length), 0)
    cols = lax.broadcasted_iota(jnp.int32, (length, length), 1)
    return rows, cols


def as_row(column):
    rows, cols = iotas(column.shape[0])
    return jnp.sum(jnp.where(rows == cols, column, 0.0), axis=0, keepdims=True)


def unit_inverses(lowers):
    length = lowers[0].shape[0]
    rows, cols = iotas(length)
    eye = jnp.where(rows == cols, 1.0, 0.0)
    near = [jnp.where((rows >> 3) == (cols >> 3), lower, 0.0) for lower in lowers]
    results = [eye - part for part in near]
    squares = [dot_nn(part, part) for part in near]
    steps = [dot_nn(result, square) for result, square in zip(results, squares)]
    squares = [dot_nn(square, square) for square in squares]
    results = [result + step for result, step in zip(results, steps)]
    steps = [dot_nn(result, square) for result, square in zip(results, squares)]
    results = [result + step for result, step in zip(results, steps)]
    shift = 3
    while (1 << shift) < length:
        off = ((rows >> (shift + 1)) == (cols >> (shift + 1))) & ((rows >> shift) != (cols >> shift))
        steps = [
            dot_nn(jnp.where(off, lower, 0.0), result) for lower, result in zip(lowers, results)
        ]
        steps = [dot_nn(result, step) for result, step in zip(results, steps)]
        results = [result - step for result, step in zip(results, steps)]
        shift += 1
    return results


@jax.custom_vjp
def inverse_known(lower, inverse):
    return inverse


def inverse_known_fwd(lower, inverse):
    return inverse, inverse


def inverse_known_bwd(inverse, grad):
    return -dot_nt(dot_tn(inverse, grad), inverse), jnp.zeros_like(grad)


inverse_known.defvjp(inverse_known_fwd, inverse_known_bwd)


def silu(values):
    return values / (1.0 + jnp.exp(-values))


def sigmoid(values):
    return 1.0 / (1.0 + jnp.exp(-values))


@jax.custom_vjp
def softplus(values):
    return jnp.maximum(values, 0.0) + jnp.log1p(jnp.exp(-jnp.abs(values)))


def softplus_fwd(values):
    return softplus(values), values


def softplus_bwd(values, grad):
    return (grad * sigmoid(values),)


softplus.defvjp(softplus_fwd, softplus_bwd)


def block_front(window, mix_decay, mix_write, taps, decay_log, decay_bias, aux):
    summed = shifted(window, 0) * taps[3]
    for steps in range(1, CONVK):
        summed = summed + jnp.where(aux[:, steps : steps + 1] > 0.0, shifted(window, steps), 0.0) * taps[3 - steps]
    active = silu(summed)
    queries = unit_rows(active[:, :HEAD_K]) * HEAD_K ** (-0.5)
    keys = unit_rows(active[:, HEAD_K : 2 * HEAD_K])
    values = active[:, 2 * HEAD_K :]
    write = sigmoid(mix_write)
    log_decay = -jnp.exp(decay_log) * softplus(mix_decay + decay_bias)
    rows, cols = iotas(BLOCK)
    cum = jnp.sum(jnp.where(cols <= rows, as_row(log_decay), 0.0), axis=1, keepdims=True)
    total = jnp.sum(log_decay, axis=0, keepdims=True)
    doc = aux[:, 0:1]
    same = (doc == as_row(doc)) & (cols <= rows)
    decay = jnp.where(same, jnp.exp(jnp.where(same, cum - as_row(cum), 0.0)), 0.0)
    entry = jnp.where(aux[:, 4:5] > 0.0, jnp.exp(cum), 0.0)
    leave = jnp.where(aux[:, 5:6] > 0.0, jnp.exp(total - cum), 0.0)
    through = jnp.where(aux[BLOCK - 1 : BLOCK, 4:5] > 0.0, jnp.exp(total), 0.0)
    grams = dot_nt(jnp.concatenate([keys, queries], axis=0), keys)
    lower = jnp.where(cols < rows, write * decay * grams[:BLOCK], 0.0)
    mixing = grams[BLOCK:] * decay
    scaled = jnp.concatenate([write * values, (write * entry) * keys], axis=1)
    return lower, mixing, scaled, entry * queries, leave * keys, through


def block_prepare(window, mix_decay, mix_write, taps, decay_log, decay_bias, aux, inverse):
    lower, mixing, scaled, queries, keys, through = block_front(
        window, mix_decay, mix_write, taps, decay_log, decay_bias, aux
    )
    return mixing, dot_nn(inverse_known(lower, inverse), scaled), queries, keys, through


def block_core(mixing, resolved, queries, keys, through, state):
    read = dot_nn(jnp.concatenate([resolved[:, HEAD_V:], queries], axis=0), state)
    written = resolved[:, :HEAD_V] - read[:BLOCK]
    mixed = read[BLOCK:] + dot_nn(mixing, written)
    return mixed, through * state + dot_tn(keys, written)


def each_slice(piece_ref, refs, parts):
    shards, slices = parts
    sub = refs[0].shape[0] // shards
    for number, ref in enumerate(refs):
        for shard in range(shards):
            start = (shard * slices + (piece_ref[0] ^ number)) * sub
            yield pl.multiple_of(start, sub), pl.ds(shard * sub, sub), sub, ref


def fill_inputs(piece_ref, xh_refs, parts, xbuf, mixbuf):
    width = xbuf.shape[1]
    xbuf[0:HALO, :] = jnp.zeros((HALO, width), jnp.float32)
    for start, there, sub, ref in each_slice(piece_ref, xh_refs, parts):
        here = pl.ds(pl.multiple_of(start + HALO, HALO), sub)
        xbuf[here, :] = ref[there, :width].astype(jnp.float32)
        mixbuf[pl.ds(start, sub), :] = ref[there, width:].astype(jnp.float32)


def load_block(aux_ref, xbuf, mixbuf, base):
    window = xbuf[pl.ds(base, BLOCK + HALO), :]
    mix = mixbuf[pl.ds(base, BLOCK), :]
    aux = aux_ref[pl.ds(base, BLOCK), :]
    return window, mix[:, 0:1] + mix[:, 2:3], mix[:, 1:2] + mix[:, 3:4], aux


def load_taps(taps_ref):
    return [taps_ref[j : j + 1, :] for j in range(CONVK)]


def forward_kernel(parts, piece_ref, *refs):
    slices = parts[1]
    xh_refs, refs = refs[:slices], refs[slices:]
    aux_ref, taps_ref, scal_ref, *mixed_refs = refs[: 3 + slices]
    states_ref, inverse_ref, xbuf, mixbuf, mixed_buf, state_ref = refs[3 + slices :]
    fill_inputs(piece_ref, xh_refs, parts, xbuf, mixbuf)
    state_ref[...] = jnp.zeros_like(state_ref)
    blocks = aux_ref.shape[0] // BLOCK
    taps = load_taps(taps_ref)
    decay_log = scal_ref[0:1, 0:1]
    decay_bias = scal_ref[0:1, 1:2]

    def group(index, carry):
        state = state_ref[...]
        places, fronts = [], []
        for inner in range(GROUP):
            number = index * GROUP + inner
            base = pl.multiple_of(number * BLOCK, BLOCK)
            window, mix_decay, mix_write, aux = load_block(aux_ref, xbuf, mixbuf, base)
            places.append((number, base))
            fronts.append(block_front(window, mix_decay, mix_write, taps, decay_log, decay_bias, aux))
        inverses = unit_inverses([front[0] for front in fronts])
        resolved = [dot_nn(inverse, front[2]) for inverse, front in zip(inverses, fronts)]
        for (number, base), front, inverse, solved in zip(places, fronts, inverses, resolved):
            states_ref[number] = state
            inverse_ref[pl.ds(base, BLOCK), :] = inverse
            mixed, state = block_core(front[1], solved, *front[3:], state)
            mixed_buf[pl.ds(base, BLOCK), :] = mixed.astype(mixed_buf.dtype)
        state_ref[...] = state
        return carry

    lax.fori_loop(0, blocks // GROUP, group, 0)
    for start, there, sub, ref in each_slice(piece_ref, mixed_refs, parts):
        ref[there, :] = mixed_buf[pl.ds(start, sub), :]


def backward_kernel(parts, piece_ref, *refs):
    slices = parts[1]
    xh_refs, grad_refs, refs = refs[:slices], refs[slices : 2 * slices], refs[2 * slices :]
    aux_ref, taps_ref, scal_ref, states_ref, inverse_ref, *dxh_refs = refs[: 5 + slices]
    dtaps_ref, dscal_ref, xbuf, mixbuf, grad_buf, dxh_buf, adjoint_ref, halo_ref = refs[5 + slices :]
    fill_inputs(piece_ref, xh_refs, parts, xbuf, mixbuf)
    for start, there, sub, ref in each_slice(piece_ref, grad_refs, parts):
        grad_buf[pl.ds(start, sub), :] = ref[there, :]
    adjoint_ref[...] = jnp.zeros_like(adjoint_ref)
    halo_ref[...] = jnp.zeros_like(halo_ref)
    dtaps_ref[...] = jnp.zeros_like(dtaps_ref)
    dscal_ref[...] = jnp.zeros_like(dscal_ref)
    blocks = aux_ref.shape[0] // BLOCK
    width = xbuf.shape[1]
    taps = load_taps(taps_ref)
    decay_log = scal_ref[0:1, 0:1]
    decay_bias = scal_ref[0:1, 1:2]
    lanes = lax.broadcasted_iota(jnp.int32, (BLOCK, EXTRA), 1)

    def group(index, carry):
        adjoint = adjoint_ref[...]
        halo = halo_ref[...]
        dtaps = [dtaps_ref[j : j + 1, :] for j in range(CONVK)]
        dlog = dscal_ref[0:1, 0:1]
        dbias = dscal_ref[0:1, 1:2]
        places, prepares, cores = [], [], []
        for inner in range(GROUP):
            number = blocks - 1 - (index * GROUP + inner)
            base = pl.multiple_of(number * BLOCK, BLOCK)
            window, mix_decay, mix_write, aux = load_block(aux_ref, xbuf, mixbuf, base)
            inverse = inverse_ref[pl.ds(base, BLOCK), :]
            prepared, pull = jax.vjp(
                functools.partial(block_prepare, aux=aux, inverse=inverse),
                window, mix_decay, mix_write, taps, decay_log, decay_bias,
            )
            places.append(base)
            prepares.append(pull)
            cores.append(jax.vjp(block_core, *prepared, states_ref[number])[1])
        dprepared = []
        for base, pull in zip(places, cores):
            grad = grad_buf[pl.ds(base, BLOCK), :].astype(jnp.float32)
            *dparts, adjoint = pull((grad, adjoint))
            dprepared.append(tuple(dparts))
        for base, pull, dparts in zip(places, prepares, dprepared):
            dwindow, ddecay, dwrite, dtaps_now, dlog_now, dbias_now = pull(dparts)
            own = dwindow[HALO:]
            own = jnp.concatenate([own[: BLOCK - HALO], own[BLOCK - HALO :] + halo], axis=0)
            halo = dwindow[:HALO]
            dtaps = [a + b for a, b in zip(dtaps, dtaps_now)]
            dlog = dlog + dlog_now
            dbias = dbias + dbias_now
            dxh_buf[pl.ds(base, BLOCK), :width] = own.astype(dxh_buf.dtype)
            high_decay = ddecay.astype(jnp.bfloat16).astype(jnp.float32)
            high_write = dwrite.astype(jnp.bfloat16).astype(jnp.float32)
            mix = jnp.where(lanes == 0, high_decay, jnp.where(lanes == 1, high_write, 0.0))
            mix = jnp.where(lanes == 2, ddecay - high_decay, jnp.where(lanes == 3, dwrite - high_write, mix))
            dxh_buf[pl.ds(base, BLOCK), width:] = mix.astype(dxh_buf.dtype)
        adjoint_ref[...] = adjoint
        halo_ref[...] = halo
        for j in range(CONVK):
            dtaps_ref[j : j + 1, :] = dtaps[j]
        dscal_ref[0:1, 0:1] = dlog
        dscal_ref[0:1, 1:2] = dbias
        return carry

    lax.fori_loop(0, blocks // GROUP, group, 0)
    for start, there, sub, ref in each_slice(piece_ref, dxh_refs, parts):
        ref[there, :] = dxh_buf[pl.ds(start, sub), :]


WIDTH = 2 * HEAD_K + HEAD_V


def whole():
    return pl.BlockSpec(memory_space=pltpu.VMEM)


def recur_cost(length):
    return pl.CostEstimate(flops=length * RECUR_FLOPS, bytes_accessed=length * 8192, transcendentals=0)


def recur_forward(piece, xh, aux, taps, scal, parts):
    length = aux.shape[0]
    blocks = length // BLOCK
    slices = len(xh)
    *mixed, states, inverse = pl.pallas_call(
        functools.partial(forward_kernel, parts),
        out_shape=(jax.ShapeDtypeStruct((length // slices, HEAD_V), jnp.bfloat16),) * slices
        + (
            jax.ShapeDtypeStruct((blocks, HEAD_K, HEAD_V), jnp.float32),
            jax.ShapeDtypeStruct((length, BLOCK), jnp.float32),
        ),
        in_specs=[pl.BlockSpec(memory_space=pltpu.SMEM)] + [whole()] * (slices + 3),
        out_specs=(whole(),) * (slices + 2),
        scratch_shapes=[
            pltpu.VMEM((length + HALO, WIDTH), jnp.float32),
            pltpu.VMEM((length, EXTRA), jnp.float32),
            pltpu.VMEM((length, HEAD_V), jnp.bfloat16),
            pltpu.VMEM((HEAD_K, HEAD_V), jnp.float32),
        ],
        compiler_params=pltpu.CompilerParams(vmem_limit_bytes=VMEM_LIMIT),
        cost_estimate=recur_cost(length),
        name="recur_forward",
    )(piece, *xh, aux, taps, scal)
    return mixed, states, inverse


def recur_backward(piece, xh, grad, aux, taps, scal, states, inverse, parts):
    length = aux.shape[0]
    slices = len(xh)
    *dxh, dtaps, dscal = pl.pallas_call(
        functools.partial(backward_kernel, parts),
        out_shape=(jax.ShapeDtypeStruct((length // slices, WIDTH + EXTRA), jnp.bfloat16),) * slices
        + (
            jax.ShapeDtypeStruct((8, WIDTH), jnp.float32),
            jax.ShapeDtypeStruct((8, 128), jnp.float32),
        ),
        in_specs=[pl.BlockSpec(memory_space=pltpu.SMEM)] + [whole()] * (2 * slices + 5),
        out_specs=(whole(),) * (slices + 2),
        scratch_shapes=[
            pltpu.VMEM((length + HALO, WIDTH), jnp.float32),
            pltpu.VMEM((length, EXTRA), jnp.float32),
            pltpu.VMEM((length, HEAD_V), jnp.bfloat16),
            pltpu.VMEM((length, WIDTH + EXTRA), jnp.bfloat16),
            pltpu.VMEM((HEAD_K, HEAD_V), jnp.float32),
            pltpu.VMEM((HALO, WIDTH), jnp.float32),
        ],
        compiler_params=pltpu.CompilerParams(vmem_limit_bytes=VMEM_LIMIT),
        cost_estimate=recur_cost(length),
        name="recur_backward",
    )(piece, *xh, *grad, aux, taps, scal, states, inverse)
    return dxh, dtaps, dscal


def make_aux(starts, length):
    positions = jnp.arange(length, dtype=jnp.int32)
    doc = jnp.sum((starts[None, :] <= positions[:, None]).astype(jnp.int32), axis=1)
    def back(steps):
        earlier = jnp.concatenate([jnp.full((steps,), -1, jnp.int32), doc[:-steps]])
        return (earlier == doc).astype(jnp.float32)
    blocks = doc.reshape(-1, BLOCK)
    before = jnp.concatenate([jnp.full((1,), -1, jnp.int32), blocks[:-1, -1]])
    entering = (blocks == before[:, None]).reshape(-1).astype(jnp.float32)
    leaving = (blocks == blocks[:, -1:]).reshape(-1).astype(jnp.float32)
    zero = jnp.zeros((length,), jnp.float32)
    return jnp.stack([doc.astype(jnp.float32), back(1), back(2), back(3), entering, leaving, zero, zero], axis=1)


def dot(left, right):
    return lax.dot_general(
        left, right, (((1,), (0,)), ((), ())), preferred_element_type=jnp.float32
    )


def in_vmem():
    return pl.BlockSpec(memory_space=pltpu.VMEM)


def in_smem():
    return pl.BlockSpec(memory_space=pltpu.SMEM)


def held(shape):
    return pl.BlockSpec(shape, lambda step: (0,) * len(shape))


def slab(shape, axis):
    return pl.BlockSpec(shape, lambda step: tuple(step if d == axis else 0 for d in range(len(shape))))


def like(shape, dtype):
    return jax.ShapeDtypeStruct(shape, dtype)


def run(kernel, grid, in_specs, out_specs, out_shape, scratch, name, flops, moved, args):
    return pl.pallas_call(
        kernel,
        grid=grid,
        in_specs=in_specs,
        out_specs=out_specs,
        out_shape=out_shape,
        scratch_shapes=scratch,
        compiler_params=pltpu.CompilerParams(vmem_limit_bytes=VMEM_LIMIT),
        cost_estimate=pl.CostEstimate(flops=flops, bytes_accessed=moved, transcendentals=0),
        name=name,
    )(*args)


def row_scale(value):
    return lax.rsqrt(jnp.mean(value * value, axis=-1, keepdims=True) + epsilon)


def mean_square(value, valid):
    return jnp.sum(valid * jnp.mean(value * value, axis=-1, keepdims=True), axis=0, keepdims=True)


def norm_adjoint(value, gain, grad):
    scale = row_scale(value)
    unit = value * scale
    scaled = grad * gain
    dvalue = scale * (scaled - unit * jnp.mean(scaled * unit, axis=-1, keepdims=True))
    return dvalue, jnp.sum(grad * unit, axis=0, keepdims=True)


def each_piece(me_ref, part_refs):
    rows = part_refs[0].shape[0]
    for number, part in enumerate(part_refs):
        start = (me_ref[0] ^ number) * rows
        yield pl.ds(pl.multiple_of(start, rows), rows), part


def hand_out(me_ref, total_ref, piece_refs):
    for where, piece in each_piece(me_ref, piece_refs):
        piece[...] = total_ref[where, :].astype(piece.dtype)


def put_stat(stat_ref, column, value):
    stat_ref[0:1, column : column + 1] += value


def mix_rows(mix_ref):
    mix = mix_ref[0]
    return jnp.concatenate([mix, jnp.zeros((EXTRA - mix.shape[0], mix.shape[1]), mix.dtype)], axis=0)


def project_kernel(kind, pieces, *refs):
    me_ref, valid_ref, gain_ref = refs[:3]
    part_refs = refs[3 : 3 + pieces]
    refs = refs[3 + pieces :]
    if kind == "next":
        base_ref, refs = refs[0], refs[1:]
    w_ref, mix_ref, resid_ref, normed_ref, packed_ref, gate_ref, stat_ref = refs

    @pl.when(pl.program_id(0) == 0)
    def _():
        stat_ref[...] = jnp.zeros_like(stat_ref)
        for where, part in each_piece(me_ref, part_refs):
            value = part[...].astype(jnp.float32)
            if kind == "next":
                valid = valid_ref[where, :]
                put_stat(stat_ref, 1, mean_square(value, valid))
                value = value + base_ref[where, :]
                put_stat(stat_ref, 0, mean_square(value, valid))
            rounded = value.astype(jnp.bfloat16)
            resid_ref[where, :] = rounded
            value = rounded.astype(jnp.float32)
            normed_ref[where, :] = (value * row_scale(value) * gain_ref[...]).astype(jnp.bfloat16)

    normed = normed_ref[...]
    result = dot(normed, w_ref[0])
    packed_ref[0, :, :WIDTH] = result[:, :WIDTH].astype(jnp.bfloat16)
    gate_ref[0] = result[:, WIDTH:]
    mix = proj_t(normed, mix_rows(mix_ref))
    lanes = lax.broadcasted_iota(jnp.int32, mix.shape, 1)
    low = mix - mix.astype(jnp.bfloat16).astype(jnp.float32)
    mix = jnp.where(lanes < 2, mix, jnp.where(lanes < 4, low, 0.0))
    packed_ref[0, :, WIDTH:] = mix.astype(jnp.bfloat16)


def project(me, valid, gain, parts, base, w_proj, w_mix):
    slices, width, columns = w_proj.shape
    sub = parts[0].shape[0]
    rows = sub * len(parts)
    kind = "first" if base is None else "next"
    return run(
        functools.partial(project_kernel, kind, len(parts)),
        (slices,),
        [in_smem(), held((rows, 1)), held((1, width))]
        + [held((sub, width))] * len(parts)
        + ([] if base is None else [held((rows, width))])
        + [slab((1, width, columns), 0), slab((1, 16, width), 0)],
        (
            held((rows, width)),
            held((rows, width)),
            slab((1, rows, WIDTH + EXTRA), 0),
            slab((1, rows, HEAD_V), 0),
            held((8, 128)),
        ),
        (
            like((rows, width), jnp.bfloat16),
            like((rows, width), jnp.bfloat16),
            like((slices, rows, WIDTH + EXTRA), jnp.bfloat16),
            like((slices, rows, HEAD_V), jnp.float32),
            like((8, 128), jnp.float32),
        ),
        [],
        "project_" + kind,
        2 * rows * width * columns * slices,
        w_proj.size * 2 + rows * width * 12,
        [me, valid, gain] + list(parts) + ([] if base is None else [base]) + [w_proj, w_mix],
    )


def output_kernel(slices, me_ref, piece_ref, *refs):
    mixed_refs, refs = refs[:slices], refs[slices:]
    gate_ref, norm_ref, w_ref, gated_ref, kept_ref, *piece_refs, total = refs

    @pl.when(pl.program_id(0) == 0)
    def _():
        for number, mixed_ref in enumerate(mixed_refs):
            j = piece_ref[0] ^ number
            kept_ref[j] = mixed_ref[...]
            value = mixed_ref[...].astype(jnp.float32)
            normed = value * row_scale(value) * norm_ref[...] * silu(gate_ref[j])
            start = pl.multiple_of(j * HEAD_V, HEAD_V)
            gated_ref[:, pl.ds(start, HEAD_V)] = normed.astype(jnp.bfloat16)

    weight = w_ref[0].reshape(gated_ref.shape[1], w_ref.shape[3])
    total[...] = dot(gated_ref[...], weight)
    hand_out(me_ref, total, piece_refs)


def output(me, piece, mixed, gate_pre, norm_weight, w_cols, shards):
    slices, rows, _ = gate_pre.shape
    inner, half = slices * HEAD_V, w_cols.shape[3]
    sub = rows // shards
    gated, kept, *pieces = run(
        functools.partial(output_kernel, slices),
        (2,),
        [in_smem(), in_smem()]
        + [held((rows, HEAD_V))] * slices
        + [held(gate_pre.shape), held((1, HEAD_V)), slab((1, slices, HEAD_V, half), 0)],
        (held((rows, inner)), held(gate_pre.shape)) + (slab((sub, half), 1),) * shards,
        (like((rows, inner), jnp.bfloat16), like(gate_pre.shape, jnp.bfloat16))
        + (like((sub, 2 * half), jnp.bfloat16),) * shards,
        [pltpu.VMEM((rows, half), jnp.float32)],
        "output",
        4 * rows * inner * half,
        inner * half * 4 + rows * inner * 12,
        [me, piece] + list(mixed) + [gate_pre, norm_weight, w_cols],
    )
    return gated, kept, pieces


def feed_kernel(pieces, *refs):
    me_ref, valid_ref, gain_ref = refs[:3]
    part_refs = refs[3 : 3 + pieces]
    base_ref, w_gu_ref = refs[3 + pieces : 5 + pieces]
    down_refs = refs[5 + pieces : -6 - pieces]
    mid_ref, normed_ref, gate_up_ref, hidden_ref, *piece_refs, stat_ref, total = refs[-6 - pieces :]
    step = pl.program_id(0)
    half = down_refs[0].shape[3]

    @pl.when(step == 0)
    def _():
        stat_ref[...] = jnp.zeros_like(stat_ref)
        total[...] = jnp.zeros_like(total)
        for where, part in each_piece(me_ref, part_refs):
            value = part[...].astype(jnp.float32)
            put_stat(stat_ref, 0, mean_square(value, valid_ref[where, :]))
            value = value + base_ref[where, :].astype(jnp.float32)
            mid_ref[where, :] = value
            normed_ref[where, :] = (value * row_scale(value) * gain_ref[...]).astype(jnp.bfloat16)

    result = dot(normed_ref[...], w_gu_ref[0])
    gate_up_ref[0] = result
    width = result.shape[1] // 2
    hidden = (silu(result[:, :width]) * result[:, width:]).astype(jnp.bfloat16)
    hidden_ref[...] = hidden
    for c in range(2):
        part = sum(
            dot(hidden[:, k * LANES : (k + 1) * LANES], ref[c, 0]) for k, ref in enumerate(down_refs)
        )
        total[:, c * half : (c + 1) * half] += part

    @pl.when(step == pl.num_programs(0) - 1)
    def _():
        hand_out(me_ref, total, piece_refs)


def down_slabs(w_cols, hidden):
    half = w_cols.shape[3]

    def block(number):
        return pl.BlockSpec((2, 1, LANES, half), lambda step: (0, step, number, 0))

    first = HEAD_V // LANES
    return [block(first + k) for k in range(hidden // LANES)]


def feed(me, valid, gain, parts, base, w_gu, w_cols):
    slices, width, columns = w_gu.shape
    sub = parts[0].shape[0]
    rows = sub * len(parts)
    hidden = columns // 2
    mid, normed, gate_up, hidden, *pieces, stat = run(
        functools.partial(feed_kernel, len(parts)),
        (slices,),
        [in_smem(), held((rows, 1)), held((1, width))]
        + [held((sub, width))] * len(parts)
        + [held((rows, width)), slab((1, width, columns), 0)]
        + down_slabs(w_cols, hidden),
        (
            held((rows, width)),
            held((rows, width)),
            slab((1, rows, columns), 0),
            slab((rows, hidden), 1),
        )
        + (held((sub, width)),) * len(parts)
        + (held((8, 128)),),
        (
            like((rows, width), jnp.float32),
            like((rows, width), jnp.bfloat16),
            like((slices, rows, columns), jnp.float32),
            like((rows, slices * hidden), jnp.bfloat16),
        )
        + (like((sub, width), jnp.bfloat16),) * len(parts)
        + (like((8, 128), jnp.float32),),
        [pltpu.VMEM((rows, width), jnp.float32)],
        "feed",
        2 * rows * width * (columns + hidden) * slices,
        (w_gu.size + hidden * slices * width) * 2 + rows * width * 16,
        [me, valid, gain] + list(parts) + [base, w_gu] + [w_cols] * (hidden // LANES),
    )
    return mid, normed, gate_up, hidden, pieces, stat


def close_kernel(valid_ref, part_ref, base_ref, out_ref, stat_ref):
    stat_ref[...] = jnp.zeros_like(stat_ref)
    value = part_ref[...].astype(jnp.float32)
    valid = valid_ref[...]
    put_stat(stat_ref, 1, mean_square(value, valid))
    value = value + base_ref[...]
    put_stat(stat_ref, 0, mean_square(value, valid))
    out_ref[...] = value.astype(jnp.bfloat16)


def close(valid, part, base):
    return run(
        close_kernel,
        (),
        [in_vmem()] * 3,
        (in_vmem(), in_vmem()),
        (like(base.shape, jnp.bfloat16), like((8, 128), jnp.float32)),
        [],
        "close",
        base.size * 6,
        base.size * 8,
        [valid, part, base],
    )


def sum_kernel(*refs):
    total = refs[0][...].astype(jnp.float32)
    for ref in refs[1:-1]:
        total = total + ref[...].astype(jnp.float32)
    refs[-1][...] = total.astype(refs[-1].dtype)


def sum_pieces(pieces):
    size = pieces[0].size
    return run(
        sum_kernel,
        (),
        [in_vmem()] * len(pieces),
        in_vmem(),
        like(pieces[0].shape, pieces[0].dtype),
        [],
        "sum_pieces",
        size * len(pieces),
        size * 2 * (len(pieces) + 1),
        list(pieces),
    )


def feed_back_kernel(shards, me_ref, up_ref, gate_up_ref, w_gu_ref, *refs):
    down_refs, (grad_ref, *piece_refs, total) = refs[: -2 - shards], refs[-2 - shards :]
    step = pl.program_id(0)
    half = down_refs[0].shape[3]
    width = gate_up_ref.shape[2] // 2
    upstream = up_ref[...]
    grad_hidden = jnp.concatenate(
        [
            proj_t(upstream[:, :half], ref[0, 0]) + proj_t(upstream[:, half:], ref[1, 0])
            for ref in down_refs
        ],
        axis=1,
    )
    gate = gate_up_ref[0, :, :width]
    up = gate_up_ref[0, :, width:]
    sig = sigmoid(gate)
    grad_ref[0, :, :width] = (grad_hidden * up * (sig * (1.0 + gate * (1.0 - sig)))).astype(jnp.bfloat16)
    grad_ref[0, :, width:] = (grad_hidden * (gate * sig)).astype(jnp.bfloat16)
    part = proj_t(grad_ref[0], w_gu_ref[0])

    @pl.when(step == 0)
    def _():
        total[...] = part

    @pl.when(step > 0)
    def _():
        total[...] += part

    @pl.when(step == pl.num_programs(0) - 1)
    def _():
        hand_out(me_ref, total, piece_refs)


def feed_back(me, upstream, gate_up, w_gu, w_cols, shards):
    slices, width, columns = w_gu.shape
    rows = upstream.shape[0]
    hidden = columns // 2
    sub = rows // shards
    grad, *pieces = run(
        functools.partial(feed_back_kernel, shards),
        (slices,),
        [
            in_smem(),
            held((rows, width)),
            slab((1, rows, columns), 0),
            slab((1, width, columns), 0),
        ]
        + down_slabs(w_cols, hidden),
        (slab((1, rows, columns), 0),) + (held((sub, width)),) * shards,
        (like((slices, rows, columns), jnp.bfloat16),) + (like((sub, width), jnp.bfloat16),) * shards,
        [pltpu.VMEM((rows, width), jnp.float32)],
        "feed_back",
        2 * rows * width * (columns + hidden) * slices,
        (w_gu.size + hidden * slices * width) * 2 + gate_up.size * 6 + rows * width * 4,
        [me, upstream, gate_up, w_gu] + [w_cols] * (hidden // LANES),
    )
    return grad, pieces


def mid_back_kernel(pieces, *refs):
    me_ref, gain_ref = refs[:2]
    part_refs = refs[2 : 2 + pieces]
    (
        mid_ref, up_ref, w_ref, mixed_ref, gate_ref, norm_ref,
        grad_mid_ref, grad_attn_ref, dgain_ref, dmixed_ref, dgate_ref, dnorm_ref,
    ) = refs[2 + pieces :]
    half = w_ref.shape[3]

    @pl.when(pl.program_id(0) == 0)
    def _():
        dgain_ref[...] = jnp.zeros_like(dgain_ref)
        dnorm_ref[...] = jnp.zeros_like(dnorm_ref)
        for where, part in each_piece(me_ref, part_refs):
            dvalue, dgain = norm_adjoint(mid_ref[where, :], gain_ref[...], part[...].astype(jnp.float32))
            dvalue = dvalue + up_ref[where, :].astype(jnp.float32)
            grad_mid_ref[where, :] = dvalue
            grad_attn_ref[where, :] = dvalue.astype(jnp.bfloat16)
            dgain_ref[...] += dgain

    grad = grad_attn_ref[...]
    grad_gated = proj_t(grad[:, :half], w_ref[0, 0]) + proj_t(grad[:, half:], w_ref[1, 0])
    value = mixed_ref[0].astype(jnp.float32)
    scale = row_scale(value)
    unit = value * scale
    weight = norm_ref[...]
    gate = gate_ref[0]
    sig = sigmoid(gate)
    dgate_ref[0] = (grad_gated * unit * weight * (sig * (1.0 + gate * (1.0 - sig)))).astype(jnp.bfloat16)
    dscaled = grad_gated * (gate * sig)
    dnorm_ref[...] += jnp.sum(dscaled * unit, axis=0, keepdims=True)
    dunit = dscaled * weight
    dmixed = scale * (dunit - unit * jnp.mean(dunit * unit, axis=-1, keepdims=True))
    dmixed_ref[0] = dmixed.astype(jnp.bfloat16)


def mid_back(me, gain, parts, mid, upstream, w_cols, mixed, gate_pre, norm_weight):
    slices, rows, _ = mixed.shape
    width = mid.shape[1]
    half = width // 2
    sub = parts[0].shape[0]
    return run(
        functools.partial(mid_back_kernel, len(parts)),
        (slices,),
        [in_smem(), held((1, width))]
        + [held((sub, width))] * len(parts)
        + [
            held((rows, width)),
            held((rows, width)),
            slab((2, 1, HEAD_V, half), 1),
            slab((1, rows, HEAD_V), 0),
            slab((1, rows, HEAD_V), 0),
            held((1, HEAD_V)),
        ],
        (
            held((rows, width)),
            held((rows, width)),
            held((1, width)),
            slab((1, rows, HEAD_V), 0),
            slab((1, rows, HEAD_V), 0),
            held((1, HEAD_V)),
        ),
        (
            like((rows, width), jnp.float32),
            like((rows, width), jnp.bfloat16),
            like((1, width), jnp.float32),
            like((slices, rows, HEAD_V), jnp.bfloat16),
            like((slices, rows, HEAD_V), jnp.bfloat16),
            like((1, HEAD_V), jnp.float32),
        ),
        [],
        "mid_back",
        2 * rows * width * HEAD_V * slices,
        slices * HEAD_V * width * 2 + rows * width * 20,
        [me, gain] + list(parts) + [mid, upstream, w_cols, mixed, gate_pre, norm_weight],
    )


def project_back_kernel(shards, slices, me_ref, piece_ref, *refs):
    part_refs, refs = refs[:slices], refs[slices:]
    dgate_ref, w_ref, mix_ref, normed_ref, grad_ref, dmix_ref, *piece_refs, packed, total = refs
    step = pl.program_id(0)

    @pl.when(step == 0)
    def _():
        for number, part in enumerate(part_refs):
            packed[piece_ref[0] ^ number] = part[...]
        total[...] = jnp.zeros_like(total)

    grad_ref[0, :, :WIDTH] = packed[step, :, :WIDTH]
    grad_ref[0, :, WIDTH:] = dgate_ref[0]
    mix = packed[step, :, WIDTH:]
    total[...] += proj_t(grad_ref[0], w_ref[0]) + dot(mix, mix_rows(mix_ref))
    dmix = inner_t(mix, normed_ref[...])
    dmix_ref[0] = jnp.concatenate([dmix[0:2] + dmix[2:4], dmix[2:8]], axis=0)

    @pl.when(step == pl.num_programs(0) - 1)
    def _():
        hand_out(me_ref, total, piece_refs)


def project_back(me, piece, packed, dgate, w_proj, w_mix, normed, shards):
    slices, width, columns = w_proj.shape
    rows = normed.shape[0]
    sub = rows // shards
    grad, dmix, *pieces = run(
        functools.partial(project_back_kernel, shards, slices),
        (slices,),
        [in_smem(), in_smem()]
        + [held((rows, WIDTH + EXTRA))] * slices
        + [
            slab((1, rows, HEAD_V), 0),
            slab((1, width, columns), 0),
            slab((1, 16, width), 0),
            held((rows, width)),
        ],
        (slab((1, rows, columns), 0), slab((1, 8, width), 0)) + (held((sub, width)),) * shards,
        (like((slices, rows, columns), jnp.bfloat16), like((slices, 8, width), jnp.float32))
        + (like((sub, width), jnp.bfloat16),) * shards,
        [
            pltpu.VMEM((slices, rows, WIDTH + EXTRA), jnp.bfloat16),
            pltpu.VMEM((rows, width), jnp.float32),
        ],
        "project_back",
        2 * rows * width * columns * slices,
        w_proj.size * 2 + rows * width * 12,
        [me, piece] + list(packed) + [dgate, w_proj, w_mix, normed],
    )
    return grad, pieces, dmix


def norm_back_kernel(pieces, *refs):
    me_ref, gain_ref = refs[:2]
    part_refs = refs[2 : 2 + pieces]
    resid_ref, mid_ref, out_ref, dgain_ref = refs[2 + pieces :]
    dgain_ref[...] = jnp.zeros_like(dgain_ref)
    for where, part in each_piece(me_ref, part_refs):
        value = resid_ref[where, :].astype(jnp.float32)
        dvalue, dgain = norm_adjoint(value, gain_ref[...], part[...].astype(jnp.float32))
        out_ref[where, :] = (dvalue + mid_ref[where, :]).astype(jnp.bfloat16)
        dgain_ref[...] += dgain


def norm_back(me, gain, parts, resid, grad_mid):
    return run(
        functools.partial(norm_back_kernel, len(parts)),
        (),
        [in_smem()] + [in_vmem()] * (3 + len(parts)),
        (in_vmem(), in_vmem()),
        (like(resid.shape, jnp.bfloat16), like(gain.shape, jnp.float32)),
        [],
        "norm_back",
        resid.size * 10,
        resid.size * 10,
        [me, gain] + list(parts) + [resid, grad_mid],
    )


def weight_grad_kernel(left_ref, right_ref, out_ref):
    right = right_ref[0] if len(right_ref.shape) == 3 else right_ref[...]
    out_ref[0] = inner_t(left_ref[...], right).astype(jnp.bfloat16)


def grad_rows(left, right):
    rows, width = left.shape
    slices, _, columns = right.shape
    return run(
        weight_grad_kernel,
        (slices,),
        [held((rows, width)), slab((1, rows, columns), 0)],
        slab((1, width, columns), 0),
        like((slices, width, columns), jnp.bfloat16),
        [],
        "grad_rows",
        2 * rows * width * columns * slices,
        slices * width * columns * 2 + rows * width * 2 + right.size * 2,
        [left, right],
    )


def grad_cols_kernel(hidden_ref, up_ref, gated_ref, grad_ref, out_ref):
    rows = hidden_ref.shape[1]
    out_ref[0, 0, :-rows] = inner_t(gated_ref[...], grad_ref[...]).astype(jnp.bfloat16)
    out_ref[0, 0, -rows:] = inner_t(hidden_ref[...], up_ref[...]).astype(jnp.bfloat16)


def grad_cols(hidden, upstream, gated, grad_attn, slices):
    rows, width = upstream.shape
    half = width // 2
    first, second = hidden.shape[1] // slices, gated.shape[1] // slices

    def piece(columns):
        return pl.BlockSpec((rows, columns), lambda c, j: (0, j))

    def side():
        return pl.BlockSpec((rows, half), lambda c, j: (0, c))

    result = run(
        grad_cols_kernel,
        (2, slices),
        [piece(first), side(), piece(second), side()],
        pl.BlockSpec((1, 1, first + second, half), lambda c, j: (c, j, 0, 0)),
        like((2, slices, first + second, half), jnp.bfloat16),
        [],
        "grad_cols",
        4 * rows * (first + second) * slices * half,
        2 * slices * (first + second) * half * 2 + rows * width * 4,
        [hidden, upstream, gated, grad_attn],
    )
    return result.reshape(2, slices * (first + second), half)


def place_kernel(pieces, *refs):
    me_ref, out_ref = refs[0], refs[-1]
    for where, part in each_piece(me_ref, refs[1:-1]):
        out_ref[where, :] = part[...]


def place(me, parts):
    sub, width = parts[0].shape
    shape = (sub * len(parts), width)
    return run(
        functools.partial(place_kernel, len(parts)),
        (),
        [in_smem()] + [in_vmem()] * len(parts),
        in_vmem(),
        like(shape, parts[0].dtype),
        [],
        "place",
        0,
        4 * sub * width * len(parts),
        [me] + list(parts),
    )


def place_cols_kernel(pieces, *refs):
    me_ref, out_ref = refs[0], refs[-1]
    width = refs[1].shape[1]
    for number, part in enumerate(refs[1:-1]):
        start = pl.multiple_of((me_ref[0] ^ number) * width, width)
        out_ref[:, pl.ds(start, width)] = part[...]


def place_cols(me, parts):
    rows, width = parts[0].shape
    shape = (rows, width * len(parts))
    return run(
        functools.partial(place_cols_kernel, len(parts)),
        (),
        [in_smem()] + [in_vmem()] * len(parts),
        in_vmem(),
        like(shape, parts[0].dtype),
        [],
        "place_cols",
        0,
        4 * rows * width * len(parts),
        [me] + list(parts),
    )


def finish_rows_kernel(widths, side_ref, layer0_ref, layer1_ref, received_ref, *out_refs):
    side = side_ref[0]
    own = jnp.where(side == 0, layer0_ref[0], layer1_ref[0]).astype(jnp.float32)
    other = received_ref[0].astype(jnp.float32)
    rows = own.shape[0]
    start = 0
    for width, out_ref in zip(widths, out_refs):
        out_ref[pl.ds(pl.multiple_of(side * rows, rows), rows), :] = own[:, start : start + width]
        out_ref[pl.ds(pl.multiple_of((1 - side) * rows, rows), rows), :] = other[:, start : start + width]
        start += width


def finish_rows(side, layer0, layer1, received, widths):
    shards, rows, columns = layer0.shape
    return run(
        functools.partial(finish_rows_kernel, widths),
        (shards,),
        [in_smem()] + [slab((1, rows, columns), 0)] * 3,
        tuple(slab((2 * rows, width), 1) for width in widths),
        tuple(like((2 * rows, shards * width), jnp.float32) for width in widths),
        [],
        "finish_rows",
        0,
        layer0.size * 14,
        [side, layer0, layer1, received],
    )


def finish_cols_kernel(hidden, side_ref, layer0_ref, layer1_ref, received_ref, down_ref, out_ref):
    side = side_ref[0]
    own = jnp.where(side == 0, layer0_ref[0], layer1_ref[0]).astype(jnp.float32)
    other = received_ref[0].astype(jnp.float32)
    first = out_ref.shape[0]
    columns = own.shape[1]
    here = pl.ds(pl.multiple_of(side * columns, columns), columns)
    there = pl.ds(pl.multiple_of((1 - side) * columns, columns), columns)
    down_ref[:, here] = own[first : first + hidden]
    down_ref[:, there] = other[first : first + hidden]
    out_ref[:, here] = own[:first]
    out_ref[:, there] = other[:first]


def finish_cols(side, layer0, layer1, received, hidden):
    shards, rows, columns = layer0.shape
    return run(
        functools.partial(finish_cols_kernel, hidden),
        (shards,),
        [in_smem()] + [slab((1, rows, columns), 0)] * 3,
        (slab((hidden, 2 * columns), 0), slab((HEAD_V, 2 * columns), 0)),
        (
            like((shards * hidden, 2 * columns), jnp.float32),
            like((shards * HEAD_V, 2 * columns), jnp.float32),
        ),
        [],
        "finish_cols",
        0,
        layer0.size * 14,
        [side, layer0, layer1, received],
    )


def finish_gu_kernel(hidden, side_ref, layer0_ref, layer1_ref, received_ref, gate_ref, up_ref):
    side = side_ref[0]
    shards, rows, columns = layer0_ref.shape
    here = pl.ds(pl.multiple_of(side * rows, rows), rows)
    there = pl.ds(pl.multiple_of((1 - side) * rows, rows), rows)
    for s in range(shards):
        own = jnp.where(side == 0, layer0_ref[s], layer1_ref[s]).astype(jnp.float32)
        other = received_ref[s].astype(jnp.float32)
        for start, out_ref in ((0, gate_ref), (columns // 2, up_ref)):
            out_ref[here, s * hidden : (s + 1) * hidden] = own[:, start : start + hidden]
            out_ref[there, s * hidden : (s + 1) * hidden] = other[:, start : start + hidden]


def finish_gu(side, layer0, layer1, received, hidden):
    shards, rows, _ = layer0.shape
    return run(
        functools.partial(finish_gu_kernel, hidden),
        (),
        [in_smem()] + [in_vmem()] * 3,
        (in_vmem(), in_vmem()),
        (like((2 * rows, shards * hidden), jnp.float32),) * 2,
        [],
        "finish_gu",
        0,
        layer0.size * 14,
        [side, layer0, layer1, received],
    )


def place_tokens_kernel(shards, me_ref, *refs):
    part_refs, out_ref = refs[:-1], refs[-1]
    micros, rows, width = part_refs[0].shape
    columns = width // (2 * shards)
    for number, part in enumerate(part_refs):
        where = pl.ds(pl.multiple_of((me_ref[0] ^ number) * rows, rows), rows)
        for half in range(2):
            for s in range(shards):
                source = (half * shards + s) * columns
                target = (s * 2 + half) * columns
                for m in range(micros):
                    out_ref[m, where, target : target + columns] = part[m, :, source : source + columns]


def place_tokens(me, parts, shards):
    micros, sub, width = parts[0].shape
    shape = (micros, sub * len(parts), width)
    return run(
        functools.partial(place_tokens_kernel, shards),
        (),
        [in_smem()] + [in_vmem()] * len(parts),
        in_vmem(),
        like(shape, parts[0].dtype),
        [],
        "place_tokens",
        0,
        4 * micros * sub * width * len(parts),
        [me] + list(parts),
    )


def join_cols_kernel(part_ref, out_ref):
    out_ref[...] = part_ref[0]


def join_cols(part):
    shards, rows, columns = part.shape
    return run(
        join_cols_kernel,
        (shards,),
        [slab((1, rows, columns), 0)],
        slab((rows, columns), 1),
        like((rows, shards * columns), part.dtype),
        [],
        "join_cols",
        0,
        part.size * 4,
        [part],
    )


def split_cols_kernel(whole_ref, out_ref):
    out_ref[0] = whole_ref[...]


def split_cols(whole, shards):
    rows, width = whole.shape
    columns = width // shards
    return run(
        split_cols_kernel,
        (shards,),
        [slab((rows, columns), 1)],
        slab((1, rows, columns), 0),
        like((shards, rows, columns), whole.dtype),
        [],
        "split_cols",
        0,
        whole.size * 4,
        [whole],
    )


def halves(value, axis):
    step = 1
    while step < lax.axis_size(axis):
        value = value + swapped(value, axis, step.bit_length() - 1)
        step *= 2
    return value


def by_partner(value, axis):
    size = lax.axis_size(axis)
    return [value] + [
        lax.ppermute(value, axis, [(i, i ^ k) for i in range(size)]) for k in range(1, size)
    ]


def in_order(parts, axis):
    position = lax.axis_index(axis)
    parts = list(parts)
    step = 1
    while step < len(parts):
        odd = (position & step) != 0
        parts = [jnp.where(odd, parts[i ^ step], parts[i]) for i in range(len(parts))]
        step *= 2
    return parts


def gathered(value, axis):
    return jnp.concatenate(in_order(by_partner(value, axis), axis), axis=0)


def swap_pieces(pieces, axis):
    size = lax.axis_size(axis)
    return [pieces[0]] + [
        lax.ppermute(pieces[n], axis, [(i, i ^ n) for i in range(size)]) for n in range(1, size)
    ]


def for_partners(parts, me):
    return [lax.dynamic_index_in_dim(parts, me[0] ^ n, 0, False) for n in range(parts.shape[0])]


def exchange(pieces):
    return by_partner(sum_pieces(swap_pieces(pieces, SEQ)), SEQ)


def pick(flag, when, otherwise):
    return jnp.where(flag, when, otherwise)


def both_layers(local, axis):
    core = lax.axis_index(SECTION)
    half = local.shape[axis] // 2
    own = lax.dynamic_slice_in_dim(local, core * half, half, axis)
    received = partner(lax.dynamic_slice_in_dim(local, (1 - core) * half, half, axis))
    first = core == 0
    return pick(first, own, received), pick(first, received, own)


def move_rows(part):
    return lax.all_to_all(part, SEQ, 0, 0).reshape(-1, part.shape[2])


def move_cols(part):
    return join_cols(lax.all_to_all(part, SEQ, 0, 0))


def spread_rows(part):
    full = lax.all_gather(part, (HEAD, SECTION), axis=0, tiled=True)
    return full.reshape(lax.axis_size(HEAD), -1, part.shape[1])


def spread_cols(part):
    full = lax.all_gather(part, (SECTION, HEAD), axis=0, tiled=True)
    return full.reshape(2, lax.axis_size(HEAD), -1, part.shape[1])


def reduce_rows(grad):
    return lax.psum_scatter(
        grad.reshape(-1, grad.shape[2]), (HEAD, SECTION), scatter_dimension=0, tiled=True
    )


def reduce_cols(grad):
    return lax.psum_scatter(
        grad.reshape(-1, grad.shape[2]), (SECTION, HEAD), scatter_dimension=0, tiled=True
    )


def collect_rows(part):
    shards = lax.axis_size(SEQ)
    return lax.all_to_all(part.reshape(shards, -1, part.shape[1]), SEQ, 0, 0)


def collect_cols(part):
    return lax.all_to_all(split_cols(part, lax.axis_size(SEQ)), SEQ, 0, 0)


def after(value, other):
    return lax.optimization_barrier((value, other))[0]


def layer_backward_fast(me, piece, upstream, saved, gains, weights, small, aux, parts, plan):
    at_mid, sum_rows, start, at_end, at_out, sum_cols, before_end, last_due = plan
    attn_gain, mlp_gain = gains
    w_proj, w_mix, w_cols, w_gu = weights
    taps, scal, norm_weight = small
    resid, normed, gate_pre, mixer, mid, ffn_in, gate_up, hidden = saved
    xh, states, inverse, mixed, gated = mixer
    shards = parts[0]
    slices, rows, _ = mixed.shape
    grad_gate_up, pieces = feed_back(me, upstream, gate_up, w_gu, w_cols, shards)
    grad_gu = grad_rows(ffn_in, grad_gate_up)
    pieces = swap_pieces(pieces, SEQ)
    pieces, _ = lax.optimization_barrier((pieces, grad_gu))
    sums = at_mid(by_partner(sum_pieces(pieces), SEQ))
    grad_mid, grad_attn, dmlp, dmixed, dgate, dnorm = mid_back(
        me, mlp_gain, sums, mid, upstream, w_cols, mixed, gate_pre, norm_weight
    )
    grad_both = grad_cols(hidden, upstream, gated, grad_attn, slices)
    grad_head = swap_pieces(for_partners(dmixed, piece), HEAD)
    grad_head, grad_both = lax.optimization_barrier((grad_head, grad_both))
    sum_gu = sum_rows(grad_gu, dmixed)
    running = start(grad_head, sum_gu)
    dxh, dtaps, dscal = recur_backward(piece, xh, grad_head, aux, taps, scal, states, inverse, parts)
    dxh, running = at_end(dxh, running, sum_gu)
    packed = swap_pieces(dxh, HEAD)
    grad_pre, pieces, dmix = project_back(me, piece, packed, dgate, w_proj, w_mix, normed, shards)
    pieces, running = at_out(pieces, running)
    grad_proj = grad_rows(normed, grad_pre)
    pieces = swap_pieces(pieces, SEQ)
    pieces, _ = lax.optimization_barrier((pieces, grad_proj))
    sums, sum_both = sum_cols(grad_both, (sum_gu, dxh), grad_pre, pieces)
    sums, running = lax.optimization_barrier((sums, running))
    sums = before_end(sums)
    grad_resid, dattn = norm_back(me, attn_gain, sums, resid, grad_mid)
    sum_proj = reduce_rows(after(grad_proj, last_due(sum_both, sums, sum_gu, grad_resid)))
    small_grads = (dtaps[:CONVK], dscal[0, :2], dnorm[0], dattn[0], dmlp[0], dmix[:, :2])
    return grad_resid, (sum_proj, sum_gu, sum_both), small_grads, running


def fast_shards(
    tokens,
    cotangent,
    doc_starts,
    valid_mask,
    gain_attn,
    w_query,
    w_key,
    w_value,
    w_gate_out,
    w_decay,
    w_beta,
    conv_query,
    conv_key,
    conv_value,
    decay_log,
    decay_bias,
    out_norm,
    w_output,
    gain_mlp,
    w_gate,
    w_up,
    w_down,
):
    core = lax.axis_index(SECTION)
    first = core == 0
    shard = lax.axis_index(SEQ)
    piece = lax.axis_index(HEAD)
    shards, slices = lax.axis_size(SEQ), lax.axis_size(HEAD)
    parts = (shards, slices)
    shard_rows = w_query.shape[1]
    model_width = tokens.shape[2]
    sub = tokens.shape[1] // slices
    length = tokens.shape[1] * shards
    hidden_width = w_gate.shape[2] // shards
    hidden_padded = -(-hidden_width // 128) * 128

    def columns(value, width):
        return jnp.stack([value[:, s * width : (s + 1) * width] for s in range(shards)])

    def halved(value):
        shape = value.shape[:-1]
        value = value.reshape(shape + (shards, 2, model_width // (2 * shards)))
        return jnp.swapaxes(value, -3, -2).reshape(shape + (model_width,))

    proj_local = jnp.concatenate(
        [
            columns(w_query[0], HEAD_K),
            columns(w_key[0], HEAD_K),
            columns(w_value[0], HEAD_V),
            columns(w_gate_out[0], HEAD_V),
        ],
        axis=2,
    )
    fill = ((0, 0), (0, 0), (0, hidden_padded - hidden_width))
    gu_local = jnp.concatenate(
        [jnp.pad(columns(w_gate[0], hidden_width), fill), jnp.pad(columns(w_up[0], hidden_width), fill)],
        axis=2,
    )
    cols_local = jnp.concatenate(
        [
            w_output[0].reshape(shards, HEAD_V, shard_rows),
            w_down[0].reshape(shards, hidden_width, shard_rows),
            jnp.zeros((shards, hidden_padded - hidden_width, shard_rows), jnp.bfloat16),
        ],
        axis=1,
    )
    proj_parts = both_layers(proj_local, 1)
    cols_parts = both_layers(cols_local, 2)
    gu_parts = both_layers(gu_local, 1)

    conv = jnp.concatenate(
        [
            columns(conv_query[0], HEAD_K),
            columns(conv_key[0], HEAD_K),
            columns(conv_value[0], HEAD_V),
        ],
        axis=2,
    )
    taps_own = lax.dynamic_index_in_dim(conv, shard, 0, False).astype(jnp.float32)
    small_own = jnp.concatenate(
        [
            taps_own.reshape(-1),
            jnp.stack([decay_log[0, shard], decay_bias[0, shard]]),
            out_norm[0].astype(jnp.float32),
            gain_attn[0].astype(jnp.float32),
            gain_mlp[0].astype(jnp.float32),
            w_decay[0].astype(jnp.float32).T.reshape(-1),
            w_beta[0].astype(jnp.float32).T.reshape(-1),
        ]
    )
    small_own = after(small_own, proj_parts[0])
    small_other = partner(small_own)
    small_layers = (pick(first, small_own, small_other), pick(first, small_other, small_own))
    taps_size = CONVK * WIDTH
    norm_at = taps_size + 2
    gain_at = norm_at + HEAD_V
    wide = jnp.stack([vector[gain_at:] for vector in small_layers])
    wide = jnp.concatenate([wide.reshape(-1), valid_mask[core].astype(jnp.float32)])
    wide = gathered(wide[None], SEQ)
    valid_all = wide[:, wide.shape[1] - tokens.shape[1] :].reshape(shards, slices, sub)
    valid = lax.dynamic_index_in_dim(valid_all, piece, 1, False).reshape(-1)
    wide = wide[:, : wide.shape[1] - tokens.shape[1]].reshape(shards, 2, 2 + 2 * shards, 2, shard_rows // 2)
    gains_all = jnp.transpose(wide[:, :, :2], (1, 2, 3, 0, 4)).reshape(2, 2, model_width)
    mix_all = wide[:, :, 2:].reshape(shards, 2, 2, shards, 2, shard_rows // 2)
    mix_all = lax.dynamic_index_in_dim(mix_all, shard, 3, False)
    mix_all = jnp.transpose(mix_all, (1, 2, 3, 0, 4)).reshape(2, 2, model_width).astype(jnp.bfloat16)
    mix_all = gathered(mix_all[None], HEAD)
    mix_all = jnp.swapaxes(mix_all, 0, 1)
    mix_all = jnp.concatenate(
        [mix_all, mix_all, jnp.zeros((2, slices, 12, model_width), jnp.bfloat16)], axis=2
    )
    small = []
    gains = []
    weights = []
    for layer in range(2):
        vector = small_layers[layer]
        taps = jnp.pad(vector[:taps_size].reshape(CONVK, WIDTH), ((0, 8 - CONVK), (0, 0)))
        scal = jnp.pad(vector[taps_size:norm_at][None], ((0, 7), (0, 126)))
        small.append((taps, scal, vector[None, norm_at:gain_at]))
        gains.append((gains_all[layer, 0][None], gains_all[layer, 1][None]))

    def my_tokens(value):
        mine = lax.dynamic_slice_in_dim(value, piece * sub, sub, 0)
        return by_partner(halved(mine), SEQ)

    me = shard[None].astype(jnp.int32)
    place_at = piece[None].astype(jnp.int32)
    valid = valid[:, None]
    aux = make_aux(doc_starts[core], length)
    masked = cotangent[core] * valid_mask[core].astype(jnp.bfloat16)[:, None]

    token_parts, base = my_tokens(tokens[core]), None
    proj0 = after(move_rows(proj_parts[0]), (small_layers, cols_parts, gu_parts))
    cols0 = lax.all_to_all(after(cols_parts[0], proj0), SEQ, 0, 0)
    cols0 = join_cols(after(cols0, (token_parts, gains, small, valid, mix_all)))
    gu0 = move_rows(after(gu_parts[0], cols0))
    weights = [(spread_rows(proj0), mix_all[0], spread_cols(cols0), None)]

    saved = []
    stats = []
    for layer in range(2):
        w_proj, w_mix, w_cols, w_gu = weights[layer]
        attn_gain, mlp_gain = gains[layer]
        resid, normed, packed, gate_pre, stat = project(
            me, valid, attn_gain, token_parts, base, w_proj, w_mix
        )
        stats.append(stat)
        xh = swap_pieces(for_partners(packed, place_at), HEAD)
        if layer == 0:
            xh, gu0 = lax.optimization_barrier((xh, gu0))
            w_gu = spread_rows(gu0)
            weights[0] = (w_proj, w_mix, w_cols, w_gu)
            proj1 = move_rows(after(proj_parts[1], gu0))
            cols1 = move_cols(after(cols_parts[1], proj1))
        mixed, states, inverse = recur_forward(place_at, xh, aux, *small[layer][:2], parts)
        mixed = swap_pieces(mixed, HEAD)
        if layer == 0:
            mixed, proj1, cols1 = lax.optimization_barrier((mixed, proj1, cols1))
        else:
            mixed, gu1, masked = lax.optimization_barrier((mixed, gu1, masked))
            w_gu = spread_rows(gu1)
            weights[1] = (w_proj, w_mix, w_cols, w_gu)
        gated, kept, pieces = output(me, place_at, mixed, gate_pre, small[layer][2], w_cols, shards)
        mixer = (xh, states, inverse, kept, gated)
        mix_parts = exchange(pieces)
        base, ffn_in, gate_up, hidden, pieces, stat = feed(
            me, valid, mlp_gain, mix_parts, resid, w_gu, w_cols
        )
        stats.append(stat)
        saved.append((resid, normed, gate_pre, mixer, base, ffn_in, gate_up, hidden))
        if layer == 0:
            token_parts = exchange(pieces)
            gu1 = move_rows(after(gu_parts[1], token_parts))
            masked = my_tokens(after(masked, token_parts))
            weights.append((spread_rows(proj1), mix_all[1], spread_cols(cols1), None))
    h1 = saved[1][0]
    stats0 = jnp.stack([stats[2][0, 0], stats[1][0, 0], stats[2][0, 1]]) / shards
    upstream = place(me, masked)
    def placed_tokens(layer0, layer1):
        layer0, layer1 = (
            value if value.shape[0] == sub else lax.dynamic_slice_in_dim(value, shard * sub, sub, 0)
            for value in (layer0, layer1)
        )
        keep = pick(first, layer0, layer1)
        received = partner(pick(first, layer1, layer0))
        both = jnp.stack([pick(first, keep, received), pick(first, received, keep)])
        return place_tokens(piece[None].astype(jnp.int32), by_partner(both, HEAD), shards)

    early = {}

    def all_sums(pieces):
        return by_partner(sum_pieces(pieces), SEQ)

    def plan_last():
        def at_mid(sums):
            return sums

        def sum_rows(grad_gu, anchor):
            return reduce_rows(grad_gu)

        def start(anchor, sum_gu):
            return swap_pieces(after(pieces, anchor), SEQ)

        def at_end(dxh, running, sum_gu):
            dxh, running = lax.optimization_barrier((dxh, running))
            return dxh, (running, collect_rows(after(sum_gu, dxh)))

        def at_out(pieces, running):
            return lax.optimization_barrier((pieces, running))

        def sum_cols(grad_both, due, grad_pre, pieces):
            sum_both = reduce_cols(after(grad_both, due))
            return lax.optimization_barrier((all_sums(pieces), sum_both))

        def before_end(sums):
            return sums

        def last_due(sum_both, sums, sum_gu, grad_resid):
            return sum_both, sums

        return at_mid, sum_rows, start, at_end, at_out, sum_cols, before_end, last_due

    grad_h1, big1, small1, (last_sum, moved_gu1) = layer_backward_fast(
        me, place_at, upstream, saved[1], gains[1], weights[1], small[1], aux, parts, plan_last()
    )
    sum_proj1, sum_gu1, sum_both1 = big1
    last_sum = sum_pieces(last_sum)
    moved_both1 = collect_cols(after(sum_both1, grad_h1))
    here = shard * sub
    valid_here = lax.dynamic_slice_in_dim(valid, here, sub, 0)
    act1, stat = close(valid_here, last_sum, lax.dynamic_slice_in_dim(base, here, sub, 0))
    stats1 = jnp.stack([stat[0, 0], stats[3][0, 0] / shards, stat[0, 1]])
    activations = placed_tokens(h1, act1)

    def plan_first():
        def at_mid(sums):
            sums, early["both"] = lax.optimization_barrier((sums, moved_both1))
            return sums

        def sum_rows(grad_gu, anchor):
            return reduce_rows(after(grad_gu, (sum_proj1, anchor)))

        def start(anchor, sum_gu):
            return collect_rows(after(sum_proj1, anchor))

        def at_end(dxh, running, sum_gu):
            return lax.optimization_barrier((dxh, running))

        def at_out(pieces, running):
            return pieces, running

        def sum_cols(grad_both, due, grad_pre, pieces):
            sum_both = reduce_cols(after(grad_both, (due, grad_pre)))
            return all_sums(pieces), sum_both

        def before_end(sums):
            return sums

        def last_due(sum_both, sums, sum_gu, grad_resid):
            early["gu"] = collect_rows(after(sum_gu, grad_resid))
            early["grads"] = placed_tokens(grad_resid, grad_h1)
            return sum_both, early["gu"], early["grads"]

        return at_mid, sum_rows, start, at_end, at_out, sum_cols, before_end, last_due

    grad_tokens, big0, small0, moved_proj1 = layer_backward_fast(
        me, place_at, grad_h1, saved[0], gains[0], weights[0], small[0], aux, parts, plan_first()
    )
    sum_proj0, sum_gu0, sum_both0 = big0
    moved_both1 = early["both"]
    moved_gu0 = early["gu"]
    moved_both0 = collect_cols(after(sum_both0, moved_gu0))
    input_grads = early["grads"]
    side = core[None].astype(jnp.int32)
    grad_down, grad_out = finish_cols(
        side, moved_both0, moved_both1, partner(pick(first, moved_both1, moved_both0)), hidden_width
    )
    grad_gate, grad_up = finish_gu(
        side, moved_gu0, moved_gu1, partner(pick(first, moved_gu1, moved_gu0)), hidden_width
    )

    def pack(grads, sums):
        dtaps, dscal, dnorm, dattn, dmlp, dmix = grads
        place = (jnp.arange(2) == core)[:, None]
        marked = jnp.where(place, jnp.concatenate([sums, (jnp.sum(valid) / shards)[None]])[None], 0.0)
        return jnp.concatenate(
            [dtaps.reshape(-1), dscal, dnorm, marked.reshape(-1), dattn, dmlp, dmix.reshape(-1)]
        )

    packs = (pack(small0, stats0), pack(small1, stats1))
    vector = pick(first, packs[0], packs[1]) + partner(pick(first, packs[1], packs[0]))
    gain_end = norm_at + HEAD_V + 8 + 2 * model_width
    per_head = gathered(vector[None, :norm_at], SEQ)
    sums_all = halves(vector[norm_at:gain_end], HEAD)
    norm_sum = halves(sums_all[: HEAD_V + 8], SEQ)
    stat_sums = norm_sum[HEAD_V:].reshape(2, 4)
    norm_sum = norm_sum[:HEAD_V]
    gain_sums = sums_all[HEAD_V + 8 :].reshape(2, 2, shards, shard_rows // 2)
    gain_sums = lax.dynamic_index_in_dim(gain_sums, shard, 2, False).reshape(2, shard_rows)
    branch_rms = jnp.sqrt(stat_sums[:, :3] / jnp.maximum(stat_sums[:, 3:], 1.0))
    mix_grad = vector[gain_end:].reshape(slices, 2, 2, shards, shard_rows // 2)
    mix_grad = jnp.sum(lax.all_to_all(mix_grad, HEAD, 0, 0), axis=0)
    mix_grad = lax.all_to_all(jnp.transpose(mix_grad, (2, 0, 1, 3)), SEQ, 0, 0)
    mix_grad = jnp.transpose(mix_grad, (1, 2, 3, 0)).reshape(2, shard_rows, shards)
    others = (input_grads, grad_down, grad_out, grad_gate, grad_up, mix_grad, norm_sum, gain_sums, per_head)
    sum_proj0, others = lax.optimization_barrier((sum_proj0, others))
    input_grads, grad_down, grad_out, grad_gate, grad_up, mix_grad, norm_sum, gain_sums, per_head = others
    moved_proj0 = collect_rows(sum_proj0)
    grad_proj = finish_rows(
        side, moved_proj0, moved_proj1, partner(pick(first, moved_proj1, moved_proj0)),
        (HEAD_K, HEAD_K, HEAD_V, HEAD_V),
    )
    conv_grad = jnp.swapaxes(per_head[:, :taps_size].reshape(shards, CONVK, WIDTH), 0, 1)

    def conv_part(start, width):
        return conv_grad[:, :, start : start + width].reshape(1, CONVK, shards * width)

    return (
        activations[None],
        input_grads[None],
        branch_rms[None],
        gain_sums[0][None],
        grad_proj[0][None],
        grad_proj[1][None],
        grad_proj[2][None],
        grad_proj[3][None],
        mix_grad[0][None],
        mix_grad[1][None],
        conv_part(0, HEAD_K),
        conv_part(HEAD_K, HEAD_K),
        conv_part(2 * HEAD_K, HEAD_V),
        per_head[:, taps_size][None],
        per_head[:, taps_size + 1][None],
        norm_sum[None],
        grad_out[None],
        gain_sums[1][None],
        grad_gate[None],
        grad_up[None],
        grad_down[None],
    )


def per_device(*args):
    tokens, w_decay = args[0], args[9]
    rows = tokens.shape[1]
    seq, head, section = (lax.axis_size(axis) for axis in (SEQ, HEAD, SECTION))
    one_head_each = w_decay.shape[2] == seq
    micro_each = tokens.shape[0] == section == 2
    powers = seq & (seq - 1) == 0 and head & (head - 1) == 0
    even = rows % (head * BLOCK) == 0 and rows * seq % (BLOCK * GROUP) == 0
    if one_head_each and micro_each and powers and even:
        return fast_shards(*args)
    return shards(*args)


def solution(mesh):
    placed = (
        P(None, SEQ, None),
        P(None, SEQ, None),
        P(),
        P(None, SEQ),
        P(SECTION, SEQ),
        P(SECTION, SEQ, HEAD),
        P(SECTION, SEQ, HEAD),
        P(SECTION, SEQ, HEAD),
        P(SECTION, SEQ, HEAD),
        P(SECTION, SEQ, HEAD),
        P(SECTION, SEQ, HEAD),
        P(SECTION, None, HEAD),
        P(SECTION, None, HEAD),
        P(SECTION, None, HEAD),
        P(SECTION, HEAD),
        P(SECTION, HEAD),
        P(SECTION, None),
        P(SECTION, HEAD, SEQ),
        P(SECTION, SEQ),
        P(SECTION, SEQ, HEAD),
        P(SECTION, SEQ, HEAD),
        P(SECTION, HEAD, SEQ),
    )
    return jax.shard_map(
        per_device,
        mesh=mesh,
        in_specs=placed,
        out_specs=(
            P(SECTION, None, SEQ, None),
            P(SECTION, None, SEQ, None),
            P(SECTION, None, None),
            P(SECTION, SEQ),
            P(SECTION, SEQ, HEAD),
            P(SECTION, SEQ, HEAD),
            P(SECTION, SEQ, HEAD),
            P(SECTION, SEQ, HEAD),
            P(SECTION, SEQ, HEAD),
            P(SECTION, SEQ, HEAD),
            P(SECTION, None, HEAD),
            P(SECTION, None, HEAD),
            P(SECTION, None, HEAD),
            P(SECTION, HEAD),
            P(SECTION, HEAD),
            P(SECTION, None),
            P(SECTION, HEAD, SEQ),
            P(SECTION, SEQ),
            P(SECTION, SEQ, HEAD),
            P(SECTION, SEQ, HEAD),
            P(SECTION, HEAD, SEQ),
        ),
        check_vma=False,
    )
```

```python
import functools

import jax
import jax.numpy as jnp
from jax import lax
from jax.experimental import pallas as pl
from jax.experimental.pallas import tpu as pltpu
from jax.sharding import PartitionSpec as P

HEAD_K = 128
HEAD_V = 256
CONVK = 4
BLOCK = 64
SECTION = "section"
SEQ = "seq"
HEAD = "head"
LANES = 128
RECUR_FLOPS = 40_000_000
VMEM_LIMIT = 62 * 1024 * 1024
HALO = 8
EXTRA = 128
GROUP = 8


epsilon = 1e-06
highest_precision = lax.Precision.HIGHEST


def swapped(value, axis, stride):
    return lax.ppermute(value, axis, [(i, i ^ 1 << stride) for i in range(lax.axis_size(axis))])


def carried_in(value, axis, combine, identity):
    devices, position = (lax.axis_size(axis), lax.axis_index(axis))
    everything = jax.tree.map(
        lambda part, kind: lax.all_gather(part.astype(kind), axis),
        value,
        (jnp.bfloat16, jnp.bfloat16),
    )
    start = jax.tree.map(
        lambda part, zero: jnp.broadcast_to(jnp.asarray(zero, part.dtype), part.shape),
        value,
        identity,
    )

    def step(k, before):
        reached = k < position
        new = combine(
            before, jax.tree.map(lambda part, own: part[k].astype(own.dtype), everything, value)
        )
        return jax.tree.map(lambda a, b: jnp.where(reached, a, b), new, before)

    return lax.fori_loop(0, devices, step, start)


def entering(value, axis, join, neutral):
    count = lax.axis_size(axis)
    place = lax.axis_index(axis)
    ahead = count - 1 - place
    gathered = jax.tree.map(
        lambda a, kind: lax.all_gather(a.astype(kind), axis),
        value,
        jax.tree.map(lambda a: jnp.bfloat16 if a.dtype == jnp.float32 else a.dtype, value),
    )
    state = jax.tree.map(lambda a, e: jnp.zeros_like(a) + jnp.asarray(e, a.dtype), value, neutral)

    def one(step, state):
        source = count - 1 - step
        return join(
            state,
            jax.tree.map(
                lambda a, own: lax.dynamic_index_in_dim(a, source, 0, False).astype(own.dtype),
                gathered,
                value,
            ),
        )

    return lax.fori_loop(0, ahead, one, state)


def passed_along(value, axis, steps):
    count = lax.axis_size(axis)
    first, last = (max(0, -steps), min(count, count - steps))
    return lax.ppermute(value, axis, [(source, source + steps) for source in range(first, last)])


def rms_norm(values, weight):
    return values * lax.rsqrt(jnp.mean(values * values, axis=-1, keepdims=True) + epsilon) * weight


def doc_index(starts, positions):
    counted = jnp.sum(
        (starts[None, :] <= positions[:, None]).astype(jnp.int32), axis=1, dtype=jnp.int32
    )
    return counted - 1


def unit_rows(values):
    return values * lax.rsqrt(jnp.sum(values * values, axis=-1, keepdims=True) + epsilon)


def conv_front(extended, doc_ext, conv_weight):
    length = extended.shape[0] - (CONVK - 1)
    summed = jnp.zeros((length, extended.shape[1]), extended.dtype)
    for tap_index in range(CONVK):
        same_doc = doc_ext[tap_index : tap_index + length] == doc_ext[CONVK - 1 :]
        summed = (
            summed
            + jnp.where(same_doc[:, None], extended[tap_index : tap_index + length], 0.0)
            * conv_weight[tap_index]
        )
    return jax.nn.silu(summed)


def heads_front(extended, doc_ext, mix_pre, conv_weight, decay_scale, decay_shift, head_count):
    activated = conv_front(extended, doc_ext, conv_weight)
    length = activated.shape[0]
    width_k = head_count * HEAD_K
    queries = unit_rows(activated[:, :width_k].reshape(length, head_count, HEAD_K)) * HEAD_K ** (
        -0.5
    )
    key_rows = unit_rows(activated[:, width_k : 2 * width_k].reshape(length, head_count, HEAD_K))
    value_rows = activated[:, 2 * width_k :].reshape(length, head_count, HEAD_V)
    write_rate = jax.nn.sigmoid(mix_pre[:, head_count:])
    log_decay = -jnp.exp(decay_scale) * jax.nn.softplus(mix_pre[:, :head_count] + decay_shift)
    return (queries, key_rows, value_rows, write_rate, log_decay)


def block_terms(queries, key_rows, value_rows, write_rate, log_decay, doc_ids, prev_doc):
    length = queries.shape[1]
    cumulated = jnp.cumsum(log_decay, axis=1)
    row_iota = lax.broadcasted_iota(jnp.int32, (length, length), 0)
    col_iota = lax.broadcasted_iota(jnp.int32, (length, length), 1)
    same_doc = (doc_ids[:, :, None] == doc_ids[:, None, :]) & (col_iota <= row_iota)[None]
    same_mask = same_doc[:, :, :, None]
    exponent = jnp.where(same_mask, cumulated[:, :, None, :] - cumulated[:, None, :, :], 0.0)
    decay_full = jnp.where(same_mask, jnp.exp(exponent), 0.0)
    initial_decay = jnp.where((doc_ids == prev_doc[:, None])[:, :, None], jnp.exp(cumulated), 0.0)
    decay_heads = jnp.transpose(decay_full, (0, 3, 1, 2))
    key_gram = jnp.einsum("nthk,nihk->nhti", key_rows, key_rows, precision=highest_precision)
    strict_mask = (col_iota < row_iota)[None, None]
    lower_part = jnp.where(
        strict_mask,
        jnp.transpose(write_rate, (0, 2, 1))[:, :, :, None] * decay_heads * key_gram,
        0.0,
    )
    system = lower_part + jnp.eye(length, dtype=lower_part.dtype)
    scaled_values = jnp.transpose(write_rate[..., None] * value_rows, (0, 2, 1, 3))
    scaled_keys = jnp.transpose((write_rate * initial_decay)[..., None] * key_rows, (0, 2, 1, 3))
    resolved_values = lax.linalg.triangular_solve(
        system, scaled_values, left_side=True, lower=True, unit_diagonal=True
    )
    resolved_keys = lax.linalg.triangular_solve(
        system, scaled_keys, left_side=True, lower=True, unit_diagonal=True
    )
    query_key = (
        jnp.einsum("nthk,nihk->nhti", queries, key_rows, precision=highest_precision) * decay_heads
    )
    return (resolved_values, resolved_keys, query_key, decay_heads, initial_decay)


def gate_norm(mixed_out, gate_pre, norm_weight, head_count):
    length = mixed_out.shape[0]
    per_head = mixed_out.reshape(length, head_count, HEAD_V)
    gates = gate_pre.reshape(length, head_count, HEAD_V)
    normed = rms_norm(per_head, norm_weight) * jax.nn.silu(gates)
    return normed.reshape(length, head_count * HEAD_V)


def summary(
    extended, mix_pre, conv_weight, decay_scale, decay_shift, doc_ext, prev_docs, head_count
):
    queries, key_rows, value_rows, write_rate, log_decay = heads_front(
        extended, doc_ext, mix_pre, conv_weight, decay_scale, decay_shift, head_count
    )
    length = write_rate.shape[0]
    blocks = length // BLOCK

    def as_blocks(values):
        return values.reshape((blocks, BLOCK) + values.shape[1:])

    block_query_rows = as_blocks(queries)
    block_key_rows = as_blocks(key_rows)
    resolved_values, resolved_keys, query_key, decay_heads, initial_decay = block_terms(
        block_query_rows,
        block_key_rows,
        as_blocks(value_rows),
        as_blocks(write_rate),
        as_blocks(log_decay),
        as_blocks(doc_ext[CONVK - 1 :]),
        prev_docs,
    )
    final_row = decay_heads[:, :, -1, :]
    identity = jnp.eye(HEAD_K, dtype=extended.dtype)
    transfer_blocks = initial_decay[:, -1, :][:, :, None, None] * identity - jnp.einsum(
        "nhi,nihk,nhil->nhkl", final_row, block_key_rows, resolved_keys, precision=highest_precision
    )
    add_blocks = jnp.einsum(
        "nhi,nihk,nhiv->nhkv",
        final_row,
        block_key_rows,
        resolved_values,
        precision=highest_precision,
    )
    local_out = jnp.einsum(
        "nhti,nhiv->nhtv", query_key, resolved_values, precision=highest_precision
    )
    response = jnp.transpose(initial_decay, (0, 2, 1))[..., None] * jnp.transpose(
        block_query_rows, (0, 2, 1, 3)
    ) - jnp.einsum("nhti,nhik->nhtk", query_key, resolved_keys, precision=highest_precision)
    carry_map = jnp.broadcast_to(identity, (head_count, HEAD_K, HEAD_K))
    carried_addend = jnp.zeros((head_count, HEAD_K, HEAD_V), extended.dtype)
    entry_maps = []
    entry_adds = []
    for block_number in range(blocks):
        entry_maps.append(carry_map)
        entry_adds.append(carried_addend)
        carried_addend = (
            jnp.einsum(
                "jme,jed->jmd",
                transfer_blocks[block_number],
                carried_addend,
                precision=highest_precision,
            )
            + add_blocks[block_number]
        )
        carry_map = jnp.einsum(
            "hkl,hlm->hkm", transfer_blocks[block_number], carry_map, precision=highest_precision
        )
    kept = (local_out, response, jnp.stack(entry_maps), jnp.stack(entry_adds))
    return (carry_map, carried_addend, kept)


def finish(kept, running_state):
    local_out, response, entry_maps, entry_adds = kept
    entry_states = (
        jnp.einsum("nhkl,hlv->nhkv", entry_maps, running_state, precision=highest_precision)
        + entry_adds
    )
    result = local_out + jnp.einsum(
        "nhck,nhkv->nhcv", response, entry_states, precision=highest_precision
    )
    blocks, head_count, length, width_v = result.shape
    return jnp.transpose(result, (0, 2, 1, 3)).reshape(blocks * length, head_count * width_v)


def compose(earlier_blocks, later_blocks):
    return (
        jnp.einsum("hkl,hlm->hkm", later_blocks[0], earlier_blocks[0], precision=highest_precision),
        jnp.einsum("jme,jed->jmd", later_blocks[0], earlier_blocks[1], precision=highest_precision)
        + later_blocks[1],
    )


def head_total(values):
    return lax.psum(values.astype(jnp.bfloat16), HEAD).astype(jnp.float32)


def partner(values):
    return swapped(values, SECTION, 0)


def proj_t(left, right):
    return lax.dot_general(
        left, right, (((1,), (1,)), ((), ())), preferred_element_type=jnp.float32
    )


def inner_t(left, right):
    return lax.dot_general(
        left, right, (((0,), (0,)), ((), ())), preferred_element_type=jnp.float32
    )


def spread(rows_grads, cols_grads):
    rows_part = (
        lax.psum_scatter(
            rows_grads[0].astype(jnp.bfloat16), SEQ, scatter_dimension=0, tiled=True
        ).astype(jnp.float32),
        lax.psum_scatter(
            rows_grads[1].astype(jnp.bfloat16), SEQ, scatter_dimension=0, tiled=True
        ).astype(jnp.float32),
        lax.psum_scatter(
            rows_grads[2].astype(jnp.bfloat16), SEQ, scatter_dimension=0, tiled=True
        ).astype(jnp.float32),
        lax.psum_scatter(
            rows_grads[3].astype(jnp.bfloat16), SEQ, scatter_dimension=0, tiled=True
        ).astype(jnp.float32),
        lax.psum_scatter(
            rows_grads[4].astype(jnp.bfloat16), SEQ, scatter_dimension=0, tiled=True
        ).astype(jnp.float32),
    )
    cols_part = (
        lax.psum_scatter(
            cols_grads[0].astype(jnp.bfloat16), SEQ, scatter_dimension=1, tiled=True
        ).astype(jnp.float32),
        lax.psum_scatter(
            cols_grads[1].astype(jnp.bfloat16), SEQ, scatter_dimension=1, tiled=True
        ).astype(jnp.float32),
    )
    return (rows_part, cols_part)


def shards(
    tokens,
    cotangent,
    doc_starts,
    valid_mask,
    gain_attn,
    w_query,
    w_key,
    w_value,
    w_gate_out,
    w_decay,
    w_beta,
    conv_query,
    conv_key,
    conv_value,
    decay_log,
    decay_bias,
    out_norm,
    w_output,
    gain_mlp,
    w_gate,
    w_up,
    w_down,
):
    micro_count = tokens.shape[0]
    row_count = tokens.shape[1]
    model_width = tokens.shape[2]
    head_count = w_decay.shape[2]
    width_qk = w_query.shape[2]
    width_qkv = 2 * width_qk + w_value.shape[2]
    hidden_width = w_gate.shape[2]
    block_count = row_count // BLOCK
    section_index = lax.axis_index(SECTION)
    shard_index = lax.axis_index(SEQ)
    full_rows = (
        lax.all_gather(gain_attn[0], SEQ, axis=0, tiled=True),
        lax.all_gather(gain_mlp[0], SEQ, axis=0, tiled=True),
        lax.all_gather(w_query[0], SEQ, axis=0, tiled=True),
        lax.all_gather(w_key[0], SEQ, axis=0, tiled=True),
        lax.all_gather(w_value[0], SEQ, axis=0, tiled=True),
        lax.all_gather(w_gate_out[0], SEQ, axis=0, tiled=True),
        lax.all_gather(w_decay[0], SEQ, axis=0, tiled=True),
        lax.all_gather(w_beta[0], SEQ, axis=0, tiled=True),
        lax.all_gather(w_gate[0], SEQ, axis=0, tiled=True),
        lax.all_gather(w_up[0], SEQ, axis=0, tiled=True),
    )
    full_cols = (
        lax.all_gather(w_output[0], SEQ, axis=1, tiled=True),
        lax.all_gather(w_down[0], SEQ, axis=1, tiled=True),
    )
    attn_gain = full_rows[0].astype(jnp.float32)
    mlp_gain = full_rows[1].astype(jnp.float32)
    proj_weight = jnp.concatenate([full_rows[2], full_rows[3], full_rows[4], full_rows[5]], axis=1)
    mix_weight = jnp.concatenate([full_rows[6], full_rows[7]], axis=1).astype(jnp.float32)
    gate_up_weight = jnp.concatenate([full_rows[8], full_rows[9]], axis=1)
    out_weight = full_cols[0]
    down_weight = full_cols[1]
    conv_weight = jnp.concatenate([conv_query[0], conv_key[0], conv_value[0]], axis=1).astype(
        jnp.float32
    )
    decay_scale = decay_log[0]
    decay_shift = decay_bias[0]
    norm_weight = out_norm[0].astype(jnp.float32)
    ext_pos = (
        shard_index * row_count - (CONVK - 1) + jnp.arange(row_count + CONVK - 1, dtype=jnp.int32)
    )
    block_pos = shard_index * row_count + jnp.arange(block_count, dtype=jnp.int32) * BLOCK - 1

    def carry_backward(shard_map_t, shard_adj):
        identity = jnp.broadcast_to(
            jnp.eye(shard_map_t.shape[1], dtype=jnp.float32), shard_map_t.shape
        )
        suffix = entering(
            (shard_map_t, shard_adj), SEQ, compose, (identity, jnp.zeros_like(shard_adj))
        )
        result = suffix[1]
        return result

    def layer_backward(saved, upstream, starts):
        (
            resid_in,
            normed,
            mix_pre,
            extended,
            gate_pre,
            kept,
            running_state,
            shard_map,
            mixed_out,
            gated,
            resid_mid,
            ffn_in,
            gate_up,
            hidden,
        ) = saved
        doc_ext = doc_index(starts, ext_pos)
        prev_docs = doc_index(starts, block_pos)
        grad_ffn = upstream.astype(jnp.bfloat16)
        grad_hidden = proj_t(grad_ffn, down_weight)
        grad_down = inner_t(hidden, grad_ffn)
        _, act_back = jax.vjp(
            lambda gate_in, up_in: jax.nn.silu(gate_in) * up_in,
            gate_up[:, :hidden_width],
            gate_up[:, hidden_width:],
        )
        grad_gate, grad_up = act_back(grad_hidden)
        grad_gate_up = jnp.concatenate([grad_gate, grad_up], axis=1).astype(jnp.bfloat16)
        grad_gu_weight = inner_t(ffn_in, grad_gate_up)
        grad_ffn_in = head_total(proj_t(grad_gate_up, gate_up_weight))
        _, mlp_norm_back = jax.vjp(rms_norm, resid_mid, mlp_gain)
        grad_mid_norm, grad_mlp_gain = mlp_norm_back(grad_ffn_in)
        grad_mid = upstream + grad_mid_norm
        grad_attn = grad_mid.astype(jnp.bfloat16)
        grad_gated = proj_t(grad_attn, out_weight)
        grad_out_weight = inner_t(gated, grad_attn)
        _, gate_back = jax.vjp(
            lambda mixed_in, gate_in, weight_in: gate_norm(
                mixed_in, gate_in, weight_in, head_count
            ),
            mixed_out,
            gate_pre,
            norm_weight,
        )
        grad_mixed, grad_gate_pre, grad_norm_weight = gate_back(grad_gated)
        _, finish_back = jax.vjp(finish, kept, running_state)
        grad_kept, grad_state = finish_back(grad_mixed)
        later_blocks = carry_backward(jnp.swapaxes(shard_map, 1, 2), grad_state)
        gradient_transfer = jnp.einsum(
            "rgm,ram->rga", later_blocks, running_state, precision=highest_precision
        )

        def local_summary(ext_in, mix_in, conv_in, scale_in, shift_in):
            return summary(
                ext_in, mix_in, conv_in, scale_in, shift_in, doc_ext, prev_docs, head_count
            )

        _, summary_back = jax.vjp(
            local_summary, extended, mix_pre, conv_weight, decay_scale, decay_shift
        )
        grad_ext, grad_mix, grad_conv, grad_scale, grad_shift = summary_back(
            (gradient_transfer, later_blocks, grad_kept)
        )
        returned = passed_along(grad_ext[: CONVK - 1], SEQ, -1)
        grad_qkv = grad_ext[CONVK - 1 :] + jnp.pad(returned, ((row_count - (CONVK - 1), 0), (0, 0)))
        grad_pre = jnp.concatenate([grad_qkv, grad_gate_pre], axis=1).astype(jnp.bfloat16)
        grad_proj_weight = inner_t(normed, grad_pre)
        normed_float = normed.astype(jnp.float32)
        grad_mix_weight = lax.dot_general(
            normed_float, grad_mix, (((0,), (0,)), ((), ())), precision=highest_precision
        )
        grad_normed = head_total(
            proj_t(grad_pre, proj_weight)
            + lax.dot_general(
                grad_mix, mix_weight, (((1,), (1,)), ((), ())), precision=highest_precision
            )
        )
        _, attn_norm_back = jax.vjp(rms_norm, resid_in.astype(jnp.float32), attn_gain)
        grad_resid_norm, grad_attn_gain = attn_norm_back(grad_normed)
        grad_resid = grad_mid + grad_resid_norm
        rows_grads = (
            grad_attn_gain,
            grad_mlp_gain,
            grad_proj_weight,
            grad_mix_weight,
            grad_gu_weight,
        )
        cols_grads = (grad_out_weight, grad_down)
        small_grads = (grad_conv, grad_scale, grad_shift, grad_norm_weight)
        return (grad_resid, rows_grads, cols_grads, small_grads)

    zero_in = jnp.zeros((row_count, model_width), jnp.bfloat16)
    incoming = zero_in
    stored = None
    activations_buf = jnp.zeros(tokens.shape, jnp.bfloat16)
    stat_sums = jnp.zeros((micro_count, 3), jnp.float32)
    stat_counts = jnp.zeros((micro_count,), jnp.float32)
    for slot_index in range(micro_count + 1):
        chosen_raw = slot_index - section_index
        active = (chosen_raw >= 0) & (chosen_raw < micro_count)
        chosen = jnp.clip(chosen_raw, 0, micro_count - 1)
        resid_in = jnp.where(section_index == 0, tokens[min(slot_index, micro_count - 1)], incoming)
        layer_starts = doc_starts[chosen]
        layer_doc_ext = doc_index(layer_starts, ext_pos)
        layer_prev_docs = doc_index(layer_starts, block_pos)
        resid = resid_in.astype(jnp.float32)
        layer_normed = rms_norm(resid, attn_gain).astype(jnp.bfloat16)
        projected = jnp.dot(layer_normed, proj_weight, preferred_element_type=jnp.float32)
        layer_mix_pre = jnp.dot(
            layer_normed.astype(jnp.float32), mix_weight, precision=highest_precision
        )
        qkv_pre = projected[:, :width_qkv]
        layer_gate_pre = projected[:, width_qkv:]
        rim_rows = passed_along(qkv_pre[row_count - (CONVK - 1) :], SEQ, 1)
        layer_extended = jnp.concatenate([rim_rows, qkv_pre], axis=0)
        layer_shard_map, layer_shard_add, layer_kept = summary(
            layer_extended,
            layer_mix_pre,
            conv_weight,
            decay_scale,
            decay_shift,
            layer_doc_ext,
            layer_prev_docs,
            head_count,
        )
        carry_identity = jnp.broadcast_to(
            jnp.eye(layer_shard_map.shape[1], dtype=jnp.float32), layer_shard_map.shape
        )
        prefix = carried_in(
            (layer_shard_map, layer_shard_add),
            SEQ,
            compose,
            (carry_identity, jnp.zeros_like(layer_shard_add)),
        )
        carry_result = prefix[1]
        layer_mixed_out = finish(layer_kept, carry_result)
        layer_gated = gate_norm(layer_mixed_out, layer_gate_pre, norm_weight, head_count).astype(
            jnp.bfloat16
        )
        attn = head_total(jnp.dot(layer_gated, out_weight, preferred_element_type=jnp.float32))
        layer_resid_mid = resid + attn
        layer_ffn_in = rms_norm(layer_resid_mid, mlp_gain).astype(jnp.bfloat16)
        layer_gate_up = jnp.dot(layer_ffn_in, gate_up_weight, preferred_element_type=jnp.float32)
        layer_hidden = (
            jax.nn.silu(layer_gate_up[:, :hidden_width]) * layer_gate_up[:, hidden_width:]
        ).astype(jnp.bfloat16)
        ffn = head_total(jnp.dot(layer_hidden, down_weight, preferred_element_type=jnp.float32))
        layer_out = layer_resid_mid + ffn
        layer_saved = (
            resid_in,
            layer_normed,
            layer_mix_pre,
            layer_extended,
            layer_gate_pre,
            layer_kept,
            carry_result,
            layer_shard_map,
            layer_mixed_out,
            layer_gated,
            layer_resid_mid,
            layer_ffn_in,
            layer_gate_up,
            layer_hidden,
        )
        saved, layer_out, attn_out, ffn_out = (layer_saved, layer_out, attn, ffn)
        if stored is None:
            stored = jax.tree.map(
                lambda part_new: jnp.zeros((micro_count,) + part_new.shape, part_new.dtype), saved
            )
        stored = jax.tree.map(
            lambda buffer, part_new: buffer.at[chosen].set(
                jnp.where(active, part_new, buffer[chosen])
            ),
            stored,
            saved,
        )
        outgoing = layer_out.astype(jnp.bfloat16)
        activations_buf = activations_buf.at[chosen].set(
            jnp.where(active, outgoing, activations_buf[chosen])
        )
        weights_valid = valid_mask[chosen].astype(jnp.float32)
        sums_now = jnp.stack(
            [
                jnp.sum(weights_valid * jnp.mean(branch_val * branch_val, axis=-1))
                for branch_val in (layer_out, attn_out, ffn_out)
            ]
        )
        stat_sums = stat_sums.at[chosen].set(jnp.where(active, sums_now, stat_sums[chosen]))
        stat_counts = stat_counts.at[chosen].set(
            jnp.where(active, jnp.sum(weights_valid), stat_counts[chosen])
        )
        if slot_index < micro_count:
            incoming = partner(outgoing)
    rows_acc = None
    cols_acc = None
    small_acc = None
    back_in = zero_in
    grad_inputs = jnp.zeros(tokens.shape, jnp.bfloat16)
    for slot_index in range(micro_count + 1):
        chosen_raw = slot_index - (1 - section_index)
        active = (chosen_raw >= 0) & (chosen_raw < micro_count)
        chosen = jnp.clip(chosen_raw, 0, micro_count - 1)
        saved = jax.tree.map(lambda buffer: buffer[chosen], stored)
        from_loss = (
            cotangent[chosen].astype(jnp.float32) * valid_mask[chosen].astype(jnp.float32)[:, None]
        )
        upstream = jnp.where(section_index == 1, from_loss, back_in.astype(jnp.float32))
        grad_resid, rows_grads, cols_grads, small_grads = layer_backward(
            saved, upstream, doc_starts[chosen]
        )
        rows_grads = jax.tree.map(lambda grad_part: jnp.where(active, grad_part, 0.0), rows_grads)
        cols_grads = jax.tree.map(lambda grad_part: jnp.where(active, grad_part, 0.0), cols_grads)
        small_grads = jax.tree.map(lambda grad_part: jnp.where(active, grad_part, 0.0), small_grads)
        if rows_acc is None:
            rows_acc, cols_acc, small_acc = (rows_grads, cols_grads, small_grads)
        else:
            rows_acc = jax.tree.map(jnp.add, rows_acc, rows_grads)
            cols_acc = jax.tree.map(jnp.add, cols_acc, cols_grads)
            small_acc = jax.tree.map(jnp.add, small_acc, small_grads)
        outgoing = grad_resid.astype(jnp.bfloat16)
        grad_inputs = grad_inputs.at[chosen].set(jnp.where(active, outgoing, grad_inputs[chosen]))
        if slot_index < micro_count:
            back_in = partner(outgoing)
    rows_part, cols_part = spread(rows_acc, cols_acc)
    norm_heads = lax.psum(small_acc[3], HEAD)
    conv_sum, scale_sum, shift_sum, norm_sum, sums_all, counts_all = (
        lax.psum(small_acc[0].astype(jnp.bfloat16), SEQ).astype(jnp.float32),
        lax.psum(small_acc[1].astype(jnp.bfloat16), SEQ).astype(jnp.float32),
        lax.psum(small_acc[2].astype(jnp.bfloat16), SEQ).astype(jnp.float32),
        lax.psum(norm_heads.astype(jnp.bfloat16), SEQ).astype(jnp.float32),
        lax.psum(stat_sums.astype(jnp.bfloat16), SEQ).astype(jnp.float32),
        lax.psum(stat_counts.astype(jnp.bfloat16), SEQ).astype(jnp.float32),
    )
    branch_rms = jnp.sqrt(sums_all / jnp.maximum(counts_all, 1.0)[:, None])
    proj_part = rows_part[2]
    mix_part = rows_part[3]
    gu_part = rows_part[4]
    return (
        activations_buf[None],
        grad_inputs[None],
        branch_rms[None],
        rows_part[0][None],
        proj_part[:, :width_qk][None],
        proj_part[:, width_qk : 2 * width_qk][None],
        proj_part[:, 2 * width_qk : width_qkv][None],
        proj_part[:, width_qkv:][None],
        mix_part[:, :head_count][None],
        mix_part[:, head_count:][None],
        conv_sum[:, :width_qk][None],
        conv_sum[:, width_qk : 2 * width_qk][None],
        conv_sum[:, 2 * width_qk :][None],
        scale_sum[None],
        shift_sum[None],
        norm_sum[None],
        cols_part[0][None],
        rows_part[1][None],
        gu_part[:, :hidden_width][None],
        gu_part[:, hidden_width:][None],
        cols_part[1][None],
    )


def high_low(value):
    high = value.astype(jnp.bfloat16)
    return high, (value - high.astype(jnp.float32)).astype(jnp.bfloat16)


@functools.partial(jax.custom_vjp, nondiff_argnums=(2,))
def fine_dot(a, b, dims):
    a_high, a_low = high_low(a)
    b_high, b_low = high_low(b)

    def part(x, y):
        return lax.dot_general(x, y, (dims, ((), ())), preferred_element_type=jnp.float32)

    return part(a_high, b_high) + (part(a_high, b_low) + part(a_low, b_high))


def fine_dot_fwd(a, b, dims):
    return fine_dot(a, b, dims), (a, b)


def fine_dot_bwd(dims, kept, grad):
    a, b = kept
    (a_dim,), (b_dim,) = dims
    if a_dim == 1:
        da = fine_dot(grad, b, ((1,), (1 - b_dim,)))
    else:
        da = fine_dot(b, grad, ((1 - b_dim,), (1,)))
    if b_dim == 0:
        db = fine_dot(a, grad, ((1 - a_dim,), (0,)))
    else:
        db = fine_dot(grad, a, ((0,), (1 - a_dim,)))
    return da, db


fine_dot.defvjp(fine_dot_fwd, fine_dot_bwd)


def dot_nn(a, b):
    return fine_dot(a, b, ((1,), (0,)))


def dot_nt(a, b):
    return fine_dot(a, b, ((1,), (1,)))


def dot_tn(a, b):
    return fine_dot(a, b, ((0,), (0,)))


@functools.partial(jax.custom_vjp, nondiff_argnums=(1,))
def shifted(window, steps):
    if steps == 0:
        return window[HALO:]
    return pltpu.roll(window, steps, 0)[HALO:]


def shifted_fwd(window, steps):
    return shifted(window, steps), None


def shifted_bwd(steps, _, grad):
    padded = jnp.concatenate([jnp.zeros((HALO, grad.shape[1]), grad.dtype), grad], axis=0)
    if steps == 0:
        return (padded,)
    return (pltpu.roll(padded, padded.shape[0] - steps, 0),)


shifted.defvjp(shifted_fwd, shifted_bwd)


def iotas(length):
    rows = lax.broadcasted_iota(jnp.int32, (length, length), 0)
    cols = lax.broadcasted_iota(jnp.int32, (length, length), 1)
    return rows, cols


def as_row(column):
    rows, cols = iotas(column.shape[0])
    return jnp.sum(jnp.where(rows == cols, column, 0.0), axis=0, keepdims=True)


def unit_inverses(lowers):
    length = lowers[0].shape[0]
    rows, cols = iotas(length)
    eye = jnp.where(rows == cols, 1.0, 0.0)
    near = [jnp.where((rows >> 3) == (cols >> 3), lower, 0.0) for lower in lowers]
    results = [eye - part for part in near]
    squares = [dot_nn(part, part) for part in near]
    steps = [dot_nn(result, square) for result, square in zip(results, squares)]
    squares = [dot_nn(square, square) for square in squares]
    results = [result + step for result, step in zip(results, steps)]
    steps = [dot_nn(result, square) for result, square in zip(results, squares)]
    results = [result + step for result, step in zip(results, steps)]
    shift = 3
    while (1 << shift) < length:
        off = ((rows >> (shift + 1)) == (cols >> (shift + 1))) & ((rows >> shift) != (cols >> shift))
        steps = [
            dot_nn(jnp.where(off, lower, 0.0), result) for lower, result in zip(lowers, results)
        ]
        steps = [dot_nn(result, step) for result, step in zip(results, steps)]
        results = [result - step for result, step in zip(results, steps)]
        shift += 1
    return results


@jax.custom_vjp
def inverse_known(lower, inverse):
    return inverse


def inverse_known_fwd(lower, inverse):
    return inverse, inverse


def inverse_known_bwd(inverse, grad):
    return -dot_nt(dot_tn(inverse, grad), inverse), jnp.zeros_like(grad)


inverse_known.defvjp(inverse_known_fwd, inverse_known_bwd)


def silu(values):
    return values / (1.0 + jnp.exp(-values))


def sigmoid(values):
    return 1.0 / (1.0 + jnp.exp(-values))


@jax.custom_vjp
def softplus(values):
    return jnp.maximum(values, 0.0) + jnp.log1p(jnp.exp(-jnp.abs(values)))


def softplus_fwd(values):
    return softplus(values), values


def softplus_bwd(values, grad):
    return (grad * sigmoid(values),)


softplus.defvjp(softplus_fwd, softplus_bwd)


def block_front(window, mix_decay, mix_write, taps, decay_log, decay_bias, aux):
    summed = shifted(window, 0) * taps[3]
    for steps in range(1, CONVK):
        summed = summed + jnp.where(aux[:, steps : steps + 1] > 0.0, shifted(window, steps), 0.0) * taps[3 - steps]
    active = silu(summed)
    queries = unit_rows(active[:, :HEAD_K]) * HEAD_K ** (-0.5)
    keys = unit_rows(active[:, HEAD_K : 2 * HEAD_K])
    values = active[:, 2 * HEAD_K :]
    write = sigmoid(mix_write)
    log_decay = -jnp.exp(decay_log) * softplus(mix_decay + decay_bias)
    rows, cols = iotas(BLOCK)
    cum = jnp.sum(jnp.where(cols <= rows, as_row(log_decay), 0.0), axis=1, keepdims=True)
    total = jnp.sum(log_decay, axis=0, keepdims=True)
    doc = aux[:, 0:1]
    same = (doc == as_row(doc)) & (cols <= rows)
    decay = jnp.where(same, jnp.exp(jnp.where(same, cum - as_row(cum), 0.0)), 0.0)
    entry = jnp.where(aux[:, 4:5] > 0.0, jnp.exp(cum), 0.0)
    leave = jnp.where(aux[:, 5:6] > 0.0, jnp.exp(total - cum), 0.0)
    through = jnp.where(aux[BLOCK - 1 : BLOCK, 4:5] > 0.0, jnp.exp(total), 0.0)
    grams = dot_nt(jnp.concatenate([keys, queries], axis=0), keys)
    lower = jnp.where(cols < rows, write * decay * grams[:BLOCK], 0.0)
    mixing = grams[BLOCK:] * decay
    scaled = jnp.concatenate([write * values, (write * entry) * keys], axis=1)
    return lower, mixing, scaled, entry * queries, leave * keys, through


def block_prepare(window, mix_decay, mix_write, taps, decay_log, decay_bias, aux, inverse):
    lower, mixing, scaled, queries, keys, through = block_front(
        window, mix_decay, mix_write, taps, decay_log, decay_bias, aux
    )
    return mixing, dot_nn(inverse_known(lower, inverse), scaled), queries, keys, through


def block_core(mixing, resolved, queries, keys, through, state):
    read = dot_nn(jnp.concatenate([resolved[:, HEAD_V:], queries], axis=0), state)
    written = resolved[:, :HEAD_V] - read[:BLOCK]
    mixed = read[BLOCK:] + dot_nn(mixing, written)
    return mixed, through * state + dot_tn(keys, written)


def each_slice(piece_ref, refs, parts):
    shards, slices = parts
    sub = refs[0].shape[0] // shards
    for number, ref in enumerate(refs):
        for shard in range(shards):
            start = (shard * slices + (piece_ref[0] ^ number)) * sub
            yield pl.multiple_of(start, sub), pl.ds(shard * sub, sub), sub, ref


def fill_inputs(piece_ref, xh_refs, parts, xbuf, mixbuf):
    width = xbuf.shape[1]
    xbuf[0:HALO, :] = jnp.zeros((HALO, width), jnp.float32)
    for start, there, sub, ref in each_slice(piece_ref, xh_refs, parts):
        here = pl.ds(pl.multiple_of(start + HALO, HALO), sub)
        xbuf[here, :] = ref[there, :width].astype(jnp.float32)
        mixbuf[pl.ds(start, sub), :] = ref[there, width:].astype(jnp.float32)


def load_block(aux_ref, xbuf, mixbuf, base):
    window = xbuf[pl.ds(base, BLOCK + HALO), :]
    mix = mixbuf[pl.ds(base, BLOCK), :]
    aux = aux_ref[pl.ds(base, BLOCK), :]
    return window, mix[:, 0:1] + mix[:, 2:3], mix[:, 1:2] + mix[:, 3:4], aux


def load_taps(taps_ref):
    return [taps_ref[j : j + 1, :] for j in range(CONVK)]


def forward_kernel(parts, piece_ref, *refs):
    slices = parts[1]
    xh_refs, refs = refs[:slices], refs[slices:]
    aux_ref, taps_ref, scal_ref, *mixed_refs = refs[: 3 + slices]
    states_ref, inverse_ref, xbuf, mixbuf, mixed_buf, state_ref = refs[3 + slices :]
    fill_inputs(piece_ref, xh_refs, parts, xbuf, mixbuf)
    state_ref[...] = jnp.zeros_like(state_ref)
    blocks = aux_ref.shape[0] // BLOCK
    taps = load_taps(taps_ref)
    decay_log = scal_ref[0:1, 0:1]
    decay_bias = scal_ref[0:1, 1:2]

    def group(index, carry):
        state = state_ref[...]
        places, fronts = [], []
        for inner in range(GROUP):
            number = index * GROUP + inner
            base = pl.multiple_of(number * BLOCK, BLOCK)
            window, mix_decay, mix_write, aux = load_block(aux_ref, xbuf, mixbuf, base)
            places.append((number, base))
            fronts.append(block_front(window, mix_decay, mix_write, taps, decay_log, decay_bias, aux))
        inverses = unit_inverses([front[0] for front in fronts])
        resolved = [dot_nn(inverse, front[2]) for inverse, front in zip(inverses, fronts)]
        for (number, base), front, inverse, solved in zip(places, fronts, inverses, resolved):
            states_ref[number] = state
            inverse_ref[pl.ds(base, BLOCK), :] = inverse
            mixed, state = block_core(front[1], solved, *front[3:], state)
            mixed_buf[pl.ds(base, BLOCK), :] = mixed.astype(mixed_buf.dtype)
        state_ref[...] = state
        return carry

    lax.fori_loop(0, blocks // GROUP, group, 0)
    for start, there, sub, ref in each_slice(piece_ref, mixed_refs, parts):
        ref[there, :] = mixed_buf[pl.ds(start, sub), :]


def backward_kernel(parts, piece_ref, *refs):
    slices = parts[1]
    xh_refs, grad_refs, refs = refs[:slices], refs[slices : 2 * slices], refs[2 * slices :]
    aux_ref, taps_ref, scal_ref, states_ref, inverse_ref, *dxh_refs = refs[: 5 + slices]
    dtaps_ref, dscal_ref, xbuf, mixbuf, grad_buf, dxh_buf, adjoint_ref, halo_ref = refs[5 + slices :]
    fill_inputs(piece_ref, xh_refs, parts, xbuf, mixbuf)
    for start, there, sub, ref in each_slice(piece_ref, grad_refs, parts):
        grad_buf[pl.ds(start, sub), :] = ref[there, :]
    adjoint_ref[...] = jnp.zeros_like(adjoint_ref)
    halo_ref[...] = jnp.zeros_like(halo_ref)
    dtaps_ref[...] = jnp.zeros_like(dtaps_ref)
    dscal_ref[...] = jnp.zeros_like(dscal_ref)
    blocks = aux_ref.shape[0] // BLOCK
    width = xbuf.shape[1]
    taps = load_taps(taps_ref)
    decay_log = scal_ref[0:1, 0:1]
    decay_bias = scal_ref[0:1, 1:2]
    lanes = lax.broadcasted_iota(jnp.int32, (BLOCK, EXTRA), 1)

    def group(index, carry):
        adjoint = adjoint_ref[...]
        halo = halo_ref[...]
        dtaps = [dtaps_ref[j : j + 1, :] for j in range(CONVK)]
        dlog = dscal_ref[0:1, 0:1]
        dbias = dscal_ref[0:1, 1:2]
        places, prepares, cores = [], [], []
        for inner in range(GROUP):
            number = blocks - 1 - (index * GROUP + inner)
            base = pl.multiple_of(number * BLOCK, BLOCK)
            window, mix_decay, mix_write, aux = load_block(aux_ref, xbuf, mixbuf, base)
            inverse = inverse_ref[pl.ds(base, BLOCK), :]
            prepared, pull = jax.vjp(
                functools.partial(block_prepare, aux=aux, inverse=inverse),
                window, mix_decay, mix_write, taps, decay_log, decay_bias,
            )
            places.append(base)
            prepares.append(pull)
            cores.append(jax.vjp(block_core, *prepared, states_ref[number])[1])
        dprepared = []
        for base, pull in zip(places, cores):
            grad = grad_buf[pl.ds(base, BLOCK), :].astype(jnp.float32)
            *dparts, adjoint = pull((grad, adjoint))
            dprepared.append(tuple(dparts))
        for base, pull, dparts in zip(places, prepares, dprepared):
            dwindow, ddecay, dwrite, dtaps_now, dlog_now, dbias_now = pull(dparts)
            own = dwindow[HALO:]
            own = jnp.concatenate([own[: BLOCK - HALO], own[BLOCK - HALO :] + halo], axis=0)
            halo = dwindow[:HALO]
            dtaps = [a + b for a, b in zip(dtaps, dtaps_now)]
            dlog = dlog + dlog_now
            dbias = dbias + dbias_now
            dxh_buf[pl.ds(base, BLOCK), :width] = own.astype(dxh_buf.dtype)
            high_decay = ddecay.astype(jnp.bfloat16).astype(jnp.float32)
            high_write = dwrite.astype(jnp.bfloat16).astype(jnp.float32)
            mix = jnp.where(lanes == 0, high_decay, jnp.where(lanes == 1, high_write, 0.0))
            mix = jnp.where(lanes == 2, ddecay - high_decay, jnp.where(lanes == 3, dwrite - high_write, mix))
            dxh_buf[pl.ds(base, BLOCK), width:] = mix.astype(dxh_buf.dtype)
        adjoint_ref[...] = adjoint
        halo_ref[...] = halo
        for j in range(CONVK):
            dtaps_ref[j : j + 1, :] = dtaps[j]
        dscal_ref[0:1, 0:1] = dlog
        dscal_ref[0:1, 1:2] = dbias
        return carry

    lax.fori_loop(0, blocks // GROUP, group, 0)
    for start, there, sub, ref in each_slice(piece_ref, dxh_refs, parts):
        ref[there, :] = dxh_buf[pl.ds(start, sub), :]


WIDTH = 2 * HEAD_K + HEAD_V


def whole():
    return pl.BlockSpec(memory_space=pltpu.VMEM)


def recur_cost(length):
    return pl.CostEstimate(flops=length * RECUR_FLOPS, bytes_accessed=length * 8192, transcendentals=0)


def recur_forward(piece, xh, aux, taps, scal, parts):
    length = aux.shape[0]
    blocks = length // BLOCK
    slices = len(xh)
    *mixed, states, inverse = pl.pallas_call(
        functools.partial(forward_kernel, parts),
        out_shape=(jax.ShapeDtypeStruct((length // slices, HEAD_V), jnp.bfloat16),) * slices
        + (
            jax.ShapeDtypeStruct((blocks, HEAD_K, HEAD_V), jnp.float32),
            jax.ShapeDtypeStruct((length, BLOCK), jnp.float32),
        ),
        in_specs=[pl.BlockSpec(memory_space=pltpu.SMEM)] + [whole()] * (slices + 3),
        out_specs=(whole(),) * (slices + 2),
        scratch_shapes=[
            pltpu.VMEM((length + HALO, WIDTH), jnp.float32),
            pltpu.VMEM((length, EXTRA), jnp.float32),
            pltpu.VMEM((length, HEAD_V), jnp.bfloat16),
            pltpu.VMEM((HEAD_K, HEAD_V), jnp.float32),
        ],
        compiler_params=pltpu.CompilerParams(vmem_limit_bytes=VMEM_LIMIT),
        cost_estimate=recur_cost(length),
        name="recur_forward",
    )(piece, *xh, aux, taps, scal)
    return mixed, states, inverse


def recur_backward(piece, xh, grad, aux, taps, scal, states, inverse, parts):
    length = aux.shape[0]
    slices = len(xh)
    *dxh, dtaps, dscal = pl.pallas_call(
        functools.partial(backward_kernel, parts),
        out_shape=(jax.ShapeDtypeStruct((length // slices, WIDTH + EXTRA), jnp.bfloat16),) * slices
        + (
            jax.ShapeDtypeStruct((8, WIDTH), jnp.float32),
            jax.ShapeDtypeStruct((8, 128), jnp.float32),
        ),
        in_specs=[pl.BlockSpec(memory_space=pltpu.SMEM)] + [whole()] * (2 * slices + 5),
        out_specs=(whole(),) * (slices + 2),
        scratch_shapes=[
            pltpu.VMEM((length + HALO, WIDTH), jnp.float32),
            pltpu.VMEM((length, EXTRA), jnp.float32),
            pltpu.VMEM((length, HEAD_V), jnp.bfloat16),
            pltpu.VMEM((length, WIDTH + EXTRA), jnp.bfloat16),
            pltpu.VMEM((HEAD_K, HEAD_V), jnp.float32),
            pltpu.VMEM((HALO, WIDTH), jnp.float32),
        ],
        compiler_params=pltpu.CompilerParams(vmem_limit_bytes=VMEM_LIMIT),
        cost_estimate=recur_cost(length),
        name="recur_backward",
    )(piece, *xh, *grad, aux, taps, scal, states, inverse)
    return dxh, dtaps, dscal


def make_aux(starts, length):
    positions = jnp.arange(length, dtype=jnp.int32)
    doc = jnp.sum((starts[None, :] <= positions[:, None]).astype(jnp.int32), axis=1)
    def back(steps):
        earlier = jnp.concatenate([jnp.full((steps,), -1, jnp.int32), doc[:-steps]])
        return (earlier == doc).astype(jnp.float32)
    blocks = doc.reshape(-1, BLOCK)
    before = jnp.concatenate([jnp.full((1,), -1, jnp.int32), blocks[:-1, -1]])
    entering = (blocks == before[:, None]).reshape(-1).astype(jnp.float32)
    leaving = (blocks == blocks[:, -1:]).reshape(-1).astype(jnp.float32)
    zero = jnp.zeros((length,), jnp.float32)
    return jnp.stack([doc.astype(jnp.float32), back(1), back(2), back(3), entering, leaving, zero, zero], axis=1)


def dot(left, right):
    return lax.dot_general(
        left, right, (((1,), (0,)), ((), ())), preferred_element_type=jnp.float32
    )


def in_vmem():
    return pl.BlockSpec(memory_space=pltpu.VMEM)


def in_smem():
    return pl.BlockSpec(memory_space=pltpu.SMEM)


def held(shape):
    return pl.BlockSpec(shape, lambda step: (0,) * len(shape))


def slab(shape, axis):
    return pl.BlockSpec(shape, lambda step: tuple(step if d == axis else 0 for d in range(len(shape))))


def like(shape, dtype):
    return jax.ShapeDtypeStruct(shape, dtype)


def run(kernel, grid, in_specs, out_specs, out_shape, scratch, name, flops, moved, args):
    return pl.pallas_call(
        kernel,
        grid=grid,
        in_specs=in_specs,
        out_specs=out_specs,
        out_shape=out_shape,
        scratch_shapes=scratch,
        compiler_params=pltpu.CompilerParams(vmem_limit_bytes=VMEM_LIMIT),
        cost_estimate=pl.CostEstimate(flops=flops, bytes_accessed=moved, transcendentals=0),
        name=name,
    )(*args)


def row_scale(value):
    return lax.rsqrt(jnp.mean(value * value, axis=-1, keepdims=True) + epsilon)


def mean_square(value, valid):
    return jnp.sum(valid * jnp.mean(value * value, axis=-1, keepdims=True), axis=0, keepdims=True)


def norm_adjoint(value, gain, grad):
    scale = row_scale(value)
    unit = value * scale
    scaled = grad * gain
    dvalue = scale * (scaled - unit * jnp.mean(scaled * unit, axis=-1, keepdims=True))
    return dvalue, jnp.sum(grad * unit, axis=0, keepdims=True)


def each_piece(me_ref, part_refs):
    rows = part_refs[0].shape[0]
    for number, part in enumerate(part_refs):
        start = (me_ref[0] ^ number) * rows
        yield pl.ds(pl.multiple_of(start, rows), rows), part


def hand_out(me_ref, total_ref, piece_refs):
    for where, piece in each_piece(me_ref, piece_refs):
        piece[...] = total_ref[where, :].astype(piece.dtype)


def put_stat(stat_ref, column, value):
    stat_ref[0:1, column : column + 1] += value


def mix_rows(mix_ref):
    mix = mix_ref[0]
    return jnp.concatenate([mix, jnp.zeros((EXTRA - mix.shape[0], mix.shape[1]), mix.dtype)], axis=0)


def project_kernel(kind, pieces, *refs):
    me_ref, valid_ref, gain_ref = refs[:3]
    part_refs = refs[3 : 3 + pieces]
    refs = refs[3 + pieces :]
    if kind == "next":
        base_ref, refs = refs[0], refs[1:]
    w_ref, mix_ref, resid_ref, normed_ref, packed_ref, gate_ref, stat_ref = refs

    @pl.when(pl.program_id(0) == 0)
    def _():
        stat_ref[...] = jnp.zeros_like(stat_ref)
        for where, part in each_piece(me_ref, part_refs):
            value = part[...].astype(jnp.float32)
            if kind == "next":
                valid = valid_ref[where, :]
                put_stat(stat_ref, 1, mean_square(value, valid))
                value = value + base_ref[where, :]
                put_stat(stat_ref, 0, mean_square(value, valid))
            rounded = value.astype(jnp.bfloat16)
            resid_ref[where, :] = rounded
            value = rounded.astype(jnp.float32)
            normed_ref[where, :] = (value * row_scale(value) * gain_ref[...]).astype(jnp.bfloat16)

    normed = normed_ref[...]
    result = dot(normed, w_ref[0])
    packed_ref[0, :, :WIDTH] = result[:, :WIDTH].astype(jnp.bfloat16)
    gate_ref[0] = result[:, WIDTH:]
    mix = proj_t(normed, mix_rows(mix_ref))
    lanes = lax.broadcasted_iota(jnp.int32, mix.shape, 1)
    low = mix - mix.astype(jnp.bfloat16).astype(jnp.float32)
    mix = jnp.where(lanes < 2, mix, jnp.where(lanes < 4, low, 0.0))
    packed_ref[0, :, WIDTH:] = mix.astype(jnp.bfloat16)


def project(me, valid, gain, parts, base, w_proj, w_mix):
    slices, width, columns = w_proj.shape
    sub = parts[0].shape[0]
    rows = sub * len(parts)
    kind = "first" if base is None else "next"
    return run(
        functools.partial(project_kernel, kind, len(parts)),
        (slices,),
        [in_smem(), held((rows, 1)), held((1, width))]
        + [held((sub, width))] * len(parts)
        + ([] if base is None else [held((rows, width))])
        + [slab((1, width, columns), 0), slab((1, 16, width), 0)],
        (
            held((rows, width)),
            held((rows, width)),
            slab((1, rows, WIDTH + EXTRA), 0),
            slab((1, rows, HEAD_V), 0),
            held((8, 128)),
        ),
        (
            like((rows, width), jnp.bfloat16),
            like((rows, width), jnp.bfloat16),
            like((slices, rows, WIDTH + EXTRA), jnp.bfloat16),
            like((slices, rows, HEAD_V), jnp.float32),
            like((8, 128), jnp.float32),
        ),
        [],
        "project_" + kind,
        2 * rows * width * columns * slices,
        w_proj.size * 2 + rows * width * 12,
        [me, valid, gain] + list(parts) + ([] if base is None else [base]) + [w_proj, w_mix],
    )


def output_kernel(slices, me_ref, piece_ref, *refs):
    mixed_refs, refs = refs[:slices], refs[slices:]
    gate_ref, norm_ref, w_ref, gated_ref, kept_ref, *piece_refs, total = refs

    @pl.when(pl.program_id(0) == 0)
    def _():
        for number, mixed_ref in enumerate(mixed_refs):
            j = piece_ref[0] ^ number
            kept_ref[j] = mixed_ref[...]
            value = mixed_ref[...].astype(jnp.float32)
            normed = value * row_scale(value) * norm_ref[...] * silu(gate_ref[j])
            start = pl.multiple_of(j * HEAD_V, HEAD_V)
            gated_ref[:, pl.ds(start, HEAD_V)] = normed.astype(jnp.bfloat16)

    weight = w_ref[0].reshape(gated_ref.shape[1], w_ref.shape[3])
    total[...] = dot(gated_ref[...], weight)
    hand_out(me_ref, total, piece_refs)


def output(me, piece, mixed, gate_pre, norm_weight, w_cols, shards):
    slices, rows, _ = gate_pre.shape
    inner, half = slices * HEAD_V, w_cols.shape[3]
    sub = rows // shards
    gated, kept, *pieces = run(
        functools.partial(output_kernel, slices),
        (2,),
        [in_smem(), in_smem()]
        + [held((rows, HEAD_V))] * slices
        + [held(gate_pre.shape), held((1, HEAD_V)), slab((1, slices, HEAD_V, half), 0)],
        (held((rows, inner)), held(gate_pre.shape)) + (slab((sub, half), 1),) * shards,
        (like((rows, inner), jnp.bfloat16), like(gate_pre.shape, jnp.bfloat16))
        + (like((sub, 2 * half), jnp.bfloat16),) * shards,
        [pltpu.VMEM((rows, half), jnp.float32)],
        "output",
        4 * rows * inner * half,
        inner * half * 4 + rows * inner * 12,
        [me, piece] + list(mixed) + [gate_pre, norm_weight, w_cols],
    )
    return gated, kept, pieces


def feed_kernel(pieces, *refs):
    me_ref, valid_ref, gain_ref = refs[:3]
    part_refs = refs[3 : 3 + pieces]
    base_ref, w_gu_ref = refs[3 + pieces : 5 + pieces]
    down_refs = refs[5 + pieces : -6 - pieces]
    mid_ref, normed_ref, gate_up_ref, hidden_ref, *piece_refs, stat_ref, total = refs[-6 - pieces :]
    step = pl.program_id(0)
    half = down_refs[0].shape[3]

    @pl.when(step == 0)
    def _():
        stat_ref[...] = jnp.zeros_like(stat_ref)
        total[...] = jnp.zeros_like(total)
        for where, part in each_piece(me_ref, part_refs):
            value = part[...].astype(jnp.float32)
            put_stat(stat_ref, 0, mean_square(value, valid_ref[where, :]))
            value = value + base_ref[where, :].astype(jnp.float32)
            mid_ref[where, :] = value
            normed_ref[where, :] = (value * row_scale(value) * gain_ref[...]).astype(jnp.bfloat16)

    result = dot(normed_ref[...], w_gu_ref[0])
    gate_up_ref[0] = result
    width = result.shape[1] // 2
    hidden = (silu(result[:, :width]) * result[:, width:]).astype(jnp.bfloat16)
    hidden_ref[...] = hidden
    for c in range(2):
        part = sum(
            dot(hidden[:, k * LANES : (k + 1) * LANES], ref[c, 0]) for k, ref in enumerate(down_refs)
        )
        total[:, c * half : (c + 1) * half] += part

    @pl.when(step == pl.num_programs(0) - 1)
    def _():
        hand_out(me_ref, total, piece_refs)


def down_slabs(w_cols, hidden):
    half = w_cols.shape[3]

    def block(number):
        return pl.BlockSpec((2, 1, LANES, half), lambda step: (0, step, number, 0))

    first = HEAD_V // LANES
    return [block(first + k) for k in range(hidden // LANES)]


def feed(me, valid, gain, parts, base, w_gu, w_cols):
    slices, width, columns = w_gu.shape
    sub = parts[0].shape[0]
    rows = sub * len(parts)
    hidden = columns // 2
    mid, normed, gate_up, hidden, *pieces, stat = run(
        functools.partial(feed_kernel, len(parts)),
        (slices,),
        [in_smem(), held((rows, 1)), held((1, width))]
        + [held((sub, width))] * len(parts)
        + [held((rows, width)), slab((1, width, columns), 0)]
        + down_slabs(w_cols, hidden),
        (
            held((rows, width)),
            held((rows, width)),
            slab((1, rows, columns), 0),
            slab((rows, hidden), 1),
        )
        + (held((sub, width)),) * len(parts)
        + (held((8, 128)),),
        (
            like((rows, width), jnp.float32),
            like((rows, width), jnp.bfloat16),
            like((slices, rows, columns), jnp.float32),
            like((rows, slices * hidden), jnp.bfloat16),
        )
        + (like((sub, width), jnp.bfloat16),) * len(parts)
        + (like((8, 128), jnp.float32),),
        [pltpu.VMEM((rows, width), jnp.float32)],
        "feed",
        2 * rows * width * (columns + hidden) * slices,
        (w_gu.size + hidden * slices * width) * 2 + rows * width * 16,
        [me, valid, gain] + list(parts) + [base, w_gu] + [w_cols] * (hidden // LANES),
    )
    return mid, normed, gate_up, hidden, pieces, stat


def close_kernel(valid_ref, part_ref, base_ref, out_ref, stat_ref):
    stat_ref[...] = jnp.zeros_like(stat_ref)
    value = part_ref[...].astype(jnp.float32)
    valid = valid_ref[...]
    put_stat(stat_ref, 1, mean_square(value, valid))
    value = value + base_ref[...]
    put_stat(stat_ref, 0, mean_square(value, valid))
    out_ref[...] = value.astype(jnp.bfloat16)


def close(valid, part, base):
    return run(
        close_kernel,
        (),
        [in_vmem()] * 3,
        (in_vmem(), in_vmem()),
        (like(base.shape, jnp.bfloat16), like((8, 128), jnp.float32)),
        [],
        "close",
        base.size * 6,
        base.size * 8,
        [valid, part, base],
    )


def sum_kernel(*refs):
    total = refs[0][...].astype(jnp.float32)
    for ref in refs[1:-1]:
        total = total + ref[...].astype(jnp.float32)
    refs[-1][...] = total.astype(refs[-1].dtype)


def sum_pieces(pieces):
    size = pieces[0].size
    return run(
        sum_kernel,
        (),
        [in_vmem()] * len(pieces),
        in_vmem(),
        like(pieces[0].shape, pieces[0].dtype),
        [],
        "sum_pieces",
        size * len(pieces),
        size * 2 * (len(pieces) + 1),
        list(pieces),
    )


def feed_back_kernel(shards, me_ref, up_ref, gate_up_ref, w_gu_ref, *refs):
    down_refs, (grad_ref, *piece_refs, total) = refs[: -2 - shards], refs[-2 - shards :]
    step = pl.program_id(0)
    half = down_refs[0].shape[3]
    width = gate_up_ref.shape[2] // 2
    upstream = up_ref[...]
    grad_hidden = jnp.concatenate(
        [
            proj_t(upstream[:, :half], ref[0, 0]) + proj_t(upstream[:, half:], ref[1, 0])
            for ref in down_refs
        ],
        axis=1,
    )
    gate = gate_up_ref[0, :, :width]
    up = gate_up_ref[0, :, width:]
    sig = sigmoid(gate)
    grad_ref[0, :, :width] = (grad_hidden * up * (sig * (1.0 + gate * (1.0 - sig)))).astype(jnp.bfloat16)
    grad_ref[0, :, width:] = (grad_hidden * (gate * sig)).astype(jnp.bfloat16)
    part = proj_t(grad_ref[0], w_gu_ref[0])

    @pl.when(step == 0)
    def _():
        total[...] = part

    @pl.when(step > 0)
    def _():
        total[...] += part

    @pl.when(step == pl.num_programs(0) - 1)
    def _():
        hand_out(me_ref, total, piece_refs)


def feed_back(me, upstream, gate_up, w_gu, w_cols, shards):
    slices, width, columns = w_gu.shape
    rows = upstream.shape[0]
    hidden = columns // 2
    sub = rows // shards
    grad, *pieces = run(
        functools.partial(feed_back_kernel, shards),
        (slices,),
        [
            in_smem(),
            held((rows, width)),
            slab((1, rows, columns), 0),
            slab((1, width, columns), 0),
        ]
        + down_slabs(w_cols, hidden),
        (slab((1, rows, columns), 0),) + (held((sub, width)),) * shards,
        (like((slices, rows, columns), jnp.bfloat16),) + (like((sub, width), jnp.bfloat16),) * shards,
        [pltpu.VMEM((rows, width), jnp.float32)],
        "feed_back",
        2 * rows * width * (columns + hidden) * slices,
        (w_gu.size + hidden * slices * width) * 2 + gate_up.size * 6 + rows * width * 4,
        [me, upstream, gate_up, w_gu] + [w_cols] * (hidden // LANES),
    )
    return grad, pieces


def mid_back_kernel(pieces, *refs):
    me_ref, gain_ref = refs[:2]
    part_refs = refs[2 : 2 + pieces]
    (
        mid_ref, up_ref, w_ref, mixed_ref, gate_ref, norm_ref,
        grad_mid_ref, grad_attn_ref, dgain_ref, dmixed_ref, dgate_ref, dnorm_ref,
    ) = refs[2 + pieces :]
    half = w_ref.shape[3]

    @pl.when(pl.program_id(0) == 0)
    def _():
        dgain_ref[...] = jnp.zeros_like(dgain_ref)
        dnorm_ref[...] = jnp.zeros_like(dnorm_ref)
        for where, part in each_piece(me_ref, part_refs):
            dvalue, dgain = norm_adjoint(mid_ref[where, :], gain_ref[...], part[...].astype(jnp.float32))
            dvalue = dvalue + up_ref[where, :].astype(jnp.float32)
            grad_mid_ref[where, :] = dvalue
            grad_attn_ref[where, :] = dvalue.astype(jnp.bfloat16)
            dgain_ref[...] += dgain

    grad = grad_attn_ref[...]
    grad_gated = proj_t(grad[:, :half], w_ref[0, 0]) + proj_t(grad[:, half:], w_ref[1, 0])
    value = mixed_ref[0].astype(jnp.float32)
    scale = row_scale(value)
    unit = value * scale
    weight = norm_ref[...]
    gate = gate_ref[0]
    sig = sigmoid(gate)
    dgate_ref[0] = (grad_gated * unit * weight * (sig * (1.0 + gate * (1.0 - sig)))).astype(jnp.bfloat16)
    dscaled = grad_gated * (gate * sig)
    dnorm_ref[...] += jnp.sum(dscaled * unit, axis=0, keepdims=True)
    dunit = dscaled * weight
    dmixed = scale * (dunit - unit * jnp.mean(dunit * unit, axis=-1, keepdims=True))
    dmixed_ref[0] = dmixed.astype(jnp.bfloat16)


def mid_back(me, gain, parts, mid, upstream, w_cols, mixed, gate_pre, norm_weight):
    slices, rows, _ = mixed.shape
    width = mid.shape[1]
    half = width // 2
    sub = parts[0].shape[0]
    return run(
        functools.partial(mid_back_kernel, len(parts)),
        (slices,),
        [in_smem(), held((1, width))]
        + [held((sub, width))] * len(parts)
        + [
            held((rows, width)),
            held((rows, width)),
            slab((2, 1, HEAD_V, half), 1),
            slab((1, rows, HEAD_V), 0),
            slab((1, rows, HEAD_V), 0),
            held((1, HEAD_V)),
        ],
        (
            held((rows, width)),
            held((rows, width)),
            held((1, width)),
            slab((1, rows, HEAD_V), 0),
            slab((1, rows, HEAD_V), 0),
            held((1, HEAD_V)),
        ),
        (
            like((rows, width), jnp.float32),
            like((rows, width), jnp.bfloat16),
            like((1, width), jnp.float32),
            like((slices, rows, HEAD_V), jnp.bfloat16),
            like((slices, rows, HEAD_V), jnp.bfloat16),
            like((1, HEAD_V), jnp.float32),
        ),
        [],
        "mid_back",
        2 * rows * width * HEAD_V * slices,
        slices * HEAD_V * width * 2 + rows * width * 20,
        [me, gain] + list(parts) + [mid, upstream, w_cols, mixed, gate_pre, norm_weight],
    )


def project_back_kernel(shards, slices, me_ref, piece_ref, *refs):
    part_refs, refs = refs[:slices], refs[slices:]
    dgate_ref, w_ref, mix_ref, normed_ref, grad_ref, dmix_ref, *piece_refs, packed, total = refs
    step = pl.program_id(0)

    @pl.when(step == 0)
    def _():
        for number, part in enumerate(part_refs):
            packed[piece_ref[0] ^ number] = part[...]
        total[...] = jnp.zeros_like(total)

    grad_ref[0, :, :WIDTH] = packed[step, :, :WIDTH]
    grad_ref[0, :, WIDTH:] = dgate_ref[0]
    mix = packed[step, :, WIDTH:]
    total[...] += proj_t(grad_ref[0], w_ref[0]) + dot(mix, mix_rows(mix_ref))
    dmix = inner_t(mix, normed_ref[...])
    dmix_ref[0] = jnp.concatenate([dmix[0:2] + dmix[2:4], dmix[2:8]], axis=0)

    @pl.when(step == pl.num_programs(0) - 1)
    def _():
        hand_out(me_ref, total, piece_refs)


def project_back(me, piece, packed, dgate, w_proj, w_mix, normed, shards):
    slices, width, columns = w_proj.shape
    rows = normed.shape[0]
    sub = rows // shards
    grad, dmix, *pieces = run(
        functools.partial(project_back_kernel, shards, slices),
        (slices,),
        [in_smem(), in_smem()]
        + [held((rows, WIDTH + EXTRA))] * slices
        + [
            slab((1, rows, HEAD_V), 0),
            slab((1, width, columns), 0),
            slab((1, 16, width), 0),
            held((rows, width)),
        ],
        (slab((1, rows, columns), 0), slab((1, 8, width), 0)) + (held((sub, width)),) * shards,
        (like((slices, rows, columns), jnp.bfloat16), like((slices, 8, width), jnp.float32))
        + (like((sub, width), jnp.bfloat16),) * shards,
        [
            pltpu.VMEM((slices, rows, WIDTH + EXTRA), jnp.bfloat16),
            pltpu.VMEM((rows, width), jnp.float32),
        ],
        "project_back",
        2 * rows * width * columns * slices,
        w_proj.size * 2 + rows * width * 12,
        [me, piece] + list(packed) + [dgate, w_proj, w_mix, normed],
    )
    return grad, pieces, dmix


def norm_back_kernel(pieces, *refs):
    me_ref, gain_ref = refs[:2]
    part_refs = refs[2 : 2 + pieces]
    resid_ref, mid_ref, out_ref, dgain_ref = refs[2 + pieces :]
    dgain_ref[...] = jnp.zeros_like(dgain_ref)
    for where, part in each_piece(me_ref, part_refs):
        value = resid_ref[where, :].astype(jnp.float32)
        dvalue, dgain = norm_adjoint(value, gain_ref[...], part[...].astype(jnp.float32))
        out_ref[where, :] = (dvalue + mid_ref[where, :]).astype(jnp.bfloat16)
        dgain_ref[...] += dgain


def norm_back(me, gain, parts, resid, grad_mid):
    return run(
        functools.partial(norm_back_kernel, len(parts)),
        (),
        [in_smem()] + [in_vmem()] * (3 + len(parts)),
        (in_vmem(), in_vmem()),
        (like(resid.shape, jnp.bfloat16), like(gain.shape, jnp.float32)),
        [],
        "norm_back",
        resid.size * 10,
        resid.size * 10,
        [me, gain] + list(parts) + [resid, grad_mid],
    )


def weight_grad_kernel(left_ref, right_ref, out_ref):
    right = right_ref[0] if len(right_ref.shape) == 3 else right_ref[...]
    out_ref[0] = inner_t(left_ref[...], right).astype(jnp.bfloat16)


def grad_rows(left, right):
    rows, width = left.shape
    slices, _, columns = right.shape
    return run(
        weight_grad_kernel,
        (slices,),
        [held((rows, width)), slab((1, rows, columns), 0)],
        slab((1, width, columns), 0),
        like((slices, width, columns), jnp.bfloat16),
        [],
        "grad_rows",
        2 * rows * width * columns * slices,
        slices * width * columns * 2 + rows * width * 2 + right.size * 2,
        [left, right],
    )


def grad_cols_kernel(hidden_ref, up_ref, gated_ref, grad_ref, out_ref):
    rows = hidden_ref.shape[1]
    out_ref[0, 0, :-rows] = inner_t(gated_ref[...], grad_ref[...]).astype(jnp.bfloat16)
    out_ref[0, 0, -rows:] = inner_t(hidden_ref[...], up_ref[...]).astype(jnp.bfloat16)


def grad_cols(hidden, upstream, gated, grad_attn, slices):
    rows, width = upstream.shape
    half = width // 2
    first, second = hidden.shape[1] // slices, gated.shape[1] // slices

    def piece(columns):
        return pl.BlockSpec((rows, columns), lambda c, j: (0, j))

    def side():
        return pl.BlockSpec((rows, half), lambda c, j: (0, c))

    result = run(
        grad_cols_kernel,
        (2, slices),
        [piece(first), side(), piece(second), side()],
        pl.BlockSpec((1, 1, first + second, half), lambda c, j: (c, j, 0, 0)),
        like((2, slices, first + second, half), jnp.bfloat16),
        [],
        "grad_cols",
        4 * rows * (first + second) * slices * half,
        2 * slices * (first + second) * half * 2 + rows * width * 4,
        [hidden, upstream, gated, grad_attn],
    )
    return result.reshape(2, slices * (first + second), half)


def run_sided(kernel, grid, side, in_specs, out_specs, out_shape, name, flops, moved, args):
    return pl.pallas_call(
        kernel,
        grid_spec=pltpu.PrefetchScalarGridSpec(
            num_scalar_prefetch=1, grid=grid, in_specs=in_specs, out_specs=out_specs
        ),
        out_shape=out_shape,
        compiler_params=pltpu.CompilerParams(vmem_limit_bytes=VMEM_LIMIT),
        cost_estimate=pl.CostEstimate(flops=flops, bytes_accessed=moved, transcendentals=0),
        name=name,
    )(side, *args)


def half_of(rows, width):
    return pl.BlockSpec((rows, width // 2), lambda step, side: (0, side[0]))


def pair_rows_kernel(side_ref, left_ref, left_other_ref, right_ref, right_other_ref, out_ref):
    total = inner_t(left_ref[...], right_ref[0]) + inner_t(left_other_ref[...], right_other_ref[0])
    out_ref[0] = total.astype(jnp.bfloat16)


def pair_rows(side, left, right):
    rows, width = left[0].shape
    slices, _, columns = right[0].shape
    piece = pl.BlockSpec((1, rows, columns), lambda step, side: (step, 0, 0))
    return run_sided(
        pair_rows_kernel,
        (slices,),
        side,
        [half_of(rows, width)] * 2 + [piece] * 2,
        pl.BlockSpec((1, width // 2, columns), lambda step, side: (step, 0, 0)),
        like((slices, width // 2, columns), jnp.bfloat16),
        "pair_rows",
        2 * rows * width * columns * slices,
        slices * width * columns + rows * width * 2 + right[0].size * 4,
        list(left) + list(right),
    )


def pair_cols_kernel(side_ref, *refs):
    hidden, up, gated, grad = refs[0:2], refs[2:4], refs[4:6], refs[6:8]
    out_ref = refs[8]
    rows = hidden[0].shape[1]
    out_ref[0, :-rows] = sum(inner_t(x[...], y[...]) for x, y in zip(gated, grad)).astype(jnp.bfloat16)
    out_ref[0, -rows:] = sum(inner_t(x[...], y[...]) for x, y in zip(hidden, up)).astype(jnp.bfloat16)


def pair_cols(side, hidden, upstream, gated, grad_attn, slices):
    rows, width = upstream[0].shape
    half = width // 2
    first, second = hidden[0].shape[1] // slices, gated[0].shape[1] // slices

    def piece(columns):
        return [pl.BlockSpec((rows, columns), lambda step, side: (0, step))] * 2

    result = run_sided(
        pair_cols_kernel,
        (slices,),
        side,
        piece(first) + [half_of(rows, width)] * 2 + piece(second) + [half_of(rows, width)] * 2,
        pl.BlockSpec((1, first + second, half), lambda step, side: (step, 0, 0)),
        like((slices, first + second, half), jnp.bfloat16),
        "pair_cols",
        4 * rows * (first + second) * slices * half,
        slices * (first + second) * half * 2 + rows * width * 8,
        list(hidden) + list(upstream) + list(gated) + list(grad_attn),
    )
    return result.reshape(slices * (first + second), half)


def place_kernel(pieces, *refs):
    me_ref, out_ref = refs[0], refs[-1]
    for where, part in each_piece(me_ref, refs[1:-1]):
        out_ref[where, :] = part[...]


def place(me, parts):
    sub, width = parts[0].shape
    shape = (sub * len(parts), width)
    return run(
        functools.partial(place_kernel, len(parts)),
        (),
        [in_smem()] + [in_vmem()] * len(parts),
        in_vmem(),
        like(shape, parts[0].dtype),
        [],
        "place",
        0,
        4 * sub * width * len(parts),
        [me] + list(parts),
    )


def place_cols_kernel(pieces, *refs):
    me_ref, out_ref = refs[0], refs[-1]
    width = refs[1].shape[1]
    for number, part in enumerate(refs[1:-1]):
        start = pl.multiple_of((me_ref[0] ^ number) * width, width)
        out_ref[:, pl.ds(start, width)] = part[...]


def place_cols(me, parts):
    rows, width = parts[0].shape
    shape = (rows, width * len(parts))
    return run(
        functools.partial(place_cols_kernel, len(parts)),
        (),
        [in_smem()] + [in_vmem()] * len(parts),
        in_vmem(),
        like(shape, parts[0].dtype),
        [],
        "place_cols",
        0,
        4 * rows * width * len(parts),
        [me] + list(parts),
    )


def finish_rows_kernel(widths, side_ref, layer0_ref, layer1_ref, received0_ref, received1_ref, *out_refs):
    side = side_ref[0]
    own = jnp.where(side == 0, layer0_ref[0], layer1_ref[0]).astype(jnp.float32)
    other = jnp.where(side == 0, received0_ref[0], received1_ref[0]).astype(jnp.float32)
    rows = own.shape[0]
    start = 0
    for width, out_ref in zip(widths, out_refs):
        out_ref[pl.ds(pl.multiple_of(side * rows, rows), rows), :] = own[:, start : start + width]
        out_ref[pl.ds(pl.multiple_of((1 - side) * rows, rows), rows), :] = other[:, start : start + width]
        start += width


def finish_rows(side, layer0, layer1, received0, received1, widths):
    shards, rows, columns = layer0.shape
    return run(
        functools.partial(finish_rows_kernel, widths),
        (shards,),
        [in_smem()] + [slab((1, rows, columns), 0)] * 4,
        tuple(slab((2 * rows, width), 1) for width in widths),
        tuple(like((2 * rows, shards * width), jnp.float32) for width in widths),
        [],
        "finish_rows",
        0,
        layer0.size * 14,
        [side, layer0, layer1, received0, received1],
    )


def finish_cols_kernel(hidden, side_ref, layer0_ref, layer1_ref, received_ref, down_ref, out_ref):
    side = side_ref[0]
    own = jnp.where(side == 0, layer0_ref[0], layer1_ref[0]).astype(jnp.float32)
    other = received_ref[0].astype(jnp.float32)
    first = out_ref.shape[0]
    columns = own.shape[1]
    here = pl.ds(pl.multiple_of(side * columns, columns), columns)
    there = pl.ds(pl.multiple_of((1 - side) * columns, columns), columns)
    down_ref[:, here] = own[first : first + hidden]
    down_ref[:, there] = other[first : first + hidden]
    out_ref[:, here] = own[:first]
    out_ref[:, there] = other[:first]


def finish_cols(side, layer0, layer1, received, hidden):
    shards, rows, columns = layer0.shape
    return run(
        functools.partial(finish_cols_kernel, hidden),
        (shards,),
        [in_smem()] + [slab((1, rows, columns), 0)] * 3,
        (slab((hidden, 2 * columns), 0), slab((HEAD_V, 2 * columns), 0)),
        (
            like((shards * hidden, 2 * columns), jnp.float32),
            like((shards * HEAD_V, 2 * columns), jnp.float32),
        ),
        [],
        "finish_cols",
        0,
        layer0.size * 14,
        [side, layer0, layer1, received],
    )


def finish_gu_kernel(hidden, side_ref, layer0_ref, layer1_ref, received_ref, gate_ref, up_ref):
    side = side_ref[0]
    shards, rows, columns = layer0_ref.shape
    here = pl.ds(pl.multiple_of(side * rows, rows), rows)
    there = pl.ds(pl.multiple_of((1 - side) * rows, rows), rows)
    for s in range(shards):
        own = jnp.where(side == 0, layer0_ref[s], layer1_ref[s]).astype(jnp.float32)
        other = received_ref[s].astype(jnp.float32)
        for start, out_ref in ((0, gate_ref), (columns // 2, up_ref)):
            out_ref[here, s * hidden : (s + 1) * hidden] = own[:, start : start + hidden]
            out_ref[there, s * hidden : (s + 1) * hidden] = other[:, start : start + hidden]


def finish_gu(side, layer0, layer1, received, hidden):
    shards, rows, _ = layer0.shape
    return run(
        functools.partial(finish_gu_kernel, hidden),
        (),
        [in_smem()] + [in_vmem()] * 3,
        (in_vmem(), in_vmem()),
        (like((2 * rows, shards * hidden), jnp.float32),) * 2,
        [],
        "finish_gu",
        0,
        layer0.size * 14,
        [side, layer0, layer1, received],
    )


def place_tokens_kernel(shards, me_ref, *refs):
    part_refs, out_ref = refs[:-1], refs[-1]
    micros, rows, width = part_refs[0].shape
    columns = width // (2 * shards)
    for number, part in enumerate(part_refs):
        where = pl.ds(pl.multiple_of((me_ref[0] ^ number) * rows, rows), rows)
        for half in range(2):
            for s in range(shards):
                source = (half * shards + s) * columns
                target = (s * 2 + half) * columns
                for m in range(micros):
                    out_ref[m, where, target : target + columns] = part[m, :, source : source + columns]


def place_tokens(me, parts, shards):
    micros, sub, width = parts[0].shape
    shape = (micros, sub * len(parts), width)
    return run(
        functools.partial(place_tokens_kernel, shards),
        (),
        [in_smem()] + [in_vmem()] * len(parts),
        in_vmem(),
        like(shape, parts[0].dtype),
        [],
        "place_tokens",
        0,
        4 * micros * sub * width * len(parts),
        [me] + list(parts),
    )


def join_cols_kernel(part_ref, out_ref):
    out_ref[...] = part_ref[0]


def join_cols(part):
    shards, rows, columns = part.shape
    return run(
        join_cols_kernel,
        (shards,),
        [slab((1, rows, columns), 0)],
        slab((rows, columns), 1),
        like((rows, shards * columns), part.dtype),
        [],
        "join_cols",
        0,
        part.size * 4,
        [part],
    )


def split_cols_kernel(whole_ref, out_ref):
    out_ref[0] = whole_ref[...]


def split_cols(whole, shards):
    rows, width = whole.shape
    columns = width // shards
    return run(
        split_cols_kernel,
        (shards,),
        [slab((rows, columns), 1)],
        slab((1, rows, columns), 0),
        like((shards, rows, columns), whole.dtype),
        [],
        "split_cols",
        0,
        whole.size * 4,
        [whole],
    )


def halves(value, axis):
    step = 1
    while step < lax.axis_size(axis):
        value = value + swapped(value, axis, step.bit_length() - 1)
        step *= 2
    return value


def by_partner(value, axis):
    size = lax.axis_size(axis)
    return [value] + [
        lax.ppermute(value, axis, [(i, i ^ k) for i in range(size)]) for k in range(1, size)
    ]


def in_order(parts, axis):
    position = lax.axis_index(axis)
    parts = list(parts)
    step = 1
    while step < len(parts):
        odd = (position & step) != 0
        parts = [jnp.where(odd, parts[i ^ step], parts[i]) for i in range(len(parts))]
        step *= 2
    return parts


def gathered(value, axis):
    return jnp.concatenate(in_order(by_partner(value, axis), axis), axis=0)


def swap_pieces(pieces, axis):
    size = lax.axis_size(axis)
    return [pieces[0]] + [
        lax.ppermute(pieces[n], axis, [(i, i ^ n) for i in range(size)]) for n in range(1, size)
    ]


def for_partners(parts, me):
    return [lax.dynamic_index_in_dim(parts, me[0] ^ n, 0, False) for n in range(parts.shape[0])]


def exchange(pieces):
    return by_partner(sum_pieces(swap_pieces(pieces, SEQ)), SEQ)


def pick(flag, when, otherwise):
    return jnp.where(flag, when, otherwise)


def both_layers(local, axis):
    core = lax.axis_index(SECTION)
    half = local.shape[axis] // 2
    own = lax.dynamic_slice_in_dim(local, core * half, half, axis)
    received = partner(lax.dynamic_slice_in_dim(local, (1 - core) * half, half, axis))
    first = core == 0
    return pick(first, own, received), pick(first, received, own)


def move_rows(part):
    return lax.all_to_all(part, SEQ, 0, 0).reshape(-1, part.shape[2])


def move_cols(part):
    return join_cols(lax.all_to_all(part, SEQ, 0, 0))


def spread_rows(part):
    full = lax.all_gather(part, (HEAD, SECTION), axis=0, tiled=True)
    return full.reshape(lax.axis_size(HEAD), -1, part.shape[1])


def spread_cols(part):
    full = lax.all_gather(part, (SECTION, HEAD), axis=0, tiled=True)
    return full.reshape(2, lax.axis_size(HEAD), -1, part.shape[1])


def reduce_rows(grad):
    return lax.psum_scatter(
        grad.reshape(-1, grad.shape[2]), (HEAD, SECTION), scatter_dimension=0, tiled=True
    )


def reduce_cols(grad):
    return lax.psum_scatter(
        grad.reshape(-1, grad.shape[2]), (SECTION, HEAD), scatter_dimension=0, tiled=True
    )


def reduce_halves(grad):
    return lax.psum_scatter(grad, HEAD, scatter_dimension=0, tiled=True)


def with_other(value):
    return value, partner(value)


def collect_rows(part):
    shards = lax.axis_size(SEQ)
    return lax.all_to_all(part.reshape(shards, -1, part.shape[1]), SEQ, 0, 0)


def collect_cols(part):
    return lax.all_to_all(split_cols(part, lax.axis_size(SEQ)), SEQ, 0, 0)


def after(value, other):
    return lax.optimization_barrier((value, other))[0]


def layer_backward_fast(me, piece, upstream, saved, gains, weights, small, aux, parts, plan, pairs):
    at_mid, sum_rows, start, at_end, at_out, sum_cols, before_end, last_due = plan
    attn_gain, mlp_gain = gains
    w_proj, w_mix, w_cols, w_gu = weights
    taps, scal, norm_weight = small
    resid, normed, gate_pre, mixer, mid, ffn_in, gate_up, hidden = saved
    xh, states, inverse, mixed, gated = mixer
    shards = parts[0]
    slices, rows, _ = mixed.shape
    grad_gate_up, pieces = feed_back(me, upstream, gate_up, w_gu, w_cols, shards)
    grad_gu = grad_rows(ffn_in, grad_gate_up)
    pieces = swap_pieces(pieces, SEQ)
    pieces, _ = lax.optimization_barrier((pieces, grad_gu))
    sums = at_mid(by_partner(sum_pieces(pieces), SEQ))
    grad_mid, grad_attn, dmlp, dmixed, dgate, dnorm = mid_back(
        me, mlp_gain, sums, mid, upstream, w_cols, mixed, gate_pre, norm_weight
    )
    if pairs is None:
        grad_both = grad_cols(hidden, upstream, gated, grad_attn, slices)
    else:
        grad_both = pair_cols(
            pairs[0], pairs[2], with_other(upstream), pairs[1], with_other(grad_attn), slices
        )
    grad_head = swap_pieces(for_partners(dmixed, piece), HEAD)
    grad_head, grad_both = lax.optimization_barrier((grad_head, grad_both))
    sum_gu = sum_rows(grad_gu, dmixed)
    running = start(grad_head, sum_gu)
    dxh, dtaps, dscal = recur_backward(piece, xh, grad_head, aux, taps, scal, states, inverse, parts)
    dxh, running = at_end(dxh, running, sum_gu)
    packed = swap_pieces(dxh, HEAD)
    grad_pre, pieces, dmix = project_back(me, piece, packed, dgate, w_proj, w_mix, normed, shards)
    pieces, running = at_out(pieces, running)
    grad_proj = grad_rows(normed, grad_pre)
    pieces = swap_pieces(pieces, SEQ)
    pieces, _ = lax.optimization_barrier((pieces, grad_proj))
    sums, sum_both = sum_cols(grad_both, (sum_gu, dxh), grad_pre, pieces)
    sums, running = lax.optimization_barrier((sums, running))
    sums = before_end(sums)
    grad_resid, dattn = norm_back(me, attn_gain, sums, resid, grad_mid)
    sum_proj = reduce_rows(after(grad_proj, last_due(sum_both, sums, sum_gu, grad_resid)))
    small_grads = (dtaps[:CONVK], dscal[0, :2], dnorm[0], dattn[0], dmlp[0], dmix[:, :2])
    return grad_resid, (sum_proj, sum_gu, sum_both), small_grads, running


def fast_shards(
    tokens,
    cotangent,
    doc_starts,
    valid_mask,
    gain_attn,
    w_query,
    w_key,
    w_value,
    w_gate_out,
    w_decay,
    w_beta,
    conv_query,
    conv_key,
    conv_value,
    decay_log,
    decay_bias,
    out_norm,
    w_output,
    gain_mlp,
    w_gate,
    w_up,
    w_down,
):
    core = lax.axis_index(SECTION)
    first = core == 0
    shard = lax.axis_index(SEQ)
    piece = lax.axis_index(HEAD)
    shards, slices = lax.axis_size(SEQ), lax.axis_size(HEAD)
    parts = (shards, slices)
    shard_rows = w_query.shape[1]
    model_width = tokens.shape[2]
    sub = tokens.shape[1] // slices
    length = tokens.shape[1] * shards
    hidden_width = w_gate.shape[2] // shards
    hidden_padded = -(-hidden_width // 128) * 128

    def columns(value, width):
        return jnp.stack([value[:, s * width : (s + 1) * width] for s in range(shards)])

    def halved(value):
        shape = value.shape[:-1]
        value = value.reshape(shape + (shards, 2, model_width // (2 * shards)))
        return jnp.swapaxes(value, -3, -2).reshape(shape + (model_width,))

    proj_local = jnp.concatenate(
        [
            columns(w_query[0], HEAD_K),
            columns(w_key[0], HEAD_K),
            columns(w_value[0], HEAD_V),
            columns(w_gate_out[0], HEAD_V),
        ],
        axis=2,
    )
    fill = ((0, 0), (0, 0), (0, hidden_padded - hidden_width))
    gu_local = jnp.concatenate(
        [jnp.pad(columns(w_gate[0], hidden_width), fill), jnp.pad(columns(w_up[0], hidden_width), fill)],
        axis=2,
    )
    cols_local = jnp.concatenate(
        [
            w_output[0].reshape(shards, HEAD_V, shard_rows),
            w_down[0].reshape(shards, hidden_width, shard_rows),
            jnp.zeros((shards, hidden_padded - hidden_width, shard_rows), jnp.bfloat16),
        ],
        axis=1,
    )
    proj_parts = both_layers(proj_local, 1)
    cols_parts = both_layers(cols_local, 2)
    gu_parts = both_layers(gu_local, 1)

    conv = jnp.concatenate(
        [
            columns(conv_query[0], HEAD_K),
            columns(conv_key[0], HEAD_K),
            columns(conv_value[0], HEAD_V),
        ],
        axis=2,
    )
    taps_own = lax.dynamic_index_in_dim(conv, shard, 0, False).astype(jnp.float32)
    small_own = jnp.concatenate(
        [
            taps_own.reshape(-1),
            jnp.stack([decay_log[0, shard], decay_bias[0, shard]]),
            out_norm[0].astype(jnp.float32),
            gain_attn[0].astype(jnp.float32),
            gain_mlp[0].astype(jnp.float32),
            w_decay[0].astype(jnp.float32).T.reshape(-1),
            w_beta[0].astype(jnp.float32).T.reshape(-1),
        ]
    )
    small_own = after(small_own, proj_parts[0])
    small_other = partner(small_own)
    small_layers = (pick(first, small_own, small_other), pick(first, small_other, small_own))
    taps_size = CONVK * WIDTH
    norm_at = taps_size + 2
    gain_at = norm_at + HEAD_V
    wide = jnp.stack([vector[gain_at:] for vector in small_layers])
    wide = jnp.concatenate([wide.reshape(-1), valid_mask[core].astype(jnp.float32)])
    wide = gathered(wide[None], SEQ)
    valid_all = wide[:, wide.shape[1] - tokens.shape[1] :].reshape(shards, slices, sub)
    valid = lax.dynamic_index_in_dim(valid_all, piece, 1, False).reshape(-1)
    wide = wide[:, : wide.shape[1] - tokens.shape[1]].reshape(shards, 2, 2 + 2 * shards, 2, shard_rows // 2)
    gains_all = jnp.transpose(wide[:, :, :2], (1, 2, 3, 0, 4)).reshape(2, 2, model_width)
    mix_all = wide[:, :, 2:].reshape(shards, 2, 2, shards, 2, shard_rows // 2)
    mix_all = lax.dynamic_index_in_dim(mix_all, shard, 3, False)
    mix_all = jnp.transpose(mix_all, (1, 2, 3, 0, 4)).reshape(2, 2, model_width).astype(jnp.bfloat16)
    mix_all = gathered(mix_all[None], HEAD)
    mix_all = jnp.swapaxes(mix_all, 0, 1)
    mix_all = jnp.concatenate(
        [mix_all, mix_all, jnp.zeros((2, slices, 12, model_width), jnp.bfloat16)], axis=2
    )
    small = []
    gains = []
    weights = []
    for layer in range(2):
        vector = small_layers[layer]
        taps = jnp.pad(vector[:taps_size].reshape(CONVK, WIDTH), ((0, 8 - CONVK), (0, 0)))
        scal = jnp.pad(vector[taps_size:norm_at][None], ((0, 7), (0, 126)))
        small.append((taps, scal, vector[None, norm_at:gain_at]))
        gains.append((gains_all[layer, 0][None], gains_all[layer, 1][None]))

    def my_tokens(value):
        mine = lax.dynamic_slice_in_dim(value, piece * sub, sub, 0)
        return by_partner(halved(mine), SEQ)

    side = core[None].astype(jnp.int32)
    me = shard[None].astype(jnp.int32)
    place_at = piece[None].astype(jnp.int32)
    valid = valid[:, None]
    aux = make_aux(doc_starts[core], length)
    masked = cotangent[core] * valid_mask[core].astype(jnp.bfloat16)[:, None]

    token_parts, base = my_tokens(tokens[core]), None
    proj0 = after(move_rows(proj_parts[0]), (small_layers, cols_parts, gu_parts))
    cols0 = lax.all_to_all(after(cols_parts[0], proj0), SEQ, 0, 0)
    cols0 = join_cols(after(cols0, (token_parts, gains, small, valid, mix_all)))
    gu0 = move_rows(after(gu_parts[0], cols0))
    weights = [(spread_rows(proj0), mix_all[0], spread_cols(cols0), None)]

    saved = []
    stats = []
    for layer in range(2):
        w_proj, w_mix, w_cols, w_gu = weights[layer]
        attn_gain, mlp_gain = gains[layer]
        resid, normed, packed, gate_pre, stat = project(
            me, valid, attn_gain, token_parts, base, w_proj, w_mix
        )
        stats.append(stat)
        xh = swap_pieces(for_partners(packed, place_at), HEAD)
        if layer == 0:
            xh, gu0 = lax.optimization_barrier((xh, gu0))
            w_gu = spread_rows(gu0)
            weights[0] = (w_proj, w_mix, w_cols, w_gu)
            proj1 = move_rows(after(proj_parts[1], gu0))
            cols1 = move_cols(after(cols_parts[1], proj1))
        mixed, states, inverse = recur_forward(place_at, xh, aux, *small[layer][:2], parts)
        mixed = swap_pieces(mixed, HEAD)
        if layer == 0:
            mixed, proj1, cols1 = lax.optimization_barrier((mixed, proj1, cols1))
        else:
            mixed, gu1, masked = lax.optimization_barrier((mixed, gu1, masked))
            w_gu = spread_rows(gu1)
            weights[1] = (w_proj, w_mix, w_cols, w_gu)
        gated, kept, pieces = output(me, place_at, mixed, gate_pre, small[layer][2], w_cols, shards)
        mixer = (xh, states, inverse, kept, gated)
        mix_parts = exchange(pieces)
        base, ffn_in, gate_up, hidden, pieces, stat = feed(
            me, valid, mlp_gain, mix_parts, resid, w_gu, w_cols
        )
        stats.append(stat)
        saved.append((resid, normed, gate_pre, mixer, base, ffn_in, gate_up, hidden))
        if layer == 0:
            pairs = (side, with_other(gated), with_other(hidden))
        if layer == 0:
            token_parts = exchange(pieces)
            gu1 = move_rows(after(gu_parts[1], token_parts))
            masked = my_tokens(after(masked, token_parts))
            weights.append((spread_rows(proj1), mix_all[1], spread_cols(cols1), None))
    h1 = saved[1][0]
    stats0 = jnp.stack([stats[2][0, 0], stats[1][0, 0], stats[2][0, 1]]) / shards
    upstream = place(me, masked)
    def placed_tokens(layer0, layer1):
        layer0, layer1 = (
            value if value.shape[0] == sub else lax.dynamic_slice_in_dim(value, shard * sub, sub, 0)
            for value in (layer0, layer1)
        )
        keep = pick(first, layer0, layer1)
        received = partner(pick(first, layer1, layer0))
        both = jnp.stack([pick(first, keep, received), pick(first, received, keep)])
        return place_tokens(piece[None].astype(jnp.int32), by_partner(both, HEAD), shards)

    early = {}

    def all_sums(pieces):
        return by_partner(sum_pieces(pieces), SEQ)

    def plan_last():
        def at_mid(sums):
            return sums

        def sum_rows(grad_gu, anchor):
            return reduce_rows(grad_gu)

        def start(anchor, sum_gu):
            return swap_pieces(after(pieces, anchor), SEQ)

        def at_end(dxh, running, sum_gu):
            dxh, running = lax.optimization_barrier((dxh, running))
            return dxh, (running, collect_rows(after(sum_gu, dxh)))

        def at_out(pieces, running):
            return lax.optimization_barrier((pieces, running))

        def sum_cols(grad_both, due, grad_pre, pieces):
            sum_both = reduce_cols(after(grad_both, due))
            return lax.optimization_barrier((all_sums(pieces), sum_both))

        def before_end(sums):
            return sums

        def last_due(sum_both, sums, sum_gu, grad_resid):
            return sum_both, sums

        return at_mid, sum_rows, start, at_end, at_out, sum_cols, before_end, last_due

    grad_h1, big1, small1, (last_sum, moved_gu1) = layer_backward_fast(
        me, place_at, upstream, saved[1], gains[1], weights[1], small[1], aux, parts, plan_last(), None
    )
    sum_proj1, sum_gu1, sum_both1 = big1
    last_sum = sum_pieces(last_sum)
    moved_both1 = collect_cols(after(sum_both1, grad_h1))
    here = shard * sub
    valid_here = lax.dynamic_slice_in_dim(valid, here, sub, 0)
    act1, stat = close(valid_here, last_sum, lax.dynamic_slice_in_dim(base, here, sub, 0))
    stats1 = jnp.stack([stat[0, 0], stats[3][0, 0] / shards, stat[0, 1]])
    activations = placed_tokens(h1, act1)

    def plan_first():
        def at_mid(sums):
            sums, early["both"] = lax.optimization_barrier((sums, moved_both1))
            return sums

        def sum_rows(grad_gu, anchor):
            return reduce_rows(after(grad_gu, (sum_proj1, anchor)))

        def start(anchor, sum_gu):
            return collect_rows(after(sum_proj1, anchor))

        def at_end(dxh, running, sum_gu):
            return lax.optimization_barrier((dxh, running))

        def at_out(pieces, running):
            return pieces, running

        def sum_cols(grad_both, due, grad_pre, pieces):
            sum_both = reduce_halves(after(grad_both, (due, grad_pre)))
            return all_sums(pieces), sum_both

        def before_end(sums):
            return sums

        def last_due(sum_both, sums, sum_gu, grad_resid):
            early["gu"] = collect_rows(after(sum_gu, grad_resid))
            early["grads"] = placed_tokens(grad_resid, grad_h1)
            return sum_both, early["gu"], early["grads"]

        return at_mid, sum_rows, start, at_end, at_out, sum_cols, before_end, last_due

    grad_tokens, big0, small0, moved_proj1 = layer_backward_fast(
        me, place_at, grad_h1, saved[0], gains[0], weights[0], small[0], aux, parts, plan_first(), pairs
    )
    sum_proj0, sum_gu0, sum_both0 = big0
    moved_both1 = early["both"]
    moved_gu0 = early["gu"]
    moved_both0 = collect_cols(after(sum_both0, moved_gu0))
    input_grads = early["grads"]
    grad_down, grad_out = finish_cols(
        side, moved_both0, moved_both1, partner(pick(first, moved_both1, moved_both0)), hidden_width
    )
    grad_gate, grad_up = finish_gu(
        side, moved_gu0, moved_gu1, partner(pick(first, moved_gu1, moved_gu0)), hidden_width
    )

    def pack(grads, sums):
        dtaps, dscal, dnorm, dattn, dmlp, dmix = grads
        place = (jnp.arange(2) == core)[:, None]
        marked = jnp.where(place, jnp.concatenate([sums, (jnp.sum(valid) / shards)[None]])[None], 0.0)
        return jnp.concatenate(
            [dtaps.reshape(-1), dscal, dnorm, marked.reshape(-1), dattn, dmlp, dmix.reshape(-1)]
        )

    packs = (pack(small0, stats0), pack(small1, stats1))
    vector = pick(first, packs[0], packs[1]) + partner(pick(first, packs[1], packs[0]))
    gain_end = norm_at + HEAD_V + 8 + 2 * model_width
    per_head = gathered(vector[None, :norm_at], SEQ)
    sums_all = halves(vector[norm_at:gain_end], HEAD)
    norm_sum = halves(sums_all[: HEAD_V + 8], SEQ)
    stat_sums = norm_sum[HEAD_V:].reshape(2, 4)
    norm_sum = norm_sum[:HEAD_V]
    gain_sums = sums_all[HEAD_V + 8 :].reshape(2, 2, shards, shard_rows // 2)
    gain_sums = lax.dynamic_index_in_dim(gain_sums, shard, 2, False).reshape(2, shard_rows)
    branch_rms = jnp.sqrt(stat_sums[:, :3] / jnp.maximum(stat_sums[:, 3:], 1.0))
    mix_grad = vector[gain_end:].reshape(slices, 2, 2, shards, shard_rows // 2)
    mix_grad = jnp.sum(lax.all_to_all(mix_grad, HEAD, 0, 0), axis=0)
    mix_grad = lax.all_to_all(jnp.transpose(mix_grad, (2, 0, 1, 3)), SEQ, 0, 0)
    mix_grad = jnp.transpose(mix_grad, (1, 2, 3, 0)).reshape(2, shard_rows, shards)
    received_proj1 = partner(moved_proj1)
    others = (input_grads, grad_down, grad_out, grad_gate, grad_up, mix_grad, norm_sum, gain_sums)
    sum_proj0, others, per_head, received_proj1 = lax.optimization_barrier(
        (sum_proj0, others, per_head, received_proj1)
    )
    input_grads, grad_down, grad_out, grad_gate, grad_up, mix_grad, norm_sum, gain_sums = others
    moved_proj0 = collect_rows(sum_proj0)
    grad_proj = finish_rows(
        side, moved_proj0, moved_proj1, partner(moved_proj0), received_proj1,
        (HEAD_K, HEAD_K, HEAD_V, HEAD_V),
    )
    conv_grad = jnp.swapaxes(per_head[:, :taps_size].reshape(shards, CONVK, WIDTH), 0, 1)

    def conv_part(start, width):
        return conv_grad[:, :, start : start + width].reshape(1, CONVK, shards * width)

    return (
        activations[None],
        input_grads[None],
        branch_rms[None],
        gain_sums[0][None],
        grad_proj[0][None],
        grad_proj[1][None],
        grad_proj[2][None],
        grad_proj[3][None],
        mix_grad[0][None],
        mix_grad[1][None],
        conv_part(0, HEAD_K),
        conv_part(HEAD_K, HEAD_K),
        conv_part(2 * HEAD_K, HEAD_V),
        per_head[:, taps_size][None],
        per_head[:, taps_size + 1][None],
        norm_sum[None],
        grad_out[None],
        gain_sums[1][None],
        grad_gate[None],
        grad_up[None],
        grad_down[None],
    )


def per_device(*args):
    tokens, w_decay = args[0], args[9]
    rows = tokens.shape[1]
    seq, head, section = (lax.axis_size(axis) for axis in (SEQ, HEAD, SECTION))
    one_head_each = w_decay.shape[2] == seq
    micro_each = tokens.shape[0] == section == 2
    powers = seq & (seq - 1) == 0 and head & (head - 1) == 0
    even = rows % (head * BLOCK) == 0 and rows * seq % (BLOCK * GROUP) == 0
    if one_head_each and micro_each and powers and even:
        return fast_shards(*args)
    return shards(*args)


def solution(mesh):
    placed = (
        P(None, SEQ, None),
        P(None, SEQ, None),
        P(),
        P(None, SEQ),
        P(SECTION, SEQ),
        P(SECTION, SEQ, HEAD),
        P(SECTION, SEQ, HEAD),
        P(SECTION, SEQ, HEAD),
        P(SECTION, SEQ, HEAD),
        P(SECTION, SEQ, HEAD),
        P(SECTION, SEQ, HEAD),
        P(SECTION, None, HEAD),
        P(SECTION, None, HEAD),
        P(SECTION, None, HEAD),
        P(SECTION, HEAD),
        P(SECTION, HEAD),
        P(SECTION, None),
        P(SECTION, HEAD, SEQ),
        P(SECTION, SEQ),
        P(SECTION, SEQ, HEAD),
        P(SECTION, SEQ, HEAD),
        P(SECTION, HEAD, SEQ),
    )
    return jax.shard_map(
        per_device,
        mesh=mesh,
        in_specs=placed,
        out_specs=(
            P(SECTION, None, SEQ, None),
            P(SECTION, None, SEQ, None),
            P(SECTION, None, None),
            P(SECTION, SEQ),
            P(SECTION, SEQ, HEAD),
            P(SECTION, SEQ, HEAD),
            P(SECTION, SEQ, HEAD),
            P(SECTION, SEQ, HEAD),
            P(SECTION, SEQ, HEAD),
            P(SECTION, SEQ, HEAD),
            P(SECTION, None, HEAD),
            P(SECTION, None, HEAD),
            P(SECTION, None, HEAD),
            P(SECTION, HEAD),
            P(SECTION, HEAD),
            P(SECTION, None),
            P(SECTION, HEAD, SEQ),
            P(SECTION, SEQ),
            P(SECTION, SEQ, HEAD),
            P(SECTION, SEQ, HEAD),
            P(SECTION, HEAD, SEQ),
        ),
        check_vma=False,
    )
```
